32 devices in a mesh: section: 2 (over y), dp: 2 (over core), expert: 4 (over z), tensor: 2 (over x).
Axes of the slice: x: 2, y: 2, z: 4, core: 2. Of those that a mesh axis runs over, the one named last changes fastest.
Arguments:
- boundary: bfloat16 [2, 2, 4096, 1536], P('section', None, ('dp', 'expert')), may hold values from -6 to 6
- segments: int32 [2, 4096], P(None, ('dp', 'expert')), may hold values from 0 to 19, never falling along the last dimension, each value on 1 to 800 neighbouring positions
- expert_ids: int32 [2, 2, 4096, 8], P('section', None, ('dp', 'expert', 'tensor')), may hold values from 0 to 31, all different within a row; in each aligned block of 256 rows (0 to 255, 256 to 511, ..., all dimensions but the last counted through in order) at most 96 rows name the same one
- attn_gain: float32 [2, 1536], P('section'), may hold values from 0.5 to 1.5
- query_weight: bfloat16 [2, 1536, 1536], P('section', None, 'tensor'), may hold values from -0.15625 to 0.15625
- key_weight: bfloat16 [2, 1536, 512], P('section', None, 'tensor'), may hold values from -0.15625 to 0.15625
- value_weight: bfloat16 [2, 1536, 512], P('section', None, 'tensor'), may hold values from -0.15625 to 0.15625
- out_weight: bfloat16 [2, 1536, 1536], P('section', 'tensor'), may hold values from -0.625 to 0.625
- ffn_gain: float32 [2, 1536], P('section'), may hold values from 0.5 to 1.5
- router_weight: bfloat16 [2, 1536, 32], P('section'), may hold values from -0.078125 to 0.078125
- gate_weight: bfloat16 [2, 32, 1536, 512], P('section', ('expert', 'tensor')), may hold values from -0.15625 to 0.15625
- up_weight: bfloat16 [2, 32, 1536, 512], P('section', ('expert', 'tensor')), may hold values from -0.15625 to 0.15625
- down_weight: bfloat16 [2, 32, 512, 1536], P('section', ('expert', 'tensor')), may hold values from -0.75 to 0.75
Outputs:
- ends_out: bfloat16 [2, 2, 4096, 1536], P('section', None, ('dp', 'expert'))
- attn_gain_grad: float32 [2, 1536], P('section')
- query_grad: float32 [2, 1536, 1536], P('section', None, 'tensor')
- key_grad: float32 [2, 1536, 512], P('section', None, 'tensor')
- value_grad: float32 [2, 1536, 512], P('section', None, 'tensor')
- out_grad: float32 [2, 1536, 1536], P('section', 'tensor')
- ffn_gain_grad: float32 [2, 1536], P('section')
- router_grad: float32 [2, 1536, 32], P('section')
- gate_grad: float32 [2, 32, 1536, 512], P('section', ('expert', 'tensor'))
- up_grad: float32 [2, 32, 1536, 512], P('section', ('expert', 'tensor'))
- down_grad: float32 [2, 32, 512, 1536], P('section', ('expert', 'tensor'))
The draws below stay inside these ranges and needn't reach their ends.
Inputs may be any that keep to these rules, and one draw needn't show every extreme that they name: `expert_ids`: in each aligned block of 256 rows (one device's tokens of one layer and micro-batch), no expert is named by more than 96 rows, a bound that some block reaches; the 8 experts of a row differ. `segments`: document numbers never fall along a row; a document holds 1 to 800 positions, some exactly 800.
All inputs are finite; a program needn't handle non-finite values.
Results may differ from the reference program's by a relative error of at most 0.03.
Values may be sent and summed in bfloat16 or wider, within the bound.
A program may use at most 448 MiB of HBM per device.

```python
import math
import jax
import jax.numpy as jnp
import numpy as np
from jax import lax

D = 1536
HQ = 24
HK = 8
HD = 64
FF = 512
TOPK = 8
EXPERTS = 32
LEN = 256
MB = 2
DOC_MOST = 800
LAYERS = 2
TOKENS = 4096
SHARE = 256
CAP = 96
DOCS = 20


def steps_of(rng, shape, shards, low, largest):
    gain, own = 1.0, jax.random.fold_in(rng, 6)
    for dim, shards_of in shards:
        steps = jnp.exp(jax.random.uniform(jax.random.fold_in(own, dim), (shards_of,), jnp.float32, low / len(shards), largest / len(shards)))
        gain = gain * jnp.repeat(steps, shape[dim] // shards_of).reshape([-1 if axis == dim else 1 for axis in range(len(shape))])
    return gain


def length_profile(number_of, total, limit, slope):
    weights = [(1 << 20) // math.isqrt(standing ** slope) + 1 for standing in range(2, number_of + 1)]
    surplus, holding = total - limit - (number_of - 1), [1] * (number_of - 1)
    while surplus > 0:
        free = [i for i in range(number_of - 1) if holding[i] < limit]
        mass, budget = sum([weights[i] for i in free]), surplus
        for i in free:
            addition = min(limit - holding[i], max(1, budget * weights[i] // mass), surplus)
            holding[i] = holding[i] + addition
            surplus = surplus - addition
    return np.array([limit] + holding)


def uneven(key, number_of, total, bound, skew):
    if number_of == 2:
        one = jax.random.randint(key, (), max(1, total - bound), min(bound, total - 1) + 1)
        return jnp.stack([one, total - one])
    sizes = jnp.asarray(length_profile(number_of, total, bound, skew), jnp.int32)
    couples = (number_of - 1) // 2
    donor, receiver = sizes[1:1 + 2 * couples:2], sizes[2:2 + 2 * couples:2]
    margin = jnp.minimum(donor - 1, bound - receiver)
    shifted = jax.random.randint(jax.random.fold_in(key, 1), (couples,), 0, 1 << 20) % (margin + 1)
    sizes = sizes.at[1:1 + 2 * couples:2].set(donor - shifted).at[2:2 + 2 * couples:2].set(receiver + shifted)
    return sizes[jax.random.permutation(jax.random.fold_in(key, 2), number_of)]


def routed_block(stream_key, own, number, rows, count, top, reach, lean):
    sequence = jax.random.permutation(stream_key, count)
    packed, ordinary = load_shares(count, rows * top, reach, lean, True), load_shares(count, rows * top, reach, lean, False)
    places = jnp.arange(count)

    def named(lengths, rotation):
        used = int((lengths > 0).sum())
        fixed = max(1, used // 4)
        shifted = fixed + (places - fixed + rotation * (used - fixed)) % max(1, count - fixed)
        return jnp.zeros((count,), jnp.int32).at[sequence[jnp.where(places < fixed, places, shifted)]].set(jnp.asarray(lengths, jnp.int32))

    lengths = jnp.where(number % 4 == 0, named(packed, number // 4), named(ordinary, number - number // 4 - 1))
    mixed = jax.random.permutation(jax.random.fold_in(own, 3), count)
    source_of, sink = mixed[0:count // 2 * 2:2], mixed[1:count // 2 * 2:2]
    slack = jnp.minimum(lengths[source_of] - 1, reach - lengths[sink]) // 2
    slack = jnp.where((source_of == sequence[0]) | (sink == sequence[0]) | (lengths[sink] == 0), 0, jnp.maximum(slack, 0))
    shifted = jax.random.randint(jax.random.fold_in(own, 4), (count // 2,), 0, 1 << 20) % (slack + 1)
    lengths = lengths.at[source_of].add(-shifted).at[sink].add(shifted)
    labels = jnp.searchsorted(jnp.cumsum(lengths), jnp.arange(rows * top), side="right").astype(jnp.int32)
    listing = labels.reshape(top, rows).T
    listing = listing[jax.random.permutation(jax.random.fold_in(own, 1), rows)]
    rotation = jax.random.randint(jax.random.fold_in(own, 2), (rows, 1), 0, top)
    return jnp.take_along_axis(listing, (jnp.arange(top)[None, :] + rotation) % top, axis=1)


def load_shares(amount, total, most, slope, full):
    weights = [(1 << 20) // math.isqrt(standing ** slope) + 1 for standing in range(1, amount + 1)]
    largest = most if full else min(most, max(-(-total // amount), total * weights[0] // sum(weights)))
    least = 1 if total - largest >= amount - 1 else 0
    holding, spare = [largest] + [least] * (amount - 1), total - largest - least * (amount - 1)
    while spare > 0:
        candidates = [i for i in range(1, amount) if holding[i] < largest] or [i for i in range(1, amount) if holding[i] < most]
        whole, left = sum([weights[i] for i in candidates]), spare
        for i in candidates:
            more = min(most - holding[i], max(1, left * weights[i] // whole), spare)
            holding[i] = holding[i] + more
            spare = spare - more
    return np.array(holding)


def centred(own_key, extent, spread, bound, pieces=(), kind=jnp.bfloat16):
    array = spread * jax.random.normal(own_key, extent, jnp.float32)
    if pieces:
        array = array * steps_of(own_key, extent, pieces, -0.22, 0.18)
    return jnp.clip(array, -bound, bound).astype(kind)


def setup_inputs(seed: int = 0) -> dict:
    seeds = jax.random.split(jax.random.key(seed), 14)
    boundary = centred(seeds[0], (2, MB, TOKENS, D), 1.0, 6.0, ((0, 2), (2, 8)))
    segments = jax.vmap(lambda own: jnp.searchsorted(jnp.cumsum(uneven(own, DOCS, TOKENS, DOC_MOST, 1)), jnp.arange(TOKENS), side="right"))(jax.random.split(seeds[1], MB)).reshape((MB, TOKENS)).astype(jnp.int32)
    expert_ids_keys = jax.random.split(jax.random.fold_in(seeds[2], 1), LAYERS * MB * TOKENS // SHARE)
    expert_ids_turns = jax.random.permutation(jax.random.fold_in(seeds[2], 3), LAYERS * MB * TOKENS // SHARE)
    expert_ids = jax.vmap(lambda own, number: routed_block(jax.random.fold_in(seeds[2], 2), own, number, SHARE, EXPERTS, TOPK, CAP, 2))(expert_ids_keys, expert_ids_turns).reshape((LAYERS, MB, TOKENS, TOPK))
    attn_gain = jnp.clip(1.0 + 0.1 * jax.random.normal(seeds[3], (LAYERS, D), jnp.float32), 0.5, 1.5)
    query_weight = centred(seeds[4], (LAYERS, D, HQ * HD), D ** -0.5, 0.15625, ((0, 2), (2, 2)))
    key_weight = centred(seeds[5], (LAYERS, D, HK * HD), D ** -0.5, 0.15625, ((0, 2), (2, 2)))
    value_weight = centred(seeds[6], (LAYERS, D, HK * HD), D ** -0.5, 0.15625, ((0, 2), (2, 2)))
    out_weight = centred(seeds[7], (LAYERS, HQ * HD, D), (HQ * HD // 16) ** -0.5, 0.625, ((0, 2), (1, 2)))
    ffn_gain = jnp.clip(1.0 + 0.1 * jax.random.normal(seeds[8], (LAYERS, D), jnp.float32), 0.5, 1.5)
    router_weight = centred(seeds[9], (LAYERS, D, EXPERTS), (4 * D) ** -0.5, 0.078125, ((0, 2),))
    gate_weight = centred(seeds[10], (LAYERS, EXPERTS, D, FF), D ** -0.5, 0.15625, ((0, 2), (1, 8)))
    up_weight = centred(seeds[11], (LAYERS, EXPERTS, D, FF), D ** -0.5, 0.15625, ((0, 2), (1, 8)))
    down_weight = centred(seeds[12], (LAYERS, EXPERTS, FF, D), (FF // 8) ** -0.5, 0.75, ((0, 2), (1, 8)))
    return {"boundary": boundary, "segments": segments, "expert_ids": expert_ids, "attn_gain": attn_gain, "query_weight": query_weight, "key_weight": key_weight, "value_weight": value_weight, "out_weight": out_weight, "ffn_gain": ffn_gain, "router_weight": router_weight, "gate_weight": gate_weight, "up_weight": up_weight, "down_weight": down_weight}


@jax.custom_vjp
def low(v):
    return lax.optimization_barrier(v.astype(jnp.bfloat16)).astype(jnp.float32)

@jax.custom_vjp
def low_back(v):
    return v

def low_keep(v):
    return (low(v), None)

def low_pass(kept, grad):
    return (grad,)

def back_keep(v):
    return (v, None)

def back_low(kept, grad):
    return (low(grad),)
low.defvjp(low_keep, low_pass)
low_back.defvjp(back_keep, back_low)
EPS = 1e-06
THETA = 10000.0
HIGH = lax.Precision.HIGHEST

def matmul(left_op, right_op):
    return jnp.dot(left_op, right_op, precision=HIGH, preferred_element_type=jnp.float32)

def rms_norm(values, gain_vec):
    return values * lax.rsqrt(lax.optimization_barrier(jnp.mean(values * values, axis=-1, keepdims=True)) + EPS) * gain_vec

def rope_tables(row_count, head_width, length):
    position = (jnp.arange(row_count) % length).astype(jnp.float32)
    frequency = THETA ** (-2.0 * jnp.arange(head_width // 2).astype(jnp.float32) / head_width)
    angles = position[:, None] * frequency[None, :]
    return (jnp.cos(angles), jnp.sin(angles))

def rotate(matrix, cosine_table, sine_table, head_width, direction):
    row_count = matrix.shape[0]
    by_head = matrix.reshape(row_count, -1, head_width)
    half_width = head_width // 2
    first_half = by_head[..., :half_width]
    second_half = by_head[..., half_width:]
    cosine = cosine_table[:, None, :]
    sine_val = sine_table[:, None, :] * direction
    turned = jnp.concatenate([first_half * cosine - second_half * sine_val, second_half * cosine + first_half * sine_val], axis=-1)
    return turned.reshape(row_count, -1)

def attend(bundle):
    query_rot, key_rot, value_rot, seg_row = bundle
    length = query_rot.shape[0]
    query_heads = query_rot.reshape(length, HK, HQ // HK, HD)
    key_heads = key_rot.reshape(length, HK, HD)
    value_heads = value_rot.reshape(length, HK, HD)
    scores = jnp.einsum('qkgd,skd->kgqs', query_heads, key_heads, precision=HIGH) * HD ** (-0.5)
    scores = low_back(scores)
    position = jnp.arange(length)
    allowed = (position[:, None] >= position[None, :]) & (seg_row[:, None] == seg_row[None, :])
    scores = jnp.where(allowed, scores, -1e+30)
    exponent = jnp.exp(scores - lax.optimization_barrier(jnp.max(scores, axis=-1, keepdims=True)))
    probability = low(exponent / lax.optimization_barrier(jnp.sum(exponent, axis=-1, keepdims=True)))
    mixture = jnp.einsum('kgqs,skd->qkgd', probability, value_heads, precision=HIGH)
    return mixture.reshape(length, -1)

def expert_apply(bundle):
    expert_rows, gate_mat, up_mat, down_mat = bundle
    gate_pre = low_back(matmul(expert_rows, gate_mat))
    up_pre = low_back(matmul(expert_rows, up_mat))
    hidden = low(jax.nn.silu(gate_pre) * up_pre)
    return low_back(low(matmul(hidden, down_mat)))

def dispatch_plan(route, token_count):
    block_count = token_count // SHARE
    pair_ids = route.reshape(block_count, SHARE * TOPK)
    onehot = (pair_ids[:, :, None] == jnp.arange(EXPERTS).astype(jnp.int32)[None, None, :]).astype(jnp.int32)
    earlier = jnp.cumsum(onehot, axis=1) - onehot
    slot_pos = lax.optimization_barrier(jnp.sum(earlier * onehot, axis=2)).astype(jnp.int32)
    block_ids = jnp.arange(block_count).astype(jnp.int32)[:, None]
    target = pair_ids * (block_count * CAP) + block_ids * CAP + slot_pos
    source = jnp.zeros((EXPERTS * block_count * CAP,), jnp.int32).at[target.reshape(-1)].set(jnp.arange(token_count * TOPK).astype(jnp.int32) + 1)
    return (target.reshape(token_count, TOPK), source)

def block(hidden_in, seg_all, route, params):
    attn_gain, query_weight, key_weight, value_weight, out_weight, ffn_gain, router_weight, gate_weight, up_weight, down_weight = params
    token_count = hidden_in.shape[0]
    normed = low(rms_norm(hidden_in, attn_gain))
    query_proj = low_back(matmul(normed, query_weight))
    key_proj = low_back(matmul(normed, key_weight))
    value_rot = low(low_back(matmul(normed, value_weight)))
    cosine_table, sine_table = rope_tables(token_count, HD, LEN)
    query_rot = low(rotate(query_proj, cosine_table, sine_table, HD, 1.0))
    key_rot = low(rotate(key_proj, cosine_table, sine_table, HD, 1.0))
    seq_count = token_count // LEN
    attended = lax.map(jax.checkpoint(attend), (query_rot.reshape(seq_count, LEN, -1), key_rot.reshape(seq_count, LEN, -1), value_rot.reshape(seq_count, LEN, -1), seg_all.reshape(seq_count, LEN)))
    attended = low_back(low(attended.reshape(token_count, -1)))
    middle = hidden_in + low_back(matmul(attended, out_weight))
    normed_two = low(rms_norm(middle, ffn_gain))
    logits = low_back(matmul(normed_two, router_weight))
    chosen = jnp.take_along_axis(logits, route, axis=1)
    exponent = jnp.exp(chosen - lax.optimization_barrier(jnp.max(chosen, axis=1, keepdims=True)))
    gates = exponent / lax.optimization_barrier(jnp.sum(exponent, axis=1, keepdims=True))
    slot_index, source = dispatch_plan(route, token_count)
    source_row = jnp.maximum(source - 1, 0) // TOPK
    filled = (source > 0)[:, None]
    gathered = normed_two[source_row]
    buffer = low_back(jnp.where(filled, gathered, jnp.zeros_like(gathered)))
    block_count = token_count // SHARE
    buffer = buffer.reshape(EXPERTS, block_count * CAP, -1)
    expert_out = lax.map(jax.checkpoint(expert_apply), (buffer, gate_weight, up_weight, down_weight))
    flat_out = expert_out.reshape(EXPERTS * block_count * CAP, -1)
    result = middle
    for column in range(TOPK):
        result = result + gates[:, column:column + 1] * flat_out[slot_index[:, column]]
    return result

def reference(boundary, segments, expert_ids, attn_gain, query_weight, key_weight, value_weight, out_weight, ffn_gain, router_weight, gate_weight, up_weight, down_weight):
    weights = tuple((array_in.astype(jnp.float32) for array_in in (attn_gain, query_weight, key_weight, value_weight, out_weight, ffn_gain, router_weight, gate_weight, up_weight, down_weight)))
    inputs = boundary[0].astype(jnp.float32)
    cotangent = boundary[1].astype(jnp.float32)

    def network(start_rows, params):
        finals = []
        for micro_idx in range(MB):
            hidden_state = start_rows[micro_idx]
            for layer_idx in range(LAYERS):
                if layer_idx > 0:
                    hidden_state = low_back(low(hidden_state))
                hidden_state = block(hidden_state, segments[micro_idx], expert_ids[layer_idx, micro_idx], tuple((array_in[layer_idx] for array_in in params)))
            finals.append(hidden_state)
        return jnp.stack(finals)
    outputs, pullback = jax.vjp(network, inputs, weights)
    grad_inputs, grad_weights = pullback(cotangent)
    ends_out = jnp.stack([grad_inputs.astype(jnp.bfloat16), outputs.astype(jnp.bfloat16)])
    return (ends_out, grad_weights[0], grad_weights[1], grad_weights[2], grad_weights[3], grad_weights[4], grad_weights[5], grad_weights[6], grad_weights[7], grad_weights[8], grad_weights[9])
```

```python
import functools

import jax
import jax.numpy as jnp
from jax import lax
from jax.experimental import pallas as pl
from jax.experimental.pallas import tpu as pltpu
from jax.sharding import PartitionSpec as P

SECTION, DP, EXPERT, TENSOR = "section", "dp", "expert", "tensor"
HD = 64
TOPK = 8
EXPERTS = 32
LEN = 256


EPS = 1e-06
THETA = 10000.0
NEG_BIG = -1e30


def shifted(block, axis, distance):
    devices = range(lax.axis_size(axis))
    route = [(i - distance, i) for i in devices if i - distance in devices]
    return lax.ppermute(block, axis, route)


def rms_scale(values):
    return lax.rsqrt(jnp.mean(values * values, axis=-1, keepdims=True) + EPS)


def norm_back(grad_out, values, scale_col, gain_vec):
    weighted = grad_out * gain_vec
    inner_mean = jnp.mean(weighted * values, axis=-1, keepdims=True)
    grad_values = scale_col * weighted - values * (scale_col * scale_col * scale_col) * inner_mean
    grad_gain = jnp.sum(grad_out * values * scale_col, axis=0)
    return (grad_values, grad_gain)


def rope_tables(row_count, head_width, length):
    position = (jnp.arange(row_count) % length).astype(jnp.float32)
    frequency = THETA ** (-2.0 * jnp.arange(head_width // 2).astype(jnp.float32) / head_width)
    angles = position[:, None] * frequency[None, :]
    return (jnp.cos(angles), jnp.sin(angles))


def rotate(matrix, cosine_table, sine_table, head_width, direction):
    row_count = matrix.shape[0]
    by_head = matrix.reshape(row_count, -1, head_width)
    half_width = head_width // 2
    first_half = by_head[..., :half_width]
    second_half = by_head[..., half_width:]
    cosine = cosine_table[:, None, :]
    sine_val = sine_table[:, None, :] * direction
    turned = jnp.concatenate(
        [
            first_half * cosine - second_half * sine_val,
            second_half * cosine + first_half * sine_val,
        ],
        axis=-1,
    )
    return turned.reshape(row_count, -1)


def slot_count(share_rows):
    return share_rows * 3 // 8


def score_block(query_blk, key_blk, seg_row):
    length = query_blk.shape[0]
    kv_heads = key_blk.shape[1] // HD
    query_heads = query_blk.reshape(length, kv_heads, -1, HD)
    key_heads = key_blk.reshape(length, kv_heads, HD)
    scores = jnp.einsum(
        "qkgd,skd->kgqs", query_heads, key_heads, preferred_element_type=jnp.float32
    ) * HD ** (-0.5)
    position = jnp.arange(length)
    allowed = (position[:, None] >= position[None, :]) & (seg_row[:, None] == seg_row[None, :])
    return (jnp.where(allowed, scores, NEG_BIG), query_heads, key_heads)


def attend_forward(bundle):
    query_blk, key_blk, value_blk, seg_row = bundle
    length = query_blk.shape[0]
    scores, query_heads, key_heads = score_block(query_blk, key_blk, seg_row)
    top_score = jnp.max(scores, axis=-1, keepdims=True)
    exponent = jnp.exp(scores - top_score)
    row_total = jnp.sum(exponent, axis=-1, keepdims=True)
    probability = (exponent / row_total).astype(jnp.bfloat16)
    value_heads = value_blk.reshape(length, key_heads.shape[1], HD)
    mixture = jnp.einsum(
        "kgqs,skd->qkgd", probability, value_heads, preferred_element_type=jnp.float32
    )
    return (mixture.astype(jnp.bfloat16).reshape(length, -1), top_score + jnp.log(row_total))


def attend_backward(bundle):
    query_blk, key_blk, value_blk, seg_row, log_total, grad_mix = bundle
    length = query_blk.shape[0]
    scores, query_heads, key_heads = score_block(query_blk, key_blk, seg_row)
    kv_heads = key_heads.shape[1]
    probability = jnp.exp(scores - log_total)
    prob_low = probability.astype(jnp.bfloat16)
    grad_heads = grad_mix.reshape(length, kv_heads, -1, HD)
    value_heads = value_blk.reshape(length, kv_heads, HD)
    grad_value = jnp.einsum(
        "kgqs,qkgd->skd", prob_low, grad_heads, preferred_element_type=jnp.float32
    )
    grad_prob = jnp.einsum(
        "qkgd,skd->kgqs", grad_heads, value_heads, preferred_element_type=jnp.float32
    )
    centre = jnp.sum(probability * grad_prob, axis=-1, keepdims=True)
    grad_scores = (probability * (grad_prob - centre)).astype(jnp.bfloat16)
    grad_query = jnp.einsum(
        "kgqs,skd->qkgd", grad_scores, key_heads, preferred_element_type=jnp.float32
    ) * HD ** (-0.5)
    grad_key = jnp.einsum(
        "kgqs,qkgd->skd", grad_scores, query_heads, preferred_element_type=jnp.float32
    ) * HD ** (-0.5)
    return (
        grad_query.reshape(length, -1),
        grad_key.reshape(length, -1),
        grad_value.reshape(length, -1),
    )


def attention_forward(hidden_in, seg_rows, params):
    attn_gain, query_weight, key_weight, value_weight = params[:4]
    row_count = hidden_in.shape[0]
    scale_one = rms_scale(hidden_in)
    normed = (hidden_in * scale_one * attn_gain).astype(jnp.bfloat16)
    query_proj = jnp.dot(normed, query_weight, preferred_element_type=jnp.float32)
    key_proj = jnp.dot(normed, key_weight, preferred_element_type=jnp.float32)
    value_rot = jnp.dot(normed, value_weight, preferred_element_type=jnp.float32).astype(
        jnp.bfloat16
    )
    cosine_table, sine_table = rope_tables(row_count, HD, LEN)
    query_rot = rotate(query_proj, cosine_table, sine_table, HD, 1.0).astype(jnp.bfloat16)
    key_rot = rotate(key_proj, cosine_table, sine_table, HD, 1.0).astype(jnp.bfloat16)
    seq_count = row_count // LEN
    mixed, log_total = lax.map(
        attend_forward,
        (
            query_rot.reshape(seq_count, LEN, -1),
            key_rot.reshape(seq_count, LEN, -1),
            value_rot.reshape(seq_count, LEN, -1),
            seg_rows.reshape(seq_count, LEN),
        ),
    )
    attended = mixed.reshape(row_count, -1)
    return (
        scale_one,
        normed,
        query_rot,
        key_rot,
        value_rot,
        attended,
        log_total,
        cosine_table,
        sine_table,
    )


def expert_plan(route_rows, capacity):
    pair_ids = route_rows.reshape(-1)
    onehot = (pair_ids[:, None] == jnp.arange(EXPERTS, dtype=jnp.int32)[None, :]).astype(jnp.int32)
    earlier = jnp.cumsum(onehot, axis=0) - onehot
    slot_pos = jnp.sum(earlier * onehot, axis=1)
    target = pair_ids * capacity + slot_pos
    source = (
        jnp.zeros((EXPERTS * capacity,), jnp.int32)
        .at[target]
        .set(jnp.arange(pair_ids.shape[0], dtype=jnp.int32) + 1)
    )
    return (target.reshape(route_rows.shape), source)


def send_out(buffer):
    return lax.all_to_all(buffer, (EXPERT, TENSOR), split_axis=0, concat_axis=1, tiled=True)


def send_home(produced):
    return lax.all_to_all(produced, (EXPERT, TENSOR), split_axis=1, concat_axis=0, tiled=True)


def moe_forward(middle_share, route_rows, params, outward, homeward):
    ffn_gain, router_weight, gate_weight, up_weight, down_weight = params[5:]
    share_rows = middle_share.shape[0]
    capacity = slot_count(share_rows)
    scale_two = rms_scale(middle_share)
    normed_two = (middle_share * scale_two * ffn_gain).astype(jnp.bfloat16)
    logits = jnp.dot(normed_two, router_weight, preferred_element_type=jnp.float32)
    member = route_rows[:, :, None] == jnp.arange(EXPERTS, dtype=jnp.int32)[None, None, :]
    chosen = jnp.sum(jnp.where(member, logits[:, None, :], 0.0), axis=2)
    exponent = jnp.exp(chosen - jnp.max(chosen, axis=1, keepdims=True))
    gates = exponent / jnp.sum(exponent, axis=1, keepdims=True)
    target, source = expert_plan(route_rows, capacity)
    filled = (source > 0)[:, None]
    gathered = normed_two[jnp.maximum(source - 1, 0) // TOPK]
    buffer = jnp.where(filled, gathered, jnp.zeros_like(gathered)).reshape(EXPERTS, capacity, -1)
    received = outward(buffer)
    gate_pre = jnp.einsum("erd,edf->erf", received, gate_weight, preferred_element_type=jnp.float32)
    up_pre = jnp.einsum("erd,edf->erf", received, up_weight, preferred_element_type=jnp.float32)
    hidden = (jax.nn.silu(gate_pre) * up_pre).astype(jnp.bfloat16)
    produced = jnp.einsum(
        "erf,efd->erd", hidden, down_weight, preferred_element_type=jnp.float32
    ).astype(jnp.bfloat16)
    returned = homeward(produced)
    picked = returned.reshape(EXPERTS * capacity, -1)[target]
    addition = jnp.einsum("tk,tkd->td", gates, picked, preferred_element_type=jnp.float32)
    return (
        scale_two,
        normed_two,
        member,
        gates,
        target,
        source,
        received,
        gate_pre,
        up_pre,
        hidden,
        picked,
        addition,
    )


def section_forward(layer_in, seg_rows, route_rows, params, share_start, share_rows):
    hidden_in = layer_in.astype(jnp.float32)
    attn_parts = attention_forward(hidden_in, seg_rows, params)
    partial_sum = jnp.dot(attn_parts[5], params[4], preferred_element_type=jnp.float32)
    own_share = lax.dynamic_slice_in_dim(hidden_in, share_start, share_rows, 0)
    summed = lax.psum(partial_sum.astype(jnp.bfloat16), TENSOR).astype(jnp.float32)
    branch = lax.dynamic_slice_in_dim(summed, share_start, share_rows, 0)
    middle_share = own_share + branch
    moe_parts = moe_forward(middle_share, route_rows, params, send_out, send_home)
    block_share = middle_share + moe_parts[-1]
    block_full = lax.all_gather(
        block_share.astype(jnp.bfloat16), TENSOR, axis=0, tiled=True
    ).astype(block_share.dtype)
    return (block_full, middle_share, moe_parts)


def section_backward(layer_in, middle_share, grad_top, seg_rows, params, share_start, kept_parts):
    (
        attn_gain,
        query_weight,
        key_weight,
        value_weight,
        out_weight,
        ffn_gain,
        router_weight,
        gate_weight,
        up_weight,
        down_weight,
    ) = params
    hidden_in = layer_in.astype(jnp.float32)
    row_count = hidden_in.shape[0]
    share_rows = middle_share.shape[0]
    capacity = slot_count(share_rows)
    (
        scale_one,
        normed,
        query_rot,
        key_rot,
        value_rot,
        attended,
        log_total,
        cosine_table,
        sine_table,
    ) = attention_forward(hidden_in, seg_rows, params)
    (
        scale_two,
        normed_two,
        member,
        gates,
        target,
        source,
        received,
        gate_pre,
        up_pre,
        hidden,
        picked,
        addition,
    ) = kept_parts
    grad_share = lax.dynamic_slice_in_dim(grad_top, share_start, share_rows, 0)
    grad_picked = (gates[:, :, None] * grad_share[:, None, :]).astype(jnp.bfloat16)
    grad_gates = jnp.einsum("td,tkd->tk", grad_share, picked, preferred_element_type=jnp.float32)
    grad_chosen = gates * (grad_gates - jnp.sum(gates * grad_gates, axis=1, keepdims=True))
    grad_logits = jnp.sum(jnp.where(member, grad_chosen[:, :, None], 0.0), axis=1).astype(
        jnp.bfloat16
    )
    router_grad = jnp.einsum(
        "td,te->de", normed_two, grad_logits, preferred_element_type=jnp.float32
    )
    grad_normed = jnp.einsum(
        "te,de->td", grad_logits, router_weight, preferred_element_type=jnp.float32
    )
    filled = (source > 0)[:, None]
    flat_grad = grad_picked.reshape(share_rows * TOPK, -1)
    gathered = flat_grad[jnp.maximum(source - 1, 0)]
    grad_buffer = jnp.where(filled, gathered, jnp.zeros_like(gathered)).reshape(
        EXPERTS, capacity, -1
    )
    sent = lax.all_to_all(
        grad_buffer, (EXPERT, TENSOR), split_axis=0, concat_axis=1, tiled=True
    )
    grad_hidden = jnp.einsum("erd,efd->erf", sent, down_weight, preferred_element_type=jnp.float32)
    sigmoid_gate = jax.nn.sigmoid(gate_pre)
    grad_gate = (
        grad_hidden * up_pre * sigmoid_gate * (1.0 + gate_pre * (1.0 - sigmoid_gate))
    ).astype(jnp.bfloat16)
    grad_up = (grad_hidden * gate_pre * sigmoid_gate).astype(jnp.bfloat16)
    down_grad = jnp.einsum("erf,erd->efd", hidden, sent, preferred_element_type=jnp.float32)
    gate_grad = jnp.einsum("erd,erf->edf", received, grad_gate, preferred_element_type=jnp.float32)
    up_grad = jnp.einsum("erd,erf->edf", received, grad_up, preferred_element_type=jnp.float32)
    grad_rows = jnp.einsum(
        "erf,edf->erd", grad_gate, gate_weight, preferred_element_type=jnp.float32
    )
    grad_rows = (
        grad_rows
        + jnp.einsum("erf,edf->erd", grad_up, up_weight, preferred_element_type=jnp.float32)
    ).astype(jnp.bfloat16)
    back_rows = lax.all_to_all(
        grad_rows, (EXPERT, TENSOR), split_axis=1, concat_axis=0, tiled=True
    )
    grad_normed = grad_normed + jnp.sum(
        back_rows.reshape(EXPERTS * capacity, -1)[target].astype(jnp.float32), axis=1
    )
    grad_middle, ffn_gain_grad = norm_back(grad_normed, middle_share, scale_two, ffn_gain)
    grad_middle = grad_middle + grad_share
    grad_mid_full = lax.all_gather(
        grad_middle.astype(jnp.bfloat16), TENSOR, axis=0, tiled=True
    ).astype(grad_middle.dtype)
    grad_mid_low = grad_mid_full.astype(jnp.bfloat16)
    out_grad = jnp.einsum("rh,rd->hd", attended, grad_mid_low, preferred_element_type=jnp.float32)
    grad_attended = jnp.einsum(
        "rd,hd->rh", grad_mid_low, out_weight, preferred_element_type=jnp.float32
    ).astype(jnp.bfloat16)
    seq_count = row_count // LEN
    grad_query, grad_key, grad_value = lax.map(
        attend_backward,
        (
            query_rot.reshape(seq_count, LEN, -1),
            key_rot.reshape(seq_count, LEN, -1),
            value_rot.reshape(seq_count, LEN, -1),
            seg_rows.reshape(seq_count, LEN),
            log_total,
            grad_attended.reshape(seq_count, LEN, -1),
        ),
    )
    grad_query = rotate(
        grad_query.reshape(row_count, -1), cosine_table, sine_table, HD, -1.0
    ).astype(jnp.bfloat16)
    grad_key = rotate(grad_key.reshape(row_count, -1), cosine_table, sine_table, HD, -1.0).astype(
        jnp.bfloat16
    )
    grad_value = grad_value.reshape(row_count, -1).astype(jnp.bfloat16)
    query_grad = jnp.einsum("rd,rh->dh", normed, grad_query, preferred_element_type=jnp.float32)
    key_grad = jnp.einsum("rd,rh->dh", normed, grad_key, preferred_element_type=jnp.float32)
    value_grad = jnp.einsum("rd,rh->dh", normed, grad_value, preferred_element_type=jnp.float32)
    grad_normed_one = jnp.einsum(
        "rh,dh->rd", grad_query, query_weight, preferred_element_type=jnp.float32
    )
    grad_normed_one = grad_normed_one + jnp.einsum(
        "rh,dh->rd", grad_key, key_weight, preferred_element_type=jnp.float32
    )
    grad_normed_one = grad_normed_one + jnp.einsum(
        "rh,dh->rd", grad_value, value_weight, preferred_element_type=jnp.float32
    )
    grad_normed_one = lax.psum(grad_normed_one.astype(jnp.bfloat16), TENSOR).astype(jnp.float32)
    grad_input, attn_gain_grad = norm_back(grad_normed_one, hidden_in, scale_one, attn_gain)
    grad_input = grad_input + grad_mid_full
    return (
        grad_input,
        (
            attn_gain_grad,
            query_grad,
            key_grad,
            value_grad,
            out_grad,
            ffn_gain_grad,
            router_grad,
            gate_grad,
            up_grad,
            down_grad,
        ),
    )


def stack_zeros(piece_arr, count):
    return jnp.zeros((count,) + piece_arr.shape, piece_arr.dtype)


def on_device(
    boundary,
    segments,
    expert_ids,
    attn_gain,
    query_weight,
    key_weight,
    value_weight,
    out_weight,
    ffn_gain,
    router_weight,
    gate_weight,
    up_weight,
    down_weight,
):
    params = tuple(
        (
            array_in[0]
            for array_in in (
                attn_gain,
                query_weight,
                key_weight,
                value_weight,
                out_weight,
                ffn_gain,
                router_weight,
                gate_weight,
                up_weight,
                down_weight,
            )
        )
    )
    section_index = lax.axis_index(SECTION)
    tensor_index = lax.axis_index(TENSOR)
    own_rows = boundary[0]
    micro_count = own_rows.shape[0]
    row_count = own_rows.shape[1]
    model_width = own_rows.shape[2]
    share_rows = expert_ids.shape[2]
    share_start = tensor_index * share_rows
    routes = expert_ids[0]
    kept_inputs = jnp.zeros((micro_count, row_count, model_width), jnp.bfloat16)
    kept_middle = jnp.zeros((micro_count, share_rows, model_width), jnp.float32)
    block_outputs = jnp.zeros((micro_count, row_count, model_width), jnp.bfloat16)
    arrived = jnp.zeros((row_count, model_width), jnp.bfloat16)
    kept_moe = None
    for tick_idx in range(micro_count + 1):
        micro_idx = tick_idx - section_index
        is_valid = (micro_idx >= 0) & (micro_idx < micro_count)
        slot_idx = jnp.clip(micro_idx, 0, micro_count - 1)
        layer_in = jnp.where(section_index == 0, own_rows[min(tick_idx, micro_count - 1)], arrived)
        seg_rows = lax.dynamic_index_in_dim(segments, slot_idx, 0, keepdims=False)
        route_rows = lax.dynamic_index_in_dim(routes, slot_idx, 0, keepdims=False)
        block_full, middle_share, moe_parts = section_forward(
            layer_in, seg_rows, route_rows, params, share_start, share_rows
        )
        block_low = block_full.astype(jnp.bfloat16)
        kept_inputs = jnp.where(
            is_valid,
            lax.dynamic_update_index_in_dim(kept_inputs, layer_in, slot_idx, 0),
            kept_inputs,
        )
        kept_middle = jnp.where(
            is_valid,
            lax.dynamic_update_index_in_dim(kept_middle, middle_share, slot_idx, 0),
            kept_middle,
        )
        block_outputs = jnp.where(
            is_valid,
            lax.dynamic_update_index_in_dim(block_outputs, block_low, slot_idx, 0),
            block_outputs,
        )
        if kept_moe is None:
            kept_moe = tuple((stack_zeros(piece_arr, micro_count) for piece_arr in moe_parts))
        kept_moe = tuple(
            (
                jnp.where(
                    is_valid,
                    lax.dynamic_update_index_in_dim(stack_arr, piece_arr, slot_idx, 0),
                    stack_arr,
                )
                for stack_arr, piece_arr in zip(kept_moe, moe_parts)
            )
        )
        arrived = shifted(block_low, SECTION, 1)
    grads = tuple((jnp.zeros(param_arr.shape, jnp.float32) for param_arr in params))
    input_grads = jnp.zeros((micro_count, row_count, model_width), jnp.bfloat16)
    grad_arrived = jnp.zeros((row_count, model_width), jnp.bfloat16)
    for tick_idx in range(micro_count + 1):
        micro_idx = tick_idx - (1 - section_index)
        is_valid = (micro_idx >= 0) & (micro_idx < micro_count)
        slot_idx = jnp.clip(micro_idx, 0, micro_count - 1)
        grad_top = jnp.where(
            section_index == 1, own_rows[min(tick_idx, micro_count - 1)], grad_arrived
        ).astype(jnp.float32)
        layer_in = lax.dynamic_index_in_dim(kept_inputs, slot_idx, 0, keepdims=False)
        middle_share = lax.dynamic_index_in_dim(kept_middle, slot_idx, 0, keepdims=False)
        seg_rows = lax.dynamic_index_in_dim(segments, slot_idx, 0, keepdims=False)
        route_rows = lax.dynamic_index_in_dim(routes, slot_idx, 0, keepdims=False)
        tick_moe = tuple(
            (
                lax.dynamic_index_in_dim(stack_arr, slot_idx, 0, keepdims=False)
                for stack_arr in kept_moe
            )
        )
        grad_input, tick_grads = section_backward(
            layer_in, middle_share, grad_top, seg_rows, params, share_start, tick_moe
        )
        valid_weight = is_valid.astype(jnp.float32)
        grads = tuple(
            (
                total_grad + valid_weight * tick_part
                for total_grad, tick_part in zip(grads, tick_grads)
            )
        )
        grad_low = grad_input.astype(jnp.bfloat16)
        input_grads = jnp.where(
            is_valid,
            lax.dynamic_update_index_in_dim(input_grads, grad_low, slot_idx, 0),
            input_grads,
        )
        grad_arrived = shifted(grad_low, SECTION, -1)
    dense = (
        lax.psum(grads[0].astype(jnp.bfloat16), (DP, EXPERT)).astype(jnp.float32),
        lax.psum(grads[1].astype(jnp.bfloat16), (DP, EXPERT)).astype(jnp.float32),
        lax.psum(grads[2].astype(jnp.bfloat16), (DP, EXPERT)).astype(jnp.float32),
        lax.psum(grads[3].astype(jnp.bfloat16), (DP, EXPERT)).astype(jnp.float32),
        lax.psum(grads[4].astype(jnp.bfloat16), (DP, EXPERT)).astype(jnp.float32),
    )
    shared = lax.psum((grads[5], grads[6]), (DP, EXPERT, TENSOR))
    expert_sums = (
        lax.psum(grads[7].astype(jnp.bfloat16), DP).astype(jnp.float32),
        lax.psum(grads[8].astype(jnp.bfloat16), DP).astype(jnp.float32),
        lax.psum(grads[9].astype(jnp.bfloat16), DP).astype(jnp.float32),
    )
    ends_out = jnp.where(section_index == 0, input_grads, block_outputs)[None]
    return (
        ends_out,
        dense[0][None],
        dense[1][None],
        dense[2][None],
        dense[3][None],
        dense[4][None],
        shared[0][None],
        shared[1][None],
        expert_sums[0][None],
        expert_sums[1][None],
        expert_sums[2][None],
    )


MIB = 1024 * 1024
NT = (((1,), (1,)), ((), ()))
TN = (((0,), (0,)), ((), ()))


def dot(left, right, dims=None):
    if dims is None:
        return jnp.dot(left, right, preferred_element_type=jnp.float32)
    return lax.dot_general(left, right, dims, preferred_element_type=jnp.float32)


def lane_grid(rows):
    return lax.broadcasted_iota(jnp.int32, (rows, 2 * HD), 1)


def turn_pair(slab, cosine, sine):
    low_half = (lane_grid(slab.shape[0]) % HD) < HD // 2
    partner = jnp.where(
        low_half, pltpu.roll(slab, 2 * HD - HD // 2, 1), pltpu.roll(slab, HD // 2, 1)
    )
    return slab * cosine + partner * sine


def pair_tables(length):
    cosine, sine = rope_tables(length, HD, length)
    return (
        jnp.concatenate([cosine] * 4, axis=1),
        jnp.concatenate([-sine, sine, -sine, sine], axis=1),
    )


def aligned_head(slabs, head, side, scale):
    slab = slabs[head // 2]
    if head % 2 != side:
        slab = pltpu.roll(slab, HD, 1)
    keep = (lane_grid(slab.shape[0]) // HD) == side
    return jnp.where(keep, slab * scale, 0.0).astype(jnp.bfloat16)


def one_side(slab, side):
    return jnp.where((lane_grid(slab.shape[0]) // HD) == side, slab, jnp.zeros_like(slab))


def slabs_of(matrix, start, count):
    return [matrix[:, start + 2 * HD * i : start + 2 * HD * (i + 1)] for i in range(count)]


def attend_part(group, rows, weights, tables, allowed):
    width = weights.shape[1]
    query_width = width * group // (group + 2)
    key_width = (width - query_width) // 2
    cosine, sine = tables
    projected = dot(rows, weights)
    query = [
        turn_pair(slab, cosine, sine) for slab in slabs_of(projected, 0, query_width // (2 * HD))
    ]
    key = [
        turn_pair(slab, cosine, sine).astype(jnp.bfloat16)
        for slab in slabs_of(projected, query_width, key_width // (2 * HD))
    ]
    value = [
        slab.astype(jnp.bfloat16)
        for slab in slabs_of(projected, query_width + key_width, key_width // (2 * HD))
    ]
    turned = jnp.concatenate([slab.astype(jnp.bfloat16) for slab in query] + key + value, axis=1)
    query = [slab.astype(jnp.bfloat16).astype(jnp.float32) for slab in query]
    mixed = [None] * len(query)
    for kv_head in range(key_width // HD):
        side = kv_head % 2
        key_slab = key[kv_head // 2]
        value_side = one_side(value[kv_head // 2], side)
        for head in range(group * kv_head, group * (kv_head + 1)):
            scores = dot(aligned_head(query, head, side, HD**-0.5), key_slab, NT)
            scores = jnp.where(allowed, scores, NEG_BIG)
            exponent = jnp.exp(scores - jnp.max(scores, axis=1, keepdims=True))
            probability = exponent / jnp.sum(exponent, axis=1, keepdims=True)
            part = dot(probability.astype(jnp.bfloat16), value_side)
            if head % 2 != side:
                part = pltpu.roll(part, HD, 1)
            mixed[head // 2] = part if head % 2 == 0 else mixed[head // 2] + part
    return turned, jnp.concatenate([part.astype(jnp.bfloat16) for part in mixed], axis=1)


def allowed_pairs(seg_col, seg_row):
    length = seg_row.shape[1]
    row = lax.broadcasted_iota(jnp.int32, (length, length), 0)
    column = lax.broadcasted_iota(jnp.int32, (length, length), 1)
    return (row >= column) & (seg_col == seg_row)


def of_section(first, second):
    return jnp.where(lax.axis_index(SECTION) == 0, first[...], second[...])


def start_of_section(first, second, to, sem):
    @pl.when(lax.axis_index(SECTION) == 0)
    def _():
        pltpu.make_async_copy(first, to, sem).start()

    @pl.when(lax.axis_index(SECTION) != 0)
    def _():
        pltpu.make_async_copy(second, to, sem).start()


def attn_forward_kernel(
    group,
    x_first,
    x_second,
    gain_one_ref,
    wqkv_hbm,
    wo_hbm,
    cos_ref,
    sin_ref,
    seg_col_ref,
    seg_row_ref,
    gain_two_ref,
    h1_ref,
    xn1_ref,
    qkv_ref,
    att_ref,
    xn2_ref,
    x_ref,
    wqkv_ref,
    wo_ref,
    x_sem,
    weight_sem,
):
    parts = wqkv_ref.shape[0]

    def weight_copies(half):
        return [
            pltpu.make_async_copy(hbm.at[half], ref.at[half], weight_sem.at[i, half])
            for i, (hbm, ref) in enumerate(((wqkv_hbm, wqkv_ref), (wo_hbm, wo_ref)))
        ]

    start_of_section(x_first, x_second, x_ref, x_sem)
    for copy in weight_copies(0):
        copy.start()
    pltpu.make_async_copy(x_first, x_ref, x_sem).wait()
    rows = x_ref[...].astype(jnp.float32)
    xn1_ref[...] = (rows * rms_scale(rows) * gain_one_ref[...]).astype(jnp.bfloat16)
    h1_ref[...] = rows

    def one(half, carry):
        for copy in weight_copies(half):
            copy.wait()

        @pl.when(half + 1 < parts)
        def _():
            for copy in weight_copies(half + 1):
                copy.start()

        turned, attended = attend_part(
            group,
            xn1_ref[...],
            wqkv_ref[half],
            (cos_ref[...], sin_ref[...]),
            allowed_pairs(seg_col_ref[...], seg_row_ref[...]),
        )
        qkv_ref[half] = turned
        att_ref[half] = attended
        h1_ref[...] += dot(attended, wo_ref[half])
        return carry

    lax.fori_loop(0, parts, one, 0)
    middle = h1_ref[...]
    xn2_ref[...] = (middle * rms_scale(middle) * gain_two_ref[...]).astype(jnp.bfloat16)


def attn_forward(first, second, seg, gains, wqkv, wo, tables, group):
    length, width = first.shape
    parts, _, qkv_width = wqkv.shape
    att_width = wo.shape[1]
    vmem = pl.BlockSpec(memory_space=pltpu.VMEM)
    anywhere = pl.BlockSpec(memory_space=pl.ANY)
    return pl.pallas_call(
        functools.partial(attn_forward_kernel, group),
        in_specs=[anywhere] * 2 + [vmem] + [anywhere] * 2 + [vmem] * 5,
        out_specs=[vmem] * 5,
        out_shape=[
            jax.ShapeDtypeStruct((length, width), jnp.float32),
            jax.ShapeDtypeStruct((length, width), jnp.bfloat16),
            jax.ShapeDtypeStruct((parts, length, qkv_width), jnp.bfloat16),
            jax.ShapeDtypeStruct((parts, length, att_width), jnp.bfloat16),
            jax.ShapeDtypeStruct((length, width), jnp.bfloat16),
        ],
        scratch_shapes=[
            pltpu.VMEM((length, width), jnp.bfloat16),
            pltpu.VMEM(wqkv.shape, wqkv.dtype),
            pltpu.VMEM(wo.shape, wo.dtype),
            pltpu.SemaphoreType.DMA,
            pltpu.SemaphoreType.DMA((2, parts)),
        ],
        compiler_params=pltpu.CompilerParams(vmem_limit_bytes=62 * MIB),
        cost_estimate=pl.CostEstimate(
            flops=4 * 10**9, bytes_accessed=20 * 10**6, transcendentals=2 * 10**6
        ),
        name="attn_forward",
    )(first, second, gains[0], wqkv, wo, *tables, seg[:, None], seg[None, :], gains[1])


def attn_again_kernel(
    group,
    x_ref,
    gain_ref,
    wqkv_hbm,
    cos_ref,
    sin_ref,
    seg_col_ref,
    seg_row_ref,
    xn1_ref,
    qkv_ref,
    att_ref,
    wqkv_ref,
    sem,
):
    @pl.when(lax.axis_index(SECTION) == 0)
    def _():
        parts = wqkv_ref.shape[0]

        def copy(half):
            return pltpu.make_async_copy(wqkv_hbm.at[half], wqkv_ref.at[half], sem.at[half])

        for half in range(parts):
            copy(half).start()
        rows = x_ref[...].astype(jnp.float32)
        xn1_ref[...] = (rows * rms_scale(rows) * gain_ref[...]).astype(jnp.bfloat16)

        def one(half, carry):
            copy(half).wait()
            qkv_ref[half], att_ref[half] = attend_part(
                group,
                xn1_ref[...],
                wqkv_ref[half],
                (cos_ref[...], sin_ref[...]),
                allowed_pairs(seg_col_ref[...], seg_row_ref[...]),
            )
            return carry

        lax.fori_loop(0, parts, one, 0)


def attn_again(layer_in, seg, gain, wqkv, tables, group):
    length, width = layer_in.shape
    parts, _, qkv_width = wqkv.shape
    vmem = pl.BlockSpec(memory_space=pltpu.VMEM)
    return pl.pallas_call(
        functools.partial(attn_again_kernel, group),
        in_specs=[vmem] * 2 + [pl.BlockSpec(memory_space=pl.ANY)] + [vmem] * 4,
        out_specs=[vmem] * 3,
        out_shape=[
            jax.ShapeDtypeStruct((length, width), jnp.bfloat16),
            jax.ShapeDtypeStruct((parts, length, qkv_width), jnp.bfloat16),
            jax.ShapeDtypeStruct((parts, length, width // parts), jnp.bfloat16),
        ],
        scratch_shapes=[
            pltpu.VMEM(wqkv.shape, wqkv.dtype),
            pltpu.SemaphoreType.DMA((parts,)),
        ],
        compiler_params=pltpu.CompilerParams(vmem_limit_bytes=62 * MIB),
        cost_estimate=pl.CostEstimate(
            flops=3 * 10**9, bytes_accessed=12 * 10**6, transcendentals=2 * 10**6
        ),
        name="attn_again",
    )(layer_in, gain, wqkv, tables[0], tables[1], seg[:, None], seg[None, :])


def attn_split_kernel(
    group,
    x_ref,
    gain_one_ref,
    wqkv_ref,
    wo_ref,
    cos_ref,
    sin_ref,
    seg_col_ref,
    seg_row_ref,
    gain_two_ref,
    h1_ref,
    xn2_ref,
    part,
    arrived,
    send_sem,
    recv_sem,
):
    x = lax.axis_index(TENSOR)
    aside = {TENSOR: 1 - x}

    @pl.when(lax.axis_index(SECTION) == 0)
    def _():
        barrier = pltpu.get_barrier_semaphore()
        pl.semaphore_signal(barrier, inc=1, device_id=aside, device_id_type=pl.DeviceIdType.MESH)

        def one(i, carry):
            at = jnp.where(i == 0, 1 - x, x)
            rows = x_ref[at].astype(jnp.float32)
            normed = (rows * rms_scale(rows) * gain_one_ref[...]).astype(jnp.bfloat16)
            _, attended = attend_part(
                group,
                normed,
                wqkv_ref[...],
                (cos_ref[...], sin_ref[...]),
                allowed_pairs(seg_col_ref[at], seg_row_ref[at]),
            )
            branch = dot(attended, wo_ref[...])

            @pl.when(i == 0)
            def _():
                part[...] = branch.astype(jnp.bfloat16)
                pl.semaphore_wait(barrier, 1)
                copy().start()

            @pl.when(i == 1)
            def _():
                h1_ref[...] = rows + branch

            return carry

        def copy():
            return pltpu.make_async_remote_copy(
                src_ref=part,
                dst_ref=arrived,
                send_sem=send_sem,
                recv_sem=recv_sem,
                device_id=aside,
                device_id_type=pl.DeviceIdType.MESH,
            )

        lax.fori_loop(0, 2, one, 0)
        copy().wait()
        middle = h1_ref[...] + arrived[...].astype(jnp.float32)
        h1_ref[...] = middle
        xn2_ref[...] = (middle * rms_scale(middle) * gain_two_ref[...]).astype(jnp.bfloat16)


def attn_split(rows, seg, gains, wqkv, wo, tables, group):
    _, length, width = rows.shape
    vmem = pl.BlockSpec(memory_space=pltpu.VMEM)
    return pl.pallas_call(
        functools.partial(attn_split_kernel, group),
        in_specs=[vmem] * 9,
        out_specs=[vmem] * 2,
        out_shape=[
            jax.ShapeDtypeStruct((length, width), jnp.float32),
            jax.ShapeDtypeStruct((length, width), jnp.bfloat16),
        ],
        scratch_shapes=[
            pltpu.VMEM((length, width), jnp.bfloat16),
            pltpu.VMEM((length, width), jnp.bfloat16),
            pltpu.SemaphoreType.DMA,
            pltpu.SemaphoreType.DMA,
        ],
        compiler_params=pltpu.CompilerParams(
            collective_id=8, has_side_effects=True, vmem_limit_bytes=48 * MIB
        ),
        cost_estimate=pl.CostEstimate(
            flops=4 * 10**9, bytes_accessed=20 * 10**6, transcendentals=2 * 10**6
        ),
        name="attn_split",
    )(
        rows,
        gains[0],
        wqkv,
        wo,
        tables[0],
        tables[1],
        seg[:, :, None],
        seg[:, None, :],
        gains[1],
    )


def both_halves_kernel(
    chunks,
    wqkv,
    wo,
    after,
    wqkv_before,
    wo_before,
    wqkv_all,
    wo_all,
    wqkv_held,
    wo_held,
    own_sem,
    out_sem,
    x_send,
    x_recv,
    core_send,
    core_recv,
):
    del after, wqkv_before, wo_before
    x = lax.axis_index(TENSOR)
    core = lax.axis_index(DP)
    aside, partner = {TENSOR: 1 - x}, {DP: 1 - core}
    pairs = ((wqkv, wqkv_held, wqkv_all), (wo, wo_held, wo_all))

    def span(i, of_core, chunk):
        rows = pairs[i][0].shape[0] // (2 * chunks)
        return pl.ds((of_core * chunks + chunk) * rows, rows)

    def own_copy(i, of_core, chunk):
        shard, held, _ = pairs[i]
        at = span(i, of_core, chunk)
        return pltpu.make_async_copy(shard.at[at], held.at[x, at], own_sem.at[i, of_core, chunk])

    def out_copy(i, half):
        _, held, out = pairs[i]
        return pltpu.make_async_copy(held.at[half], out.at[half], out_sem.at[i, half])

    def x_copy(i, chunk, half):
        _, held, _ = pairs[i]
        at = held.at[half, span(i, core, chunk)]
        return pltpu.make_async_remote_copy(
            src_ref=at,
            dst_ref=at,
            send_sem=x_send.at[i, chunk],
            recv_sem=x_recv.at[i, chunk],
            device_id=aside,
            device_id_type=pl.DeviceIdType.MESH,
        )

    def core_copy(i, chunk, of_core):
        _, held, _ = pairs[i]
        at = held.at[1 - x, span(i, of_core, chunk)]
        return pltpu.make_async_remote_copy(
            src_ref=at,
            dst_ref=at,
            send_sem=core_send.at[i, chunk],
            recv_sem=core_recv.at[i, chunk],
            device_id=partner,
            device_id_type=pl.DeviceIdType.MESH,
        )

    steps = [(i, chunk) for i in range(2) for chunk in range(chunks)]

    @pl.when(lax.axis_index(SECTION) == 0)
    def _():
        for of_core in (core, 1 - core):
            for i, chunk in steps:
                own_copy(i, of_core, chunk).start()
        barrier = pltpu.get_barrier_semaphore()
        for other in (aside, partner):
            pl.semaphore_signal(barrier, inc=1, device_id=other, device_id_type=pl.DeviceIdType.MESH)
        pl.semaphore_wait(barrier, 2)
        for i, chunk in steps:
            own_copy(i, core, chunk).wait()
            x_copy(i, chunk, x).start()
        for i, chunk in steps:
            own_copy(i, 1 - core, chunk).wait()
        for i in range(2):
            out_copy(i, x).start()
        for i, chunk in steps:
            x_copy(i, chunk, 1 - x).wait_recv()
            core_copy(i, chunk, core).start()
        for i in range(2):
            for chunk in range(chunks):
                core_copy(i, chunk, 1 - core).wait_recv()
            out_copy(i, 1 - x).start()
        for i, chunk in steps:
            x_copy(i, chunk, x).wait_send()
            core_copy(i, chunk, core).wait_send()
        for i in range(2):
            for half in range(2):
                out_copy(i, half).wait()


def both_halves(wqkv, wo, after, before, chunks=4):
    anywhere = pl.BlockSpec(memory_space=pl.ANY)
    dma = pltpu.SemaphoreType.DMA
    return pl.pallas_call(
        functools.partial(both_halves_kernel, chunks),
        in_specs=[anywhere] * 5,
        out_specs=[anywhere] * 2,
        input_output_aliases={3: 0, 4: 1},
        out_shape=[
            jax.ShapeDtypeStruct((2,) + wqkv.shape, wqkv.dtype),
            jax.ShapeDtypeStruct((2,) + wo.shape, wo.dtype),
        ],
        scratch_shapes=[
            pltpu.VMEM((2,) + wqkv.shape, wqkv.dtype),
            pltpu.VMEM((2,) + wo.shape, wo.dtype),
            dma((2, 2, chunks)),
            dma((2, 2)),
        ]
        + [dma((2, chunks))] * 4,
        compiler_params=pltpu.CompilerParams(
            collective_id=9, has_side_effects=True, vmem_limit_bytes=62 * MIB
        ),
        cost_estimate=pl.CostEstimate(flops=0, bytes_accessed=30 * 10**6, transcendentals=0),
        name="both_halves",
    )(wqkv, wo, after, *before)


def attn_backward_kernel(group, *refs):
    pairs = [refs[2 * i : 2 * i + 2] for i in range(6)]
    (
        wqkv_hbm,
        wo_hbm,
        rows_ref,
        grad_gates_ref,
        router_ref,
        gain_one_ref,
        gain_two_ref,
        cos_ref,
        sin_ref,
        seg_col_ref,
        seg_row_ref,
        grad_in_ref,
        mid_ref,
        dqkv_ref,
        small_ref,
        x_ref,
        h1_ref,
        xn2_ref,
        gates_ref,
        qkv_ref,
        top_ref,
        wqkv_ref,
        wo_ref,
        middle_acc,
        normed_acc,
        taken_sem,
        weight_sem,
    ) = refs[12:]
    taken = (x_ref, h1_ref, xn2_ref, gates_ref, qkv_ref, top_ref)
    experts = grad_gates_ref.shape[0]
    parts = wqkv_ref.shape[0]

    def weight_copies(half):
        return [
            pltpu.make_async_copy(hbm.at[half], ref.at[half], weight_sem.at[i, half])
            for i, (hbm, ref) in enumerate(((wqkv_hbm, wqkv_ref), (wo_hbm, wo_ref)))
        ]

    for i in (3, 2, 1, 5, 4, 0):
        start_of_section(*pairs[i], taken[i], taken_sem.at[i])

    def arrived(i):
        pltpu.make_async_copy(pairs[i][0], taken[i], taken_sem.at[i]).wait()
        return taken[i]

    gates = arrived(3)[...]
    grad_gates = grad_gates_ref[...]
    chosen = gates * (grad_gates - jnp.sum(gates * grad_gates, axis=0, keepdims=True))
    logits = chosen.astype(jnp.bfloat16)
    small_ref[0:experts, :] = dot(logits, arrived(2)[...])
    for copy in weight_copies(0):
        copy.start()
    grad_normed = dot(logits, router_ref[...], TN) + rows_ref[...].astype(jnp.float32)
    middle = arrived(1)[...]
    grad_middle, gain_grad = norm_back(grad_normed, middle, rms_scale(middle), gain_two_ref[...])
    small_ref[experts : experts + 1, :] = gain_grad[None, :]
    grad_middle = grad_middle + arrived(5)[...].astype(jnp.float32)
    middle_acc[...] = grad_middle
    mid_ref[...] = grad_middle.astype(jnp.bfloat16)
    normed_acc[...] = jnp.zeros_like(normed_acc)
    arrived(4)

    def one(half, carry):
        for copy in weight_copies(half):
            copy.wait()

        @pl.when(half + 1 < parts)
        def _():
            for copy in weight_copies(half + 1):
                copy.start()

        attn_backward_part(
            group,
            half,
            mid_ref,
            wqkv_ref,
            wo_ref,
            (cos_ref[...], -sin_ref[...]),
            (seg_col_ref[...], seg_row_ref[...]),
            qkv_ref,
            dqkv_ref,
            normed_acc,
        )
        return carry

    lax.fori_loop(0, parts, one, 0)
    rows = arrived(0)[...].astype(jnp.float32)
    grad_rows, gain_grad = norm_back(normed_acc[...], rows, rms_scale(rows), gain_one_ref[...])
    grad_in_ref[...] = (grad_rows + middle_acc[...]).astype(jnp.bfloat16)
    small_ref[experts + 1 : experts + 2, :] = gain_grad[None, :]
    small_ref[experts + 2 :, :] = jnp.zeros_like(small_ref[experts + 2 :, :])


def attn_backward_part(
    group, part, mid_ref, wqkv_ref, wo_ref, tables, segs, qkv_ref, dqkv_ref, normed_acc
):
    length = mid_ref.shape[0]
    width = wqkv_ref.shape[2]
    query_width = width * group // (group + 2)
    key_width = (width - query_width) // 2
    cosine, sine = tables
    seg_col, seg_row = segs
    grad_att = dot(mid_ref[...], wo_ref[part], NT).astype(jnp.bfloat16).astype(jnp.float32)
    grad_out = slabs_of(grad_att, 0, query_width // (2 * HD))
    kept = qkv_ref[part]
    query = [slab.astype(jnp.float32) for slab in slabs_of(kept, 0, query_width // (2 * HD))]
    key = slabs_of(kept, query_width, key_width // (2 * HD))
    value = slabs_of(kept, query_width + key_width, key_width // (2 * HD))
    key_at = lax.broadcasted_iota(jnp.int32, (length, length), 0)
    query_at = lax.broadcasted_iota(jnp.int32, (length, length), 1)
    allowed = (query_at >= key_at) & (seg_col == seg_row)
    grad_query = [None] * len(query)
    grad_key = [None] * len(key)
    grad_value = [None] * len(value)
    for kv_head in range(key_width // HD):
        side = kv_head % 2
        slab_at = kv_head // 2
        key_slab = key[slab_at]
        key_side = one_side(key_slab, side)
        value_slab = value[slab_at]
        for head in range(group * kv_head, group * (kv_head + 1)):
            query_head = aligned_head(query, head, side, HD**-0.5)
            out_head = aligned_head(grad_out, head, side, 1.0)
            scores = dot(key_slab, query_head, NT)
            scores = jnp.where(allowed, scores, NEG_BIG)
            exponent = jnp.exp(scores - jnp.max(scores, axis=0, keepdims=True))
            probability = exponent / jnp.sum(exponent, axis=0, keepdims=True)
            grad_prob = dot(value_slab, out_head, NT)
            value_part = dot(probability.astype(jnp.bfloat16), out_head)
            centre = jnp.sum(probability * grad_prob, axis=0, keepdims=True)
            grad_scores = (probability * (grad_prob - centre)).astype(jnp.bfloat16)
            key_part = dot(grad_scores, query_head)
            query_part = dot(grad_scores, key_side, TN) * HD**-0.5
            if head % 2 != side:
                query_part = pltpu.roll(query_part, HD, 1)
            at = head // 2
            grad_query[at] = query_part if head % 2 == 0 else grad_query[at] + query_part
            first = head == 2 * group * slab_at
            grad_key[slab_at] = key_part if first else grad_key[slab_at] + key_part
            grad_value[slab_at] = value_part if first else grad_value[slab_at] + value_part
    turned = [turn_pair(slab, cosine, sine).astype(jnp.bfloat16) for slab in grad_query + grad_key]
    dqkv = jnp.concatenate(turned + [slab.astype(jnp.bfloat16) for slab in grad_value], axis=1)
    dqkv_ref[part] = dqkv
    normed_acc[...] += dot(dqkv, wqkv_ref[part], NT)


def attn_backward(kept, rows, grad_gates, seg, gains, router, wqkv, wo, tables, group):
    length, width = rows.shape
    parts, _, qkv_width = wqkv.shape
    experts = router.shape[0]
    vmem = pl.BlockSpec(memory_space=pltpu.VMEM)
    anywhere = pl.BlockSpec(memory_space=pl.ANY)
    dma = pltpu.SemaphoreType.DMA
    return pl.pallas_call(
        functools.partial(attn_backward_kernel, group),
        in_specs=[anywhere] * 14 + [vmem] * 9,
        out_specs=[vmem] * 4,
        out_shape=[
            jax.ShapeDtypeStruct((length, width), jnp.bfloat16),
            jax.ShapeDtypeStruct((length, width), jnp.bfloat16),
            jax.ShapeDtypeStruct((parts, length, qkv_width), jnp.bfloat16),
            jax.ShapeDtypeStruct((experts + 8, width), jnp.float32),
        ],
        scratch_shapes=[pltpu.VMEM(one.shape, one.dtype) for one, _ in kept]
        + [
            pltpu.VMEM(wqkv.shape, wqkv.dtype),
            pltpu.VMEM(wo.shape, wo.dtype),
            pltpu.VMEM((length, width), jnp.float32),
            pltpu.VMEM((length, width), jnp.float32),
            dma((len(kept),)),
            dma((2, parts)),
        ],
        compiler_params=pltpu.CompilerParams(vmem_limit_bytes=62 * MIB),
        cost_estimate=pl.CostEstimate(
            flops=8 * 10**9, bytes_accessed=20 * 10**6, transcendentals=2 * 10**6
        ),
        name="attn_backward",
    )(
        *[one for pair in kept for one in pair],
        wqkv,
        wo,
        rows,
        grad_gates,
        router,
        gains[0],
        gains[1],
        tables[0],
        tables[1],
        seg[:, None],
        seg[None, :],
    )


def attn_weights_kernel(*refs):
    groups, out_ref = [refs[3 * i : 3 * i + 3] for i in range(4)], refs[12]
    width = out_ref.shape[1]

    def kept(group):
        one, both, three = group
        return jnp.concatenate([of_section(one, three), both[...]], axis=-2)

    def found(group):
        one, both, three = group
        return jnp.concatenate([both[...], of_section(three, one)], axis=-2)

    xn1, att = kept(groups[0]), kept(groups[1])[0]
    mid, dqkv = found(groups[2]), found(groups[3])[0]
    qkv_width = dqkv.shape[1]
    out_ref[0, :, :qkv_width] = dot(xn1, dqkv, TN).astype(jnp.bfloat16)
    half = width // 2
    for i in range(2):
        out_ref[0, i * half : (i + 1) * half, qkv_width:] = dot(
            att, mid[:, i * half : (i + 1) * half], TN
        ).astype(jnp.bfloat16)


def attn_weights(xn1, att, mid, dqkv):
    rows, width = xn1[0].shape
    parts, _, att_width = att[0].shape
    qkv_width = dqkv[0].shape[2]

    def whole(*shape):
        return pl.BlockSpec(shape, lambda i: (0,) * len(shape))

    def part(*shape):
        return pl.BlockSpec((1,) + shape, lambda i: (i, 0, 0))

    return pl.pallas_call(
        attn_weights_kernel,
        grid=(parts,),
        in_specs=[whole(rows, width)] * 3
        + [part(rows, att_width)] * 3
        + [whole(rows, width)] * 3
        + [part(rows, qkv_width)] * 3,
        out_specs=part(width, qkv_width + width // 2),
        out_shape=jax.ShapeDtypeStruct((parts, width, qkv_width + width // 2), jnp.bfloat16),
        compiler_params=pltpu.CompilerParams(vmem_limit_bytes=56 * MIB),
        cost_estimate=pl.CostEstimate(
            flops=7 * 10**9, bytes_accessed=20 * 10**6, transcendentals=0
        ),
        name="attn_weights",
    )(*xn1, *att, *mid, *dqkv)


def looked_up(place, values):
    found = values[0]
    for i, value in enumerate(values[1:]):
        found = jnp.where(place == i + 1, value, found)
    return found


def nearest_first(place, reach):
    table = []
    for at in range(reach):
        table.append(sorted(range(reach), key=lambda other: (abs(other - at), other)))
    return [looked_up(place, [table[at][k] for at in range(reach)]) for k in range(reach)]


MESH_ID = pl.DeviceIdType.MESH


class Chain:
    def __init__(self, reach):
        self.reach = reach
        self.z = lax.axis_index(EXPERT)
        self.x = lax.axis_index(TENSOR)
        self.me = 2 * self.z + self.x
        self.aside = {TENSOR: 1 - self.x}
        self.above = {EXPERT: self.z + 1}
        self.below = {EXPERT: self.z - 1}
        self.has_above = self.z < reach - 1
        self.has_below = self.z > 0
        self.order = nearest_first(self.z, reach)

    def near(self, k):
        return self.order[k] if isinstance(k, int) else looked_up(k, self.order)

    def greet_group(self, partner=None):
        barrier = pltpu.get_barrier_semaphore()
        if partner is not None:
            pl.semaphore_signal(barrier, inc=1, device_id=partner, device_id_type=MESH_ID)
        for other in range(2 * self.reach):

            @pl.when(other != self.me)
            def _():
                pl.semaphore_signal(
                    barrier,
                    inc=1,
                    device_id={EXPERT: other // 2, TENSOR: other % 2},
                    device_id_type=MESH_ID,
                )

        pl.semaphore_wait(barrier, 2 * self.reach - (1 if partner is None else 0))


def is_end(chain, source):
    return jnp.logical_or(source == 0, source == chain.reach - 1)


class Gather:
    def __init__(self, chain, blocks, send_sem, recv_sem, paired=False):
        self.chain, self.blocks, self.send_sem, self.recv_sem = chain, blocks, send_sem, recv_sem
        self.paired = paired

    def copy(self, source, column, piece, way, target):
        at = 2 * source + column
        return pltpu.make_async_remote_copy(
            src_ref=self.blocks.at[at, piece],
            dst_ref=self.blocks.at[at, piece],
            send_sem=self.send_sem.at[way, source, piece],
            recv_sem=self.recv_sem.at[at, piece],
            device_id=target,
            device_id_type=MESH_ID,
        )

    def over_x(self, source, piece, act):
        c = self.chain
        crosses = jnp.logical_and(is_end(c, source), source != c.z)
        if piece == 0:
            act(self.copy(source, c.x, 0, 0, c.aside))
        else:

            @pl.when(jnp.logical_not(crosses))
            def _():
                act(self.copy(source, c.x, piece, 0, c.aside))

    def each_way(self, source, piece, up, down, act):
        c = self.chain
        if up:

            @pl.when(c.has_above)
            def _():
                act(self.copy(source, c.x, piece, 1, c.above))

        if down:

            @pl.when(c.has_below)
            def _():
                act(self.copy(source, c.x, piece, 2, c.below))

        if not (self.paired and up and down):
            self.over_x(source, piece, act)

    def start(self):
        for piece in range(PIECES):
            self.each_way(self.chain.z, piece, True, True, lambda copy: copy.start())
        if self.paired:
            self.cross_out()

    def relay(self, distance):
        c = self.chain
        for piece in range(PIECES):

            @pl.when(c.z - distance >= 0)
            def _():
                self.copy(c.z - distance, c.x, piece, 1, c.below).wait_recv()
                self.each_way(c.z - distance, piece, True, False, lambda copy: copy.start())

            @pl.when(c.z + distance <= c.reach - 1)
            def _():
                self.copy(c.z + distance, c.x, piece, 2, c.above).wait_recv()
                self.each_way(c.z + distance, piece, False, True, lambda copy: copy.start())

    def cross_copy(self, end):
        c = self.chain
        return self.copy(end, 1 - c.x, PIECES - 1, 3, c.below if end else c.above)

    def cross_out(self):
        c = self.chain
        for end in (0, c.reach - 1):

            @pl.when(c.z == end)
            def _():
                self.cross_copy(end).start()

    def cross_relay(self, distance):
        c = self.chain
        for end in (0, c.reach - 1):
            last = c.reach - 1 - end

            @pl.when(jnp.where(c.z > end, c.z - end, end - c.z) == distance)
            def _():
                self.cross_copy(end).wait_recv()

                @pl.when(c.z != last)
                def _():
                    self.cross_copy(end).start()

    def wait_aside(self, source):
        c = self.chain
        self.copy(source, 1 - c.x, 0, 0, c.aside).wait_recv()

        @pl.when(jnp.logical_not(jnp.logical_and(is_end(c, source), source != c.z)))
        def _():
            self.copy(source, 1 - c.x, PIECES - 1, 0, c.aside).wait_recv()

    def drain(self):
        c = self.chain
        for piece in range(PIECES):
            self.each_way(c.z, piece, True, True, lambda copy: copy.wait_send())
            for distance in range(1, c.reach):

                @pl.when(c.z - distance >= 0)
                def _():
                    self.each_way(
                        c.z - distance, piece, True, False, lambda copy: copy.wait_send()
                    )

                @pl.when(c.z + distance <= c.reach - 1)
                def _():
                    self.each_way(
                        c.z + distance, piece, False, True, lambda copy: copy.wait_send()
                    )

        for end in (0, c.reach - 1):

            @pl.when(c.z != c.reach - 1 - end)
            def _():
                self.cross_copy(end).wait_send()


PIECES = 2
TAIL_PIECES = 4


class Reduce:
    def __init__(self, chain, part_at, from_x, from_z, sems, pieces=PIECES, cross=None):
        self.chain, self.part_at, self.from_x, self.from_z = chain, part_at, from_x, from_z
        self.pieces = pieces
        self.cross = cross
        self.x_send, self.x_recv, self.z_send, self.z_recv = sems

    def part_copy(self, home, piece):
        c = self.chain
        return pltpu.make_async_remote_copy(
            src_ref=self.part_at(home, 1 - c.x, piece),
            dst_ref=self.from_x.at[home, piece],
            send_sem=self.x_send.at[home, piece],
            recv_sem=self.x_recv.at[home, piece],
            device_id=c.aside,
            device_id_type=MESH_ID,
        )

    def sum_copy(self, home, piece, slot, target):
        return pltpu.make_async_remote_copy(
            src_ref=self.part_at(home, self.chain.x, piece),
            dst_ref=self.from_z.at[slot, piece],
            send_sem=self.z_send.at[home, piece],
            recv_sem=self.z_recv.at[slot, piece],
            device_id=target,
            device_id_type=MESH_ID,
        )

    def over_x(self, home, piece, act):
        c = self.chain
        if self.cross is None:
            act()
        else:
            crosses = jnp.logical_and(is_end(c, home), home != c.z)

            @pl.when(jnp.logical_not(jnp.logical_and(crosses, piece == self.pieces - 1)))
            def _():
                act()

    def start(self, k, piece):
        home = self.chain.near(k)
        self.over_x(home, piece, lambda: self.part_copy(home, piece).start())

    def arrive(self, k, piece):
        home = self.chain.near(k)
        self.over_x(home, piece, lambda: self.part_copy(home, piece).wait_recv())

    def own(self, home, piece):
        c = self.chain
        mine = self.part_at(home, c.x, piece)[...].astype(jnp.float32)
        came = self.from_x[home, piece].astype(jnp.float32)
        if self.cross is not None:
            crosses = jnp.logical_and(is_end(c, home), home != c.z)
            came = jnp.where(jnp.logical_and(crosses, piece == self.pieces - 1), 0.0, came)
        return mine + came

    def cross_copy(self, end):
        c = self.chain
        from_cross, send_sem, recv_sem = self.cross
        at = 1 if end else 0
        return pltpu.make_async_remote_copy(
            src_ref=self.part_at(end, 1 - c.x, self.pieces - 1),
            dst_ref=from_cross.at[at],
            send_sem=send_sem.at[at],
            recv_sem=recv_sem.at[at],
            device_id=c.above if end else c.below,
            device_id_type=MESH_ID,
        )

    def cross_step(self, distance):
        c = self.chain
        for end in (0, c.reach - 1):

            @pl.when(jnp.where(c.z > end, c.z - end, end - c.z) == distance)
            def _():
                @pl.when(c.z != c.reach - 1 - end)
                def _():
                    self.cross_copy(end).wait_recv()
                    mine = self.part_at(end, 1 - c.x, self.pieces - 1)
                    mine[...] = (
                        mine[...].astype(jnp.float32)
                        + self.cross[0][1 if end else 0].astype(jnp.float32)
                    ).astype(mine.dtype)

                @pl.when(c.z != end)
                def _():
                    self.cross_copy(end).start()

    def pass_on(self, k, piece):
        c = self.chain
        home = c.near(k)
        up = home > c.z
        comes = jnp.logical_or(
            jnp.logical_and(up, c.has_below), jnp.logical_and(home < c.z, c.has_above)
        )
        mine = self.part_at(home, c.x, piece)

        @pl.when(comes)
        def _():
            self.sum_copy(home, piece, home, c.above).wait_recv()
            mine[...] = (
                self.own(home, piece) + self.from_z[home, piece].astype(jnp.float32)
            ).astype(mine.dtype)

        @pl.when(jnp.logical_not(comes))
        def _():
            mine[...] = self.own(home, piece).astype(mine.dtype)

        @pl.when(up)
        def _():
            self.sum_copy(home, piece, home, c.above).start()

        @pl.when(home < c.z)
        def _():
            slot = jnp.where(home == c.z - 1, c.reach, home)
            self.sum_copy(home, piece, slot, c.below).start()

    def finish(self, piece, act):
        c = self.chain
        home = c.z

        @pl.when(c.has_below)
        def _():
            self.sum_copy(home, piece, home, c.below).wait_recv()

        @pl.when(c.has_above)
        def _():
            self.sum_copy(home, piece, c.reach, c.above).wait_recv()

        @pl.when(c.has_below & c.has_above)
        def _():
            act(
                piece,
                self.own(home, piece)
                + self.from_z[home, piece].astype(jnp.float32)
                + self.from_z[c.reach, piece].astype(jnp.float32),
            )

        @pl.when(jnp.logical_not(c.has_above))
        def _():
            act(piece, self.own(home, piece) + self.from_z[home, piece].astype(jnp.float32))

        @pl.when(jnp.logical_not(c.has_below))
        def _():
            act(piece, self.own(home, piece) + self.from_z[c.reach, piece].astype(jnp.float32))

    def drain(self):
        c = self.chain

        def one(home, carry):
            for piece in range(self.pieces):
                self.over_x(home, piece, lambda: self.part_copy(home, piece).wait_send())

                @pl.when(home != c.z)
                def _():
                    self.sum_copy(home, piece, home, c.above).wait_send()

            return carry

        lax.fori_loop(0, c.reach, one, 0)
        if self.cross is not None:
            for end in (0, c.reach - 1):

                @pl.when(c.z != end)
                def _():
                    self.cross_copy(end).wait_send()


def masked_softmax(logits, kept):
    top = jnp.max(jnp.where(kept, logits, NEG_BIG), axis=0, keepdims=True)
    exponent = jnp.where(kept, jnp.exp(jnp.where(kept, logits - top, 0.0)), 0.0)
    return exponent / jnp.sum(exponent, axis=0, keepdims=True)


def slot_gates(picks, gate_row):
    return jnp.sum(picks.astype(jnp.float32) * gate_row, axis=1, keepdims=True)


def one_hot_slots(slot_row, cap):
    length = slot_row.shape[1]
    at = lax.broadcasted_iota(jnp.int32, (cap, length), 0).astype(jnp.float32)
    return jnp.where(at == slot_row, 1.0, 0.0).astype(jnp.bfloat16)


def finish_pieces(summed, act):
    def one(piece, carry):
        summed.arrive(0, piece)
        summed.finish(piece, act)
        return carry

    lax.fori_loop(0, PIECES, one, 0)


def reduced_in_order(reach, summed, act):
    count = PIECES * (reach - 1)
    ahead = 3

    def place(i):
        return reach - 1 - i // PIECES, i % PIECES

    summed.cross_step(reach - 1)
    for i in range(ahead):
        summed.start(*place(i))

    def step(i, carry):
        summed.arrive(*place(i))

        @pl.when(i + ahead < count)
        def _():
            summed.start(*place(i + ahead))

        summed.pass_on(*place(i))

        @pl.when(jnp.logical_and(i % PIECES == 1, i < count - 1))
        def _():
            summed.cross_step(reach - 2 - i // PIECES)

        return carry

    lax.fori_loop(0, count, step, 0)
    summed.cross_step(0)
    summed.start(0, PIECES - 1)
    finish_pieces(summed, act)


def gathered_steps(reach, chain, rows, summed, compute):
    rows.start()

    def step(k, carry):
        @pl.when(k + 1 < reach)
        def _():
            rows.relay(k + 1)

        source = chain.near(k)
        rows.wait_aside(source)

        @pl.when(k == 0)
        def _():
            rows.cross_out()

        @pl.when(k > 0)
        def _():
            rows.cross_relay(k)

        @pl.when(k + 1 == reach)
        def _():
            summed.start(0, 0)

        compute(k, source)
        return carry

    lax.fori_loop(0, reach, step, 0)


def whole_rows(block):
    return block.reshape(-1, block.shape[-1])


def moe_forward_kernel(
    reach,
    tick,
    last,
    own_ref,
    h1_ref,
    ids_ref,
    router_ref,
    wg_hbm,
    wu_hbm,
    wd_hbm,
    *refs,
):
    refs = list(refs)
    if tick == 0:
        tops_ref, *shards = refs[:3]
        refs = refs[3:]
    out_ref, gates_ref, slots_ref, own_gates_ref, picked_hbm, g_hbm, u_hbm = refs[:7]
    refs = refs[7:]
    if tick == 0:
        tops_hbm, *halves = refs[:3]
        refs = refs[3:]
    (
        blocks,
        parts,
        from_x,
        from_z,
        from_cross,
        wg_ref,
        wu_ref,
        wd_ref,
        rows_in,
        rows_out,
        g_slots,
        u_slots,
        picks_of,
        ids_all,
        gather_send,
        gather_recv,
        x_send,
        x_recv,
        z_send,
        z_recv,
        cross_send,
        cross_recv,
        weight_sem,
        keep_sem,
        id_send,
        id_recv,
    ) = refs[:26]
    local = wg_ref.shape[0]
    cap = rows_in.shape[2] // 2
    experts = router_ref.shape[0]
    length = own_ref.shape[0]
    section = lax.axis_index(SECTION)
    chain = Chain(reach)

    def weight_copies():
        return [
            pltpu.make_async_copy(hbm, vmem, weight_sem.at[i])
            for i, (hbm, vmem) in enumerate(
                ((wg_hbm, wg_ref), (wu_hbm, wu_ref), (wd_hbm, wd_ref))
            )
        ]

    def keep_copies(k):
        source = chain.near(k)
        slot = k % 2 if isinstance(k, int) else lax.rem(k, 2)
        return [
            pltpu.make_async_copy(rows_in.at[slot], picked_hbm.at[source], keep_sem.at[0, k]),
            pltpu.make_async_copy(g_slots.at[slot], g_hbm.at[source], keep_sem.at[1, k]),
            pltpu.make_async_copy(u_slots.at[slot], u_hbm.at[source], keep_sem.at[2, k]),
        ]

    def id_copy(target, at):
        return pltpu.make_async_remote_copy(
            src_ref=ids_ref,
            dst_ref=ids_all.at[at],
            send_sem=id_send.at[target],
            recv_sem=id_recv.at[at],
            device_id={EXPERT: target // 2, TENSOR: target % 2},
            device_id_type=MESH_ID,
        )

    def compute(k, source):
        slot = lax.rem(k, 2)

        @pl.when(k == 0)
        def _():
            for copy in weight_copies():
                copy.wait()

        @pl.when(k >= 2)
        def _():
            for copy in keep_copies(k - 2):
                copy.wait()

        gate_of = {}
        ahead = lax.broadcasted_iota(jnp.int32, (length, length), 0)
        behind = lax.broadcasted_iota(jnp.int32, (length, length), 1)
        before = jnp.where(ahead < behind, 1.0, 0.0).astype(jnp.bfloat16)
        named = lax.rem(
            lax.broadcasted_iota(jnp.int32, (experts, length), 0) + chain.me * local, experts
        )
        for i in range(2):
            at = 2 * source + i

            @pl.when(at != chain.me)
            def _():
                id_copy(at, at).wait_recv()

            ids = ids_all[at]
            member = ids[0:1, :] == named
            for pick in range(1, TOPK):
                member = jnp.logical_or(member, ids[pick : pick + 1, :] == named)
            rows = whole_rows(blocks[at])
            gates = masked_softmax(dot(router_ref[...], rows, NT), member)
            gates_ref[at] = gates

            @pl.when(at == chain.me)
            def _():
                own_gates_ref[...] = gates

            mine = jnp.where(member[:8], 1.0, 0.0).astype(jnp.bfloat16)
            taken = jnp.where(member[:8], dot(mine, before), -1.0)
            slots_ref[at] = taken
            for e in range(local):
                picks = one_hot_slots(taken[e : e + 1, :], cap)
                picks_of[i, e * cap : (e + 1) * cap, :] = picks
                gate_of[i, e] = slot_gates(picks, gates[e : e + 1, :])
            gathered = dot(picks_of[i], rows).astype(jnp.bfloat16)
            for e in range(local):
                rows_in[slot, e, i * cap : (i + 1) * cap, :] = gathered[e * cap : (e + 1) * cap, :]
        for e in range(local):
            rows = rows_in[slot, e]
            gate_pre = dot(rows, wg_ref[e])
            up_pre = dot(rows, wu_ref[e])
            g_slots[slot, e] = gate_pre.astype(jnp.bfloat16)
            u_slots[slot, e] = up_pre.astype(jnp.bfloat16)
            hidden = (gate_pre * jax.nn.sigmoid(gate_pre) * up_pre).astype(jnp.bfloat16)
            produced = dot(hidden, wd_ref[e])
            for i in range(2):
                rows_out[i, e * cap : (e + 1) * cap, :] = (
                    produced[i * cap : (i + 1) * cap, :] * gate_of[i, e]
                ).astype(jnp.bfloat16)
        for i in range(2):
            share = dot(picks_of[i], rows_out[i], TN).astype(jnp.bfloat16)
            parts[2 * source + i] = share.reshape(parts.shape[1:])
        for copy in keep_copies(k):
            copy.start()

    def finish(piece, total):
        at = pl.ds(pl.multiple_of(piece * total.shape[0], total.shape[0]), total.shape[0])
        out_ref[at, :] = (h1_ref[at, :] + total).astype(jnp.bfloat16)

    def run():
        for copy in weight_copies():
            copy.start()
        blocks[chain.me] = own_ref[...].reshape(blocks.shape[1:])
        ids_all[chain.me] = ids_ref[...]
        chain.greet_group()
        for target in range(2 * reach):

            @pl.when(target != chain.me)
            def _():
                id_copy(target, chain.me).start()

        rows = Gather(chain, blocks, gather_send, gather_recv)
        summed = Reduce(
            chain,
            lambda home, column, piece: parts.at[2 * home + column, piece],
            from_x,
            from_z,
            (x_send, x_recv, z_send, z_recv),
            cross=(from_cross, cross_send, cross_recv),
        )
        gathered_steps(reach, chain, rows, summed, compute)
        reduced_in_order(reach, summed, finish)
        rows.drain()
        summed.drain()
        for target in range(2 * reach):

            @pl.when(target != chain.me)
            def _():
                id_copy(target, chain.me).wait_send()

        for k in (reach - 2, reach - 1):
            for copy in keep_copies(k):
                copy.wait()

    if tick == 0:
        second_send, second_recv, tops_sem, *refs = refs[26:]
        landed, (stage_sem, own_sem, half_sem, wx_send, wx_recv, core_send, core_recv) = (
            refs[:2],
            refs[2:],
        )
        core = lax.axis_index(DP)
        partner = {DP: 1 - core}
        chunks = local
        pieces = [(i, chunk) for i in range(2) for chunk in range(chunks)]

        def span(i, of_core, chunk):
            rows = shards[i].shape[0] // (2 * chunks)
            return pl.ds((of_core * chunks + chunk) * rows, rows)

        def stage(i, chunk, mine):
            rows, columns = shards[i].shape[0] // (2 * chunks), shards[i].shape[1]
            if mine:
                return rows_in.at[i, chunk, pl.ds(0, rows), pl.ds(0, columns)]
            if i == 0:
                return rows_out.at[chunk // 2, pl.ds(chunk % 2 * rows, rows), pl.ds(0, columns)]
            return from_x.at[chunk, 0, pl.ds(0, rows)]

        def stage_copy(i, chunk, mine):
            at = span(i, core if mine else 1 - core, chunk)
            return pltpu.make_async_copy(
                shards[i].at[at], stage(i, chunk, mine), stage_sem.at[i, chunk, 1 - mine]
            )

        def own_copy(i, chunk, mine):
            at = span(i, core if mine else 1 - core, chunk)
            return pltpu.make_async_copy(
                stage(i, chunk, mine), halves[i].at[chain.x, at], own_sem.at[i, chunk, 1 - mine]
            )

        def half_copy(i):
            return pltpu.make_async_copy(landed[i], halves[i].at[1 - chain.x], half_sem.at[i])

        def weight_x_copy(i, chunk):
            return pltpu.make_async_remote_copy(
                src_ref=stage(i, chunk, 1),
                dst_ref=landed[i].at[span(i, core, chunk)],
                send_sem=wx_send.at[i, chunk],
                recv_sem=wx_recv.at[i, chunk],
                device_id=chain.aside,
                device_id_type=MESH_ID,
            )

        def weight_core_copy(i, chunk, of_core):
            at = landed[i].at[span(i, of_core, chunk)]
            return pltpu.make_async_remote_copy(
                src_ref=at,
                dst_ref=at,
                send_sem=core_send.at[i, chunk],
                recv_sem=core_recv.at[i, chunk],
                device_id=partner,
                device_id_type=MESH_ID,
            )

        @pl.when(section == 0)
        def _():
            run()

        @pl.when(section != 0)
        def _():
            for mine in (1, 0):
                for i, chunk in pieces:
                    stage_copy(i, chunk, mine).start()
            own_tops = [
                pltpu.make_async_copy(
                    tops_ref.at[micro], buffer.at[pl.ds(2 * chain.z, 2)], tops_sem.at[micro]
                )
                for micro, buffer in enumerate((blocks, parts))
            ]
            for copy in own_tops:
                copy.start()
            chain.greet_group(partner)
            for copy in own_tops:
                copy.wait()
            both = (
                Gather(chain, blocks, gather_send, gather_recv, True),
                Gather(chain, parts, second_send, second_recv, True),
            )
            copies = [
                pltpu.make_async_copy(blocks, tops_hbm.at[0], tops_sem.at[0]),
                pltpu.make_async_copy(parts, tops_hbm.at[1], tops_sem.at[1]),
            ]
            both[0].start()
            both[1].start()
            for i, chunk in pieces:
                stage_copy(i, chunk, 1).wait()
                weight_x_copy(i, chunk).start()
                own_copy(i, chunk, 1).start()
            for i, chunk in pieces:
                stage_copy(i, chunk, 0).wait()
                own_copy(i, chunk, 0).start()
            for rows in both:
                for distance in range(1, reach):
                    rows.relay(distance)
                    rows.cross_relay(distance)
            for i, chunk in pieces:
                weight_x_copy(i, chunk).wait_recv()
                weight_core_copy(i, chunk, core).start()
            for i in range(2):
                for chunk in range(chunks):
                    weight_core_copy(i, chunk, 1 - core).wait_recv()
                half_copy(i).start()
            for rows, copy in zip(both, copies):
                for k in range(1, reach):
                    rows.wait_aside(chain.near(k))
                copy.start()
            for rows in both:
                rows.drain()
            for i, chunk in pieces:
                weight_x_copy(i, chunk).wait_send()
                weight_core_copy(i, chunk, core).wait_send()
                for mine in (1, 0):
                    own_copy(i, chunk, mine).wait()
            for i in range(2):
                half_copy(i).wait()
            for copy in copies:
                copy.wait()

    elif tick == last:

        @pl.when(section != 0)
        def _():
            run()

    else:
        run()


def exchange_scratch(reach, length, width):
    piece = (PIECES, length // PIECES, width)
    return [
        pltpu.VMEM((2 * reach,) + piece, jnp.bfloat16),
        pltpu.VMEM((2 * reach,) + piece, jnp.bfloat16),
        pltpu.VMEM((reach,) + piece, jnp.bfloat16),
        pltpu.VMEM((reach + 1,) + piece, jnp.bfloat16),
        pltpu.VMEM((2,) + piece[1:], jnp.bfloat16),
    ]


def exchange_sems(reach):
    dma = pltpu.SemaphoreType.DMA
    return [
        dma((4, reach, PIECES)),
        dma((2 * reach, PIECES)),
        dma((reach, PIECES)),
        dma((reach, PIECES)),
        dma((reach, PIECES)),
        dma((reach + 1, PIECES)),
        dma((2,)),
        dma((2,)),
    ]


def moe_forward_call(reach, tick, last, own, h1, ids, router, wg, wu, wd, firsts):
    length, width = own.shape
    local, _, hidden = wg.shape
    cap = slot_count(length)
    experts = router.shape[0]
    vmem = pl.BlockSpec(memory_space=pltpu.VMEM)
    anywhere = pl.BlockSpec(memory_space=pl.ANY)
    slots = (reach, local, 2 * cap, hidden)
    first = tick == 0
    all_rows = (2 * reach, PIECES, length // PIECES, width)
    return pl.pallas_call(
        functools.partial(moe_forward_kernel, reach, tick, last),
        in_specs=[vmem] * 4 + [anywhere] * 3 + [anywhere] * 3 * first,
        out_specs=[vmem] * 4 + [anywhere] * 3 + [anywhere] * 3 * first,
        out_shape=[
            jax.ShapeDtypeStruct((length, width), jnp.bfloat16),
            jax.ShapeDtypeStruct((2 * reach, experts, length), jnp.float32),
            jax.ShapeDtypeStruct((2 * reach, 8, length), jnp.float32),
            jax.ShapeDtypeStruct((experts, length), jnp.float32),
            jax.ShapeDtypeStruct(slots[:3] + (width,), jnp.bfloat16),
            jax.ShapeDtypeStruct(slots, jnp.bfloat16),
            jax.ShapeDtypeStruct(slots, jnp.bfloat16),
        ]
        + (
            [jax.ShapeDtypeStruct((2,) + all_rows, jnp.bfloat16)]
            + [jax.ShapeDtypeStruct((2,) + shard.shape, shard.dtype) for shard in firsts[1:]]
        )
        * first,
        scratch_shapes=exchange_scratch(reach, length, width)
        + [
            pltpu.VMEM(wg.shape, jnp.bfloat16),
            pltpu.VMEM(wu.shape, jnp.bfloat16),
            pltpu.VMEM(wd.shape, jnp.bfloat16),
            pltpu.VMEM((2, local, 2 * cap, width), jnp.bfloat16),
            pltpu.VMEM((2, local * cap, width), jnp.bfloat16),
            pltpu.VMEM((2,) + slots[1:], jnp.bfloat16),
            pltpu.VMEM((2,) + slots[1:], jnp.bfloat16),
            pltpu.VMEM((2, local * cap, length), jnp.bfloat16),
            pltpu.VMEM((2 * reach, TOPK, length), jnp.int32),
        ]
        + exchange_sems(reach)
        + [
            pltpu.SemaphoreType.DMA((3,)),
            pltpu.SemaphoreType.DMA((3, reach)),
            pltpu.SemaphoreType.DMA((2 * reach,)),
            pltpu.SemaphoreType.DMA((2 * reach,)),
        ]
        + (
            exchange_sems(reach)[:2]
            + [pltpu.SemaphoreType.DMA((2,))]
            + [pltpu.VMEM(shard.shape, shard.dtype) for shard in firsts[1:]]
            + [
                pltpu.SemaphoreType.DMA((2, local, 2)),
                pltpu.SemaphoreType.DMA((2, local, 2)),
                pltpu.SemaphoreType.DMA((2,)),
            ]
            + [pltpu.SemaphoreType.DMA((2, local))] * 4
        )
        * first,
        compiler_params=pltpu.CompilerParams(
            collective_id=1 + tick, has_side_effects=True, vmem_limit_bytes=62 * MIB
        ),
        cost_estimate=pl.CostEstimate(
            flops=20 * 10**9, bytes_accessed=45 * 10**6, transcendentals=2 * 10**6
        ),
        name="moe_forward",
    )(own, h1, ids, router, wg, wu, wd, *(firsts * first))


def moe_backward_kernel(
    reach,
    tick,
    last,
    own_ref,
    slots_first,
    slots_second,
    gates_first,
    gates_second,
    g_first,
    g_second,
    u_first,
    u_second,
    wg_hbm,
    wu_hbm,
    wd_hbm,
    tops_hbm,
    after,
    out_ref,
    home_gates_ref,
    picked_hbm,
    gg_hbm,
    gu_hbm,
    hg_hbm,
    blocks,
    parts,
    from_x,
    from_z,
    from_cross,
    wg_ref,
    wu_ref,
    wd_ref,
    rows_in,
    rows_out,
    g_slots,
    u_slots,
    gg_slots,
    gu_slots,
    hg_slots,
    picks_of,
    gate_parts,
    gate_from,
    gather_send,
    gather_recv,
    x_send,
    x_recv,
    z_send,
    z_recv,
    cross_send,
    cross_recv,
    weight_sem,
    keep_sem,
    load_sem,
    gate_send,
    gate_recv,
    tops_sem,
):
    del after
    local = wg_ref.shape[0]
    cap = rows_in.shape[2] // 2
    section = lax.axis_index(SECTION)
    chain = Chain(reach)
    me = chain.me

    def weight_copies():
        return [
            pltpu.make_async_copy(hbm, vmem, weight_sem.at[i])
            for i, (hbm, vmem) in enumerate(
                ((wd_hbm, wd_ref), (wg_hbm, wg_ref), (wu_hbm, wu_ref))
            )
        ]

    def load_copies(step, source, first):
        slot = step % 2 if isinstance(step, int) else lax.rem(step, 2)
        return [
            pltpu.make_async_copy(
                (g_first if first else g_second).at[source], g_slots.at[slot], load_sem.at[0, step]
            ),
            pltpu.make_async_copy(
                (u_first if first else u_second).at[source], u_slots.at[slot], load_sem.at[1, step]
            ),
        ]

    def keep_copies(step, source):
        slot = step % 2 if isinstance(step, int) else lax.rem(step, 2)
        return [
            pltpu.make_async_copy(rows_in.at[slot], picked_hbm.at[source], keep_sem.at[0, step]),
            pltpu.make_async_copy(gg_slots.at[slot], gg_hbm.at[source], keep_sem.at[1, step]),
            pltpu.make_async_copy(gu_slots.at[slot], gu_hbm.at[source], keep_sem.at[2, step]),
            pltpu.make_async_copy(hg_slots.at[slot], hg_hbm.at[source], keep_sem.at[3, step]),
        ]

    def gate_copy(target, at):
        return pltpu.make_async_remote_copy(
            src_ref=gate_parts.at[target],
            dst_ref=gate_from.at[at],
            send_sem=gate_send.at[target],
            recv_sem=gate_recv.at[at],
            device_id={EXPERT: target // 2, TENSOR: target % 2},
            device_id_type=MESH_ID,
        )

    def compute(step, source_of, first):
        source = source_of(step)
        slot = lax.rem(step, 2)

        @pl.when(step == 0)
        def _():
            for copy in weight_copies():
                copy.wait()

        @pl.when(step >= 2)
        def _():
            for copy in keep_copies(step - 2, source_of(step - 2)):
                copy.wait()

        for copy in load_copies(step, source, first):
            copy.wait()
        slots_ref = slots_first if first else slots_second
        gates_ref = gates_first if first else gates_second
        gate_of = {}
        for i in range(2):
            at = 2 * source + i
            for e in range(local):
                picks = one_hot_slots(slots_ref[at, e : e + 1, :], cap)
                picks_of[i, e * cap : (e + 1) * cap, :] = picks
                gate_of[i, e] = slot_gates(picks, gates_ref[at, e : e + 1, :])
            gathered = dot(picks_of[i], whole_rows(blocks[at])).astype(jnp.bfloat16)
            for e in range(local):
                rows_in[slot, e, i * cap : (i + 1) * cap, :] = gathered[e * cap : (e + 1) * cap, :]
        for e in range(local):
            plain = dot(rows_in[slot, e], wd_ref[e], NT)
            gate_pre = g_slots[slot, e].astype(jnp.float32)
            up_pre = u_slots[slot, e].astype(jnp.float32)
            sg = jax.nn.sigmoid(gate_pre)
            hidden = gate_pre * sg * up_pre
            gate_col = jnp.concatenate([gate_of[i, e] for i in range(2)], axis=0)
            grad_gate_col = jnp.sum(hidden * plain, axis=1, keepdims=True)
            grad_hidden = plain * gate_col
            grad_gate = (grad_hidden * up_pre * sg * (1.0 + gate_pre * (1.0 - sg))).astype(
                jnp.bfloat16
            )
            grad_up = (grad_hidden * gate_pre * sg).astype(jnp.bfloat16)
            gg_slots[slot, e] = grad_gate
            gu_slots[slot, e] = grad_up
            hg_slots[slot, e] = (hidden * gate_col).astype(jnp.bfloat16)
            grad_rows = dot(grad_gate, wg_ref[e], NT) + dot(grad_up, wu_ref[e], NT)
            for i in range(2):
                at = 2 * source + i
                rows = slice(i * cap, (i + 1) * cap)
                rows_out[i, e * cap : (e + 1) * cap, :] = grad_rows[rows, :].astype(jnp.bfloat16)
                picks = picks_of[i, e * cap : (e + 1) * cap, :].astype(jnp.float32)
                gate_parts[at, e : e + 1, :] = jnp.sum(
                    picks * grad_gate_col[rows, :], axis=0, keepdims=True
                )
        for i in range(2):
            share = dot(picks_of[i], rows_out[i], TN).astype(jnp.bfloat16)
            parts[2 * source + i] = share.reshape(parts.shape[1:])
        for copy in keep_copies(step, source):
            copy.start()

        @pl.when(step + 2 < reach)
        def _():
            for copy in load_copies(step + 2, source_of(step + 2), first):
                copy.start()

        for i in range(2):
            at = 2 * source + i

            @pl.when(at != me)
            def _():
                gate_copy(at, me).start()

    def finish(piece, total):
        at = pl.ds(pl.multiple_of(piece * total.shape[0], total.shape[0]), total.shape[0])
        out_ref[at, :] = total

    def run(gathered):
        first = gathered

        def source_of(step):
            if isinstance(step, int):
                return chain.near(step if gathered else reach - 1 - step)
            return chain.near(step if gathered else reach - 1 - step)

        def top_copy(step):
            pair = pl.ds(2 * source_of(step), 2)
            return pltpu.make_async_copy(
                tops_hbm.at[min(tick, 1), pair], blocks.at[pair], tops_sem.at[step]
            )

        for step in range(2):
            for copy in load_copies(step, source_of(step), first):
                copy.start()
        if not gathered:
            for step in range(reach):
                top_copy(step).start()
        for copy in weight_copies():
            copy.start()
        chain.greet_group()
        summed = Reduce(
            chain,
            lambda home, column, piece: parts.at[2 * home + column, piece],
            from_x,
            from_z,
            (x_send, x_recv, z_send, z_recv),
            cross=(from_cross, cross_send, cross_recv),
        )
        if gathered:
            blocks[me] = own_ref[...].reshape(blocks.shape[1:])
            rows = Gather(chain, blocks, gather_send, gather_recv)
            gathered_steps(
                reach, chain, rows, summed, lambda step, source: compute(step, source_of, first)
            )
            reduced_in_order(reach, summed, finish)
            rows.drain()
        else:

            def step_back(step, carry):
                k = reach - 1 - step
                top_copy(step).wait()
                compute(step, source_of, first)
                summed.start(k, 0)

                @pl.when(k > 0)
                def _():
                    summed.start(k, PIECES - 1)
                    summed.cross_step(k)

                @pl.when(step >= 1)
                def _():
                    for piece in range(PIECES):
                        summed.arrive(k + 1, piece)
                        summed.pass_on(k + 1, piece)

                return carry

            lax.fori_loop(0, reach, step_back, 0)
            summed.cross_step(0)
            summed.start(0, PIECES - 1)
            finish_pieces(summed, finish)
        summed.drain()
        home_gates_ref[0] = gate_parts[me, :local]
        for at in range(2 * reach):

            @pl.when(at != me)
            def _():
                gate_copy(at, me).wait_send()
                gate_copy(at, at).wait_recv()
                home_gates_ref[lax.rem(at - me + 2 * reach, 2 * reach)] = gate_from[at, :local]

        for step in (reach - 2, reach - 1):
            for copy in keep_copies(step, source_of(step)):
                copy.wait()

    if tick > 0:

        @pl.when(section == 0)
        def _():
            run(True)

    if tick < last:

        @pl.when(section != 0)
        def _():
            run(False)


def moe_backward_call(
    reach, tick, last, own, slots_two, gates_two, g_two, u_two, wg, wu, wd, tops, after
):
    length, width = own.shape
    local, _, hidden = wg.shape
    cap = slot_count(length)
    vmem = pl.BlockSpec(memory_space=pltpu.VMEM)
    anywhere = pl.BlockSpec(memory_space=pl.ANY)
    slot_rows = (reach, local, 2 * cap, hidden)
    kept = jax.ShapeDtypeStruct(slot_rows, jnp.bfloat16)
    return pl.pallas_call(
        functools.partial(moe_backward_kernel, reach, tick, last),
        in_specs=[vmem] * 5 + [anywhere] * 9,
        out_specs=[vmem, vmem] + [anywhere] * 4,
        out_shape=[
            jax.ShapeDtypeStruct((length, width), jnp.float32),
            jax.ShapeDtypeStruct((2 * reach, local, length), jnp.float32),
            jax.ShapeDtypeStruct(slot_rows[:3] + (width,), jnp.bfloat16),
            kept,
            kept,
            kept,
        ],
        scratch_shapes=exchange_scratch(reach, length, width)
        + [
            pltpu.VMEM(wg.shape, jnp.bfloat16),
            pltpu.VMEM(wu.shape, jnp.bfloat16),
            pltpu.VMEM(wd.shape, jnp.bfloat16),
            pltpu.VMEM((2, local, 2 * cap, width), jnp.bfloat16),
            pltpu.VMEM((2, local * cap, width), jnp.bfloat16),
        ]
        + [pltpu.VMEM((2,) + slot_rows[1:], jnp.bfloat16)] * 5
        + [
            pltpu.VMEM((2, local * cap, length), jnp.bfloat16),
            pltpu.VMEM((2 * reach, 8, length), jnp.float32),
            pltpu.VMEM((2 * reach, 8, length), jnp.float32),
        ]
        + exchange_sems(reach)
        + [
            pltpu.SemaphoreType.DMA((3,)),
            pltpu.SemaphoreType.DMA((4, reach)),
            pltpu.SemaphoreType.DMA((2, reach)),
            pltpu.SemaphoreType.DMA((2 * reach,)),
            pltpu.SemaphoreType.DMA((2 * reach,)),
            pltpu.SemaphoreType.DMA((reach,)),
        ],
        compiler_params=pltpu.CompilerParams(
            collective_id=4 + tick, has_side_effects=True, vmem_limit_bytes=62 * MIB
        ),
        cost_estimate=pl.CostEstimate(
            flops=20 * 10**9, bytes_accessed=55 * 10**6, transcendentals=2 * 10**6
        ),
        name="moe_backward",
    )(own, *slots_two, *gates_two, *g_two, *u_two, wg, wu, wd, tops, after)


def middle_weights_kernel(
    x_first, x_second, dh_ref, gg_ref, gu_ref, hg_ref, after, wg_ref, wu_ref, wd_ref
):
    del after
    hidden = gg_ref.shape[3]
    wide = dh_ref.shape[3]
    rows = of_section(x_first, x_second).reshape(-1, wide)
    wg_ref[0] = dot(rows, gg_ref[...].reshape(-1, hidden), TN).astype(jnp.bfloat16)
    wu_ref[0] = dot(rows, gu_ref[...].reshape(-1, hidden), TN).astype(jnp.bfloat16)
    wd_ref[0] = dot(
        hg_ref[...].reshape(-1, hidden), dh_ref[...].reshape(-1, wide), TN
    ).astype(jnp.bfloat16)


def middle_weights(x_two, dh, gg, gu, hg, after):
    groups, local, rows, width = dh.shape
    hidden = gg.shape[3]
    tiles = width // hidden
    wide = width // tiles
    tiled = pl.BlockSpec((groups, 1, rows, wide), lambda e, t: (0, e, 0, t))
    held = pl.BlockSpec((groups, 1, rows, hidden), lambda e, t: (0, e, 0, 0))
    up = jax.ShapeDtypeStruct((local, width, hidden), jnp.bfloat16)
    return pl.pallas_call(
        middle_weights_kernel,
        grid=(local, tiles),
        in_specs=[tiled] * 3 + [held] * 3 + [pl.BlockSpec(memory_space=pl.ANY)],
        out_specs=[
            pl.BlockSpec((1, wide, hidden), lambda e, t: (e, t, 0)),
            pl.BlockSpec((1, wide, hidden), lambda e, t: (e, t, 0)),
            pl.BlockSpec((1, hidden, wide), lambda e, t: (e, 0, t)),
        ],
        out_shape=[up, up, jax.ShapeDtypeStruct((local, hidden, width), jnp.bfloat16)],
        compiler_params=pltpu.CompilerParams(vmem_limit_bytes=62 * MIB),
        cost_estimate=pl.CostEstimate(
            flops=30 * 10**9, bytes_accessed=60 * 10**6, transcendentals=0
        ),
        name="middle_weights",
    )(*x_two, dh, gg, gu, hg, after)


def tail_kernel(
    reach,
    tiles,
    dense_hbm,
    x_hbm,
    dh_first,
    dh_last,
    gg_first,
    gg_last,
    gu_first,
    gu_last,
    hg_first,
    hg_last,
    wg_before,
    wu_before,
    wd_before,
    small_first,
    small_both,
    small_last,
    ends_back_one,
    ends_forward_one,
    ends_back_two,
    ends_forward_two,
    query_out,
    key_out,
    value_out,
    out_out,
    wg_out,
    wu_out,
    wd_out,
    small_out,
    ends_out,
    mine,
    from_core,
    from_x,
    from_z,
    whole,
    x_rows,
    dh_rows,
    slots,
    before,
    wg_tile,
    wu_tile,
    wd_tile,
    wg_from,
    wu_from,
    wd_from,
    small_held,
    small_came,
    small_z,
    ends_held,
    ends_came,
    mine_sem,
    core_send,
    core_recv,
    x_send,
    x_recv,
    z_send,
    z_recv,
    ring_send,
    ring_recv,
    last_send,
    last_recv,
    out_sem,
    row_sem,
    slot_sem,
    before_sem,
    tile_sem,
    tile_send,
    tile_recv,
    free_sem,
    small_send,
    small_recv,
    ends_load,
    ends_keep,
    ends_send,
    ends_recv,
):
    section = lax.axis_index(SECTION)
    core = lax.axis_index(DP)
    partner = {DP: 1 - core}
    chain = Chain(reach)
    x = chain.x
    z = chain.z
    quarter = mine.shape[3]
    local = gg_first.shape[1]
    width = x_hbm.shape[3]
    hidden = gg_first.shape[3]
    wide = width // tiles

    def mine_copy(half):
        return pltpu.make_async_copy(dense_hbm.at[half, core], mine.at[half], mine_sem.at[half])

    def core_copy(half, piece):
        return pltpu.make_async_remote_copy(
            src_ref=dense_hbm.at[half, 1 - core, :, piece],
            dst_ref=from_core.at[half, :, piece],
            send_sem=core_send.at[half, piece],
            recv_sem=core_recv.at[half, piece],
            device_id=partner,
            device_id_type=MESH_ID,
        )

    def add_core(half, k, piece):
        home = chain.near(k)

        @pl.when(k == reach - 1)
        def _():
            core_copy(half, piece).wait_recv()

        mine[half, home, piece] = (
            mine[half, home, piece].astype(jnp.float32)
            + from_core[half, home, piece].astype(jnp.float32)
        ).astype(jnp.bfloat16)

    summed = Reduce(
        chain,
        lambda home, column, piece: mine.at[column, home, piece],
        from_x,
        from_z,
        (x_send, x_recv, z_send, z_recv),
        TAIL_PIECES,
    )

    def ring_copy(source, piece, way, target):
        return pltpu.make_async_remote_copy(
            src_ref=whole.at[core, source, piece],
            dst_ref=whole.at[core, source, piece],
            send_sem=ring_send.at[way, source, piece],
            recv_sem=ring_recv.at[source, piece],
            device_id=target,
            device_id_type=MESH_ID,
        )

    def last_copy(source, piece, side):
        return pltpu.make_async_remote_copy(
            src_ref=whole.at[side, source, piece],
            dst_ref=whole.at[side, source, piece],
            send_sem=last_send.at[source, piece],
            recv_sem=last_recv.at[source, piece],
            device_id=partner,
            device_id_type=MESH_ID,
        )

    def out_copies(side, source):
        block = whole.at[side, source]
        at = side * reach + source
        first = query_out.shape[3]
        second = first + key_out.shape[3]
        third = second + value_out.shape[3]
        half = block.shape[2] - third
        columns = pl.ds(pl.multiple_of(side * half, half), half)
        return [
            pltpu.make_async_copy(block.at[:, :, found], to, out_sem.at[side, source, i])
            for i, (found, to) in enumerate(
                (
                    (pl.ds(0, first), query_out.at[at]),
                    (pl.ds(first, second - first), key_out.at[at]),
                    (pl.ds(second, third - second), value_out.at[at]),
                    (pl.ds(third, half), out_out.at[source, :, :, columns]),
                )
            )
        ]

    def spread_block(source, piece, up, down):
        if up:

            @pl.when(chain.has_above)
            def _():
                ring_copy(source, piece, 0, chain.above).start()

        if down:

            @pl.when(chain.has_below)
            def _():
                ring_copy(source, piece, 1, chain.below).start()

        last_copy(source, piece, core).start()

        @pl.when(piece == TAIL_PIECES - 1)
        def _():
            for copy in out_copies(core, source):
                copy.start()

    def relay(distance, piece):
        @pl.when(z - distance >= 0)
        def _():
            ring_copy(z - distance, piece, 0, chain.below).wait_recv()
            spread_block(z - distance, piece, True, False)

        @pl.when(z + distance <= reach - 1)
        def _():
            ring_copy(z + distance, piece, 1, chain.above).wait_recv()
            spread_block(z + distance, piece, False, True)

    depth = wg_tile.shape[0]

    def spot(index):
        expert = index // tiles
        return expert, pl.ds(pl.multiple_of(lax.rem(index, tiles) * wide, wide), wide)

    def tile_loads(index, first):
        expert, at = spot(index)
        slot = lax.rem(index, 2)
        back = dh_last if first else dh_first
        return [
            pltpu.make_async_copy(
                x_hbm.at[:, expert, :, at], x_rows.at[slot], row_sem.at[slot, 0]
            ),
            pltpu.make_async_copy(
                back.at[:, expert, :, at], dh_rows.at[slot], row_sem.at[slot, 1]
            ),
        ] + [
            pltpu.make_async_copy(ref, before.at[slot, i], before_sem.at[slot, i])
            for i, ref in enumerate(
                (wg_before.at[expert, at], wu_before.at[expert, at], wd_before.at[expert, :, at])
            )
        ]

    def slot_loads(expert, first):
        slot = lax.rem(expert, 2)
        return [
            pltpu.make_async_copy(
                (two if first else one).at[:, expert], slots.at[slot, i], slot_sem.at[slot, i]
            )
            for i, (one, two) in enumerate(
                ((gg_first, gg_last), (gu_first, gu_last), (hg_first, hg_last))
            )
        ]

    def start(copies):
        @pl.when(section == 0)
        def _():
            for copy in copies(True):
                copy.start()

        @pl.when(section != 0)
        def _():
            for copy in copies(False):
                copy.start()

    held = ((wg_tile, wg_from), (wu_tile, wu_from), (wd_tile, wd_from))

    def tile_sends(index):
        slot = lax.rem(index, depth)
        return [
            pltpu.make_async_remote_copy(
                src_ref=tile.at[slot],
                dst_ref=came.at[slot],
                send_sem=tile_send.at[slot, i],
                recv_sem=tile_recv.at[slot, i],
                device_id=partner,
                device_id_type=MESH_ID,
            )
            for i, (tile, came) in enumerate(held)
        ]

    def tile_stores(index):
        expert, at = spot(index)
        slot = lax.rem(index, depth)
        outs = (wg_out.at[expert, at], wu_out.at[expert, at], wd_out.at[expert, :, at])
        return [
            pltpu.make_async_copy(came.at[slot], out, tile_sem.at[slot, i])
            for i, ((_, came), out) in enumerate(zip(held, outs))
        ]

    count = local * tiles

    def sum_tile(index):
        slot = lax.rem(index, depth)
        for copy, (tile, came) in zip(tile_sends(index), held):
            copy.wait_recv()
            came[slot] = (
                tile[slot].astype(jnp.float32) + came[slot].astype(jnp.float32)
            ).astype(jnp.bfloat16)
        for copy in tile_stores(index):
            copy.start()

    def one_tile(index):
        slot = lax.rem(index, 2)
        expert = index // tiles
        taken = lax.rem(expert, 2)

        @pl.when(index + 1 < count)
        def _():
            start(functools.partial(tile_loads, index + 1))

        @pl.when(jnp.logical_and(lax.rem(index, tiles) == 0, expert + 1 < local))
        def _():
            start(functools.partial(slot_loads, expert + 1))

        @pl.when(lax.rem(index, tiles) == 0)
        def _():
            for copy in slot_loads(expert, True):
                copy.wait()

        for copy in tile_loads(index, True):
            copy.wait()

        @pl.when(index >= depth)
        def _():
            for copy in tile_sends(index - depth):
                copy.wait_send()
            for copy in tile_stores(index - depth):
                copy.wait()
            pl.semaphore_signal(free_sem, inc=1, device_id=partner, device_id_type=MESH_ID)
            pl.semaphore_wait(free_sem, 1)

        to = lax.rem(index, depth)
        rows = x_rows[slot].reshape(-1, wide)
        found = (
            dot(rows, slots[taken, 0].reshape(-1, hidden), TN),
            dot(rows, slots[taken, 1].reshape(-1, hidden), TN),
            dot(slots[taken, 2].reshape(-1, hidden), dh_rows[slot].reshape(-1, wide), TN),
        )
        for i, (one, (tile, _)) in enumerate(zip(found, held)):
            tile[to] = (one + before[slot, i].astype(jnp.float32)).astype(jnp.bfloat16)
        for copy in tile_sends(index):
            copy.start()

        @pl.when(index >= 1)
        def _():
            sum_tile(index - 1)

    def tile_run(low, high):
        lax.fori_loop(low, high, lambda index, carry: (one_tile(index), carry)[1], 0)

    def small_copy(to, i):
        if i < 2:
            return pltpu.make_async_remote_copy(
                src_ref=small_held.at[i],
                dst_ref=small_came.at[i],
                send_sem=small_send.at[i],
                recv_sem=small_recv.at[i],
                device_id=to,
                device_id_type=MESH_ID,
            )
        return pltpu.make_async_remote_copy(
            src_ref=small_z.at[z],
            dst_ref=small_z.at[z],
            send_sem=small_send.at[2 + to],
            recv_sem=small_recv.at[2 + z],
            device_id={EXPERT: to},
            device_id_type=MESH_ID,
        )

    def others(act):
        for other in range(reach):

            @pl.when(other != z)
            def _():
                act(other)

    def small_step(stage):
        if stage == 0:
            total = small_both[...] + of_section(small_last, small_first)
            experts = 2 * reach * local
            small_held[0, :experts] = pltpu.roll(total[:experts], chain.me * local, 0)
            small_held[0, experts:] = total[experts:]
            small_copy(partner, 0).start()
        elif stage == 1:
            small_copy(partner, 0).wait_recv()
            small_held[1] = small_held[0] + small_came[0]
            small_copy(chain.aside, 1).start()
        elif stage == 2:
            small_copy(chain.aside, 1).wait_recv()
            small_z[z] = small_held[1] + small_came[1]
            others(lambda other: small_copy(other, 2).start())
        else:

            def wait(other):
                pltpu.make_async_remote_copy(
                    src_ref=small_z.at[other],
                    dst_ref=small_z.at[other],
                    send_sem=small_send.at[2 + other],
                    recv_sem=small_recv.at[2 + other],
                    device_id={EXPERT: other},
                    device_id_type=MESH_ID,
                ).wait_recv()

            others(wait)
            total = small_z[0]
            for other in range(1, reach):
                total = total + small_z[other]
            small_out[...] = total

    ends_of = ((ends_back_one, ends_forward_one), (ends_back_two, ends_forward_two))

    def ends_copy(m):
        return pltpu.make_async_remote_copy(
            src_ref=ends_held.at[m],
            dst_ref=ends_came.at[m],
            send_sem=ends_send.at[m],
            recv_sem=ends_recv.at[m],
            device_id=chain.aside,
            device_id_type=MESH_ID,
        )

    def ends_store(m, other):
        found = ends_came if other else ends_held
        at = 1 - x if other else x
        return pltpu.make_async_copy(found.at[m], ends_out.at[m, at], ends_keep.at[m, int(other)])

    for half in range(2):
        mine_copy(half).start()
    for m in range(2):
        start_of_section(*ends_of[m], ends_held.at[m], ends_load.at[m])

    barrier = pltpu.get_barrier_semaphore()
    pl.semaphore_signal(barrier, inc=1, device_id=partner, device_id_type=MESH_ID)
    pl.semaphore_signal(barrier, inc=1, device_id=chain.aside, device_id_type=MESH_ID)
    others(
        lambda other: pl.semaphore_signal(
            barrier, inc=1, device_id={EXPERT: other}, device_id_type=MESH_ID
        )
    )
    pl.semaphore_wait(barrier, 1 + reach)

    def core_start(piece):
        for half in (1 - x, x):
            core_copy(half, piece).start()

    for piece in range(2):
        core_start(piece)
    small_step(0)
    start(functools.partial(slot_loads, 0))
    start(functools.partial(tile_loads, 0))
    for m in range(2):
        pltpu.make_async_copy(ends_of[m][0], ends_held.at[m], ends_load.at[m]).wait()
        ends_store(m, False).start()
    ends_copy(0).start()
    for half in range(2):
        mine_copy(half).wait()

    steps = TAIL_PIECES * reach
    ahead = 3

    def place(i):
        return reach - 1 - i % reach, i // reach

    def launch(i):
        k, piece = place(i)
        add_core(1 - x, k, piece)
        summed.start(k, piece)

    def finish(piece, total):
        whole[core, z, piece] = total.astype(jnp.bfloat16)

    def late(i):
        def due(offset, act):
            since = i - offset
            if isinstance(i, int):
                if since >= 0 and since % reach == 0 and since // reach < TAIL_PIECES:
                    act(since // reach)
            else:

                @pl.when(jnp.logical_and(since >= 0, lax.rem(since, reach) == 0))
                def _():
                    act(since // reach)

        def own(piece):
            summed.finish(piece, finish)
            spread_block(z, piece, True, True)

        due(reach + 1, own)
        for distance in range(1, reach):
            due(reach + 1 + 2 * distance, functools.partial(relay, distance))

    for i in range(ahead):
        launch(i)
    small_step(1)

    def step(i, carry):
        k, piece = place(i)

        @pl.when(jnp.logical_and(k == reach - 1, piece + 2 < TAIL_PIECES))
        def _():
            core_start(piece + 2)

        @pl.when(jnp.logical_and(k > 0, piece * (reach - 1) + reach - 1 - k < count))
        def _():
            one_tile(piece * (reach - 1) + reach - 1 - k)

        @pl.when(i == reach)
        def _():
            small_step(2)

        summed.arrive(k, piece)

        @pl.when(i + ahead < steps)
        def _():
            launch(i + ahead)

        add_core(x, k, piece)

        @pl.when(k > 0)
        def _():
            summed.pass_on(k, piece)

        late(i)
        return carry

    lax.fori_loop(0, steps, step, 0)
    done = min(count, TAIL_PIECES * (reach - 1))
    ends_copy(1).start()
    small_step(3)
    for i in range(steps, steps + 3 * reach):
        late(i)
    tile_run(done, count)
    sum_tile(count - 1)

    def settle_last(source, carry):
        for piece in range(TAIL_PIECES):
            last_copy(source, piece, 1 - core).wait_recv()
        for copy in out_copies(1 - core, source):
            copy.start()
        return carry

    lax.fori_loop(0, reach, settle_last, 0)
    for m in range(2):
        ends_copy(m).wait_recv()
        ends_store(m, True).start()

    summed.drain()

    def settle_sends(source, carry):
        for piece in range(TAIL_PIECES):
            last_copy(source, piece, core).wait_send()

            @pl.when(jnp.logical_and(chain.has_above, z >= source))
            def _():
                ring_copy(source, piece, 0, chain.above).wait_send()

            @pl.when(jnp.logical_and(chain.has_below, z <= source))
            def _():
                ring_copy(source, piece, 1, chain.below).wait_send()

        for side in range(2):
            for copy in out_copies(side, source):
                copy.wait()
        return carry

    lax.fori_loop(0, reach, settle_sends, 0)
    for piece in range(TAIL_PIECES):
        for half in range(2):
            core_copy(half, piece).wait_send()
    for m in range(2):
        ends_copy(m).wait_send()
        for other in (False, True):
            ends_store(m, other).wait()
    small_copy(partner, 0).wait_send()
    small_copy(chain.aside, 1).wait_send()
    others(lambda other: small_copy(other, 2).wait_send())
    def settle_tiles(index, carry):
        for copy in tile_sends(index):
            copy.wait_send()
        for copy in tile_stores(index):
            copy.wait()
        return carry

    lax.fori_loop(count - depth, count, settle_tiles, 0)


def tail_call(reach, widths, dense, x_rows, dh_two, gg_two, gu_two, hg_two, before, smalls, ends):
    halves, cores, _, _, quarter, columns = dense.shape
    groups, local, slot_rows, width = x_rows.shape
    hidden = gg_two[0].shape[3]
    tiles = width // hidden
    wide = width // tiles
    anywhere = pl.BlockSpec(memory_space=pl.ANY)
    vmem = pl.BlockSpec(memory_space=pltpu.VMEM)
    end = ends[0].shape
    up = jax.ShapeDtypeStruct((local, width, hidden), jnp.bfloat16)
    down = jax.ShapeDtypeStruct((local, hidden, width), jnp.bfloat16)
    block = (TAIL_PIECES, quarter, columns)
    dma = pltpu.SemaphoreType.DMA
    return pl.pallas_call(
        functools.partial(tail_kernel, reach, tiles),
        in_specs=[anywhere] * 13 + [vmem] * 3 + [anywhere] * 4,
        out_specs=[anywhere] * 7 + [vmem, anywhere],
        out_shape=[
            jax.ShapeDtypeStruct((cores * reach, TAIL_PIECES, quarter, one), jnp.bfloat16)
            for one in widths
        ]
        + [
            jax.ShapeDtypeStruct((reach, TAIL_PIECES, quarter, width), jnp.bfloat16),
            up,
            up,
            down,
            jax.ShapeDtypeStruct(smalls[0].shape, jnp.float32),
            jax.ShapeDtypeStruct((2, 2) + end, jnp.bfloat16),
        ],
        scratch_shapes=[
            pltpu.VMEM((halves, reach) + block, jnp.bfloat16),
            pltpu.VMEM((halves, reach) + block, jnp.bfloat16),
            pltpu.VMEM((reach,) + block, jnp.bfloat16),
            pltpu.VMEM((reach + 1,) + block, jnp.bfloat16),
            pltpu.VMEM((cores, reach) + block, jnp.bfloat16),
            pltpu.VMEM((2, groups, slot_rows, wide), jnp.bfloat16),
            pltpu.VMEM((2, groups, slot_rows, wide), jnp.bfloat16),
            pltpu.VMEM((2, 3, groups, slot_rows, hidden), jnp.bfloat16),
            pltpu.VMEM((2, 3, wide, hidden), jnp.bfloat16),
        ]
        + [pltpu.VMEM((3, wide, hidden), jnp.bfloat16)] * 6
        + [pltpu.VMEM((count,) + smalls[0].shape, jnp.float32) for count in (2, 2, reach)]
        + [pltpu.VMEM((2,) + end, jnp.bfloat16)] * 2
        + [
            dma((halves,)),
            dma((halves, TAIL_PIECES)),
            dma((halves, TAIL_PIECES)),
            dma((reach, TAIL_PIECES)),
            dma((reach, TAIL_PIECES)),
            dma((reach, TAIL_PIECES)),
            dma((reach + 1, TAIL_PIECES)),
            dma((2, reach, TAIL_PIECES)),
            dma((reach, TAIL_PIECES)),
            dma((reach, TAIL_PIECES)),
            dma((reach, TAIL_PIECES)),
            dma((cores, reach, 4)),
            dma((2, 2)),
            dma((2, 3)),
            dma((2, 3)),
            dma((3, 3)),
            dma((3, 3)),
            dma((3, 3)),
            pltpu.SemaphoreType.REGULAR,
            dma((2 + reach,)),
            dma((2 + reach,)),
            dma((2,)),
            dma((2, 2)),
            dma((2,)),
            dma((2,)),
        ],
        compiler_params=pltpu.CompilerParams(
            collective_id=7, has_side_effects=True, vmem_limit_bytes=62 * MIB
        ),
        cost_estimate=pl.CostEstimate(
            flops=60 * 10**9, bytes_accessed=120 * 10**6, transcendentals=0
        ),
        name="tail",
    )(dense, x_rows, *dh_two, *gg_two, *gu_two, *hg_two, *before, *smalls, *ends)


GROUP = (EXPERT, TENSOR)
ROWS = (DP, EXPERT)


def by_rows(
    boundary,
    segments,
    expert_ids,
    attn_gain,
    query_weight,
    key_weight,
    value_weight,
    out_weight,
    ffn_gain,
    router_weight,
    gate_weight,
    up_weight,
    down_weight,
):
    args = (
        boundary,
        segments,
        expert_ids,
        attn_gain,
        query_weight,
        key_weight,
        value_weight,
        out_weight,
        ffn_gain,
        router_weight,
        gate_weight,
        up_weight,
        down_weight,
    )
    share_rows = expert_ids.shape[2]
    local = gate_weight.shape[1]
    if (
        share_rows != LEN
        or lax.axis_size(TENSOR) != 2
        or lax.axis_size(SECTION) != 2
        or lax.axis_size(DP) != 2
        or query_weight.shape[2] % (4 * HD)
    ):
        return on_device(*args)
    section = lax.axis_index(SECTION)
    tensor = lax.axis_index(TENSOR)
    group_at = lax.axis_index(EXPERT) * lax.axis_size(TENSOR) + tensor
    micro_count = boundary.shape[1]
    reach = lax.axis_size(EXPERT)
    group = query_weight.shape[2] // key_weight.shape[2]
    own_rows = lax.dynamic_slice_in_dim(boundary[0], tensor * share_rows, share_rows, 1)
    own_seg = lax.dynamic_slice_in_dim(segments, tensor * share_rows, share_rows, 1)
    own_ids = jnp.swapaxes(expert_ids[0], 1, 2)
    gains = (attn_gain, ffn_gain)
    tables = pair_tables(LEN)

    wqkv_part = jnp.concatenate([query_weight[0], key_weight[0], value_weight[0]], axis=1)
    wo_part = out_weight[0]
    wqkv = wo = None
    router_local = jnp.roll(router_weight[0].T, -group_at * local, axis=0)
    wg, wu, wd = gate_weight[0], up_weight[0], down_weight[0]

    def pick(array, index):
        return lax.dynamic_index_in_dim(array, index, 0, keepdims=False)

    arrived = None
    kept = []
    wide = []
    outputs = []
    for tick in range(micro_count + 1):
        micro = jnp.clip(tick - section, 0, micro_count - 1)
        if tick == 0:
            layer_in = own_rows[0]
            h1, xn2 = attn_split(
                boundary[0, 0].reshape(2, share_rows, -1),
                segments[0].reshape(2, share_rows),
                gains,
                wqkv_part,
                wo_part,
                tables,
                group,
            )
        else:
            layer_in = arrived
            h1, xn1, qkv, att, xn2 = attn_forward(
                own_rows[tick] if tick < micro_count else arrived,
                arrived,
                pick(own_seg, micro),
                gains,
                wqkv,
                wo,
                tables,
                group,
            )
        h2, gates, slots, own_gates, picked, gate_pre, up_pre, *firsts = moe_forward_call(
            reach,
            tick,
            micro_count,
            xn2,
            h1,
            pick(own_ids, micro),
            router_local,
            wg,
            wu,
            wd,
            [
                boundary[0].reshape(micro_count, 2, PIECES, share_rows // PIECES, -1),
                wqkv_part,
                wo_part,
            ],
        )
        outputs.append(h2)
        arrived = shifted(h2, SECTION, 1)
        if tick == 0:
            tops, *before = firsts
            wqkv, wo = both_halves(wqkv_part, wo_part, h2, before)
            xn1, qkv, att = attn_again(own_rows[0], own_seg[0], attn_gain, wqkv, tables, group)
        kept.append((layer_in, h1, xn2, own_gates, qkv, slots, gates, xn1, att))
        wide.append((picked, gate_pre, up_pre))

    arrived = jnp.zeros(own_rows.shape[1:], jnp.bfloat16)
    backs = []
    slotted = []
    for tick in range(micro_count + 1):
        micro = jnp.clip(tick - (1 - section), 0, micro_count - 1)
        ticks = {0: (1, 1), 1: (0, 2), 2: (1, 1)}[tick]
        pairs = list(zip(*(kept[one] for one in ticks)))
        sides = [wide[one] for one in ticks]
        if tick == micro_count:
            pairs[0] = (own_rows[1], own_rows[1])
            pairs.insert(5, (arrived, arrived))
        elif tick == 0:
            pairs.insert(5, (own_rows[0], own_rows[0]))
        else:
            pairs.insert(5, (arrived, own_rows[1]))
        rows, grad_gates, picked, gg, gu, hg = moe_backward_call(
            reach,
            tick,
            micro_count,
            arrived,
            pairs[6],
            pairs[7],
            [side[1] for side in sides],
            [side[2] for side in sides],
            wg,
            wu,
            wd,
            tops,
            before[0] if tick == micro_count else tops,
        )
        grad_in, mid, dqkv, small = attn_backward(
            pairs[:6],
            rows,
            grad_gates.reshape(EXPERTS, LEN),
            pick(own_seg, micro),
            gains,
            router_local,
            wqkv,
            wo,
            tables,
            group,
        )
        arrived = shifted(grad_in, SECTION, -1)
        backs.append((grad_in, mid, dqkv, small))
        slotted.append((picked, gg, gu, hg))
        if tick == 1:
            before = middle_weights([side[0] for side in sides], picked, gg, gu, hg, grad_in)

    grads_in, mids, dqkvs, smalls = zip(*backs)
    dense = attn_weights([one[7] for one in kept], [one[8] for one in kept], mids, dqkvs)
    width = dense.shape[1]
    dense = dense.reshape(
        2, 2, reach, TAIL_PIECES, width // (2 * reach * TAIL_PIECES), dense.shape[2]
    )
    widths = [one.shape[2] for one in (query_weight, key_weight, value_weight)]
    ends = (grads_in[1], outputs[1], grads_in[2], outputs[2])
    *dense, wg_sum, wu_sum, wd_sum, small, ends = tail_call(
        reach, widths, dense, wide[1][0], *zip(slotted[0], slotted[2]), before, smalls, ends
    )
    return (
        ends.reshape(1, micro_count, 2 * share_rows, -1),
        small[EXPERTS + 1][None],
        *[one.astype(jnp.float32).reshape(1, -1, one.shape[3]) for one in dense],
        small[EXPERTS][None],
        small[:EXPERTS].T[None],
        *[one.astype(jnp.float32)[None] for one in (wg_sum, wu_sum, wd_sum)],
    )


def solution(mesh):
    placed = (
        P(SECTION, None, (DP, EXPERT), None),
        P(None, (DP, EXPERT)),
        P(SECTION, None, (DP, EXPERT, TENSOR), None),
        P(SECTION, None),
        P(SECTION, None, TENSOR),
        P(SECTION, None, TENSOR),
        P(SECTION, None, TENSOR),
        P(SECTION, TENSOR, None),
        P(SECTION, None),
        P(SECTION, None, None),
        P(SECTION, (EXPERT, TENSOR), None, None),
        P(SECTION, (EXPERT, TENSOR), None, None),
        P(SECTION, (EXPERT, TENSOR), None, None),
    )
    return jax.shard_map(
        by_rows,
        mesh=mesh,
        in_specs=placed,
        out_specs=(
            P(SECTION, None, (DP, EXPERT), None),
            P(SECTION, None),
            P(SECTION, None, TENSOR),
            P(SECTION, None, TENSOR),
            P(SECTION, None, TENSOR),
            P(SECTION, TENSOR, None),
            P(SECTION, None),
            P(SECTION, None, None),
            P(SECTION, (EXPERT, TENSOR), None, None),
            P(SECTION, (EXPERT, TENSOR), None, None),
            P(SECTION, (EXPERT, TENSOR), None, None),
        ),
        check_vma=False,
    )
```

```python
import functools

import jax
import jax.numpy as jnp
from jax import lax
from jax.experimental import pallas as pl
from jax.experimental.pallas import tpu as pltpu
from jax.sharding import PartitionSpec as P

SECTION, DP, EXPERT, TENSOR = "section", "dp", "expert", "tensor"
HD = 64
TOPK = 8
EXPERTS = 32
LEN = 256


EPS = 1e-06
THETA = 10000.0
NEG_BIG = -1e30


def shifted(block, axis, distance):
    devices = range(lax.axis_size(axis))
    route = [(i - distance, i) for i in devices if i - distance in devices]
    return lax.ppermute(block, axis, route)


def rms_scale(values):
    return lax.rsqrt(jnp.mean(values * values, axis=-1, keepdims=True) + EPS)


def norm_back(grad_out, values, scale_col, gain_vec):
    weighted = grad_out * gain_vec
    inner_mean = jnp.mean(weighted * values, axis=-1, keepdims=True)
    grad_values = scale_col * weighted - values * (scale_col * scale_col * scale_col) * inner_mean
    grad_gain = jnp.sum(grad_out * values * scale_col, axis=0)
    return (grad_values, grad_gain)


def rope_tables(row_count, head_width, length):
    position = (jnp.arange(row_count) % length).astype(jnp.float32)
    frequency = THETA ** (-2.0 * jnp.arange(head_width // 2).astype(jnp.float32) / head_width)
    angles = position[:, None] * frequency[None, :]
    return (jnp.cos(angles), jnp.sin(angles))


def rotate(matrix, cosine_table, sine_table, head_width, direction):
    row_count = matrix.shape[0]
    by_head = matrix.reshape(row_count, -1, head_width)
    half_width = head_width // 2
    first_half = by_head[..., :half_width]
    second_half = by_head[..., half_width:]
    cosine = cosine_table[:, None, :]
    sine_val = sine_table[:, None, :] * direction
    turned = jnp.concatenate(
        [
            first_half * cosine - second_half * sine_val,
            second_half * cosine + first_half * sine_val,
        ],
        axis=-1,
    )
    return turned.reshape(row_count, -1)


def slot_count(share_rows):
    return share_rows * 3 // 8


def score_block(query_blk, key_blk, seg_row):
    length = query_blk.shape[0]
    kv_heads = key_blk.shape[1] // HD
    query_heads = query_blk.reshape(length, kv_heads, -1, HD)
    key_heads = key_blk.reshape(length, kv_heads, HD)
    scores = jnp.einsum(
        "qkgd,skd->kgqs", query_heads, key_heads, preferred_element_type=jnp.float32
    ) * HD ** (-0.5)
    position = jnp.arange(length)
    allowed = (position[:, None] >= position[None, :]) & (seg_row[:, None] == seg_row[None, :])
    return (jnp.where(allowed, scores, NEG_BIG), query_heads, key_heads)


def attend_forward(bundle):
    query_blk, key_blk, value_blk, seg_row = bundle
    length = query_blk.shape[0]
    scores, query_heads, key_heads = score_block(query_blk, key_blk, seg_row)
    top_score = jnp.max(scores, axis=-1, keepdims=True)
    exponent = jnp.exp(scores - top_score)
    row_total = jnp.sum(exponent, axis=-1, keepdims=True)
    probability = (exponent / row_total).astype(jnp.bfloat16)
    value_heads = value_blk.reshape(length, key_heads.shape[1], HD)
    mixture = jnp.einsum(
        "kgqs,skd->qkgd", probability, value_heads, preferred_element_type=jnp.float32
    )
    return (mixture.astype(jnp.bfloat16).reshape(length, -1), top_score + jnp.log(row_total))


def attend_backward(bundle):
    query_blk, key_blk, value_blk, seg_row, log_total, grad_mix = bundle
    length = query_blk.shape[0]
    scores, query_heads, key_heads = score_block(query_blk, key_blk, seg_row)
    kv_heads = key_heads.shape[1]
    probability = jnp.exp(scores - log_total)
    prob_low = probability.astype(jnp.bfloat16)
    grad_heads = grad_mix.reshape(length, kv_heads, -1, HD)
    value_heads = value_blk.reshape(length, kv_heads, HD)
    grad_value = jnp.einsum(
        "kgqs,qkgd->skd", prob_low, grad_heads, preferred_element_type=jnp.float32
    )
    grad_prob = jnp.einsum(
        "qkgd,skd->kgqs", grad_heads, value_heads, preferred_element_type=jnp.float32
    )
    centre = jnp.sum(probability * grad_prob, axis=-1, keepdims=True)
    grad_scores = (probability * (grad_prob - centre)).astype(jnp.bfloat16)
    grad_query = jnp.einsum(
        "kgqs,skd->qkgd", grad_scores, key_heads, preferred_element_type=jnp.float32
    ) * HD ** (-0.5)
    grad_key = jnp.einsum(
        "kgqs,qkgd->skd", grad_scores, query_heads, preferred_element_type=jnp.float32
    ) * HD ** (-0.5)
    return (
        grad_query.reshape(length, -1),
        grad_key.reshape(length, -1),
        grad_value.reshape(length, -1),
    )


def attention_forward(hidden_in, seg_rows, params):
    attn_gain, query_weight, key_weight, value_weight = params[:4]
    row_count = hidden_in.shape[0]
    scale_one = rms_scale(hidden_in)
    normed = (hidden_in * scale_one * attn_gain).astype(jnp.bfloat16)
    query_proj = jnp.dot(normed, query_weight, preferred_element_type=jnp.float32)
    key_proj = jnp.dot(normed, key_weight, preferred_element_type=jnp.float32)
    value_rot = jnp.dot(normed, value_weight, preferred_element_type=jnp.float32).astype(
        jnp.bfloat16
    )
    cosine_table, sine_table = rope_tables(row_count, HD, LEN)
    query_rot = rotate(query_proj, cosine_table, sine_table, HD, 1.0).astype(jnp.bfloat16)
    key_rot = rotate(key_proj, cosine_table, sine_table, HD, 1.0).astype(jnp.bfloat16)
    seq_count = row_count // LEN
    mixed, log_total = lax.map(
        attend_forward,
        (
            query_rot.reshape(seq_count, LEN, -1),
            key_rot.reshape(seq_count, LEN, -1),
            value_rot.reshape(seq_count, LEN, -1),
            seg_rows.reshape(seq_count, LEN),
        ),
    )
    attended = mixed.reshape(row_count, -1)
    return (
        scale_one,
        normed,
        query_rot,
        key_rot,
        value_rot,
        attended,
        log_total,
        cosine_table,
        sine_table,
    )


def expert_plan(route_rows, capacity):
    pair_ids = route_rows.reshape(-1)
    onehot = (pair_ids[:, None] == jnp.arange(EXPERTS, dtype=jnp.int32)[None, :]).astype(jnp.int32)
    earlier = jnp.cumsum(onehot, axis=0) - onehot
    slot_pos = jnp.sum(earlier * onehot, axis=1)
    target = pair_ids * capacity + slot_pos
    source = (
        jnp.zeros((EXPERTS * capacity,), jnp.int32)
        .at[target]
        .set(jnp.arange(pair_ids.shape[0], dtype=jnp.int32) + 1)
    )
    return (target.reshape(route_rows.shape), source)


def send_out(buffer):
    return lax.all_to_all(buffer, (EXPERT, TENSOR), split_axis=0, concat_axis=1, tiled=True)


def send_home(produced):
    return lax.all_to_all(produced, (EXPERT, TENSOR), split_axis=1, concat_axis=0, tiled=True)


def moe_forward(middle_share, route_rows, params, outward, homeward):
    ffn_gain, router_weight, gate_weight, up_weight, down_weight = params[5:]
    share_rows = middle_share.shape[0]
    capacity = slot_count(share_rows)
    scale_two = rms_scale(middle_share)
    normed_two = (middle_share * scale_two * ffn_gain).astype(jnp.bfloat16)
    logits = jnp.dot(normed_two, router_weight, preferred_element_type=jnp.float32)
    member = route_rows[:, :, None] == jnp.arange(EXPERTS, dtype=jnp.int32)[None, None, :]
    chosen = jnp.sum(jnp.where(member, logits[:, None, :], 0.0), axis=2)
    exponent = jnp.exp(chosen - jnp.max(chosen, axis=1, keepdims=True))
    gates = exponent / jnp.sum(exponent, axis=1, keepdims=True)
    target, source = expert_plan(route_rows, capacity)
    filled = (source > 0)[:, None]
    gathered = normed_two[jnp.maximum(source - 1, 0) // TOPK]
    buffer = jnp.where(filled, gathered, jnp.zeros_like(gathered)).reshape(EXPERTS, capacity, -1)
    received = outward(buffer)
    gate_pre = jnp.einsum("erd,edf->erf", received, gate_weight, preferred_element_type=jnp.float32)
    up_pre = jnp.einsum("erd,edf->erf", received, up_weight, preferred_element_type=jnp.float32)
    hidden = (jax.nn.silu(gate_pre) * up_pre).astype(jnp.bfloat16)
    produced = jnp.einsum(
        "erf,efd->erd", hidden, down_weight, preferred_element_type=jnp.float32
    ).astype(jnp.bfloat16)
    returned = homeward(produced)
    picked = returned.reshape(EXPERTS * capacity, -1)[target]
    addition = jnp.einsum("tk,tkd->td", gates, picked, preferred_element_type=jnp.float32)
    return (
        scale_two,
        normed_two,
        member,
        gates,
        target,
        source,
        received,
        gate_pre,
        up_pre,
        hidden,
        picked,
        addition,
    )


def section_forward(layer_in, seg_rows, route_rows, params, share_start, share_rows):
    hidden_in = layer_in.astype(jnp.float32)
    attn_parts = attention_forward(hidden_in, seg_rows, params)
    partial_sum = jnp.dot(attn_parts[5], params[4], preferred_element_type=jnp.float32)
    own_share = lax.dynamic_slice_in_dim(hidden_in, share_start, share_rows, 0)
    summed = lax.psum(partial_sum.astype(jnp.bfloat16), TENSOR).astype(jnp.float32)
    branch = lax.dynamic_slice_in_dim(summed, share_start, share_rows, 0)
    middle_share = own_share + branch
    moe_parts = moe_forward(middle_share, route_rows, params, send_out, send_home)
    block_share = middle_share + moe_parts[-1]
    block_full = lax.all_gather(
        block_share.astype(jnp.bfloat16), TENSOR, axis=0, tiled=True
    ).astype(block_share.dtype)
    return (block_full, middle_share, moe_parts)


def section_backward(layer_in, middle_share, grad_top, seg_rows, params, share_start, kept_parts):
    (
        attn_gain,
        query_weight,
        key_weight,
        value_weight,
        out_weight,
        ffn_gain,
        router_weight,
        gate_weight,
        up_weight,
        down_weight,
    ) = params
    hidden_in = layer_in.astype(jnp.float32)
    row_count = hidden_in.shape[0]
    share_rows = middle_share.shape[0]
    capacity = slot_count(share_rows)
    (
        scale_one,
        normed,
        query_rot,
        key_rot,
        value_rot,
        attended,
        log_total,
        cosine_table,
        sine_table,
    ) = attention_forward(hidden_in, seg_rows, params)
    (
        scale_two,
        normed_two,
        member,
        gates,
        target,
        source,
        received,
        gate_pre,
        up_pre,
        hidden,
        picked,
        addition,
    ) = kept_parts
    grad_share = lax.dynamic_slice_in_dim(grad_top, share_start, share_rows, 0)
    grad_picked = (gates[:, :, None] * grad_share[:, None, :]).astype(jnp.bfloat16)
    grad_gates = jnp.einsum("td,tkd->tk", grad_share, picked, preferred_element_type=jnp.float32)
    grad_chosen = gates * (grad_gates - jnp.sum(gates * grad_gates, axis=1, keepdims=True))
    grad_logits = jnp.sum(jnp.where(member, grad_chosen[:, :, None], 0.0), axis=1).astype(
        jnp.bfloat16
    )
    router_grad = jnp.einsum(
        "td,te->de", normed_two, grad_logits, preferred_element_type=jnp.float32
    )
    grad_normed = jnp.einsum(
        "te,de->td", grad_logits, router_weight, preferred_element_type=jnp.float32
    )
    filled = (source > 0)[:, None]
    flat_grad = grad_picked.reshape(share_rows * TOPK, -1)
    gathered = flat_grad[jnp.maximum(source - 1, 0)]
    grad_buffer = jnp.where(filled, gathered, jnp.zeros_like(gathered)).reshape(
        EXPERTS, capacity, -1
    )
    sent = lax.all_to_all(
        grad_buffer, (EXPERT, TENSOR), split_axis=0, concat_axis=1, tiled=True
    )
    grad_hidden = jnp.einsum("erd,efd->erf", sent, down_weight, preferred_element_type=jnp.float32)
    sigmoid_gate = jax.nn.sigmoid(gate_pre)
    grad_gate = (
        grad_hidden * up_pre * sigmoid_gate * (1.0 + gate_pre * (1.0 - sigmoid_gate))
    ).astype(jnp.bfloat16)
    grad_up = (grad_hidden * gate_pre * sigmoid_gate).astype(jnp.bfloat16)
    down_grad = jnp.einsum("erf,erd->efd", hidden, sent, preferred_element_type=jnp.float32)
    gate_grad = jnp.einsum("erd,erf->edf", received, grad_gate, preferred_element_type=jnp.float32)
    up_grad = jnp.einsum("erd,erf->edf", received, grad_up, preferred_element_type=jnp.float32)
    grad_rows = jnp.einsum(
        "erf,edf->erd", grad_gate, gate_weight, preferred_element_type=jnp.float32
    )
    grad_rows = (
        grad_rows
        + jnp.einsum("erf,edf->erd", grad_up, up_weight, preferred_element_type=jnp.float32)
    ).astype(jnp.bfloat16)
    back_rows = lax.all_to_all(
        grad_rows, (EXPERT, TENSOR), split_axis=1, concat_axis=0, tiled=True
    )
    grad_normed = grad_normed + jnp.sum(
        back_rows.reshape(EXPERTS * capacity, -1)[target].astype(jnp.float32), axis=1
    )
    grad_middle, ffn_gain_grad = norm_back(grad_normed, middle_share, scale_two, ffn_gain)
    grad_middle = grad_middle + grad_share
    grad_mid_full = lax.all_gather(
        grad_middle.astype(jnp.bfloat16), TENSOR, axis=0, tiled=True
    ).astype(grad_middle.dtype)
    grad_mid_low = grad_mid_full.astype(jnp.bfloat16)
    out_grad = jnp.einsum("rh,rd->hd", attended, grad_mid_low, preferred_element_type=jnp.float32)
    grad_attended = jnp.einsum(
        "rd,hd->rh", grad_mid_low, out_weight, preferred_element_type=jnp.float32
    ).astype(jnp.bfloat16)
    seq_count = row_count // LEN
    grad_query, grad_key, grad_value = lax.map(
        attend_backward,
        (
            query_rot.reshape(seq_count, LEN, -1),
            key_rot.reshape(seq_count, LEN, -1),
            value_rot.reshape(seq_count, LEN, -1),
            seg_rows.reshape(seq_count, LEN),
            log_total,
            grad_attended.reshape(seq_count, LEN, -1),
        ),
    )
    grad_query = rotate(
        grad_query.reshape(row_count, -1), cosine_table, sine_table, HD, -1.0
    ).astype(jnp.bfloat16)
    grad_key = rotate(grad_key.reshape(row_count, -1), cosine_table, sine_table, HD, -1.0).astype(
        jnp.bfloat16
    )
    grad_value = grad_value.reshape(row_count, -1).astype(jnp.bfloat16)
    query_grad = jnp.einsum("rd,rh->dh", normed, grad_query, preferred_element_type=jnp.float32)
    key_grad = jnp.einsum("rd,rh->dh", normed, grad_key, preferred_element_type=jnp.float32)
    value_grad = jnp.einsum("rd,rh->dh", normed, grad_value, preferred_element_type=jnp.float32)
    grad_normed_one = jnp.einsum(
        "rh,dh->rd", grad_query, query_weight, preferred_element_type=jnp.float32
    )
    grad_normed_one = grad_normed_one + jnp.einsum(
        "rh,dh->rd", grad_key, key_weight, preferred_element_type=jnp.float32
    )
    grad_normed_one = grad_normed_one + jnp.einsum(
        "rh,dh->rd", grad_value, value_weight, preferred_element_type=jnp.float32
    )
    grad_normed_one = lax.psum(grad_normed_one.astype(jnp.bfloat16), TENSOR).astype(jnp.float32)
    grad_input, attn_gain_grad = norm_back(grad_normed_one, hidden_in, scale_one, attn_gain)
    grad_input = grad_input + grad_mid_full
    return (
        grad_input,
        (
            attn_gain_grad,
            query_grad,
            key_grad,
            value_grad,
            out_grad,
            ffn_gain_grad,
            router_grad,
            gate_grad,
            up_grad,
            down_grad,
        ),
    )


def stack_zeros(piece_arr, count):
    return jnp.zeros((count,) + piece_arr.shape, piece_arr.dtype)


def on_device(
    boundary,
    segments,
    expert_ids,
    attn_gain,
    query_weight,
    key_weight,
    value_weight,
    out_weight,
    ffn_gain,
    router_weight,
    gate_weight,
    up_weight,
    down_weight,
):
    params = tuple(
        (
            array_in[0]
            for array_in in (
                attn_gain,
                query_weight,
                key_weight,
                value_weight,
                out_weight,
                ffn_gain,
                router_weight,
                gate_weight,
                up_weight,
                down_weight,
            )
        )
    )
    section_index = lax.axis_index(SECTION)
    tensor_index = lax.axis_index(TENSOR)
    own_rows = boundary[0]
    micro_count = own_rows.shape[0]
    row_count = own_rows.shape[1]
    model_width = own_rows.shape[2]
    share_rows = expert_ids.shape[2]
    share_start = tensor_index * share_rows
    routes = expert_ids[0]
    kept_inputs = jnp.zeros((micro_count, row_count, model_width), jnp.bfloat16)
    kept_middle = jnp.zeros((micro_count, share_rows, model_width), jnp.float32)
    block_outputs = jnp.zeros((micro_count, row_count, model_width), jnp.bfloat16)
    arrived = jnp.zeros((row_count, model_width), jnp.bfloat16)
    kept_moe = None
    for tick_idx in range(micro_count + 1):
        micro_idx = tick_idx - section_index
        is_valid = (micro_idx >= 0) & (micro_idx < micro_count)
        slot_idx = jnp.clip(micro_idx, 0, micro_count - 1)
        layer_in = jnp.where(section_index == 0, own_rows[min(tick_idx, micro_count - 1)], arrived)
        seg_rows = lax.dynamic_index_in_dim(segments, slot_idx, 0, keepdims=False)
        route_rows = lax.dynamic_index_in_dim(routes, slot_idx, 0, keepdims=False)
        block_full, middle_share, moe_parts = section_forward(
            layer_in, seg_rows, route_rows, params, share_start, share_rows
        )
        block_low = block_full.astype(jnp.bfloat16)
        kept_inputs = jnp.where(
            is_valid,
            lax.dynamic_update_index_in_dim(kept_inputs, layer_in, slot_idx, 0),
            kept_inputs,
        )
        kept_middle = jnp.where(
            is_valid,
            lax.dynamic_update_index_in_dim(kept_middle, middle_share, slot_idx, 0),
            kept_middle,
        )
        block_outputs = jnp.where(
            is_valid,
            lax.dynamic_update_index_in_dim(block_outputs, block_low, slot_idx, 0),
            block_outputs,
        )
        if kept_moe is None:
            kept_moe = tuple((stack_zeros(piece_arr, micro_count) for piece_arr in moe_parts))
        kept_moe = tuple(
            (
                jnp.where(
                    is_valid,
                    lax.dynamic_update_index_in_dim(stack_arr, piece_arr, slot_idx, 0),
                    stack_arr,
                )
                for stack_arr, piece_arr in zip(kept_moe, moe_parts)
            )
        )
        arrived = shifted(block_low, SECTION, 1)
    grads = tuple((jnp.zeros(param_arr.shape, jnp.float32) for param_arr in params))
    input_grads = jnp.zeros((micro_count, row_count, model_width), jnp.bfloat16)
    grad_arrived = jnp.zeros((row_count, model_width), jnp.bfloat16)
    for tick_idx in range(micro_count + 1):
        micro_idx = tick_idx - (1 - section_index)
        is_valid = (micro_idx >= 0) & (micro_idx < micro_count)
        slot_idx = jnp.clip(micro_idx, 0, micro_count - 1)
        grad_top = jnp.where(
            section_index == 1, own_rows[min(tick_idx, micro_count - 1)], grad_arrived
        ).astype(jnp.float32)
        layer_in = lax.dynamic_index_in_dim(kept_inputs, slot_idx, 0, keepdims=False)
        middle_share = lax.dynamic_index_in_dim(kept_middle, slot_idx, 0, keepdims=False)
        seg_rows = lax.dynamic_index_in_dim(segments, slot_idx, 0, keepdims=False)
        route_rows = lax.dynamic_index_in_dim(routes, slot_idx, 0, keepdims=False)
        tick_moe = tuple(
            (
                lax.dynamic_index_in_dim(stack_arr, slot_idx, 0, keepdims=False)
                for stack_arr in kept_moe
            )
        )
        grad_input, tick_grads = section_backward(
            layer_in, middle_share, grad_top, seg_rows, params, share_start, tick_moe
        )
        valid_weight = is_valid.astype(jnp.float32)
        grads = tuple(
            (
                total_grad + valid_weight * tick_part
                for total_grad, tick_part in zip(grads, tick_grads)
            )
        )
        grad_low = grad_input.astype(jnp.bfloat16)
        input_grads = jnp.where(
            is_valid,
            lax.dynamic_update_index_in_dim(input_grads, grad_low, slot_idx, 0),
            input_grads,
        )
        grad_arrived = shifted(grad_low, SECTION, -1)
    dense = (
        lax.psum(grads[0].astype(jnp.bfloat16), (DP, EXPERT)).astype(jnp.float32),
        lax.psum(grads[1].astype(jnp.bfloat16), (DP, EXPERT)).astype(jnp.float32),
        lax.psum(grads[2].astype(jnp.bfloat16), (DP, EXPERT)).astype(jnp.float32),
        lax.psum(grads[3].astype(jnp.bfloat16), (DP, EXPERT)).astype(jnp.float32),
        lax.psum(grads[4].astype(jnp.bfloat16), (DP, EXPERT)).astype(jnp.float32),
    )
    shared = lax.psum((grads[5], grads[6]), (DP, EXPERT, TENSOR))
    expert_sums = (
        lax.psum(grads[7].astype(jnp.bfloat16), DP).astype(jnp.float32),
        lax.psum(grads[8].astype(jnp.bfloat16), DP).astype(jnp.float32),
        lax.psum(grads[9].astype(jnp.bfloat16), DP).astype(jnp.float32),
    )
    ends_out = jnp.where(section_index == 0, input_grads, block_outputs)[None]
    return (
        ends_out,
        dense[0][None],
        dense[1][None],
        dense[2][None],
        dense[3][None],
        dense[4][None],
        shared[0][None],
        shared[1][None],
        expert_sums[0][None],
        expert_sums[1][None],
        expert_sums[2][None],
    )


MIB = 1024 * 1024
NT = (((1,), (1,)), ((), ()))
TN = (((0,), (0,)), ((), ()))


def dot(left, right, dims=None):
    if dims is None:
        return jnp.dot(left, right, preferred_element_type=jnp.float32)
    return lax.dot_general(left, right, dims, preferred_element_type=jnp.float32)


def lane_grid(rows):
    return lax.broadcasted_iota(jnp.int32, (rows, 2 * HD), 1)


def turn_pair(slab, cosine, sine):
    low_half = (lane_grid(slab.shape[0]) % HD) < HD // 2
    partner = jnp.where(
        low_half, pltpu.roll(slab, 2 * HD - HD // 2, 1), pltpu.roll(slab, HD // 2, 1)
    )
    return slab * cosine + partner * sine


def pair_tables(length):
    cosine, sine = rope_tables(length, HD, length)
    return (
        jnp.concatenate([cosine] * 4, axis=1),
        jnp.concatenate([-sine, sine, -sine, sine], axis=1),
    )


def aligned_head(slabs, head, side, scale):
    slab = slabs[head // 2]
    if head % 2 != side:
        slab = pltpu.roll(slab, HD, 1)
    keep = (lane_grid(slab.shape[0]) // HD) == side
    return jnp.where(keep, slab * scale, 0.0).astype(jnp.bfloat16)


def one_side(slab, side):
    return jnp.where((lane_grid(slab.shape[0]) // HD) == side, slab, jnp.zeros_like(slab))


def slabs_of(matrix, start, count):
    return [matrix[:, start + 2 * HD * i : start + 2 * HD * (i + 1)] for i in range(count)]


def attend_part(group, rows, weights, tables, allowed):
    width = weights.shape[1]
    query_width = width * group // (group + 2)
    key_width = (width - query_width) // 2
    cosine, sine = tables
    projected = dot(rows, weights)
    query = [
        turn_pair(slab, cosine, sine) for slab in slabs_of(projected, 0, query_width // (2 * HD))
    ]
    key = [
        turn_pair(slab, cosine, sine).astype(jnp.bfloat16)
        for slab in slabs_of(projected, query_width, key_width // (2 * HD))
    ]
    value = [
        slab.astype(jnp.bfloat16)
        for slab in slabs_of(projected, query_width + key_width, key_width // (2 * HD))
    ]
    turned = jnp.concatenate([slab.astype(jnp.bfloat16) for slab in query] + key + value, axis=1)
    query = [slab.astype(jnp.bfloat16).astype(jnp.float32) for slab in query]
    mixed = [None] * len(query)
    for kv_head in range(key_width // HD):
        side = kv_head % 2
        key_slab = key[kv_head // 2]
        value_side = one_side(value[kv_head // 2], side)
        for head in range(group * kv_head, group * (kv_head + 1)):
            scores = dot(aligned_head(query, head, side, HD**-0.5), key_slab, NT)
            scores = jnp.where(allowed, scores, NEG_BIG)
            exponent = jnp.exp(scores - jnp.max(scores, axis=1, keepdims=True))
            probability = exponent / jnp.sum(exponent, axis=1, keepdims=True)
            part = dot(probability.astype(jnp.bfloat16), value_side)
            if head % 2 != side:
                part = pltpu.roll(part, HD, 1)
            mixed[head // 2] = part if head % 2 == 0 else mixed[head // 2] + part
    return turned, jnp.concatenate([part.astype(jnp.bfloat16) for part in mixed], axis=1)


def allowed_pairs(seg_col, seg_row):
    length = seg_row.shape[1]
    row = lax.broadcasted_iota(jnp.int32, (length, length), 0)
    column = lax.broadcasted_iota(jnp.int32, (length, length), 1)
    return (row >= column) & (seg_col == seg_row)


def of_section(first, second):
    return jnp.where(lax.axis_index(SECTION) == 0, first[...], second[...])


def start_of_section(first, second, to, sem):
    @pl.when(lax.axis_index(SECTION) == 0)
    def _():
        pltpu.make_async_copy(first, to, sem).start()

    @pl.when(lax.axis_index(SECTION) != 0)
    def _():
        pltpu.make_async_copy(second, to, sem).start()


def attn_forward_kernel(
    group,
    skipped,
    x_first,
    x_second,
    gain_one_ref,
    wqkv_hbm,
    wo_hbm,
    cos_ref,
    sin_ref,
    seg_col_ref,
    seg_row_ref,
    gain_two_ref,
    h1_ref,
    xn1_ref,
    qkv_ref,
    att_ref,
    xn2_ref,
    x_ref,
    wqkv_ref,
    wo_ref,
    x_sem,
    weight_sem,
):
    @pl.when(lax.axis_index(SECTION) != skipped)
    def _():
        parts = wqkv_ref.shape[0]

        def weight_copies(half):
            return [
                pltpu.make_async_copy(hbm.at[half], ref.at[half], weight_sem.at[i, half])
                for i, (hbm, ref) in enumerate(((wqkv_hbm, wqkv_ref), (wo_hbm, wo_ref)))
            ]

        start_of_section(x_first, x_second, x_ref, x_sem)
        for copy in weight_copies(0):
            copy.start()
        pltpu.make_async_copy(x_first, x_ref, x_sem).wait()
        rows = x_ref[...].astype(jnp.float32)
        xn1_ref[...] = (rows * rms_scale(rows) * gain_one_ref[...]).astype(jnp.bfloat16)
        h1_ref[...] = rows

        def one(half, carry):
            for copy in weight_copies(half):
                copy.wait()

            @pl.when(half + 1 < parts)
            def _():
                for copy in weight_copies(half + 1):
                    copy.start()

            turned, attended = attend_part(
                group,
                xn1_ref[...],
                wqkv_ref[half],
                (cos_ref[...], sin_ref[...]),
                allowed_pairs(seg_col_ref[...], seg_row_ref[...]),
            )
            qkv_ref[half] = turned
            att_ref[half] = attended
            h1_ref[...] += dot(attended, wo_ref[half])
            return carry

        lax.fori_loop(0, parts, one, 0)
        middle = h1_ref[...]
        xn2_ref[...] = (middle * rms_scale(middle) * gain_two_ref[...]).astype(jnp.bfloat16)


def attn_forward(first, second, seg, gains, wqkv, wo, tables, group, skipped):
    length, width = first.shape
    parts, _, qkv_width = wqkv.shape
    att_width = wo.shape[1]
    vmem = pl.BlockSpec(memory_space=pltpu.VMEM)
    anywhere = pl.BlockSpec(memory_space=pl.ANY)
    return pl.pallas_call(
        functools.partial(attn_forward_kernel, group, skipped),
        in_specs=[anywhere] * 2 + [vmem] + [anywhere] * 2 + [vmem] * 5,
        out_specs=[vmem] * 5,
        out_shape=[
            jax.ShapeDtypeStruct((length, width), jnp.float32),
            jax.ShapeDtypeStruct((length, width), jnp.bfloat16),
            jax.ShapeDtypeStruct((parts, length, qkv_width), jnp.bfloat16),
            jax.ShapeDtypeStruct((parts, length, att_width), jnp.bfloat16),
            jax.ShapeDtypeStruct((length, width), jnp.bfloat16),
        ],
        scratch_shapes=[
            pltpu.VMEM((length, width), jnp.bfloat16),
            pltpu.VMEM(wqkv.shape, wqkv.dtype),
            pltpu.VMEM(wo.shape, wo.dtype),
            pltpu.SemaphoreType.DMA,
            pltpu.SemaphoreType.DMA((2, parts)),
        ],
        compiler_params=pltpu.CompilerParams(vmem_limit_bytes=62 * MIB),
        cost_estimate=pl.CostEstimate(
            flops=4 * 10**9, bytes_accessed=20 * 10**6, transcendentals=2 * 10**6
        ),
        name="attn_forward",
    )(first, second, gains[0], wqkv, wo, *tables, seg[:, None], seg[None, :], gains[1])


def attn_again_kernel(
    group,
    x_ref,
    gain_ref,
    wqkv_hbm,
    cos_ref,
    sin_ref,
    seg_col_ref,
    seg_row_ref,
    xn1_ref,
    qkv_ref,
    att_ref,
    wqkv_ref,
    sem,
):
    @pl.when(lax.axis_index(SECTION) == 0)
    def _():
        parts = wqkv_ref.shape[0]

        def copy(half):
            return pltpu.make_async_copy(wqkv_hbm.at[half], wqkv_ref.at[half], sem.at[half])

        for half in range(parts):
            copy(half).start()
        rows = x_ref[...].astype(jnp.float32)
        xn1_ref[...] = (rows * rms_scale(rows) * gain_ref[...]).astype(jnp.bfloat16)

        def one(half, carry):
            copy(half).wait()
            qkv_ref[half], att_ref[half] = attend_part(
                group,
                xn1_ref[...],
                wqkv_ref[half],
                (cos_ref[...], sin_ref[...]),
                allowed_pairs(seg_col_ref[...], seg_row_ref[...]),
            )
            return carry

        lax.fori_loop(0, parts, one, 0)


def attn_again(layer_in, seg, gain, wqkv, tables, group):
    length, width = layer_in.shape
    parts, _, qkv_width = wqkv.shape
    vmem = pl.BlockSpec(memory_space=pltpu.VMEM)
    return pl.pallas_call(
        functools.partial(attn_again_kernel, group),
        in_specs=[vmem] * 2 + [pl.BlockSpec(memory_space=pl.ANY)] + [vmem] * 4,
        out_specs=[vmem] * 3,
        out_shape=[
            jax.ShapeDtypeStruct((length, width), jnp.bfloat16),
            jax.ShapeDtypeStruct((parts, length, qkv_width), jnp.bfloat16),
            jax.ShapeDtypeStruct((parts, length, width // parts), jnp.bfloat16),
        ],
        scratch_shapes=[
            pltpu.VMEM(wqkv.shape, wqkv.dtype),
            pltpu.SemaphoreType.DMA((parts,)),
        ],
        compiler_params=pltpu.CompilerParams(vmem_limit_bytes=62 * MIB),
        cost_estimate=pl.CostEstimate(
            flops=3 * 10**9, bytes_accessed=12 * 10**6, transcendentals=2 * 10**6
        ),
        name="attn_again",
    )(layer_in, gain, wqkv, tables[0], tables[1], seg[:, None], seg[None, :])


def attn_split_kernel(
    group,
    x_ref,
    gain_one_ref,
    wqkv_ref,
    wo_ref,
    cos_ref,
    sin_ref,
    seg_col_ref,
    seg_row_ref,
    gain_two_ref,
    h1_ref,
    xn2_ref,
    part,
    arrived,
    send_sem,
    recv_sem,
):
    x = lax.axis_index(TENSOR)
    aside = {TENSOR: 1 - x}

    @pl.when(lax.axis_index(SECTION) == 0)
    def _():
        barrier = pltpu.get_barrier_semaphore()
        pl.semaphore_signal(barrier, inc=1, device_id=aside, device_id_type=pl.DeviceIdType.MESH)

        def one(i, carry):
            at = jnp.where(i == 0, 1 - x, x)
            rows = x_ref[at].astype(jnp.float32)
            normed = (rows * rms_scale(rows) * gain_one_ref[...]).astype(jnp.bfloat16)
            _, attended = attend_part(
                group,
                normed,
                wqkv_ref[...],
                (cos_ref[...], sin_ref[...]),
                allowed_pairs(seg_col_ref[at], seg_row_ref[at]),
            )
            branch = dot(attended, wo_ref[...])

            @pl.when(i == 0)
            def _():
                part[...] = branch.astype(jnp.bfloat16)
                pl.semaphore_wait(barrier, 1)
                copy().start()

            @pl.when(i == 1)
            def _():
                h1_ref[...] = rows + branch

            return carry

        def copy():
            return pltpu.make_async_remote_copy(
                src_ref=part,
                dst_ref=arrived,
                send_sem=send_sem,
                recv_sem=recv_sem,
                device_id=aside,
                device_id_type=pl.DeviceIdType.MESH,
            )

        lax.fori_loop(0, 2, one, 0)
        copy().wait()
        middle = h1_ref[...] + arrived[...].astype(jnp.float32)
        h1_ref[...] = middle
        xn2_ref[...] = (middle * rms_scale(middle) * gain_two_ref[...]).astype(jnp.bfloat16)


def attn_split(rows, seg, gains, wqkv, wo, tables, group):
    _, length, width = rows.shape
    vmem = pl.BlockSpec(memory_space=pltpu.VMEM)
    return pl.pallas_call(
        functools.partial(attn_split_kernel, group),
        in_specs=[vmem] * 9,
        out_specs=[vmem] * 2,
        out_shape=[
            jax.ShapeDtypeStruct((length, width), jnp.float32),
            jax.ShapeDtypeStruct((length, width), jnp.bfloat16),
        ],
        scratch_shapes=[
            pltpu.VMEM((length, width), jnp.bfloat16),
            pltpu.VMEM((length, width), jnp.bfloat16),
            pltpu.SemaphoreType.DMA,
            pltpu.SemaphoreType.DMA,
        ],
        compiler_params=pltpu.CompilerParams(
            collective_id=8, has_side_effects=True, vmem_limit_bytes=48 * MIB
        ),
        cost_estimate=pl.CostEstimate(
            flops=4 * 10**9, bytes_accessed=20 * 10**6, transcendentals=2 * 10**6
        ),
        name="attn_split",
    )(
        rows,
        gains[0],
        wqkv,
        wo,
        tables[0],
        tables[1],
        seg[:, :, None],
        seg[:, None, :],
        gains[1],
    )


def both_halves_kernel(
    chunks,
    wqkv,
    wo,
    after,
    wqkv_before,
    wo_before,
    wqkv_all,
    wo_all,
    wqkv_held,
    wo_held,
    own_sem,
    out_sem,
    x_send,
    x_recv,
    core_send,
    core_recv,
):
    del after, wqkv_before, wo_before
    x = lax.axis_index(TENSOR)
    core = lax.axis_index(DP)
    aside, partner = {TENSOR: 1 - x}, {DP: 1 - core}
    pairs = ((wqkv, wqkv_held, wqkv_all), (wo, wo_held, wo_all))

    def span(i, of_core, chunk):
        rows = pairs[i][0].shape[0] // (2 * chunks)
        return pl.ds((of_core * chunks + chunk) * rows, rows)

    def own_copy(i, of_core, chunk):
        shard, held, _ = pairs[i]
        at = span(i, of_core, chunk)
        return pltpu.make_async_copy(shard.at[at], held.at[x, at], own_sem.at[i, of_core, chunk])

    def out_copy(i, half):
        _, held, out = pairs[i]
        return pltpu.make_async_copy(held.at[half], out.at[half], out_sem.at[i, half])

    def x_copy(i, chunk, half):
        _, held, _ = pairs[i]
        at = held.at[half, span(i, core, chunk)]
        return pltpu.make_async_remote_copy(
            src_ref=at,
            dst_ref=at,
            send_sem=x_send.at[i, chunk],
            recv_sem=x_recv.at[i, chunk],
            device_id=aside,
            device_id_type=pl.DeviceIdType.MESH,
        )

    def core_copy(i, chunk, of_core):
        _, held, _ = pairs[i]
        at = held.at[1 - x, span(i, of_core, chunk)]
        return pltpu.make_async_remote_copy(
            src_ref=at,
            dst_ref=at,
            send_sem=core_send.at[i, chunk],
            recv_sem=core_recv.at[i, chunk],
            device_id=partner,
            device_id_type=pl.DeviceIdType.MESH,
        )

    steps = [(i, chunk) for i in range(2) for chunk in range(chunks)]

    @pl.when(lax.axis_index(SECTION) == 0)
    def _():
        for of_core in (core, 1 - core):
            for i, chunk in steps:
                own_copy(i, of_core, chunk).start()
        barrier = pltpu.get_barrier_semaphore()
        for other in (aside, partner):
            pl.semaphore_signal(barrier, inc=1, device_id=other, device_id_type=pl.DeviceIdType.MESH)
        pl.semaphore_wait(barrier, 2)
        for i, chunk in steps:
            own_copy(i, core, chunk).wait()
            x_copy(i, chunk, x).start()
        for i, chunk in steps:
            own_copy(i, 1 - core, chunk).wait()
        for i in range(2):
            out_copy(i, x).start()
        for i, chunk in steps:
            x_copy(i, chunk, 1 - x).wait_recv()
            core_copy(i, chunk, core).start()
        for i in range(2):
            for chunk in range(chunks):
                core_copy(i, chunk, 1 - core).wait_recv()
            out_copy(i, 1 - x).start()
        for i, chunk in steps:
            x_copy(i, chunk, x).wait_send()
            core_copy(i, chunk, core).wait_send()
        for i in range(2):
            for half in range(2):
                out_copy(i, half).wait()


def both_halves(wqkv, wo, after, before, chunks=4):
    anywhere = pl.BlockSpec(memory_space=pl.ANY)
    dma = pltpu.SemaphoreType.DMA
    return pl.pallas_call(
        functools.partial(both_halves_kernel, chunks),
        in_specs=[anywhere] * 5,
        out_specs=[anywhere] * 2,
        input_output_aliases={3: 0, 4: 1},
        out_shape=[
            jax.ShapeDtypeStruct((2,) + wqkv.shape, wqkv.dtype),
            jax.ShapeDtypeStruct((2,) + wo.shape, wo.dtype),
        ],
        scratch_shapes=[
            pltpu.VMEM((2,) + wqkv.shape, wqkv.dtype),
            pltpu.VMEM((2,) + wo.shape, wo.dtype),
            dma((2, 2, chunks)),
            dma((2, 2)),
        ]
        + [dma((2, chunks))] * 4,
        compiler_params=pltpu.CompilerParams(
            collective_id=9, has_side_effects=True, vmem_limit_bytes=62 * MIB
        ),
        cost_estimate=pl.CostEstimate(flops=0, bytes_accessed=30 * 10**6, transcendentals=0),
        name="both_halves",
    )(wqkv, wo, after, *before)


def attn_backward_kernel(group, skipped, *refs):
    @pl.when(lax.axis_index(SECTION) != skipped)
    def _():
        pairs = [refs[2 * i : 2 * i + 2] for i in range(6)]
        (
            wqkv_hbm,
            wo_hbm,
            rows_ref,
            grad_gates_ref,
            router_ref,
            gain_one_ref,
            gain_two_ref,
            cos_ref,
            sin_ref,
            seg_col_ref,
            seg_row_ref,
            grad_in_ref,
            mid_ref,
            dqkv_ref,
            small_ref,
            x_ref,
            h1_ref,
            xn2_ref,
            gates_ref,
            qkv_ref,
            top_ref,
            wqkv_ref,
            wo_ref,
            middle_acc,
            normed_acc,
            taken_sem,
            weight_sem,
        ) = refs[12:]
        taken = (x_ref, h1_ref, xn2_ref, gates_ref, qkv_ref, top_ref)
        experts = grad_gates_ref.shape[0]
        parts = wqkv_ref.shape[0]

        def weight_copies(half):
            return [
                pltpu.make_async_copy(hbm.at[half], ref.at[half], weight_sem.at[i, half])
                for i, (hbm, ref) in enumerate(((wqkv_hbm, wqkv_ref), (wo_hbm, wo_ref)))
            ]

        for i in (3, 2, 1, 5, 4, 0):
            start_of_section(*pairs[i], taken[i], taken_sem.at[i])

        def arrived(i):
            pltpu.make_async_copy(pairs[i][0], taken[i], taken_sem.at[i]).wait()
            return taken[i]

        gates = arrived(3)[...]
        grad_gates = grad_gates_ref[...]
        chosen = gates * (grad_gates - jnp.sum(gates * grad_gates, axis=0, keepdims=True))
        logits = chosen.astype(jnp.bfloat16)
        small_ref[0:experts, :] = dot(logits, arrived(2)[...])
        for copy in weight_copies(0):
            copy.start()
        grad_normed = dot(logits, router_ref[...], TN) + rows_ref[...].astype(jnp.float32)
        middle = arrived(1)[...]
        grad_middle, gain_grad = norm_back(grad_normed, middle, rms_scale(middle), gain_two_ref[...])
        small_ref[experts : experts + 1, :] = gain_grad[None, :]
        grad_middle = grad_middle + arrived(5)[...].astype(jnp.float32)
        middle_acc[...] = grad_middle
        mid_ref[...] = grad_middle.astype(jnp.bfloat16)
        normed_acc[...] = jnp.zeros_like(normed_acc)
        arrived(4)

        def one(half, carry):
            for copy in weight_copies(half):
                copy.wait()

            @pl.when(half + 1 < parts)
            def _():
                for copy in weight_copies(half + 1):
                    copy.start()

            attn_backward_part(
                group,
                half,
                mid_ref,
                wqkv_ref,
                wo_ref,
                (cos_ref[...], -sin_ref[...]),
                (seg_col_ref[...], seg_row_ref[...]),
                qkv_ref,
                dqkv_ref,
                normed_acc,
            )
            return carry

        lax.fori_loop(0, parts, one, 0)
        rows = arrived(0)[...].astype(jnp.float32)
        grad_rows, gain_grad = norm_back(normed_acc[...], rows, rms_scale(rows), gain_one_ref[...])
        grad_in_ref[...] = (grad_rows + middle_acc[...]).astype(jnp.bfloat16)
        small_ref[experts + 1 : experts + 2, :] = gain_grad[None, :]
        small_ref[experts + 2 :, :] = jnp.zeros_like(small_ref[experts + 2 :, :])


def attn_backward_part(
    group, part, mid_ref, wqkv_ref, wo_ref, tables, segs, qkv_ref, dqkv_ref, normed_acc
):
    length = mid_ref.shape[0]
    width = wqkv_ref.shape[2]
    query_width = width * group // (group + 2)
    key_width = (width - query_width) // 2
    cosine, sine = tables
    seg_col, seg_row = segs
    grad_att = dot(mid_ref[...], wo_ref[part], NT).astype(jnp.bfloat16).astype(jnp.float32)
    grad_out = slabs_of(grad_att, 0, query_width // (2 * HD))
    kept = qkv_ref[part]
    query = [slab.astype(jnp.float32) for slab in slabs_of(kept, 0, query_width // (2 * HD))]
    key = slabs_of(kept, query_width, key_width // (2 * HD))
    value = slabs_of(kept, query_width + key_width, key_width // (2 * HD))
    key_at = lax.broadcasted_iota(jnp.int32, (length, length), 0)
    query_at = lax.broadcasted_iota(jnp.int32, (length, length), 1)
    allowed = (query_at >= key_at) & (seg_col == seg_row)
    grad_query = [None] * len(query)
    grad_key = [None] * len(key)
    grad_value = [None] * len(value)
    for kv_head in range(key_width // HD):
        side = kv_head % 2
        slab_at = kv_head // 2
        key_slab = key[slab_at]
        key_side = one_side(key_slab, side)
        value_slab = value[slab_at]
        for head in range(group * kv_head, group * (kv_head + 1)):
            query_head = aligned_head(query, head, side, HD**-0.5)
            out_head = aligned_head(grad_out, head, side, 1.0)
            scores = dot(key_slab, query_head, NT)
            scores = jnp.where(allowed, scores, NEG_BIG)
            exponent = jnp.exp(scores - jnp.max(scores, axis=0, keepdims=True))
            probability = exponent / jnp.sum(exponent, axis=0, keepdims=True)
            grad_prob = dot(value_slab, out_head, NT)
            value_part = dot(probability.astype(jnp.bfloat16), out_head)
            centre = jnp.sum(probability * grad_prob, axis=0, keepdims=True)
            grad_scores = (probability * (grad_prob - centre)).astype(jnp.bfloat16)
            key_part = dot(grad_scores, query_head)
            query_part = dot(grad_scores, key_side, TN) * HD**-0.5
            if head % 2 != side:
                query_part = pltpu.roll(query_part, HD, 1)
            at = head // 2
            grad_query[at] = query_part if head % 2 == 0 else grad_query[at] + query_part
            first = head == 2 * group * slab_at
            grad_key[slab_at] = key_part if first else grad_key[slab_at] + key_part
            grad_value[slab_at] = value_part if first else grad_value[slab_at] + value_part
    turned = [turn_pair(slab, cosine, sine).astype(jnp.bfloat16) for slab in grad_query + grad_key]
    dqkv = jnp.concatenate(turned + [slab.astype(jnp.bfloat16) for slab in grad_value], axis=1)
    dqkv_ref[part] = dqkv
    normed_acc[...] += dot(dqkv, wqkv_ref[part], NT)


def attn_backward(
    kept, rows, grad_gates, seg, gains, router, wqkv, wo, tables, group, skipped
):
    length, width = rows.shape
    parts, _, qkv_width = wqkv.shape
    experts = router.shape[0]
    vmem = pl.BlockSpec(memory_space=pltpu.VMEM)
    anywhere = pl.BlockSpec(memory_space=pl.ANY)
    dma = pltpu.SemaphoreType.DMA
    return pl.pallas_call(
        functools.partial(attn_backward_kernel, group, skipped),
        in_specs=[anywhere] * 14 + [vmem] * 9,
        out_specs=[vmem] * 4,
        out_shape=[
            jax.ShapeDtypeStruct((length, width), jnp.bfloat16),
            jax.ShapeDtypeStruct((length, width), jnp.bfloat16),
            jax.ShapeDtypeStruct((parts, length, qkv_width), jnp.bfloat16),
            jax.ShapeDtypeStruct((experts + 8, width), jnp.float32),
        ],
        scratch_shapes=[pltpu.VMEM(one.shape, one.dtype) for one, _ in kept]
        + [
            pltpu.VMEM(wqkv.shape, wqkv.dtype),
            pltpu.VMEM(wo.shape, wo.dtype),
            pltpu.VMEM((length, width), jnp.float32),
            pltpu.VMEM((length, width), jnp.float32),
            dma((len(kept),)),
            dma((2, parts)),
        ],
        compiler_params=pltpu.CompilerParams(vmem_limit_bytes=62 * MIB),
        cost_estimate=pl.CostEstimate(
            flops=8 * 10**9, bytes_accessed=20 * 10**6, transcendentals=2 * 10**6
        ),
        name="attn_backward",
    )(
        *[one for pair in kept for one in pair],
        wqkv,
        wo,
        rows,
        grad_gates,
        router,
        gains[0],
        gains[1],
        tables[0],
        tables[1],
        seg[:, None],
        seg[None, :],
    )


def attn_weights_kernel(*refs):
    groups, out_ref = [refs[3 * i : 3 * i + 3] for i in range(4)], refs[12]
    width = out_ref.shape[1]

    def kept(group):
        one, both, three = group
        return jnp.concatenate([of_section(one, three), both[...]], axis=-2)

    def found(group):
        one, both, three = group
        return jnp.concatenate([both[...], of_section(three, one)], axis=-2)

    xn1, att = kept(groups[0]), kept(groups[1])[0]
    mid, dqkv = found(groups[2]), found(groups[3])[0]
    qkv_width = dqkv.shape[1]
    out_ref[0, :, :qkv_width] = dot(xn1, dqkv, TN).astype(jnp.bfloat16)
    half = width // 2
    for i in range(2):
        out_ref[0, i * half : (i + 1) * half, qkv_width:] = dot(
            att, mid[:, i * half : (i + 1) * half], TN
        ).astype(jnp.bfloat16)


def attn_weights(xn1, att, mid, dqkv):
    rows, width = xn1[0].shape
    parts, _, att_width = att[0].shape
    qkv_width = dqkv[0].shape[2]

    def whole(*shape):
        return pl.BlockSpec(shape, lambda i: (0,) * len(shape))

    def part(*shape):
        return pl.BlockSpec((1,) + shape, lambda i: (i, 0, 0))

    return pl.pallas_call(
        attn_weights_kernel,
        grid=(parts,),
        in_specs=[whole(rows, width)] * 3
        + [part(rows, att_width)] * 3
        + [whole(rows, width)] * 3
        + [part(rows, qkv_width)] * 3,
        out_specs=part(width, qkv_width + width // 2),
        out_shape=jax.ShapeDtypeStruct((parts, width, qkv_width + width // 2), jnp.bfloat16),
        compiler_params=pltpu.CompilerParams(vmem_limit_bytes=56 * MIB),
        cost_estimate=pl.CostEstimate(
            flops=7 * 10**9, bytes_accessed=20 * 10**6, transcendentals=0
        ),
        name="attn_weights",
    )(*xn1, *att, *mid, *dqkv)


def looked_up(place, values):
    found = values[0]
    for i, value in enumerate(values[1:]):
        found = jnp.where(place == i + 1, value, found)
    return found


def nearest_first(place, reach):
    table = []
    for at in range(reach):
        table.append(sorted(range(reach), key=lambda other: (abs(other - at), other)))
    return [looked_up(place, [table[at][k] for at in range(reach)]) for k in range(reach)]


MESH_ID = pl.DeviceIdType.MESH


class Chain:
    def __init__(self, reach):
        self.reach = reach
        self.z = lax.axis_index(EXPERT)
        self.x = lax.axis_index(TENSOR)
        self.me = 2 * self.z + self.x
        self.aside = {TENSOR: 1 - self.x}
        self.above = {EXPERT: self.z + 1}
        self.below = {EXPERT: self.z - 1}
        self.has_above = self.z < reach - 1
        self.has_below = self.z > 0
        self.order = nearest_first(self.z, reach)

    def near(self, k):
        return self.order[k] if isinstance(k, int) else looked_up(k, self.order)

    def greet_group(self, partner=None):
        barrier = pltpu.get_barrier_semaphore()
        if partner is not None:
            pl.semaphore_signal(barrier, inc=1, device_id=partner, device_id_type=MESH_ID)
        for other in range(2 * self.reach):

            @pl.when(other != self.me)
            def _():
                pl.semaphore_signal(
                    barrier,
                    inc=1,
                    device_id={EXPERT: other // 2, TENSOR: other % 2},
                    device_id_type=MESH_ID,
                )

        pl.semaphore_wait(barrier, 2 * self.reach - (1 if partner is None else 0))


def is_end(chain, source):
    return jnp.logical_or(source == 0, source == chain.reach - 1)


class Gather:
    def __init__(self, chain, blocks, send_sem, recv_sem, paired=False):
        self.chain, self.blocks, self.send_sem, self.recv_sem = chain, blocks, send_sem, recv_sem
        self.paired = paired

    def copy(self, source, column, piece, way, target):
        at = 2 * source + column
        return pltpu.make_async_remote_copy(
            src_ref=self.blocks.at[at, piece],
            dst_ref=self.blocks.at[at, piece],
            send_sem=self.send_sem.at[way, source, piece],
            recv_sem=self.recv_sem.at[at, piece],
            device_id=target,
            device_id_type=MESH_ID,
        )

    def over_x(self, source, piece, act):
        c = self.chain
        crosses = jnp.logical_and(is_end(c, source), source != c.z)
        if piece == 0:
            act(self.copy(source, c.x, 0, 0, c.aside))
        else:

            @pl.when(jnp.logical_not(crosses))
            def _():
                act(self.copy(source, c.x, piece, 0, c.aside))

    def each_way(self, source, piece, up, down, act):
        c = self.chain
        if up:

            @pl.when(c.has_above)
            def _():
                act(self.copy(source, c.x, piece, 1, c.above))

        if down:

            @pl.when(c.has_below)
            def _():
                act(self.copy(source, c.x, piece, 2, c.below))

        if not (self.paired and up and down):
            self.over_x(source, piece, act)

    def start(self):
        for piece in range(PIECES):
            self.each_way(self.chain.z, piece, True, True, lambda copy: copy.start())
        if self.paired:
            self.cross_out()

    def relay(self, distance):
        c = self.chain
        for piece in range(PIECES):

            @pl.when(c.z - distance >= 0)
            def _():
                self.copy(c.z - distance, c.x, piece, 1, c.below).wait_recv()
                self.each_way(c.z - distance, piece, True, False, lambda copy: copy.start())

            @pl.when(c.z + distance <= c.reach - 1)
            def _():
                self.copy(c.z + distance, c.x, piece, 2, c.above).wait_recv()
                self.each_way(c.z + distance, piece, False, True, lambda copy: copy.start())

    def cross_copy(self, end):
        c = self.chain
        return self.copy(end, 1 - c.x, PIECES - 1, 3, c.below if end else c.above)

    def cross_out(self):
        c = self.chain
        for end in (0, c.reach - 1):

            @pl.when(c.z == end)
            def _():
                self.cross_copy(end).start()

    def cross_relay(self, distance):
        c = self.chain
        for end in (0, c.reach - 1):
            last = c.reach - 1 - end

            @pl.when(jnp.where(c.z > end, c.z - end, end - c.z) == distance)
            def _():
                self.cross_copy(end).wait_recv()

                @pl.when(c.z != last)
                def _():
                    self.cross_copy(end).start()

    def wait_aside(self, source):
        c = self.chain
        self.copy(source, 1 - c.x, 0, 0, c.aside).wait_recv()

        @pl.when(jnp.logical_not(jnp.logical_and(is_end(c, source), source != c.z)))
        def _():
            self.copy(source, 1 - c.x, PIECES - 1, 0, c.aside).wait_recv()

    def drain(self):
        c = self.chain
        for piece in range(PIECES):
            self.each_way(c.z, piece, True, True, lambda copy: copy.wait_send())
            for distance in range(1, c.reach):

                @pl.when(c.z - distance >= 0)
                def _():
                    self.each_way(
                        c.z - distance, piece, True, False, lambda copy: copy.wait_send()
                    )

                @pl.when(c.z + distance <= c.reach - 1)
                def _():
                    self.each_way(
                        c.z + distance, piece, False, True, lambda copy: copy.wait_send()
                    )

        for end in (0, c.reach - 1):

            @pl.when(c.z != c.reach - 1 - end)
            def _():
                self.cross_copy(end).wait_send()


PIECES = 2
TAIL_PIECES = 4


class Reduce:
    def __init__(self, chain, part_at, from_x, from_z, sems, pieces=PIECES, cross=None):
        self.chain, self.part_at, self.from_x, self.from_z = chain, part_at, from_x, from_z
        self.pieces = pieces
        self.cross = cross
        self.x_send, self.x_recv, self.z_send, self.z_recv = sems

    def part_copy(self, home, piece):
        c = self.chain
        return pltpu.make_async_remote_copy(
            src_ref=self.part_at(home, 1 - c.x, piece),
            dst_ref=self.from_x.at[home, piece],
            send_sem=self.x_send.at[home, piece],
            recv_sem=self.x_recv.at[home, piece],
            device_id=c.aside,
            device_id_type=MESH_ID,
        )

    def sum_copy(self, home, piece, slot, target):
        return pltpu.make_async_remote_copy(
            src_ref=self.part_at(home, self.chain.x, piece),
            dst_ref=self.from_z.at[slot, piece],
            send_sem=self.z_send.at[home, piece],
            recv_sem=self.z_recv.at[slot, piece],
            device_id=target,
            device_id_type=MESH_ID,
        )

    def over_x(self, home, piece, act):
        c = self.chain
        if self.cross is None:
            act()
        else:
            crosses = jnp.logical_and(is_end(c, home), home != c.z)

            @pl.when(jnp.logical_not(jnp.logical_and(crosses, piece == self.pieces - 1)))
            def _():
                act()

    def start(self, k, piece):
        home = self.chain.near(k)
        self.over_x(home, piece, lambda: self.part_copy(home, piece).start())

    def arrive(self, k, piece):
        home = self.chain.near(k)
        self.over_x(home, piece, lambda: self.part_copy(home, piece).wait_recv())

    def own(self, home, piece):
        c = self.chain
        mine = self.part_at(home, c.x, piece)[...].astype(jnp.float32)
        came = self.from_x[home, piece].astype(jnp.float32)
        if self.cross is not None:
            crosses = jnp.logical_and(is_end(c, home), home != c.z)
            came = jnp.where(jnp.logical_and(crosses, piece == self.pieces - 1), 0.0, came)
        return mine + came

    def cross_copy(self, end):
        c = self.chain
        from_cross, send_sem, recv_sem = self.cross
        at = 1 if end else 0
        return pltpu.make_async_remote_copy(
            src_ref=self.part_at(end, 1 - c.x, self.pieces - 1),
            dst_ref=from_cross.at[at],
            send_sem=send_sem.at[at],
            recv_sem=recv_sem.at[at],
            device_id=c.above if end else c.below,
            device_id_type=MESH_ID,
        )

    def cross_step(self, distance):
        c = self.chain
        for end in (0, c.reach - 1):

            @pl.when(jnp.where(c.z > end, c.z - end, end - c.z) == distance)
            def _():
                @pl.when(c.z != c.reach - 1 - end)
                def _():
                    self.cross_copy(end).wait_recv()
                    mine = self.part_at(end, 1 - c.x, self.pieces - 1)
                    mine[...] = (
                        mine[...].astype(jnp.float32)
                        + self.cross[0][1 if end else 0].astype(jnp.float32)
                    ).astype(mine.dtype)

                @pl.when(c.z != end)
                def _():
                    self.cross_copy(end).start()

    def pass_on(self, k, piece):
        c = self.chain
        home = c.near(k)
        up = home > c.z
        comes = jnp.logical_or(
            jnp.logical_and(up, c.has_below), jnp.logical_and(home < c.z, c.has_above)
        )
        mine = self.part_at(home, c.x, piece)

        @pl.when(comes)
        def _():
            self.sum_copy(home, piece, home, c.above).wait_recv()
            mine[...] = (
                self.own(home, piece) + self.from_z[home, piece].astype(jnp.float32)
            ).astype(mine.dtype)

        @pl.when(jnp.logical_not(comes))
        def _():
            mine[...] = self.own(home, piece).astype(mine.dtype)

        @pl.when(up)
        def _():
            self.sum_copy(home, piece, home, c.above).start()

        @pl.when(home < c.z)
        def _():
            slot = jnp.where(home == c.z - 1, c.reach, home)
            self.sum_copy(home, piece, slot, c.below).start()

    def finish(self, piece, act):
        c = self.chain
        home = c.z

        @pl.when(c.has_below)
        def _():
            self.sum_copy(home, piece, home, c.below).wait_recv()

        @pl.when(c.has_above)
        def _():
            self.sum_copy(home, piece, c.reach, c.above).wait_recv()

        @pl.when(c.has_below & c.has_above)
        def _():
            act(
                piece,
                self.own(home, piece)
                + self.from_z[home, piece].astype(jnp.float32)
                + self.from_z[c.reach, piece].astype(jnp.float32),
            )

        @pl.when(jnp.logical_not(c.has_above))
        def _():
            act(piece, self.own(home, piece) + self.from_z[home, piece].astype(jnp.float32))

        @pl.when(jnp.logical_not(c.has_below))
        def _():
            act(piece, self.own(home, piece) + self.from_z[c.reach, piece].astype(jnp.float32))

    def drain(self):
        c = self.chain

        def one(home, carry):
            for piece in range(self.pieces):
                self.over_x(home, piece, lambda: self.part_copy(home, piece).wait_send())

                @pl.when(home != c.z)
                def _():
                    self.sum_copy(home, piece, home, c.above).wait_send()

            return carry

        lax.fori_loop(0, c.reach, one, 0)
        if self.cross is not None:
            for end in (0, c.reach - 1):

                @pl.when(c.z != end)
                def _():
                    self.cross_copy(end).wait_send()


def masked_softmax(logits, kept):
    top = jnp.max(jnp.where(kept, logits, NEG_BIG), axis=0, keepdims=True)
    exponent = jnp.where(kept, jnp.exp(jnp.where(kept, logits - top, 0.0)), 0.0)
    return exponent / jnp.sum(exponent, axis=0, keepdims=True)


def slot_gates(picks, gate_row):
    return jnp.sum(picks.astype(jnp.float32) * gate_row, axis=1, keepdims=True)


def one_hot_slots(slot_row, cap):
    length = slot_row.shape[1]
    at = lax.broadcasted_iota(jnp.int32, (cap, length), 0).astype(jnp.float32)
    return jnp.where(at == slot_row, 1.0, 0.0).astype(jnp.bfloat16)


def finish_pieces(summed, act):
    def one(piece, carry):
        summed.arrive(0, piece)
        summed.finish(piece, act)
        return carry

    lax.fori_loop(0, PIECES, one, 0)


def reduced_in_order(reach, summed, act):
    count = PIECES * (reach - 1)
    ahead = 3

    def place(i):
        return reach - 1 - i // PIECES, i % PIECES

    summed.cross_step(reach - 1)
    for i in range(ahead):
        summed.start(*place(i))

    def step(i, carry):
        summed.arrive(*place(i))

        @pl.when(i + ahead < count)
        def _():
            summed.start(*place(i + ahead))

        summed.pass_on(*place(i))

        @pl.when(jnp.logical_and(i % PIECES == 1, i < count - 1))
        def _():
            summed.cross_step(reach - 2 - i // PIECES)

        return carry

    lax.fori_loop(0, count, step, 0)
    summed.cross_step(0)
    summed.start(0, PIECES - 1)
    finish_pieces(summed, act)


def gathered_steps(reach, chain, rows, summed, compute):
    rows.start()

    def step(k, carry):
        @pl.when(k + 1 < reach)
        def _():
            rows.relay(k + 1)

        source = chain.near(k)
        rows.wait_aside(source)

        @pl.when(k == 0)
        def _():
            rows.cross_out()

        @pl.when(k > 0)
        def _():
            rows.cross_relay(k)

        @pl.when(k + 1 == reach)
        def _():
            summed.start(0, 0)

        compute(k, source)
        return carry

    lax.fori_loop(0, reach, step, 0)


def whole_rows(block):
    return block.reshape(-1, block.shape[-1])


def moe_forward_kernel(
    reach,
    tick,
    last,
    own_ref,
    h1_ref,
    ids_ref,
    router_ref,
    wg_hbm,
    wu_hbm,
    wd_hbm,
    *refs,
):
    refs = list(refs)
    if tick == 0:
        tops_ref, *shards = refs[:3]
        refs = refs[3:]
    out_ref, gates_ref, slots_ref, own_gates_ref, picked_hbm, g_hbm, u_hbm = refs[:7]
    refs = refs[7:]
    if tick == 0:
        tops_hbm, *halves = refs[:3]
        refs = refs[3:]
    (
        blocks,
        parts,
        from_x,
        from_z,
        from_cross,
        wg_ref,
        wu_ref,
        wd_ref,
        rows_in,
        rows_out,
        g_slots,
        u_slots,
        picks_of,
        ids_all,
        gather_send,
        gather_recv,
        x_send,
        x_recv,
        z_send,
        z_recv,
        cross_send,
        cross_recv,
        weight_sem,
        keep_sem,
        id_send,
        id_recv,
    ) = refs[:26]
    local = wg_ref.shape[0]
    cap = rows_in.shape[2] // 2
    experts = router_ref.shape[0]
    length = own_ref.shape[0]
    section = lax.axis_index(SECTION)
    chain = Chain(reach)

    def weight_copies():
        return [
            pltpu.make_async_copy(hbm, vmem, weight_sem.at[i])
            for i, (hbm, vmem) in enumerate(
                ((wg_hbm, wg_ref), (wu_hbm, wu_ref), (wd_hbm, wd_ref))
            )
        ]

    def keep_copies(k):
        source = chain.near(k)
        slot = k % 2 if isinstance(k, int) else lax.rem(k, 2)
        return [
            pltpu.make_async_copy(rows_in.at[slot], picked_hbm.at[source], keep_sem.at[0, k]),
            pltpu.make_async_copy(g_slots.at[slot], g_hbm.at[source], keep_sem.at[1, k]),
            pltpu.make_async_copy(u_slots.at[slot], u_hbm.at[source], keep_sem.at[2, k]),
        ]

    def id_copy(target, at):
        return pltpu.make_async_remote_copy(
            src_ref=ids_ref,
            dst_ref=ids_all.at[at],
            send_sem=id_send.at[target],
            recv_sem=id_recv.at[at],
            device_id={EXPERT: target // 2, TENSOR: target % 2},
            device_id_type=MESH_ID,
        )

    def compute(k, source):
        slot = lax.rem(k, 2)

        @pl.when(k == 0)
        def _():
            for copy in weight_copies():
                copy.wait()

        @pl.when(k >= 2)
        def _():
            for copy in keep_copies(k - 2):
                copy.wait()

        gate_of = {}
        ahead = lax.broadcasted_iota(jnp.int32, (length, length), 0)
        behind = lax.broadcasted_iota(jnp.int32, (length, length), 1)
        before = jnp.where(ahead < behind, 1.0, 0.0).astype(jnp.bfloat16)
        named = lax.rem(
            lax.broadcasted_iota(jnp.int32, (experts, length), 0) + chain.me * local, experts
        )
        for i in range(2):
            at = 2 * source + i

            @pl.when(at != chain.me)
            def _():
                id_copy(at, at).wait_recv()

            ids = ids_all[at]
            member = ids[0:1, :] == named
            for pick in range(1, TOPK):
                member = jnp.logical_or(member, ids[pick : pick + 1, :] == named)
            rows = whole_rows(blocks[at])
            gates = masked_softmax(dot(router_ref[...], rows, NT), member)
            gates_ref[at] = gates

            @pl.when(at == chain.me)
            def _():
                own_gates_ref[...] = gates

            mine = jnp.where(member[:8], 1.0, 0.0).astype(jnp.bfloat16)
            taken = jnp.where(member[:8], dot(mine, before), -1.0)
            slots_ref[at] = taken
            for e in range(local):
                picks = one_hot_slots(taken[e : e + 1, :], cap)
                picks_of[i, e * cap : (e + 1) * cap, :] = picks
                gate_of[i, e] = slot_gates(picks, gates[e : e + 1, :])
            gathered = dot(picks_of[i], rows).astype(jnp.bfloat16)
            for e in range(local):
                rows_in[slot, e, i * cap : (i + 1) * cap, :] = gathered[e * cap : (e + 1) * cap, :]
        for e in range(local):
            rows = rows_in[slot, e]
            gate_pre = dot(rows, wg_ref[e])
            up_pre = dot(rows, wu_ref[e])
            g_slots[slot, e] = gate_pre.astype(jnp.bfloat16)
            u_slots[slot, e] = up_pre.astype(jnp.bfloat16)
            hidden = (gate_pre * jax.nn.sigmoid(gate_pre) * up_pre).astype(jnp.bfloat16)
            produced = dot(hidden, wd_ref[e])
            for i in range(2):
                rows_out[i, e * cap : (e + 1) * cap, :] = (
                    produced[i * cap : (i + 1) * cap, :] * gate_of[i, e]
                ).astype(jnp.bfloat16)
        for i in range(2):
            share = dot(picks_of[i], rows_out[i], TN).astype(jnp.bfloat16)
            parts[2 * source + i] = share.reshape(parts.shape[1:])
        for copy in keep_copies(k):
            copy.start()

    def finish(piece, total):
        at = pl.ds(pl.multiple_of(piece * total.shape[0], total.shape[0]), total.shape[0])
        out_ref[at, :] = (h1_ref[at, :] + total).astype(jnp.bfloat16)

    def run():
        for copy in weight_copies():
            copy.start()
        blocks[chain.me] = own_ref[...].reshape(blocks.shape[1:])
        ids_all[chain.me] = ids_ref[...]
        chain.greet_group()
        for target in range(2 * reach):

            @pl.when(target != chain.me)
            def _():
                id_copy(target, chain.me).start()

        rows = Gather(chain, blocks, gather_send, gather_recv)
        summed = Reduce(
            chain,
            lambda home, column, piece: parts.at[2 * home + column, piece],
            from_x,
            from_z,
            (x_send, x_recv, z_send, z_recv),
            cross=(from_cross, cross_send, cross_recv),
        )
        gathered_steps(reach, chain, rows, summed, compute)
        reduced_in_order(reach, summed, finish)
        rows.drain()
        summed.drain()
        for target in range(2 * reach):

            @pl.when(target != chain.me)
            def _():
                id_copy(target, chain.me).wait_send()

        for k in (reach - 2, reach - 1):
            for copy in keep_copies(k):
                copy.wait()

    if tick == 0:
        second_send, second_recv, tops_sem, *refs = refs[26:]
        landed, (stage_sem, own_sem, half_sem, wx_send, wx_recv, core_send, core_recv) = (
            refs[:2],
            refs[2:],
        )
        core = lax.axis_index(DP)
        partner = {DP: 1 - core}
        chunks = local
        pieces = [(i, chunk) for i in range(2) for chunk in range(chunks)]

        def span(i, of_core, chunk):
            rows = shards[i].shape[0] // (2 * chunks)
            return pl.ds((of_core * chunks + chunk) * rows, rows)

        def stage(i, chunk, mine):
            rows, columns = shards[i].shape[0] // (2 * chunks), shards[i].shape[1]
            if mine:
                return rows_in.at[i, chunk, pl.ds(0, rows), pl.ds(0, columns)]
            if i == 0:
                return rows_out.at[chunk // 2, pl.ds(chunk % 2 * rows, rows), pl.ds(0, columns)]
            return from_x.at[chunk, 0, pl.ds(0, rows)]

        def stage_copy(i, chunk, mine):
            at = span(i, core if mine else 1 - core, chunk)
            return pltpu.make_async_copy(
                shards[i].at[at], stage(i, chunk, mine), stage_sem.at[i, chunk, 1 - mine]
            )

        def own_copy(i, chunk, mine):
            at = span(i, core if mine else 1 - core, chunk)
            return pltpu.make_async_copy(
                stage(i, chunk, mine), halves[i].at[chain.x, at], own_sem.at[i, chunk, 1 - mine]
            )

        def half_copy(i):
            return pltpu.make_async_copy(landed[i], halves[i].at[1 - chain.x], half_sem.at[i])

        def weight_x_copy(i, chunk):
            return pltpu.make_async_remote_copy(
                src_ref=stage(i, chunk, 1),
                dst_ref=landed[i].at[span(i, core, chunk)],
                send_sem=wx_send.at[i, chunk],
                recv_sem=wx_recv.at[i, chunk],
                device_id=chain.aside,
                device_id_type=MESH_ID,
            )

        def weight_core_copy(i, chunk, of_core):
            at = landed[i].at[span(i, of_core, chunk)]
            return pltpu.make_async_remote_copy(
                src_ref=at,
                dst_ref=at,
                send_sem=core_send.at[i, chunk],
                recv_sem=core_recv.at[i, chunk],
                device_id=partner,
                device_id_type=MESH_ID,
            )

        @pl.when(section == 0)
        def _():
            run()

        @pl.when(section != 0)
        def _():
            for mine in (1, 0):
                for i, chunk in pieces:
                    stage_copy(i, chunk, mine).start()
            own_tops = [
                pltpu.make_async_copy(
                    tops_ref.at[micro], buffer.at[pl.ds(2 * chain.z, 2)], tops_sem.at[micro]
                )
                for micro, buffer in enumerate((blocks, parts))
            ]
            for copy in own_tops:
                copy.start()
            chain.greet_group(partner)
            for copy in own_tops:
                copy.wait()
            both = (
                Gather(chain, blocks, gather_send, gather_recv, True),
                Gather(chain, parts, second_send, second_recv, True),
            )
            copies = [
                pltpu.make_async_copy(blocks, tops_hbm.at[0], tops_sem.at[0]),
                pltpu.make_async_copy(parts, tops_hbm.at[1], tops_sem.at[1]),
            ]
            both[0].start()
            both[1].start()
            for i, chunk in pieces:
                stage_copy(i, chunk, 1).wait()
                weight_x_copy(i, chunk).start()
                own_copy(i, chunk, 1).start()
            for i, chunk in pieces:
                stage_copy(i, chunk, 0).wait()
                own_copy(i, chunk, 0).start()
            for rows in both:
                for distance in range(1, reach):
                    rows.relay(distance)
                    rows.cross_relay(distance)
            for i, chunk in pieces:
                weight_x_copy(i, chunk).wait_recv()
                weight_core_copy(i, chunk, core).start()
            for i in range(2):
                for chunk in range(chunks):
                    weight_core_copy(i, chunk, 1 - core).wait_recv()
                half_copy(i).start()
            for rows, copy in zip(both, copies):
                for k in range(1, reach):
                    rows.wait_aside(chain.near(k))
                copy.start()
            for rows in both:
                rows.drain()
            for i, chunk in pieces:
                weight_x_copy(i, chunk).wait_send()
                weight_core_copy(i, chunk, core).wait_send()
                for mine in (1, 0):
                    own_copy(i, chunk, mine).wait()
            for i in range(2):
                half_copy(i).wait()
            for copy in copies:
                copy.wait()

    elif tick == last:

        @pl.when(section != 0)
        def _():
            run()

    else:
        run()


def exchange_scratch(reach, length, width):
    piece = (PIECES, length // PIECES, width)
    return [
        pltpu.VMEM((2 * reach,) + piece, jnp.bfloat16),
        pltpu.VMEM((2 * reach,) + piece, jnp.bfloat16),
        pltpu.VMEM((reach,) + piece, jnp.bfloat16),
        pltpu.VMEM((reach + 1,) + piece, jnp.bfloat16),
        pltpu.VMEM((2,) + piece[1:], jnp.bfloat16),
    ]


def exchange_sems(reach):
    dma = pltpu.SemaphoreType.DMA
    return [
        dma((4, reach, PIECES)),
        dma((2 * reach, PIECES)),
        dma((reach, PIECES)),
        dma((reach, PIECES)),
        dma((reach, PIECES)),
        dma((reach + 1, PIECES)),
        dma((2,)),
        dma((2,)),
    ]


def moe_forward_call(reach, tick, last, own, h1, ids, router, wg, wu, wd, firsts):
    length, width = own.shape
    local, _, hidden = wg.shape
    cap = slot_count(length)
    experts = router.shape[0]
    vmem = pl.BlockSpec(memory_space=pltpu.VMEM)
    anywhere = pl.BlockSpec(memory_space=pl.ANY)
    slots = (reach, local, 2 * cap, hidden)
    first = tick == 0
    all_rows = (2 * reach, PIECES, length // PIECES, width)
    return pl.pallas_call(
        functools.partial(moe_forward_kernel, reach, tick, last),
        in_specs=[vmem] * 4 + [anywhere] * 3 + [anywhere] * 3 * first,
        out_specs=[vmem] * 4 + [anywhere] * 3 + [anywhere] * 3 * first,
        out_shape=[
            jax.ShapeDtypeStruct((length, width), jnp.bfloat16),
            jax.ShapeDtypeStruct((2 * reach, experts, length), jnp.float32),
            jax.ShapeDtypeStruct((2 * reach, 8, length), jnp.float32),
            jax.ShapeDtypeStruct((experts, length), jnp.float32),
            jax.ShapeDtypeStruct(slots[:3] + (width,), jnp.bfloat16),
            jax.ShapeDtypeStruct(slots, jnp.bfloat16),
            jax.ShapeDtypeStruct(slots, jnp.bfloat16),
        ]
        + (
            [jax.ShapeDtypeStruct((2,) + all_rows, jnp.bfloat16)]
            + [jax.ShapeDtypeStruct((2,) + shard.shape, shard.dtype) for shard in firsts[1:]]
        )
        * first,
        scratch_shapes=exchange_scratch(reach, length, width)
        + [
            pltpu.VMEM(wg.shape, jnp.bfloat16),
            pltpu.VMEM(wu.shape, jnp.bfloat16),
            pltpu.VMEM(wd.shape, jnp.bfloat16),
            pltpu.VMEM((2, local, 2 * cap, width), jnp.bfloat16),
            pltpu.VMEM((2, local * cap, width), jnp.bfloat16),
            pltpu.VMEM((2,) + slots[1:], jnp.bfloat16),
            pltpu.VMEM((2,) + slots[1:], jnp.bfloat16),
            pltpu.VMEM((2, local * cap, length), jnp.bfloat16),
            pltpu.VMEM((2 * reach, TOPK, length), jnp.int32),
        ]
        + exchange_sems(reach)
        + [
            pltpu.SemaphoreType.DMA((3,)),
            pltpu.SemaphoreType.DMA((3, reach)),
            pltpu.SemaphoreType.DMA((2 * reach,)),
            pltpu.SemaphoreType.DMA((2 * reach,)),
        ]
        + (
            exchange_sems(reach)[:2]
            + [pltpu.SemaphoreType.DMA((2,))]
            + [pltpu.VMEM(shard.shape, shard.dtype) for shard in firsts[1:]]
            + [
                pltpu.SemaphoreType.DMA((2, local, 2)),
                pltpu.SemaphoreType.DMA((2, local, 2)),
                pltpu.SemaphoreType.DMA((2,)),
            ]
            + [pltpu.SemaphoreType.DMA((2, local))] * 4
        )
        * first,
        compiler_params=pltpu.CompilerParams(
            collective_id=1 + tick, has_side_effects=True, vmem_limit_bytes=62 * MIB
        ),
        cost_estimate=pl.CostEstimate(
            flops=20 * 10**9, bytes_accessed=45 * 10**6, transcendentals=2 * 10**6
        ),
        name="moe_forward",
    )(own, h1, ids, router, wg, wu, wd, *(firsts * first))


def moe_backward_kernel(
    reach,
    tick,
    last,
    own_ref,
    slots_first,
    slots_second,
    gates_first,
    gates_second,
    g_first,
    g_second,
    u_first,
    u_second,
    wg_hbm,
    wu_hbm,
    wd_hbm,
    tops_hbm,
    after,
    out_ref,
    home_gates_ref,
    picked_hbm,
    gg_hbm,
    gu_hbm,
    hg_hbm,
    blocks,
    parts,
    from_x,
    from_z,
    from_cross,
    wg_ref,
    wu_ref,
    wd_ref,
    rows_in,
    rows_out,
    g_slots,
    u_slots,
    gg_slots,
    gu_slots,
    hg_slots,
    picks_of,
    gate_parts,
    gate_from,
    gather_send,
    gather_recv,
    x_send,
    x_recv,
    z_send,
    z_recv,
    cross_send,
    cross_recv,
    weight_sem,
    keep_sem,
    load_sem,
    gate_send,
    gate_recv,
    tops_sem,
):
    del after
    local = wg_ref.shape[0]
    cap = rows_in.shape[2] // 2
    section = lax.axis_index(SECTION)
    chain = Chain(reach)
    me = chain.me

    def weight_copies():
        return [
            pltpu.make_async_copy(hbm, vmem, weight_sem.at[i])
            for i, (hbm, vmem) in enumerate(
                ((wd_hbm, wd_ref), (wg_hbm, wg_ref), (wu_hbm, wu_ref))
            )
        ]

    def load_copies(step, source, first):
        slot = step % 2 if isinstance(step, int) else lax.rem(step, 2)
        return [
            pltpu.make_async_copy(
                (g_first if first else g_second).at[source], g_slots.at[slot], load_sem.at[0, step]
            ),
            pltpu.make_async_copy(
                (u_first if first else u_second).at[source], u_slots.at[slot], load_sem.at[1, step]
            ),
        ]

    def keep_copies(step, source):
        slot = step % 2 if isinstance(step, int) else lax.rem(step, 2)
        return [
            pltpu.make_async_copy(rows_in.at[slot], picked_hbm.at[source], keep_sem.at[0, step]),
            pltpu.make_async_copy(gg_slots.at[slot], gg_hbm.at[source], keep_sem.at[1, step]),
            pltpu.make_async_copy(gu_slots.at[slot], gu_hbm.at[source], keep_sem.at[2, step]),
            pltpu.make_async_copy(hg_slots.at[slot], hg_hbm.at[source], keep_sem.at[3, step]),
        ]

    def gate_copy(target, at):
        return pltpu.make_async_remote_copy(
            src_ref=gate_parts.at[target],
            dst_ref=gate_from.at[at],
            send_sem=gate_send.at[target],
            recv_sem=gate_recv.at[at],
            device_id={EXPERT: target // 2, TENSOR: target % 2},
            device_id_type=MESH_ID,
        )

    def compute(step, source_of, first):
        source = source_of(step)
        slot = lax.rem(step, 2)

        @pl.when(step == 0)
        def _():
            for copy in weight_copies():
                copy.wait()

        @pl.when(step >= 2)
        def _():
            for copy in keep_copies(step - 2, source_of(step - 2)):
                copy.wait()

        for copy in load_copies(step, source, first):
            copy.wait()
        slots_ref = slots_first if first else slots_second
        gates_ref = gates_first if first else gates_second
        gate_of = {}
        for i in range(2):
            at = 2 * source + i
            for e in range(local):
                picks = one_hot_slots(slots_ref[at, e : e + 1, :], cap)
                picks_of[i, e * cap : (e + 1) * cap, :] = picks
                gate_of[i, e] = slot_gates(picks, gates_ref[at, e : e + 1, :])
            gathered = dot(picks_of[i], whole_rows(blocks[at])).astype(jnp.bfloat16)
            for e in range(local):
                rows_in[slot, e, i * cap : (i + 1) * cap, :] = gathered[e * cap : (e + 1) * cap, :]
        for e in range(local):
            plain = dot(rows_in[slot, e], wd_ref[e], NT)
            gate_pre = g_slots[slot, e].astype(jnp.float32)
            up_pre = u_slots[slot, e].astype(jnp.float32)
            sg = jax.nn.sigmoid(gate_pre)
            hidden = gate_pre * sg * up_pre
            gate_col = jnp.concatenate([gate_of[i, e] for i in range(2)], axis=0)
            grad_gate_col = jnp.sum(hidden * plain, axis=1, keepdims=True)
            grad_hidden = plain * gate_col
            grad_gate = (grad_hidden * up_pre * sg * (1.0 + gate_pre * (1.0 - sg))).astype(
                jnp.bfloat16
            )
            grad_up = (grad_hidden * gate_pre * sg).astype(jnp.bfloat16)
            gg_slots[slot, e] = grad_gate
            gu_slots[slot, e] = grad_up
            hg_slots[slot, e] = (hidden * gate_col).astype(jnp.bfloat16)
            grad_rows = dot(grad_gate, wg_ref[e], NT) + dot(grad_up, wu_ref[e], NT)
            for i in range(2):
                at = 2 * source + i
                rows = slice(i * cap, (i + 1) * cap)
                rows_out[i, e * cap : (e + 1) * cap, :] = grad_rows[rows, :].astype(jnp.bfloat16)
                picks = picks_of[i, e * cap : (e + 1) * cap, :].astype(jnp.float32)
                gate_parts[at, e : e + 1, :] = jnp.sum(
                    picks * grad_gate_col[rows, :], axis=0, keepdims=True
                )
        for i in range(2):
            share = dot(picks_of[i], rows_out[i], TN).astype(jnp.bfloat16)
            parts[2 * source + i] = share.reshape(parts.shape[1:])
        for copy in keep_copies(step, source):
            copy.start()

        @pl.when(step + 2 < reach)
        def _():
            for copy in load_copies(step + 2, source_of(step + 2), first):
                copy.start()

        for i in range(2):
            at = 2 * source + i

            @pl.when(at != me)
            def _():
                gate_copy(at, me).start()

    def finish(piece, total):
        at = pl.ds(pl.multiple_of(piece * total.shape[0], total.shape[0]), total.shape[0])
        out_ref[at, :] = total

    def run(gathered):
        first = gathered

        def source_of(step):
            if isinstance(step, int):
                return chain.near(step if gathered else reach - 1 - step)
            return chain.near(step if gathered else reach - 1 - step)

        def top_copy(step):
            pair = pl.ds(2 * source_of(step), 2)
            return pltpu.make_async_copy(
                tops_hbm.at[min(tick, 1), pair], blocks.at[pair], tops_sem.at[step]
            )

        for step in range(2):
            for copy in load_copies(step, source_of(step), first):
                copy.start()
        if not gathered:
            for step in range(reach):
                top_copy(step).start()
        for copy in weight_copies():
            copy.start()
        chain.greet_group()
        summed = Reduce(
            chain,
            lambda home, column, piece: parts.at[2 * home + column, piece],
            from_x,
            from_z,
            (x_send, x_recv, z_send, z_recv),
            cross=(from_cross, cross_send, cross_recv),
        )
        if gathered:
            blocks[me] = own_ref[...].reshape(blocks.shape[1:])
            rows = Gather(chain, blocks, gather_send, gather_recv)
            gathered_steps(
                reach, chain, rows, summed, lambda step, source: compute(step, source_of, first)
            )
            reduced_in_order(reach, summed, finish)
            rows.drain()
        else:

            def step_back(step, carry):
                k = reach - 1 - step
                top_copy(step).wait()
                compute(step, source_of, first)
                summed.start(k, 0)

                @pl.when(k > 0)
                def _():
                    summed.start(k, PIECES - 1)
                    summed.cross_step(k)

                @pl.when(step >= 1)
                def _():
                    for piece in range(PIECES):
                        summed.arrive(k + 1, piece)
                        summed.pass_on(k + 1, piece)

                return carry

            lax.fori_loop(0, reach, step_back, 0)
            summed.cross_step(0)
            summed.start(0, PIECES - 1)
            finish_pieces(summed, finish)
        summed.drain()
        home_gates_ref[0] = gate_parts[me, :local]
        for at in range(2 * reach):

            @pl.when(at != me)
            def _():
                gate_copy(at, me).wait_send()
                gate_copy(at, at).wait_recv()
                home_gates_ref[lax.rem(at - me + 2 * reach, 2 * reach)] = gate_from[at, :local]

        for step in (reach - 2, reach - 1):
            for copy in keep_copies(step, source_of(step)):
                copy.wait()

    if tick > 0:

        @pl.when(section == 0)
        def _():
            run(True)

    if tick < last:

        @pl.when(section != 0)
        def _():
            run(False)


def moe_backward_call(
    reach, tick, last, own, slots_two, gates_two, g_two, u_two, wg, wu, wd, tops, after
):
    length, width = own.shape
    local, _, hidden = wg.shape
    cap = slot_count(length)
    vmem = pl.BlockSpec(memory_space=pltpu.VMEM)
    anywhere = pl.BlockSpec(memory_space=pl.ANY)
    slot_rows = (reach, local, 2 * cap, hidden)
    kept = jax.ShapeDtypeStruct(slot_rows, jnp.bfloat16)
    return pl.pallas_call(
        functools.partial(moe_backward_kernel, reach, tick, last),
        in_specs=[vmem] * 5 + [anywhere] * 9,
        out_specs=[vmem, vmem] + [anywhere] * 4,
        out_shape=[
            jax.ShapeDtypeStruct((length, width), jnp.float32),
            jax.ShapeDtypeStruct((2 * reach, local, length), jnp.float32),
            jax.ShapeDtypeStruct(slot_rows[:3] + (width,), jnp.bfloat16),
            kept,
            kept,
            kept,
        ],
        scratch_shapes=exchange_scratch(reach, length, width)
        + [
            pltpu.VMEM(wg.shape, jnp.bfloat16),
            pltpu.VMEM(wu.shape, jnp.bfloat16),
            pltpu.VMEM(wd.shape, jnp.bfloat16),
            pltpu.VMEM((2, local, 2 * cap, width), jnp.bfloat16),
            pltpu.VMEM((2, local * cap, width), jnp.bfloat16),
        ]
        + [pltpu.VMEM((2,) + slot_rows[1:], jnp.bfloat16)] * 5
        + [
            pltpu.VMEM((2, local * cap, length), jnp.bfloat16),
            pltpu.VMEM((2 * reach, 8, length), jnp.float32),
            pltpu.VMEM((2 * reach, 8, length), jnp.float32),
        ]
        + exchange_sems(reach)
        + [
            pltpu.SemaphoreType.DMA((3,)),
            pltpu.SemaphoreType.DMA((4, reach)),
            pltpu.SemaphoreType.DMA((2, reach)),
            pltpu.SemaphoreType.DMA((2 * reach,)),
            pltpu.SemaphoreType.DMA((2 * reach,)),
            pltpu.SemaphoreType.DMA((reach,)),
        ],
        compiler_params=pltpu.CompilerParams(
            collective_id=4 + tick, has_side_effects=True, vmem_limit_bytes=62 * MIB
        ),
        cost_estimate=pl.CostEstimate(
            flops=20 * 10**9, bytes_accessed=55 * 10**6, transcendentals=2 * 10**6
        ),
        name="moe_backward",
    )(own, *slots_two, *gates_two, *g_two, *u_two, wg, wu, wd, tops, after)


def middle_weights_kernel(
    x_first, x_second, dh_ref, gg_ref, gu_ref, hg_ref, after, wg_ref, wu_ref, wd_ref
):
    del after
    hidden = gg_ref.shape[3]
    wide = dh_ref.shape[3]
    rows = of_section(x_first, x_second).reshape(-1, wide)
    wg_ref[0] = dot(rows, gg_ref[...].reshape(-1, hidden), TN).astype(jnp.bfloat16)
    wu_ref[0] = dot(rows, gu_ref[...].reshape(-1, hidden), TN).astype(jnp.bfloat16)
    wd_ref[0] = dot(
        hg_ref[...].reshape(-1, hidden), dh_ref[...].reshape(-1, wide), TN
    ).astype(jnp.bfloat16)


def middle_weights(x_two, dh, gg, gu, hg, after):
    groups, local, rows, width = dh.shape
    hidden = gg.shape[3]
    tiles = width // hidden
    wide = width // tiles
    tiled = pl.BlockSpec((groups, 1, rows, wide), lambda e, t: (0, e, 0, t))
    held = pl.BlockSpec((groups, 1, rows, hidden), lambda e, t: (0, e, 0, 0))
    up = jax.ShapeDtypeStruct((local, width, hidden), jnp.bfloat16)
    return pl.pallas_call(
        middle_weights_kernel,
        grid=(local, tiles),
        in_specs=[tiled] * 3 + [held] * 3 + [pl.BlockSpec(memory_space=pl.ANY)],
        out_specs=[
            pl.BlockSpec((1, wide, hidden), lambda e, t: (e, t, 0)),
            pl.BlockSpec((1, wide, hidden), lambda e, t: (e, t, 0)),
            pl.BlockSpec((1, hidden, wide), lambda e, t: (e, 0, t)),
        ],
        out_shape=[up, up, jax.ShapeDtypeStruct((local, hidden, width), jnp.bfloat16)],
        compiler_params=pltpu.CompilerParams(vmem_limit_bytes=62 * MIB),
        cost_estimate=pl.CostEstimate(
            flops=30 * 10**9, bytes_accessed=60 * 10**6, transcendentals=0
        ),
        name="middle_weights",
    )(*x_two, dh, gg, gu, hg, after)


def tail_kernel(
    reach,
    tiles,
    dense_hbm,
    x_hbm,
    dh_first,
    dh_last,
    gg_first,
    gg_last,
    gu_first,
    gu_last,
    hg_first,
    hg_last,
    wg_before,
    wu_before,
    wd_before,
    small_first,
    small_both,
    small_last,
    ends_back_one,
    ends_forward_one,
    ends_back_two,
    ends_forward_two,
    query_out,
    key_out,
    value_out,
    out_out,
    wg_out,
    wu_out,
    wd_out,
    small_out,
    ends_out,
    mine,
    theirs,
    from_core,
    from_x,
    from_z,
    whole,
    x_rows,
    dh_rows,
    slots,
    before,
    wg_tile,
    wu_tile,
    wd_tile,
    wg_from,
    wu_from,
    wd_from,
    small_held,
    small_came,
    small_z,
    ends_held,
    ends_came,
    mine_sem,
    theirs_sem,
    core_send,
    core_recv,
    x_send,
    x_recv,
    z_send,
    z_recv,
    ring_send,
    ring_recv,
    last_send,
    last_recv,
    out_sem,
    row_sem,
    slot_sem,
    before_sem,
    tile_sem,
    tile_send,
    tile_recv,
    free_sem,
    small_send,
    small_recv,
    ends_load,
    ends_keep,
    ends_send,
    ends_recv,
):
    section = lax.axis_index(SECTION)
    core = lax.axis_index(DP)
    partner = {DP: 1 - core}
    chain = Chain(reach)
    x = chain.x
    z = chain.z
    quarter = mine.shape[3]
    local = gg_first.shape[1]
    width = x_hbm.shape[3]
    hidden = gg_first.shape[3]
    wide = width // tiles

    def mine_copy(half):
        return pltpu.make_async_copy(dense_hbm.at[half, core], mine.at[half], mine_sem.at[half])

    def theirs_copy(half, piece):
        return pltpu.make_async_copy(
            dense_hbm.at[half, 1 - core, :, piece],
            theirs.at[half, :, piece],
            theirs_sem.at[half, piece],
        )

    def core_copy(half, piece):
        return pltpu.make_async_remote_copy(
            src_ref=theirs.at[half, :, piece],
            dst_ref=from_core.at[half, :, piece],
            send_sem=core_send.at[half, piece],
            recv_sem=core_recv.at[half, piece],
            device_id=partner,
            device_id_type=MESH_ID,
        )

    def add_core(half, k, piece):
        home = chain.near(k)

        @pl.when(k == reach - 1)
        def _():
            core_copy(half, piece).wait_recv()

        mine[half, home, piece] = (
            mine[half, home, piece].astype(jnp.float32)
            + from_core[half, home, piece].astype(jnp.float32)
        ).astype(jnp.bfloat16)

    summed = Reduce(
        chain,
        lambda home, column, piece: mine.at[column, home, piece],
        from_x,
        from_z,
        (x_send, x_recv, z_send, z_recv),
        TAIL_PIECES,
    )

    def ring_copy(source, piece, way, target):
        return pltpu.make_async_remote_copy(
            src_ref=whole.at[core, source, piece],
            dst_ref=whole.at[core, source, piece],
            send_sem=ring_send.at[way, source, piece],
            recv_sem=ring_recv.at[source, piece],
            device_id=target,
            device_id_type=MESH_ID,
        )

    def last_copy(source, piece, side):
        return pltpu.make_async_remote_copy(
            src_ref=whole.at[side, source, piece],
            dst_ref=whole.at[side, source, piece],
            send_sem=last_send.at[source, piece],
            recv_sem=last_recv.at[source, piece],
            device_id=partner,
            device_id_type=MESH_ID,
        )

    def out_copies(side, source):
        block = whole.at[side, source]
        at = side * reach + source
        first = query_out.shape[3]
        second = first + key_out.shape[3]
        third = second + value_out.shape[3]
        half = block.shape[2] - third
        columns = pl.ds(pl.multiple_of(side * half, half), half)
        return [
            pltpu.make_async_copy(block.at[:, :, found], to, out_sem.at[side, source, i])
            for i, (found, to) in enumerate(
                (
                    (pl.ds(0, first), query_out.at[at]),
                    (pl.ds(first, second - first), key_out.at[at]),
                    (pl.ds(second, third - second), value_out.at[at]),
                    (pl.ds(third, half), out_out.at[source, :, :, columns]),
                )
            )
        ]

    def spread_block(source, piece, up, down):
        if up:

            @pl.when(chain.has_above)
            def _():
                ring_copy(source, piece, 0, chain.above).start()

        if down:

            @pl.when(chain.has_below)
            def _():
                ring_copy(source, piece, 1, chain.below).start()

        last_copy(source, piece, core).start()

        @pl.when(piece == TAIL_PIECES - 1)
        def _():
            for copy in out_copies(core, source):
                copy.start()

    def relay(distance, piece):
        @pl.when(z - distance >= 0)
        def _():
            ring_copy(z - distance, piece, 0, chain.below).wait_recv()
            spread_block(z - distance, piece, True, False)

        @pl.when(z + distance <= reach - 1)
        def _():
            ring_copy(z + distance, piece, 1, chain.above).wait_recv()
            spread_block(z + distance, piece, False, True)

    depth = wg_tile.shape[0]

    def spot(index):
        expert = index // tiles
        return expert, pl.ds(pl.multiple_of(lax.rem(index, tiles) * wide, wide), wide)

    def tile_loads(index, first):
        expert, at = spot(index)
        slot = lax.rem(index, 2)
        back = dh_last if first else dh_first
        return [
            pltpu.make_async_copy(
                x_hbm.at[:, expert, :, at], x_rows.at[slot], row_sem.at[slot, 0]
            ),
            pltpu.make_async_copy(
                back.at[:, expert, :, at], dh_rows.at[slot], row_sem.at[slot, 1]
            ),
        ] + [
            pltpu.make_async_copy(ref, before.at[slot, i], before_sem.at[slot, i])
            for i, ref in enumerate(
                (wg_before.at[expert, at], wu_before.at[expert, at], wd_before.at[expert, :, at])
            )
        ]

    def slot_loads(expert, first):
        slot = lax.rem(expert, 2)
        return [
            pltpu.make_async_copy(
                (two if first else one).at[:, expert], slots.at[slot, i], slot_sem.at[slot, i]
            )
            for i, (one, two) in enumerate(
                ((gg_first, gg_last), (gu_first, gu_last), (hg_first, hg_last))
            )
        ]

    def start(copies):
        @pl.when(section == 0)
        def _():
            for copy in copies(True):
                copy.start()

        @pl.when(section != 0)
        def _():
            for copy in copies(False):
                copy.start()

    held = ((wg_tile, wg_from), (wu_tile, wu_from), (wd_tile, wd_from))

    def tile_sends(index):
        slot = lax.rem(index, depth)
        return [
            pltpu.make_async_remote_copy(
                src_ref=tile.at[slot],
                dst_ref=came.at[slot],
                send_sem=tile_send.at[slot, i],
                recv_sem=tile_recv.at[slot, i],
                device_id=partner,
                device_id_type=MESH_ID,
            )
            for i, (tile, came) in enumerate(held)
        ]

    def tile_stores(index):
        expert, at = spot(index)
        slot = lax.rem(index, depth)
        outs = (wg_out.at[expert, at], wu_out.at[expert, at], wd_out.at[expert, :, at])
        return [
            pltpu.make_async_copy(came.at[slot], out, tile_sem.at[slot, i])
            for i, ((_, came), out) in enumerate(zip(held, outs))
        ]

    count = local * tiles

    def sum_tile(index):
        slot = lax.rem(index, depth)
        for copy, (tile, came) in zip(tile_sends(index), held):
            copy.wait_recv()
            came[slot] = (
                tile[slot].astype(jnp.float32) + came[slot].astype(jnp.float32)
            ).astype(jnp.bfloat16)
        for copy in tile_stores(index):
            copy.start()

    def one_tile(index):
        slot = lax.rem(index, 2)
        expert = index // tiles
        taken = lax.rem(expert, 2)

        @pl.when(index + 1 < count)
        def _():
            start(functools.partial(tile_loads, index + 1))

        @pl.when(jnp.logical_and(lax.rem(index, tiles) == 0, expert + 1 < local))
        def _():
            start(functools.partial(slot_loads, expert + 1))

        @pl.when(lax.rem(index, tiles) == 0)
        def _():
            for copy in slot_loads(expert, True):
                copy.wait()

        for copy in tile_loads(index, True):
            copy.wait()

        @pl.when(index >= depth)
        def _():
            for copy in tile_sends(index - depth):
                copy.wait_send()
            for copy in tile_stores(index - depth):
                copy.wait()
            pl.semaphore_signal(free_sem, inc=1, device_id=partner, device_id_type=MESH_ID)
            pl.semaphore_wait(free_sem, 1)

        to = lax.rem(index, depth)
        rows = x_rows[slot].reshape(-1, wide)
        found = (
            dot(rows, slots[taken, 0].reshape(-1, hidden), TN),
            dot(rows, slots[taken, 1].reshape(-1, hidden), TN),
            dot(slots[taken, 2].reshape(-1, hidden), dh_rows[slot].reshape(-1, wide), TN),
        )
        for i, (one, (tile, _)) in enumerate(zip(found, held)):
            tile[to] = (one + before[slot, i].astype(jnp.float32)).astype(jnp.bfloat16)
        for copy in tile_sends(index):
            copy.start()

        @pl.when(index >= 2)
        def _():
            sum_tile(index - 2)

    def tile_run(low, high):
        lax.fori_loop(low, high, lambda index, carry: (one_tile(index), carry)[1], 0)

    def small_copy(to, i):
        if i < 2:
            return pltpu.make_async_remote_copy(
                src_ref=small_held.at[i],
                dst_ref=small_came.at[i],
                send_sem=small_send.at[i],
                recv_sem=small_recv.at[i],
                device_id=to,
                device_id_type=MESH_ID,
            )
        return pltpu.make_async_remote_copy(
            src_ref=small_z.at[z],
            dst_ref=small_z.at[z],
            send_sem=small_send.at[2 + to],
            recv_sem=small_recv.at[2 + z],
            device_id={EXPERT: to},
            device_id_type=MESH_ID,
        )

    def others(act):
        for other in range(reach):

            @pl.when(other != z)
            def _():
                act(other)

    def small_step(stage):
        if stage == 0:
            total = small_both[...] + of_section(small_last, small_first)
            experts = 2 * reach * local
            small_held[0, :experts] = pltpu.roll(total[:experts], chain.me * local, 0)
            small_held[0, experts:] = total[experts:]
            small_copy(partner, 0).start()
        elif stage == 1:
            small_copy(partner, 0).wait_recv()
            small_held[1] = small_held[0] + small_came[0]
            small_copy(chain.aside, 1).start()
        elif stage == 2:
            small_copy(chain.aside, 1).wait_recv()
            small_z[z] = small_held[1] + small_came[1]
            others(lambda other: small_copy(other, 2).start())
        else:

            def wait(other):
                pltpu.make_async_remote_copy(
                    src_ref=small_z.at[other],
                    dst_ref=small_z.at[other],
                    send_sem=small_send.at[2 + other],
                    recv_sem=small_recv.at[2 + other],
                    device_id={EXPERT: other},
                    device_id_type=MESH_ID,
                ).wait_recv()

            others(wait)
            total = small_z[0]
            for other in range(1, reach):
                total = total + small_z[other]
            small_out[...] = total

    ends_of = ((ends_back_one, ends_forward_one), (ends_back_two, ends_forward_two))

    def ends_copy(m):
        return pltpu.make_async_remote_copy(
            src_ref=ends_held.at[m],
            dst_ref=ends_came.at[m],
            send_sem=ends_send.at[m],
            recv_sem=ends_recv.at[m],
            device_id=chain.aside,
            device_id_type=MESH_ID,
        )

    def ends_store(m, other):
        found = ends_came if other else ends_held
        at = 1 - x if other else x
        return pltpu.make_async_copy(found.at[m], ends_out.at[m, at], ends_keep.at[m, int(other)])

    for piece in range(TAIL_PIECES):
        for half in (1 - x, x):
            theirs_copy(half, piece).start()
    for half in range(2):
        mine_copy(half).start()
    for m in range(2):
        start_of_section(*ends_of[m], ends_held.at[m], ends_load.at[m])

    barrier = pltpu.get_barrier_semaphore()
    pl.semaphore_signal(barrier, inc=1, device_id=partner, device_id_type=MESH_ID)
    pl.semaphore_signal(barrier, inc=1, device_id=chain.aside, device_id_type=MESH_ID)
    others(
        lambda other: pl.semaphore_signal(
            barrier, inc=1, device_id={EXPERT: other}, device_id_type=MESH_ID
        )
    )
    pl.semaphore_wait(barrier, 1 + reach)

    def core_start(piece):
        for half in (1 - x, x):
            theirs_copy(half, piece).wait()
            core_copy(half, piece).start()

    for piece in range(2):
        core_start(piece)
    small_step(0)
    start(functools.partial(slot_loads, 0))
    start(functools.partial(tile_loads, 0))
    for m in range(2):
        pltpu.make_async_copy(ends_of[m][0], ends_held.at[m], ends_load.at[m]).wait()
        ends_store(m, False).start()
    ends_copy(0).start()
    for half in range(2):
        mine_copy(half).wait()

    steps = TAIL_PIECES * reach
    ahead = 3

    def place(i):
        return reach - 1 - i % reach, i // reach

    def launch(i):
        k, piece = place(i)
        add_core(1 - x, k, piece)
        summed.start(k, piece)

    def finish(piece, total):
        whole[core, z, piece] = total.astype(jnp.bfloat16)

    def late(i):
        def due(offset, act):
            since = i - offset
            if isinstance(i, int):
                if since >= 0 and since % reach == 0 and since // reach < TAIL_PIECES:
                    act(since // reach)
            else:

                @pl.when(jnp.logical_and(since >= 0, lax.rem(since, reach) == 0))
                def _():
                    act(since // reach)

        def own(piece):
            summed.finish(piece, finish)
            spread_block(z, piece, True, True)

        due(reach + 1, own)
        for distance in range(1, reach):
            due(reach + 1 + 2 * distance, functools.partial(relay, distance))

    for i in range(ahead):
        launch(i)
    small_step(1)

    def step(i, carry):
        k, piece = place(i)

        @pl.when(jnp.logical_and(k == reach - 1, piece + 2 < TAIL_PIECES))
        def _():
            core_start(piece + 2)

        @pl.when(jnp.logical_and(k > 0, piece * (reach - 1) + reach - 1 - k < count))
        def _():
            one_tile(piece * (reach - 1) + reach - 1 - k)

        @pl.when(i == reach)
        def _():
            small_step(2)

        summed.arrive(k, piece)

        @pl.when(i + ahead < steps)
        def _():
            launch(i + ahead)

        add_core(x, k, piece)

        @pl.when(k > 0)
        def _():
            summed.pass_on(k, piece)

        late(i)
        return carry

    lax.fori_loop(0, steps, step, 0)
    done = min(count, TAIL_PIECES * (reach - 1))
    ends_copy(1).start()
    small_step(3)
    for i in range(steps, steps + 3 * reach):
        late(i)
    tile_run(done, count)
    for index in (count - 2, count - 1):
        sum_tile(index)

    def settle_last(source, carry):
        for piece in range(TAIL_PIECES):
            last_copy(source, piece, 1 - core).wait_recv()
        for copy in out_copies(1 - core, source):
            copy.start()
        return carry

    lax.fori_loop(0, reach, settle_last, 0)
    for m in range(2):
        ends_copy(m).wait_recv()
        ends_store(m, True).start()

    summed.drain()

    def settle_sends(source, carry):
        for piece in range(TAIL_PIECES):
            last_copy(source, piece, core).wait_send()

            @pl.when(jnp.logical_and(chain.has_above, z >= source))
            def _():
                ring_copy(source, piece, 0, chain.above).wait_send()

            @pl.when(jnp.logical_and(chain.has_below, z <= source))
            def _():
                ring_copy(source, piece, 1, chain.below).wait_send()

        for side in range(2):
            for copy in out_copies(side, source):
                copy.wait()
        return carry

    lax.fori_loop(0, reach, settle_sends, 0)
    for piece in range(TAIL_PIECES):
        for half in range(2):
            core_copy(half, piece).wait_send()
    for m in range(2):
        ends_copy(m).wait_send()
        for other in (False, True):
            ends_store(m, other).wait()
    small_copy(partner, 0).wait_send()
    small_copy(chain.aside, 1).wait_send()
    others(lambda other: small_copy(other, 2).wait_send())
    def settle_tiles(index, carry):
        for copy in tile_sends(index):
            copy.wait_send()
        for copy in tile_stores(index):
            copy.wait()
        return carry

    lax.fori_loop(count - depth, count, settle_tiles, 0)


def tail_call(reach, widths, dense, x_rows, dh_two, gg_two, gu_two, hg_two, before, smalls, ends):
    halves, cores, _, _, quarter, columns = dense.shape
    groups, local, slot_rows, width = x_rows.shape
    hidden = gg_two[0].shape[3]
    tiles = width // hidden
    wide = width // tiles
    anywhere = pl.BlockSpec(memory_space=pl.ANY)
    vmem = pl.BlockSpec(memory_space=pltpu.VMEM)
    end = ends[0].shape
    up = jax.ShapeDtypeStruct((local, width, hidden), jnp.bfloat16)
    down = jax.ShapeDtypeStruct((local, hidden, width), jnp.bfloat16)
    block = (TAIL_PIECES, quarter, columns)
    dma = pltpu.SemaphoreType.DMA
    return pl.pallas_call(
        functools.partial(tail_kernel, reach, tiles),
        in_specs=[anywhere] * 13 + [vmem] * 3 + [anywhere] * 4,
        out_specs=[anywhere] * 7 + [vmem, anywhere],
        out_shape=[
            jax.ShapeDtypeStruct((cores * reach, TAIL_PIECES, quarter, one), jnp.bfloat16)
            for one in widths
        ]
        + [
            jax.ShapeDtypeStruct((reach, TAIL_PIECES, quarter, width), jnp.bfloat16),
            up,
            up,
            down,
            jax.ShapeDtypeStruct(smalls[0].shape, jnp.float32),
            jax.ShapeDtypeStruct((2, 2) + end, jnp.bfloat16),
        ],
        scratch_shapes=[
            pltpu.VMEM((halves, reach) + block, jnp.bfloat16),
            pltpu.VMEM((halves, reach) + block, jnp.bfloat16),
            pltpu.VMEM((halves, reach) + block, jnp.bfloat16),
            pltpu.VMEM((reach,) + block, jnp.bfloat16),
            pltpu.VMEM((reach + 1,) + block, jnp.bfloat16),
            pltpu.VMEM((cores, reach) + block, jnp.bfloat16),
            pltpu.VMEM((2, groups, slot_rows, wide), jnp.bfloat16),
            pltpu.VMEM((2, groups, slot_rows, wide), jnp.bfloat16),
            pltpu.VMEM((2, 3, groups, slot_rows, hidden), jnp.bfloat16),
            pltpu.VMEM((2, 3, wide, hidden), jnp.bfloat16),
        ]
        + [pltpu.VMEM((3, wide, hidden), jnp.bfloat16)] * 6
        + [pltpu.VMEM((count,) + smalls[0].shape, jnp.float32) for count in (2, 2, reach)]
        + [pltpu.VMEM((2,) + end, jnp.bfloat16)] * 2
        + [
            dma((halves,)),
            dma((halves, TAIL_PIECES)),
            dma((halves, TAIL_PIECES)),
            dma((halves, TAIL_PIECES)),
            dma((reach, TAIL_PIECES)),
            dma((reach, TAIL_PIECES)),
            dma((reach, TAIL_PIECES)),
            dma((reach + 1, TAIL_PIECES)),
            dma((2, reach, TAIL_PIECES)),
            dma((reach, TAIL_PIECES)),
            dma((reach, TAIL_PIECES)),
            dma((reach, TAIL_PIECES)),
            dma((cores, reach, 4)),
            dma((2, 2)),
            dma((2, 3)),
            dma((2, 3)),
            dma((3, 3)),
            dma((3, 3)),
            dma((3, 3)),
            pltpu.SemaphoreType.REGULAR,
            dma((2 + reach,)),
            dma((2 + reach,)),
            dma((2,)),
            dma((2, 2)),
            dma((2,)),
            dma((2,)),
        ],
        compiler_params=pltpu.CompilerParams(
            collective_id=7, has_side_effects=True, vmem_limit_bytes=62 * MIB
        ),
        cost_estimate=pl.CostEstimate(
            flops=60 * 10**9, bytes_accessed=120 * 10**6, transcendentals=0
        ),
        name="tail",
    )(dense, x_rows, *dh_two, *gg_two, *gu_two, *hg_two, *before, *smalls, *ends)


GROUP = (EXPERT, TENSOR)
ROWS = (DP, EXPERT)


def by_rows(
    boundary,
    segments,
    expert_ids,
    attn_gain,
    query_weight,
    key_weight,
    value_weight,
    out_weight,
    ffn_gain,
    router_weight,
    gate_weight,
    up_weight,
    down_weight,
):
    args = (
        boundary,
        segments,
        expert_ids,
        attn_gain,
        query_weight,
        key_weight,
        value_weight,
        out_weight,
        ffn_gain,
        router_weight,
        gate_weight,
        up_weight,
        down_weight,
    )
    share_rows = expert_ids.shape[2]
    local = gate_weight.shape[1]
    if (
        share_rows != LEN
        or lax.axis_size(TENSOR) != 2
        or lax.axis_size(SECTION) != 2
        or lax.axis_size(DP) != 2
        or query_weight.shape[2] % (4 * HD)
    ):
        return on_device(*args)
    section = lax.axis_index(SECTION)
    tensor = lax.axis_index(TENSOR)
    group_at = lax.axis_index(EXPERT) * lax.axis_size(TENSOR) + tensor
    micro_count = boundary.shape[1]
    reach = lax.axis_size(EXPERT)
    group = query_weight.shape[2] // key_weight.shape[2]
    own_rows = lax.dynamic_slice_in_dim(boundary[0], tensor * share_rows, share_rows, 1)
    own_seg = lax.dynamic_slice_in_dim(segments, tensor * share_rows, share_rows, 1)
    own_ids = jnp.swapaxes(expert_ids[0], 1, 2)
    gains = (attn_gain, ffn_gain)
    tables = pair_tables(LEN)

    wqkv_part = jnp.concatenate([query_weight[0], key_weight[0], value_weight[0]], axis=1)
    wo_part = out_weight[0]
    wqkv = wo = None
    router_local = jnp.roll(router_weight[0].T, -group_at * local, axis=0)
    wg, wu, wd = gate_weight[0], up_weight[0], down_weight[0]

    def pick(array, index):
        return lax.dynamic_index_in_dim(array, index, 0, keepdims=False)

    arrived = None
    kept = []
    wide = []
    outputs = []
    for tick in range(micro_count + 1):
        micro = jnp.clip(tick - section, 0, micro_count - 1)
        if tick == 0:
            layer_in = own_rows[0]
            h1, xn2 = attn_split(
                boundary[0, 0].reshape(2, share_rows, -1),
                segments[0].reshape(2, share_rows),
                gains,
                wqkv_part,
                wo_part,
                tables,
                group,
            )
        else:
            layer_in = arrived
            h1, xn1, qkv, att, xn2 = attn_forward(
                own_rows[tick] if tick < micro_count else arrived,
                arrived,
                pick(own_seg, micro),
                gains,
                wqkv,
                wo,
                tables,
                group,
                0 if tick == micro_count else -1,
            )
        h2, gates, slots, own_gates, picked, gate_pre, up_pre, *firsts = moe_forward_call(
            reach,
            tick,
            micro_count,
            xn2,
            h1,
            pick(own_ids, micro),
            router_local,
            wg,
            wu,
            wd,
            [
                boundary[0].reshape(micro_count, 2, PIECES, share_rows // PIECES, -1),
                wqkv_part,
                wo_part,
            ],
        )
        outputs.append(h2)
        arrived = shifted(h2, SECTION, 1)
        if tick == 0:
            tops, *before = firsts
            wqkv, wo = both_halves(wqkv_part, wo_part, h2, before)
            xn1, qkv, att = attn_again(own_rows[0], own_seg[0], attn_gain, wqkv, tables, group)
        kept.append((layer_in, h1, xn2, own_gates, qkv, slots, gates, xn1, att))
        wide.append((picked, gate_pre, up_pre))

    arrived = jnp.zeros(own_rows.shape[1:], jnp.bfloat16)
    backs = []
    slotted = []
    for tick in range(micro_count + 1):
        micro = jnp.clip(tick - (1 - section), 0, micro_count - 1)
        ticks = {0: (1, 1), 1: (0, 2), 2: (1, 1)}[tick]
        pairs = list(zip(*(kept[one] for one in ticks)))
        sides = [wide[one] for one in ticks]
        if tick == micro_count:
            pairs[0] = (own_rows[1], own_rows[1])
            pairs.insert(5, (arrived, arrived))
        elif tick == 0:
            pairs.insert(5, (own_rows[0], own_rows[0]))
        else:
            pairs.insert(5, (arrived, own_rows[1]))
        rows, grad_gates, picked, gg, gu, hg = moe_backward_call(
            reach,
            tick,
            micro_count,
            arrived,
            pairs[6],
            pairs[7],
            [side[1] for side in sides],
            [side[2] for side in sides],
            wg,
            wu,
            wd,
            tops,
            before[0] if tick == micro_count else tops,
        )
        grad_in, mid, dqkv, small = attn_backward(
            pairs[:6],
            rows,
            grad_gates.reshape(EXPERTS, LEN),
            pick(own_seg, micro),
            gains,
            router_local,
            wqkv,
            wo,
            tables,
            group,
            {0: 0, micro_count: 1}.get(tick, -1),
        )
        arrived = shifted(grad_in, SECTION, -1)
        backs.append((grad_in, mid, dqkv, small))
        slotted.append((picked, gg, gu, hg))
        if tick == 1:
            before = middle_weights([side[0] for side in sides], picked, gg, gu, hg, grad_in)

    grads_in, mids, dqkvs, smalls = zip(*backs)
    dense = attn_weights([one[7] for one in kept], [one[8] for one in kept], mids, dqkvs)
    width = dense.shape[1]
    dense = dense.reshape(
        2, 2, reach, TAIL_PIECES, width // (2 * reach * TAIL_PIECES), dense.shape[2]
    )
    widths = [one.shape[2] for one in (query_weight, key_weight, value_weight)]
    ends = (grads_in[1], outputs[1], grads_in[2], outputs[2])
    *dense, wg_sum, wu_sum, wd_sum, small, ends = tail_call(
        reach, widths, dense, wide[1][0], *zip(slotted[0], slotted[2]), before, smalls, ends
    )
    return (
        ends.reshape(1, micro_count, 2 * share_rows, -1),
        small[EXPERTS + 1][None],
        *[one.astype(jnp.float32).reshape(1, -1, one.shape[3]) for one in dense],
        small[EXPERTS][None],
        small[:EXPERTS].T[None],
        *[one.astype(jnp.float32)[None] for one in (wg_sum, wu_sum, wd_sum)],
    )


def solution(mesh):
    placed = (
        P(SECTION, None, (DP, EXPERT), None),
        P(None, (DP, EXPERT)),
        P(SECTION, None, (DP, EXPERT, TENSOR), None),
        P(SECTION, None),
        P(SECTION, None, TENSOR),
        P(SECTION, None, TENSOR),
        P(SECTION, None, TENSOR),
        P(SECTION, TENSOR, None),
        P(SECTION, None),
        P(SECTION, None, None),
        P(SECTION, (EXPERT, TENSOR), None, None),
        P(SECTION, (EXPERT, TENSOR), None, None),
        P(SECTION, (EXPERT, TENSOR), None, None),
    )
    return jax.shard_map(
        by_rows,
        mesh=mesh,
        in_specs=placed,
        out_specs=(
            P(SECTION, None, (DP, EXPERT), None),
            P(SECTION, None),
            P(SECTION, None, TENSOR),
            P(SECTION, None, TENSOR),
            P(SECTION, None, TENSOR),
            P(SECTION, TENSOR, None),
            P(SECTION, None),
            P(SECTION, None, None),
            P(SECTION, (EXPERT, TENSOR), None, None),
            P(SECTION, (EXPERT, TENSOR), None, None),
            P(SECTION, (EXPERT, TENSOR), None, None),
        ),
        check_vma=False,
    )
```

```python
import functools

import jax
import jax.numpy as jnp
from jax import lax
from jax.experimental import pallas as pl
from jax.experimental.pallas import tpu as pltpu
from jax.sharding import PartitionSpec as P

SECTION, DP, EXPERT, TENSOR = "section", "dp", "expert", "tensor"
HD = 64
TOPK = 8
EXPERTS = 32
LEN = 256


EPS = 1e-06
THETA = 10000.0
NEG_BIG = -1e30


def shifted(block, axis, distance):
    devices = range(lax.axis_size(axis))
    route = [(i - distance, i) for i in devices if i - distance in devices]
    return lax.ppermute(block, axis, route)


def rms_scale(values):
    return lax.rsqrt(jnp.mean(values * values, axis=-1, keepdims=True) + EPS)


def norm_back(grad_out, values, scale_col, gain_vec):
    weighted = grad_out * gain_vec
    inner_mean = jnp.mean(weighted * values, axis=-1, keepdims=True)
    grad_values = scale_col * weighted - values * (scale_col * scale_col * scale_col) * inner_mean
    grad_gain = jnp.sum(grad_out * values * scale_col, axis=0)
    return (grad_values, grad_gain)


def rope_tables(row_count, head_width, length):
    position = (jnp.arange(row_count) % length).astype(jnp.float32)
    frequency = THETA ** (-2.0 * jnp.arange(head_width // 2).astype(jnp.float32) / head_width)
    angles = position[:, None] * frequency[None, :]
    return (jnp.cos(angles), jnp.sin(angles))


def rotate(matrix, cosine_table, sine_table, head_width, direction):
    row_count = matrix.shape[0]
    by_head = matrix.reshape(row_count, -1, head_width)
    half_width = head_width // 2
    first_half = by_head[..., :half_width]
    second_half = by_head[..., half_width:]
    cosine = cosine_table[:, None, :]
    sine_val = sine_table[:, None, :] * direction
    turned = jnp.concatenate(
        [
            first_half * cosine - second_half * sine_val,
            second_half * cosine + first_half * sine_val,
        ],
        axis=-1,
    )
    return turned.reshape(row_count, -1)


def slot_count(share_rows):
    return share_rows * 3 // 8


def score_block(query_blk, key_blk, seg_row):
    length = query_blk.shape[0]
    kv_heads = key_blk.shape[1] // HD
    query_heads = query_blk.reshape(length, kv_heads, -1, HD)
    key_heads = key_blk.reshape(length, kv_heads, HD)
    scores = jnp.einsum(
        "qkgd,skd->kgqs", query_heads, key_heads, preferred_element_type=jnp.float32
    ) * HD ** (-0.5)
    position = jnp.arange(length)
    allowed = (position[:, None] >= position[None, :]) & (seg_row[:, None] == seg_row[None, :])
    return (jnp.where(allowed, scores, NEG_BIG), query_heads, key_heads)


def attend_forward(bundle):
    query_blk, key_blk, value_blk, seg_row = bundle
    length = query_blk.shape[0]
    scores, query_heads, key_heads = score_block(query_blk, key_blk, seg_row)
    top_score = jnp.max(scores, axis=-1, keepdims=True)
    exponent = jnp.exp(scores - top_score)
    row_total = jnp.sum(exponent, axis=-1, keepdims=True)
    probability = (exponent / row_total).astype(jnp.bfloat16)
    value_heads = value_blk.reshape(length, key_heads.shape[1], HD)
    mixture = jnp.einsum(
        "kgqs,skd->qkgd", probability, value_heads, preferred_element_type=jnp.float32
    )
    return (mixture.astype(jnp.bfloat16).reshape(length, -1), top_score + jnp.log(row_total))


def attend_backward(bundle):
    query_blk, key_blk, value_blk, seg_row, log_total, grad_mix = bundle
    length = query_blk.shape[0]
    scores, query_heads, key_heads = score_block(query_blk, key_blk, seg_row)
    kv_heads = key_heads.shape[1]
    probability = jnp.exp(scores - log_total)
    prob_low = probability.astype(jnp.bfloat16)
    grad_heads = grad_mix.reshape(length, kv_heads, -1, HD)
    value_heads = value_blk.reshape(length, kv_heads, HD)
    grad_value = jnp.einsum(
        "kgqs,qkgd->skd", prob_low, grad_heads, preferred_element_type=jnp.float32
    )
    grad_prob = jnp.einsum(
        "qkgd,skd->kgqs", grad_heads, value_heads, preferred_element_type=jnp.float32
    )
    centre = jnp.sum(probability * grad_prob, axis=-1, keepdims=True)
    grad_scores = (probability * (grad_prob - centre)).astype(jnp.bfloat16)
    grad_query = jnp.einsum(
        "kgqs,skd->qkgd", grad_scores, key_heads, preferred_element_type=jnp.float32
    ) * HD ** (-0.5)
    grad_key = jnp.einsum(
        "kgqs,qkgd->skd", grad_scores, query_heads, preferred_element_type=jnp.float32
    ) * HD ** (-0.5)
    return (
        grad_query.reshape(length, -1),
        grad_key.reshape(length, -1),
        grad_value.reshape(length, -1),
    )


def attention_forward(hidden_in, seg_rows, params):
    attn_gain, query_weight, key_weight, value_weight = params[:4]
    row_count = hidden_in.shape[0]
    scale_one = rms_scale(hidden_in)
    normed = (hidden_in * scale_one * attn_gain).astype(jnp.bfloat16)
    query_proj = jnp.dot(normed, query_weight, preferred_element_type=jnp.float32)
    key_proj = jnp.dot(normed, key_weight, preferred_element_type=jnp.float32)
    value_rot = jnp.dot(normed, value_weight, preferred_element_type=jnp.float32).astype(
        jnp.bfloat16
    )
    cosine_table, sine_table = rope_tables(row_count, HD, LEN)
    query_rot = rotate(query_proj, cosine_table, sine_table, HD, 1.0).astype(jnp.bfloat16)
    key_rot = rotate(key_proj, cosine_table, sine_table, HD, 1.0).astype(jnp.bfloat16)
    seq_count = row_count // LEN
    mixed, log_total = lax.map(
        attend_forward,
        (
            query_rot.reshape(seq_count, LEN, -1),
            key_rot.reshape(seq_count, LEN, -1),
            value_rot.reshape(seq_count, LEN, -1),
            seg_rows.reshape(seq_count, LEN),
        ),
    )
    attended = mixed.reshape(row_count, -1)
    return (
        scale_one,
        normed,
        query_rot,
        key_rot,
        value_rot,
        attended,
        log_total,
        cosine_table,
        sine_table,
    )


def expert_plan(route_rows, capacity):
    pair_ids = route_rows.reshape(-1)
    onehot = (pair_ids[:, None] == jnp.arange(EXPERTS, dtype=jnp.int32)[None, :]).astype(jnp.int32)
    earlier = jnp.cumsum(onehot, axis=0) - onehot
    slot_pos = jnp.sum(earlier * onehot, axis=1)
    target = pair_ids * capacity + slot_pos
    source = (
        jnp.zeros((EXPERTS * capacity,), jnp.int32)
        .at[target]
        .set(jnp.arange(pair_ids.shape[0], dtype=jnp.int32) + 1)
    )
    return (target.reshape(route_rows.shape), source)


def send_out(buffer):
    return lax.all_to_all(buffer, (EXPERT, TENSOR), split_axis=0, concat_axis=1, tiled=True)


def send_home(produced):
    return lax.all_to_all(produced, (EXPERT, TENSOR), split_axis=1, concat_axis=0, tiled=True)


def moe_forward(middle_share, route_rows, params, outward, homeward):
    ffn_gain, router_weight, gate_weight, up_weight, down_weight = params[5:]
    share_rows = middle_share.shape[0]
    capacity = slot_count(share_rows)
    scale_two = rms_scale(middle_share)
    normed_two = (middle_share * scale_two * ffn_gain).astype(jnp.bfloat16)
    logits = jnp.dot(normed_two, router_weight, preferred_element_type=jnp.float32)
    member = route_rows[:, :, None] == jnp.arange(EXPERTS, dtype=jnp.int32)[None, None, :]
    chosen = jnp.sum(jnp.where(member, logits[:, None, :], 0.0), axis=2)
    exponent = jnp.exp(chosen - jnp.max(chosen, axis=1, keepdims=True))
    gates = exponent / jnp.sum(exponent, axis=1, keepdims=True)
    target, source = expert_plan(route_rows, capacity)
    filled = (source > 0)[:, None]
    gathered = normed_two[jnp.maximum(source - 1, 0) // TOPK]
    buffer = jnp.where(filled, gathered, jnp.zeros_like(gathered)).reshape(EXPERTS, capacity, -1)
    received = outward(buffer)
    gate_pre = jnp.einsum("erd,edf->erf", received, gate_weight, preferred_element_type=jnp.float32)
    up_pre = jnp.einsum("erd,edf->erf", received, up_weight, preferred_element_type=jnp.float32)
    hidden = (jax.nn.silu(gate_pre) * up_pre).astype(jnp.bfloat16)
    produced = jnp.einsum(
        "erf,efd->erd", hidden, down_weight, preferred_element_type=jnp.float32
    ).astype(jnp.bfloat16)
    returned = homeward(produced)
    picked = returned.reshape(EXPERTS * capacity, -1)[target]
    addition = jnp.einsum("tk,tkd->td", gates, picked, preferred_element_type=jnp.float32)
    return (
        scale_two,
        normed_two,
        member,
        gates,
        target,
        source,
        received,
        gate_pre,
        up_pre,
        hidden,
        picked,
        addition,
    )


def section_forward(layer_in, seg_rows, route_rows, params, share_start, share_rows):
    hidden_in = layer_in.astype(jnp.float32)
    attn_parts = attention_forward(hidden_in, seg_rows, params)
    partial_sum = jnp.dot(attn_parts[5], params[4], preferred_element_type=jnp.float32)
    own_share = lax.dynamic_slice_in_dim(hidden_in, share_start, share_rows, 0)
    summed = lax.psum(partial_sum.astype(jnp.bfloat16), TENSOR).astype(jnp.float32)
    branch = lax.dynamic_slice_in_dim(summed, share_start, share_rows, 0)
    middle_share = own_share + branch
    moe_parts = moe_forward(middle_share, route_rows, params, send_out, send_home)
    block_share = middle_share + moe_parts[-1]
    block_full = lax.all_gather(
        block_share.astype(jnp.bfloat16), TENSOR, axis=0, tiled=True
    ).astype(block_share.dtype)
    return (block_full, middle_share, moe_parts)


def section_backward(layer_in, middle_share, grad_top, seg_rows, params, share_start, kept_parts):
    (
        attn_gain,
        query_weight,
        key_weight,
        value_weight,
        out_weight,
        ffn_gain,
        router_weight,
        gate_weight,
        up_weight,
        down_weight,
    ) = params
    hidden_in = layer_in.astype(jnp.float32)
    row_count = hidden_in.shape[0]
    share_rows = middle_share.shape[0]
    capacity = slot_count(share_rows)
    (
        scale_one,
        normed,
        query_rot,
        key_rot,
        value_rot,
        attended,
        log_total,
        cosine_table,
        sine_table,
    ) = attention_forward(hidden_in, seg_rows, params)
    (
        scale_two,
        normed_two,
        member,
        gates,
        target,
        source,
        received,
        gate_pre,
        up_pre,
        hidden,
        picked,
        addition,
    ) = kept_parts
    grad_share = lax.dynamic_slice_in_dim(grad_top, share_start, share_rows, 0)
    grad_picked = (gates[:, :, None] * grad_share[:, None, :]).astype(jnp.bfloat16)
    grad_gates = jnp.einsum("td,tkd->tk", grad_share, picked, preferred_element_type=jnp.float32)
    grad_chosen = gates * (grad_gates - jnp.sum(gates * grad_gates, axis=1, keepdims=True))
    grad_logits = jnp.sum(jnp.where(member, grad_chosen[:, :, None], 0.0), axis=1).astype(
        jnp.bfloat16
    )
    router_grad = jnp.einsum(
        "td,te->de", normed_two, grad_logits, preferred_element_type=jnp.float32
    )
    grad_normed = jnp.einsum(
        "te,de->td", grad_logits, router_weight, preferred_element_type=jnp.float32
    )
    filled = (source > 0)[:, None]
    flat_grad = grad_picked.reshape(share_rows * TOPK, -1)
    gathered = flat_grad[jnp.maximum(source - 1, 0)]
    grad_buffer = jnp.where(filled, gathered, jnp.zeros_like(gathered)).reshape(
        EXPERTS, capacity, -1
    )
    sent = lax.all_to_all(
        grad_buffer, (EXPERT, TENSOR), split_axis=0, concat_axis=1, tiled=True
    )
    grad_hidden = jnp.einsum("erd,efd->erf", sent, down_weight, preferred_element_type=jnp.float32)
    sigmoid_gate = jax.nn.sigmoid(gate_pre)
    grad_gate = (
        grad_hidden * up_pre * sigmoid_gate * (1.0 + gate_pre * (1.0 - sigmoid_gate))
    ).astype(jnp.bfloat16)
    grad_up = (grad_hidden * gate_pre * sigmoid_gate).astype(jnp.bfloat16)
    down_grad = jnp.einsum("erf,erd->efd", hidden, sent, preferred_element_type=jnp.float32)
    gate_grad = jnp.einsum("erd,erf->edf", received, grad_gate, preferred_element_type=jnp.float32)
    up_grad = jnp.einsum("erd,erf->edf", received, grad_up, preferred_element_type=jnp.float32)
    grad_rows = jnp.einsum(
        "erf,edf->erd", grad_gate, gate_weight, preferred_element_type=jnp.float32
    )
    grad_rows = (
        grad_rows
        + jnp.einsum("erf,edf->erd", grad_up, up_weight, preferred_element_type=jnp.float32)
    ).astype(jnp.bfloat16)
    back_rows = lax.all_to_all(
        grad_rows, (EXPERT, TENSOR), split_axis=1, concat_axis=0, tiled=True
    )
    grad_normed = grad_normed + jnp.sum(
        back_rows.reshape(EXPERTS * capacity, -1)[target].astype(jnp.float32), axis=1
    )
    grad_middle, ffn_gain_grad = norm_back(grad_normed, middle_share, scale_two, ffn_gain)
    grad_middle = grad_middle + grad_share
    grad_mid_full = lax.all_gather(
        grad_middle.astype(jnp.bfloat16), TENSOR, axis=0, tiled=True
    ).astype(grad_middle.dtype)
    grad_mid_low = grad_mid_full.astype(jnp.bfloat16)
    out_grad = jnp.einsum("rh,rd->hd", attended, grad_mid_low, preferred_element_type=jnp.float32)
    grad_attended = jnp.einsum(
        "rd,hd->rh", grad_mid_low, out_weight, preferred_element_type=jnp.float32
    ).astype(jnp.bfloat16)
    seq_count = row_count // LEN
    grad_query, grad_key, grad_value = lax.map(
        attend_backward,
        (
            query_rot.reshape(seq_count, LEN, -1),
            key_rot.reshape(seq_count, LEN, -1),
            value_rot.reshape(seq_count, LEN, -1),
            seg_rows.reshape(seq_count, LEN),
            log_total,
            grad_attended.reshape(seq_count, LEN, -1),
        ),
    )
    grad_query = rotate(
        grad_query.reshape(row_count, -1), cosine_table, sine_table, HD, -1.0
    ).astype(jnp.bfloat16)
    grad_key = rotate(grad_key.reshape(row_count, -1), cosine_table, sine_table, HD, -1.0).astype(
        jnp.bfloat16
    )
    grad_value = grad_value.reshape(row_count, -1).astype(jnp.bfloat16)
    query_grad = jnp.einsum("rd,rh->dh", normed, grad_query, preferred_element_type=jnp.float32)
    key_grad = jnp.einsum("rd,rh->dh", normed, grad_key, preferred_element_type=jnp.float32)
    value_grad = jnp.einsum("rd,rh->dh", normed, grad_value, preferred_element_type=jnp.float32)
    grad_normed_one = jnp.einsum(
        "rh,dh->rd", grad_query, query_weight, preferred_element_type=jnp.float32
    )
    grad_normed_one = grad_normed_one + jnp.einsum(
        "rh,dh->rd", grad_key, key_weight, preferred_element_type=jnp.float32
    )
    grad_normed_one = grad_normed_one + jnp.einsum(
        "rh,dh->rd", grad_value, value_weight, preferred_element_type=jnp.float32
    )
    grad_normed_one = lax.psum(grad_normed_one.astype(jnp.bfloat16), TENSOR).astype(jnp.float32)
    grad_input, attn_gain_grad = norm_back(grad_normed_one, hidden_in, scale_one, attn_gain)
    grad_input = grad_input + grad_mid_full
    return (
        grad_input,
        (
            attn_gain_grad,
            query_grad,
            key_grad,
            value_grad,
            out_grad,
            ffn_gain_grad,
            router_grad,
            gate_grad,
            up_grad,
            down_grad,
        ),
    )


def stack_zeros(piece_arr, count):
    return jnp.zeros((count,) + piece_arr.shape, piece_arr.dtype)


def on_device(
    boundary,
    segments,
    expert_ids,
    attn_gain,
    query_weight,
    key_weight,
    value_weight,
    out_weight,
    ffn_gain,
    router_weight,
    gate_weight,
    up_weight,
    down_weight,
):
    params = tuple(
        (
            array_in[0]
            for array_in in (
                attn_gain,
                query_weight,
                key_weight,
                value_weight,
                out_weight,
                ffn_gain,
                router_weight,
                gate_weight,
                up_weight,
                down_weight,
            )
        )
    )
    section_index = lax.axis_index(SECTION)
    tensor_index = lax.axis_index(TENSOR)
    own_rows = boundary[0]
    micro_count = own_rows.shape[0]
    row_count = own_rows.shape[1]
    model_width = own_rows.shape[2]
    share_rows = expert_ids.shape[2]
    share_start = tensor_index * share_rows
    routes = expert_ids[0]
    kept_inputs = jnp.zeros((micro_count, row_count, model_width), jnp.bfloat16)
    kept_middle = jnp.zeros((micro_count, share_rows, model_width), jnp.float32)
    block_outputs = jnp.zeros((micro_count, row_count, model_width), jnp.bfloat16)
    arrived = jnp.zeros((row_count, model_width), jnp.bfloat16)
    kept_moe = None
    for tick_idx in range(micro_count + 1):
        micro_idx = tick_idx - section_index
        is_valid = (micro_idx >= 0) & (micro_idx < micro_count)
        slot_idx = jnp.clip(micro_idx, 0, micro_count - 1)
        layer_in = jnp.where(section_index == 0, own_rows[min(tick_idx, micro_count - 1)], arrived)
        seg_rows = lax.dynamic_index_in_dim(segments, slot_idx, 0, keepdims=False)
        route_rows = lax.dynamic_index_in_dim(routes, slot_idx, 0, keepdims=False)
        block_full, middle_share, moe_parts = section_forward(
            layer_in, seg_rows, route_rows, params, share_start, share_rows
        )
        block_low = block_full.astype(jnp.bfloat16)
        kept_inputs = jnp.where(
            is_valid,
            lax.dynamic_update_index_in_dim(kept_inputs, layer_in, slot_idx, 0),
            kept_inputs,
        )
        kept_middle = jnp.where(
            is_valid,
            lax.dynamic_update_index_in_dim(kept_middle, middle_share, slot_idx, 0),
            kept_middle,
        )
        block_outputs = jnp.where(
            is_valid,
            lax.dynamic_update_index_in_dim(block_outputs, block_low, slot_idx, 0),
            block_outputs,
        )
        if kept_moe is None:
            kept_moe = tuple((stack_zeros(piece_arr, micro_count) for piece_arr in moe_parts))
        kept_moe = tuple(
            (
                jnp.where(
                    is_valid,
                    lax.dynamic_update_index_in_dim(stack_arr, piece_arr, slot_idx, 0),
                    stack_arr,
                )
                for stack_arr, piece_arr in zip(kept_moe, moe_parts)
            )
        )
        arrived = shifted(block_low, SECTION, 1)
    grads = tuple((jnp.zeros(param_arr.shape, jnp.float32) for param_arr in params))
    input_grads = jnp.zeros((micro_count, row_count, model_width), jnp.bfloat16)
    grad_arrived = jnp.zeros((row_count, model_width), jnp.bfloat16)
    for tick_idx in range(micro_count + 1):
        micro_idx = tick_idx - (1 - section_index)
        is_valid = (micro_idx >= 0) & (micro_idx < micro_count)
        slot_idx = jnp.clip(micro_idx, 0, micro_count - 1)
        grad_top = jnp.where(
            section_index == 1, own_rows[min(tick_idx, micro_count - 1)], grad_arrived
        ).astype(jnp.float32)
        layer_in = lax.dynamic_index_in_dim(kept_inputs, slot_idx, 0, keepdims=False)
        middle_share = lax.dynamic_index_in_dim(kept_middle, slot_idx, 0, keepdims=False)
        seg_rows = lax.dynamic_index_in_dim(segments, slot_idx, 0, keepdims=False)
        route_rows = lax.dynamic_index_in_dim(routes, slot_idx, 0, keepdims=False)
        tick_moe = tuple(
            (
                lax.dynamic_index_in_dim(stack_arr, slot_idx, 0, keepdims=False)
                for stack_arr in kept_moe
            )
        )
        grad_input, tick_grads = section_backward(
            layer_in, middle_share, grad_top, seg_rows, params, share_start, tick_moe
        )
        valid_weight = is_valid.astype(jnp.float32)
        grads = tuple(
            (
                total_grad + valid_weight * tick_part
                for total_grad, tick_part in zip(grads, tick_grads)
            )
        )
        grad_low = grad_input.astype(jnp.bfloat16)
        input_grads = jnp.where(
            is_valid,
            lax.dynamic_update_index_in_dim(input_grads, grad_low, slot_idx, 0),
            input_grads,
        )
        grad_arrived = shifted(grad_low, SECTION, -1)
    dense = (
        lax.psum(grads[0].astype(jnp.bfloat16), (DP, EXPERT)).astype(jnp.float32),
        lax.psum(grads[1].astype(jnp.bfloat16), (DP, EXPERT)).astype(jnp.float32),
        lax.psum(grads[2].astype(jnp.bfloat16), (DP, EXPERT)).astype(jnp.float32),
        lax.psum(grads[3].astype(jnp.bfloat16), (DP, EXPERT)).astype(jnp.float32),
        lax.psum(grads[4].astype(jnp.bfloat16), (DP, EXPERT)).astype(jnp.float32),
    )
    shared = lax.psum((grads[5], grads[6]), (DP, EXPERT, TENSOR))
    expert_sums = (
        lax.psum(grads[7].astype(jnp.bfloat16), DP).astype(jnp.float32),
        lax.psum(grads[8].astype(jnp.bfloat16), DP).astype(jnp.float32),
        lax.psum(grads[9].astype(jnp.bfloat16), DP).astype(jnp.float32),
    )
    ends_out = jnp.where(section_index == 0, input_grads, block_outputs)[None]
    return (
        ends_out,
        dense[0][None],
        dense[1][None],
        dense[2][None],
        dense[3][None],
        dense[4][None],
        shared[0][None],
        shared[1][None],
        expert_sums[0][None],
        expert_sums[1][None],
        expert_sums[2][None],
    )


MIB = 1024 * 1024
NT = (((1,), (1,)), ((), ()))
TN = (((0,), (0,)), ((), ()))


def dot(left, right, dims=None):
    if dims is None:
        return jnp.dot(left, right, preferred_element_type=jnp.float32)
    return lax.dot_general(left, right, dims, preferred_element_type=jnp.float32)


def lane_grid(rows):
    return lax.broadcasted_iota(jnp.int32, (rows, 2 * HD), 1)


def turn_pair(slab, cosine, sine):
    low_half = (lane_grid(slab.shape[0]) % HD) < HD // 2
    partner = jnp.where(
        low_half, pltpu.roll(slab, 2 * HD - HD // 2, 1), pltpu.roll(slab, HD // 2, 1)
    )
    return slab * cosine + partner * sine


def pair_tables(length):
    cosine, sine = rope_tables(length, HD, length)
    return (
        jnp.concatenate([cosine] * 4, axis=1),
        jnp.concatenate([-sine, sine, -sine, sine], axis=1),
    )


def aligned_head(slabs, head, side, scale):
    slab = slabs[head // 2]
    if head % 2 != side:
        slab = pltpu.roll(slab, HD, 1)
    keep = (lane_grid(slab.shape[0]) // HD) == side
    return jnp.where(keep, slab * scale, 0.0).astype(jnp.bfloat16)


def one_side(slab, side):
    return jnp.where((lane_grid(slab.shape[0]) // HD) == side, slab, jnp.zeros_like(slab))


def slabs_of(matrix, start, count):
    return [matrix[:, start + 2 * HD * i : start + 2 * HD * (i + 1)] for i in range(count)]


def attend_part(group, rows, weights, tables, allowed):
    width = weights.shape[1]
    query_width = width * group // (group + 2)
    key_width = (width - query_width) // 2
    cosine, sine = tables
    projected = dot(rows, weights)
    query = [
        turn_pair(slab, cosine, sine) for slab in slabs_of(projected, 0, query_width // (2 * HD))
    ]
    key = [
        turn_pair(slab, cosine, sine).astype(jnp.bfloat16)
        for slab in slabs_of(projected, query_width, key_width // (2 * HD))
    ]
    value = [
        slab.astype(jnp.bfloat16)
        for slab in slabs_of(projected, query_width + key_width, key_width // (2 * HD))
    ]
    turned = jnp.concatenate([slab.astype(jnp.bfloat16) for slab in query] + key + value, axis=1)
    query = [slab.astype(jnp.bfloat16).astype(jnp.float32) for slab in query]
    mixed = [None] * len(query)
    for kv_head in range(key_width // HD):
        side = kv_head % 2
        key_slab = key[kv_head // 2]
        value_side = one_side(value[kv_head // 2], side)
        for head in range(group * kv_head, group * (kv_head + 1)):
            scores = dot(aligned_head(query, head, side, HD**-0.5), key_slab, NT)
            scores = jnp.where(allowed, scores, NEG_BIG)
            exponent = jnp.exp(scores - jnp.max(scores, axis=1, keepdims=True))
            probability = exponent / jnp.sum(exponent, axis=1, keepdims=True)
            part = dot(probability.astype(jnp.bfloat16), value_side)
            if head % 2 != side:
                part = pltpu.roll(part, HD, 1)
            mixed[head // 2] = part if head % 2 == 0 else mixed[head // 2] + part
    return turned, jnp.concatenate([part.astype(jnp.bfloat16) for part in mixed], axis=1)


def allowed_pairs(seg_col, seg_row):
    length = seg_row.shape[1]
    row = lax.broadcasted_iota(jnp.int32, (length, length), 0)
    column = lax.broadcasted_iota(jnp.int32, (length, length), 1)
    return (row >= column) & (seg_col == seg_row)


def of_section(first, second):
    return jnp.where(lax.axis_index(SECTION) == 0, first[...], second[...])


def start_of_section(first, second, to, sem):
    @pl.when(lax.axis_index(SECTION) == 0)
    def _():
        pltpu.make_async_copy(first, to, sem).start()

    @pl.when(lax.axis_index(SECTION) != 0)
    def _():
        pltpu.make_async_copy(second, to, sem).start()


def attn_forward_kernel(
    group,
    skipped,
    x_first,
    x_second,
    gain_one_ref,
    wqkv_hbm,
    wo_hbm,
    cos_ref,
    sin_ref,
    seg_col_ref,
    seg_row_ref,
    gain_two_ref,
    h1_ref,
    xn1_ref,
    qkv_ref,
    att_ref,
    xn2_ref,
    x_ref,
    wqkv_ref,
    wo_ref,
    x_sem,
    weight_sem,
):
    @pl.when(lax.axis_index(SECTION) != skipped)
    def _():
        parts = wqkv_ref.shape[0]

        def weight_copies(half):
            return [
                pltpu.make_async_copy(hbm.at[half], ref.at[half], weight_sem.at[i, half])
                for i, (hbm, ref) in enumerate(((wqkv_hbm, wqkv_ref), (wo_hbm, wo_ref)))
            ]

        start_of_section(x_first, x_second, x_ref, x_sem)
        for copy in weight_copies(0):
            copy.start()
        pltpu.make_async_copy(x_first, x_ref, x_sem).wait()
        rows = x_ref[...].astype(jnp.float32)
        xn1_ref[...] = (rows * rms_scale(rows) * gain_one_ref[...]).astype(jnp.bfloat16)
        h1_ref[...] = rows

        def one(half, carry):
            for copy in weight_copies(half):
                copy.wait()

            @pl.when(half + 1 < parts)
            def _():
                for copy in weight_copies(half + 1):
                    copy.start()

            turned, attended = attend_part(
                group,
                xn1_ref[...],
                wqkv_ref[half],
                (cos_ref[...], sin_ref[...]),
                allowed_pairs(seg_col_ref[...], seg_row_ref[...]),
            )
            qkv_ref[half] = turned
            att_ref[half] = attended
            h1_ref[...] += dot(attended, wo_ref[half])
            return carry

        lax.fori_loop(0, parts, one, 0)
        middle = h1_ref[...]
        xn2_ref[...] = (middle * rms_scale(middle) * gain_two_ref[...]).astype(jnp.bfloat16)


def attn_forward(first, second, seg, gains, wqkv, wo, tables, group, skipped):
    length, width = first.shape
    parts, _, qkv_width = wqkv.shape
    att_width = wo.shape[1]
    vmem = pl.BlockSpec(memory_space=pltpu.VMEM)
    anywhere = pl.BlockSpec(memory_space=pl.ANY)
    return pl.pallas_call(
        functools.partial(attn_forward_kernel, group, skipped),
        in_specs=[anywhere] * 2 + [vmem] + [anywhere] * 2 + [vmem] * 5,
        out_specs=[vmem] * 5,
        out_shape=[
            jax.ShapeDtypeStruct((length, width), jnp.float32),
            jax.ShapeDtypeStruct((length, width), jnp.bfloat16),
            jax.ShapeDtypeStruct((parts, length, qkv_width), jnp.bfloat16),
            jax.ShapeDtypeStruct((parts, length, att_width), jnp.bfloat16),
            jax.ShapeDtypeStruct((length, width), jnp.bfloat16),
        ],
        scratch_shapes=[
            pltpu.VMEM((length, width), jnp.bfloat16),
            pltpu.VMEM(wqkv.shape, wqkv.dtype),
            pltpu.VMEM(wo.shape, wo.dtype),
            pltpu.SemaphoreType.DMA,
            pltpu.SemaphoreType.DMA((2, parts)),
        ],
        compiler_params=pltpu.CompilerParams(vmem_limit_bytes=62 * MIB),
        cost_estimate=pl.CostEstimate(
            flops=4 * 10**9, bytes_accessed=20 * 10**6, transcendentals=2 * 10**6
        ),
        name="attn_forward",
    )(first, second, gains[0], wqkv, wo, *tables, seg[:, None], seg[None, :], gains[1])


def attn_again_kernel(
    group,
    x_ref,
    gain_ref,
    wqkv_hbm,
    cos_ref,
    sin_ref,
    seg_col_ref,
    seg_row_ref,
    xn1_ref,
    qkv_ref,
    att_ref,
    wqkv_ref,
    sem,
):
    @pl.when(lax.axis_index(SECTION) == 0)
    def _():
        parts = wqkv_ref.shape[0]

        def copy(half):
            return pltpu.make_async_copy(wqkv_hbm.at[half], wqkv_ref.at[half], sem.at[half])

        for half in range(parts):
            copy(half).start()
        rows = x_ref[...].astype(jnp.float32)
        xn1_ref[...] = (rows * rms_scale(rows) * gain_ref[...]).astype(jnp.bfloat16)

        def one(half, carry):
            copy(half).wait()
            qkv_ref[half], att_ref[half] = attend_part(
                group,
                xn1_ref[...],
                wqkv_ref[half],
                (cos_ref[...], sin_ref[...]),
                allowed_pairs(seg_col_ref[...], seg_row_ref[...]),
            )
            return carry

        lax.fori_loop(0, parts, one, 0)


def attn_again(layer_in, seg, gain, wqkv, tables, group):
    length, width = layer_in.shape
    parts, _, qkv_width = wqkv.shape
    vmem = pl.BlockSpec(memory_space=pltpu.VMEM)
    return pl.pallas_call(
        functools.partial(attn_again_kernel, group),
        in_specs=[vmem] * 2 + [pl.BlockSpec(memory_space=pl.ANY)] + [vmem] * 4,
        out_specs=[vmem] * 3,
        out_shape=[
            jax.ShapeDtypeStruct((length, width), jnp.bfloat16),
            jax.ShapeDtypeStruct((parts, length, qkv_width), jnp.bfloat16),
            jax.ShapeDtypeStruct((parts, length, width // parts), jnp.bfloat16),
        ],
        scratch_shapes=[
            pltpu.VMEM(wqkv.shape, wqkv.dtype),
            pltpu.SemaphoreType.DMA((parts,)),
        ],
        compiler_params=pltpu.CompilerParams(vmem_limit_bytes=62 * MIB),
        cost_estimate=pl.CostEstimate(
            flops=3 * 10**9, bytes_accessed=12 * 10**6, transcendentals=2 * 10**6
        ),
        name="attn_again",
    )(layer_in, gain, wqkv, tables[0], tables[1], seg[:, None], seg[None, :])


def attn_split_kernel(
    group,
    x_ref,
    gain_one_ref,
    wqkv_ref,
    wo_ref,
    cos_ref,
    sin_ref,
    seg_col_ref,
    seg_row_ref,
    gain_two_ref,
    h1_ref,
    xn2_ref,
    part,
    arrived,
    send_sem,
    recv_sem,
):
    x = lax.axis_index(TENSOR)
    aside = {TENSOR: 1 - x}

    @pl.when(lax.axis_index(SECTION) == 0)
    def _():
        barrier = pltpu.get_barrier_semaphore()
        pl.semaphore_signal(barrier, inc=1, device_id=aside, device_id_type=pl.DeviceIdType.MESH)

        def one(i, carry):
            at = jnp.where(i == 0, 1 - x, x)
            rows = x_ref[at].astype(jnp.float32)
            normed = (rows * rms_scale(rows) * gain_one_ref[...]).astype(jnp.bfloat16)
            _, attended = attend_part(
                group,
                normed,
                wqkv_ref[...],
                (cos_ref[...], sin_ref[...]),
                allowed_pairs(seg_col_ref[at], seg_row_ref[at]),
            )
            branch = dot(attended, wo_ref[...])

            @pl.when(i == 0)
            def _():
                part[...] = branch.astype(jnp.bfloat16)
                pl.semaphore_wait(barrier, 1)
                copy().start()

            @pl.when(i == 1)
            def _():
                h1_ref[...] = rows + branch

            return carry

        def copy():
            return pltpu.make_async_remote_copy(
                src_ref=part,
                dst_ref=arrived,
                send_sem=send_sem,
                recv_sem=recv_sem,
                device_id=aside,
                device_id_type=pl.DeviceIdType.MESH,
            )

        lax.fori_loop(0, 2, one, 0)
        copy().wait()
        middle = h1_ref[...] + arrived[...].astype(jnp.float32)
        h1_ref[...] = middle
        xn2_ref[...] = (middle * rms_scale(middle) * gain_two_ref[...]).astype(jnp.bfloat16)


def attn_split(rows, seg, gains, wqkv, wo, tables, group):
    _, length, width = rows.shape
    vmem = pl.BlockSpec(memory_space=pltpu.VMEM)
    return pl.pallas_call(
        functools.partial(attn_split_kernel, group),
        in_specs=[vmem] * 9,
        out_specs=[vmem] * 2,
        out_shape=[
            jax.ShapeDtypeStruct((length, width), jnp.float32),
            jax.ShapeDtypeStruct((length, width), jnp.bfloat16),
        ],
        scratch_shapes=[
            pltpu.VMEM((length, width), jnp.bfloat16),
            pltpu.VMEM((length, width), jnp.bfloat16),
            pltpu.SemaphoreType.DMA,
            pltpu.SemaphoreType.DMA,
        ],
        compiler_params=pltpu.CompilerParams(
            collective_id=8, has_side_effects=True, vmem_limit_bytes=48 * MIB
        ),
        cost_estimate=pl.CostEstimate(
            flops=4 * 10**9, bytes_accessed=20 * 10**6, transcendentals=2 * 10**6
        ),
        name="attn_split",
    )(
        rows,
        gains[0],
        wqkv,
        wo,
        tables[0],
        tables[1],
        seg[:, :, None],
        seg[:, None, :],
        gains[1],
    )


def both_halves_kernel(
    chunks,
    wqkv,
    wo,
    after,
    wqkv_before,
    wo_before,
    wqkv_all,
    wo_all,
    wqkv_held,
    wo_held,
    own_sem,
    out_sem,
    x_send,
    x_recv,
    core_send,
    core_recv,
):
    del after, wqkv_before, wo_before
    x = lax.axis_index(TENSOR)
    core = lax.axis_index(DP)
    aside, partner = {TENSOR: 1 - x}, {DP: 1 - core}
    pairs = ((wqkv, wqkv_held, wqkv_all), (wo, wo_held, wo_all))

    def span(i, of_core, chunk):
        rows = pairs[i][0].shape[0] // (2 * chunks)
        return pl.ds((of_core * chunks + chunk) * rows, rows)

    def own_copy(i, of_core, chunk):
        shard, held, _ = pairs[i]
        at = span(i, of_core, chunk)
        return pltpu.make_async_copy(shard.at[at], held.at[x, at], own_sem.at[i, of_core, chunk])

    def out_copy(i, half):
        _, held, out = pairs[i]
        return pltpu.make_async_copy(held.at[half], out.at[half], out_sem.at[i, half])

    def x_copy(i, chunk, half):
        _, held, _ = pairs[i]
        at = held.at[half, span(i, core, chunk)]
        return pltpu.make_async_remote_copy(
            src_ref=at,
            dst_ref=at,
            send_sem=x_send.at[i, chunk],
            recv_sem=x_recv.at[i, chunk],
            device_id=aside,
            device_id_type=pl.DeviceIdType.MESH,
        )

    def core_copy(i, chunk, of_core):
        _, held, _ = pairs[i]
        at = held.at[1 - x, span(i, of_core, chunk)]
        return pltpu.make_async_remote_copy(
            src_ref=at,
            dst_ref=at,
            send_sem=core_send.at[i, chunk],
            recv_sem=core_recv.at[i, chunk],
            device_id=partner,
            device_id_type=pl.DeviceIdType.MESH,
        )

    steps = [(i, chunk) for i in range(2) for chunk in range(chunks)]

    @pl.when(lax.axis_index(SECTION) == 0)
    def _():
        for of_core in (core, 1 - core):
            for i, chunk in steps:
                own_copy(i, of_core, chunk).start()
        barrier = pltpu.get_barrier_semaphore()
        for other in (aside, partner):
            pl.semaphore_signal(barrier, inc=1, device_id=other, device_id_type=pl.DeviceIdType.MESH)
        pl.semaphore_wait(barrier, 2)
        for i, chunk in steps:
            own_copy(i, core, chunk).wait()
            x_copy(i, chunk, x).start()
        for i, chunk in steps:
            own_copy(i, 1 - core, chunk).wait()
        for i in range(2):
            out_copy(i, x).start()
        for i, chunk in steps:
            x_copy(i, chunk, 1 - x).wait_recv()
            core_copy(i, chunk, core).start()
        for i in range(2):
            for chunk in range(chunks):
                core_copy(i, chunk, 1 - core).wait_recv()
            out_copy(i, 1 - x).start()
        for i, chunk in steps:
            x_copy(i, chunk, x).wait_send()
            core_copy(i, chunk, core).wait_send()
        for i in range(2):
            for half in range(2):
                out_copy(i, half).wait()


def both_halves(wqkv, wo, after, before, chunks=4):
    anywhere = pl.BlockSpec(memory_space=pl.ANY)
    dma = pltpu.SemaphoreType.DMA
    return pl.pallas_call(
        functools.partial(both_halves_kernel, chunks),
        in_specs=[anywhere] * 5,
        out_specs=[anywhere] * 2,
        input_output_aliases={3: 0, 4: 1},
        out_shape=[
            jax.ShapeDtypeStruct((2,) + wqkv.shape, wqkv.dtype),
            jax.ShapeDtypeStruct((2,) + wo.shape, wo.dtype),
        ],
        scratch_shapes=[
            pltpu.VMEM((2,) + wqkv.shape, wqkv.dtype),
            pltpu.VMEM((2,) + wo.shape, wo.dtype),
            dma((2, 2, chunks)),
            dma((2, 2)),
        ]
        + [dma((2, chunks))] * 4,
        compiler_params=pltpu.CompilerParams(
            collective_id=9, has_side_effects=True, vmem_limit_bytes=62 * MIB
        ),
        cost_estimate=pl.CostEstimate(flops=0, bytes_accessed=30 * 10**6, transcendentals=0),
        name="both_halves",
    )(wqkv, wo, after, *before)


def attn_backward_kernel(group, skipped, *refs):
    @pl.when(lax.axis_index(SECTION) != skipped)
    def _():
        pairs = [refs[2 * i : 2 * i + 2] for i in range(6)]
        (
            wqkv_hbm,
            wo_hbm,
            rows_ref,
            grad_gates_ref,
            router_ref,
            gain_one_ref,
            gain_two_ref,
            cos_ref,
            sin_ref,
            seg_col_ref,
            seg_row_ref,
            grad_in_ref,
            mid_ref,
            dqkv_ref,
            small_ref,
            x_ref,
            h1_ref,
            xn2_ref,
            gates_ref,
            qkv_ref,
            top_ref,
            wqkv_ref,
            wo_ref,
            middle_acc,
            normed_acc,
            taken_sem,
            weight_sem,
        ) = refs[12:]
        taken = (x_ref, h1_ref, xn2_ref, gates_ref, qkv_ref, top_ref)
        experts = grad_gates_ref.shape[0]
        parts = wqkv_ref.shape[0]

        def weight_copies(half):
            return [
                pltpu.make_async_copy(hbm.at[half], ref.at[half], weight_sem.at[i, half])
                for i, (hbm, ref) in enumerate(((wqkv_hbm, wqkv_ref), (wo_hbm, wo_ref)))
            ]

        for i in (3, 2, 1, 5, 4, 0):
            start_of_section(*pairs[i], taken[i], taken_sem.at[i])

        def arrived(i):
            pltpu.make_async_copy(pairs[i][0], taken[i], taken_sem.at[i]).wait()
            return taken[i]

        gates = arrived(3)[...]
        grad_gates = grad_gates_ref[...]
        chosen = gates * (grad_gates - jnp.sum(gates * grad_gates, axis=0, keepdims=True))
        logits = chosen.astype(jnp.bfloat16)
        small_ref[0:experts, :] = dot(logits, arrived(2)[...])
        for copy in weight_copies(0):
            copy.start()
        grad_normed = dot(logits, router_ref[...], TN) + rows_ref[...].astype(jnp.float32)
        middle = arrived(1)[...]
        grad_middle, gain_grad = norm_back(grad_normed, middle, rms_scale(middle), gain_two_ref[...])
        small_ref[experts : experts + 1, :] = gain_grad[None, :]
        grad_middle = grad_middle + arrived(5)[...].astype(jnp.float32)
        middle_acc[...] = grad_middle
        mid_ref[...] = grad_middle.astype(jnp.bfloat16)
        normed_acc[...] = jnp.zeros_like(normed_acc)
        arrived(4)

        def one(half, carry):
            for copy in weight_copies(half):
                copy.wait()

            @pl.when(half + 1 < parts)
            def _():
                for copy in weight_copies(half + 1):
                    copy.start()

            attn_backward_part(
                group,
                half,
                mid_ref,
                wqkv_ref,
                wo_ref,
                (cos_ref[...], -sin_ref[...]),
                (seg_col_ref[...], seg_row_ref[...]),
                qkv_ref,
                dqkv_ref,
                normed_acc,
            )
            return carry

        lax.fori_loop(0, parts, one, 0)
        rows = arrived(0)[...].astype(jnp.float32)
        grad_rows, gain_grad = norm_back(normed_acc[...], rows, rms_scale(rows), gain_one_ref[...])
        grad_in_ref[...] = (grad_rows + middle_acc[...]).astype(jnp.bfloat16)
        small_ref[experts + 1 : experts + 2, :] = gain_grad[None, :]
        small_ref[experts + 2 :, :] = jnp.zeros_like(small_ref[experts + 2 :, :])


def attn_backward_part(
    group, part, mid_ref, wqkv_ref, wo_ref, tables, segs, qkv_ref, dqkv_ref, normed_acc
):
    length = mid_ref.shape[0]
    width = wqkv_ref.shape[2]
    query_width = width * group // (group + 2)
    key_width = (width - query_width) // 2
    cosine, sine = tables
    seg_col, seg_row = segs
    grad_att = dot(mid_ref[...], wo_ref[part], NT).astype(jnp.bfloat16).astype(jnp.float32)
    grad_out = slabs_of(grad_att, 0, query_width // (2 * HD))
    kept = qkv_ref[part]
    query = [slab.astype(jnp.float32) for slab in slabs_of(kept, 0, query_width // (2 * HD))]
    key = slabs_of(kept, query_width, key_width // (2 * HD))
    value = slabs_of(kept, query_width + key_width, key_width // (2 * HD))
    key_at = lax.broadcasted_iota(jnp.int32, (length, length), 0)
    query_at = lax.broadcasted_iota(jnp.int32, (length, length), 1)
    allowed = (query_at >= key_at) & (seg_col == seg_row)
    grad_query = [None] * len(query)
    grad_key = [None] * len(key)
    grad_value = [None] * len(value)
    for kv_head in range(key_width // HD):
        side = kv_head % 2
        slab_at = kv_head // 2
        key_slab = key[slab_at]
        key_side = one_side(key_slab, side)
        value_slab = value[slab_at]
        for head in range(group * kv_head, group * (kv_head + 1)):
            query_head = aligned_head(query, head, side, HD**-0.5)
            out_head = aligned_head(grad_out, head, side, 1.0)
            scores = dot(key_slab, query_head, NT)
            scores = jnp.where(allowed, scores, NEG_BIG)
            exponent = jnp.exp(scores - jnp.max(scores, axis=0, keepdims=True))
            probability = exponent / jnp.sum(exponent, axis=0, keepdims=True)
            grad_prob = dot(value_slab, out_head, NT)
            value_part = dot(probability.astype(jnp.bfloat16), out_head)
            centre = jnp.sum(probability * grad_prob, axis=0, keepdims=True)
            grad_scores = (probability * (grad_prob - centre)).astype(jnp.bfloat16)
            key_part = dot(grad_scores, query_head)
            query_part = dot(grad_scores, key_side, TN) * HD**-0.5
            if head % 2 != side:
                query_part = pltpu.roll(query_part, HD, 1)
            at = head // 2
            grad_query[at] = query_part if head % 2 == 0 else grad_query[at] + query_part
            first = head == 2 * group * slab_at
            grad_key[slab_at] = key_part if first else grad_key[slab_at] + key_part
            grad_value[slab_at] = value_part if first else grad_value[slab_at] + value_part
    turned = [turn_pair(slab, cosine, sine).astype(jnp.bfloat16) for slab in grad_query + grad_key]
    dqkv = jnp.concatenate(turned + [slab.astype(jnp.bfloat16) for slab in grad_value], axis=1)
    dqkv_ref[part] = dqkv
    normed_acc[...] += dot(dqkv, wqkv_ref[part], NT)


def attn_backward(
    kept, rows, grad_gates, seg, gains, router, wqkv, wo, tables, group, skipped
):
    length, width = rows.shape
    parts, _, qkv_width = wqkv.shape
    experts = router.shape[0]
    vmem = pl.BlockSpec(memory_space=pltpu.VMEM)
    anywhere = pl.BlockSpec(memory_space=pl.ANY)
    dma = pltpu.SemaphoreType.DMA
    return pl.pallas_call(
        functools.partial(attn_backward_kernel, group, skipped),
        in_specs=[anywhere] * 14 + [vmem] * 9,
        out_specs=[vmem] * 4,
        out_shape=[
            jax.ShapeDtypeStruct((length, width), jnp.bfloat16),
            jax.ShapeDtypeStruct((length, width), jnp.bfloat16),
            jax.ShapeDtypeStruct((parts, length, qkv_width), jnp.bfloat16),
            jax.ShapeDtypeStruct((experts + 8, width), jnp.float32),
        ],
        scratch_shapes=[pltpu.VMEM(one.shape, one.dtype) for one, _ in kept]
        + [
            pltpu.VMEM(wqkv.shape, wqkv.dtype),
            pltpu.VMEM(wo.shape, wo.dtype),
            pltpu.VMEM((length, width), jnp.float32),
            pltpu.VMEM((length, width), jnp.float32),
            dma((len(kept),)),
            dma((2, parts)),
        ],
        compiler_params=pltpu.CompilerParams(vmem_limit_bytes=62 * MIB),
        cost_estimate=pl.CostEstimate(
            flops=8 * 10**9, bytes_accessed=20 * 10**6, transcendentals=2 * 10**6
        ),
        name="attn_backward",
    )(
        *[one for pair in kept for one in pair],
        wqkv,
        wo,
        rows,
        grad_gates,
        router,
        gains[0],
        gains[1],
        tables[0],
        tables[1],
        seg[:, None],
        seg[None, :],
    )


def attn_weights_kernel(*refs):
    groups, out_ref = [refs[3 * i : 3 * i + 3] for i in range(4)], refs[12]
    width = out_ref.shape[1]

    def kept(group):
        one, both, three = group
        return jnp.concatenate([of_section(one, three), both[...]], axis=-2)

    def found(group):
        one, both, three = group
        return jnp.concatenate([both[...], of_section(three, one)], axis=-2)

    xn1, att = kept(groups[0]), kept(groups[1])[0]
    mid, dqkv = found(groups[2]), found(groups[3])[0]
    qkv_width = dqkv.shape[1]
    out_ref[0, :, :qkv_width] = dot(xn1, dqkv, TN).astype(jnp.bfloat16)
    half = width // 2
    for i in range(2):
        out_ref[0, i * half : (i + 1) * half, qkv_width:] = dot(
            att, mid[:, i * half : (i + 1) * half], TN
        ).astype(jnp.bfloat16)


def attn_weights(xn1, att, mid, dqkv):
    rows, width = xn1[0].shape
    parts, _, att_width = att[0].shape
    qkv_width = dqkv[0].shape[2]

    def whole(*shape):
        return pl.BlockSpec(shape, lambda i: (0,) * len(shape))

    def part(*shape):
        return pl.BlockSpec((1,) + shape, lambda i: (i, 0, 0))

    return pl.pallas_call(
        attn_weights_kernel,
        grid=(parts,),
        in_specs=[whole(rows, width)] * 3
        + [part(rows, att_width)] * 3
        + [whole(rows, width)] * 3
        + [part(rows, qkv_width)] * 3,
        out_specs=part(width, qkv_width + width // 2),
        out_shape=jax.ShapeDtypeStruct((parts, width, qkv_width + width // 2), jnp.bfloat16),
        compiler_params=pltpu.CompilerParams(vmem_limit_bytes=56 * MIB),
        cost_estimate=pl.CostEstimate(
            flops=7 * 10**9, bytes_accessed=20 * 10**6, transcendentals=0
        ),
        name="attn_weights",
    )(*xn1, *att, *mid, *dqkv)


def looked_up(place, values):
    found = values[0]
    for i, value in enumerate(values[1:]):
        found = jnp.where(place == i + 1, value, found)
    return found


def nearest_first(place, reach):
    table = []
    for at in range(reach):
        table.append(sorted(range(reach), key=lambda other: (abs(other - at), other)))
    return [looked_up(place, [table[at][k] for at in range(reach)]) for k in range(reach)]


MESH_ID = pl.DeviceIdType.MESH


class Chain:
    def __init__(self, reach):
        self.reach = reach
        self.z = lax.axis_index(EXPERT)
        self.x = lax.axis_index(TENSOR)
        self.me = 2 * self.z + self.x
        self.aside = {TENSOR: 1 - self.x}
        self.above = {EXPERT: self.z + 1}
        self.below = {EXPERT: self.z - 1}
        self.has_above = self.z < reach - 1
        self.has_below = self.z > 0
        self.order = nearest_first(self.z, reach)

    def near(self, k):
        return self.order[k] if isinstance(k, int) else looked_up(k, self.order)

    def greet_group(self, partner=None):
        barrier = pltpu.get_barrier_semaphore()
        if partner is not None:
            pl.semaphore_signal(barrier, inc=1, device_id=partner, device_id_type=MESH_ID)
        for other in range(2 * self.reach):

            @pl.when(other != self.me)
            def _():
                pl.semaphore_signal(
                    barrier,
                    inc=1,
                    device_id={EXPERT: other // 2, TENSOR: other % 2},
                    device_id_type=MESH_ID,
                )

        pl.semaphore_wait(barrier, 2 * self.reach - (1 if partner is None else 0))


def is_end(chain, source):
    return jnp.logical_or(source == 0, source == chain.reach - 1)


class Gather:
    def __init__(self, chain, blocks, send_sem, recv_sem, paired=False):
        self.chain, self.blocks, self.send_sem, self.recv_sem = chain, blocks, send_sem, recv_sem
        self.paired = paired

    def copy(self, source, column, piece, way, target):
        at = 2 * source + column
        return pltpu.make_async_remote_copy(
            src_ref=self.blocks.at[at, piece],
            dst_ref=self.blocks.at[at, piece],
            send_sem=self.send_sem.at[way, source, piece],
            recv_sem=self.recv_sem.at[at, piece],
            device_id=target,
            device_id_type=MESH_ID,
        )

    def over_x(self, source, piece, act):
        c = self.chain
        crosses = jnp.logical_and(is_end(c, source), source != c.z)
        if piece == 0:
            act(self.copy(source, c.x, 0, 0, c.aside))
        else:

            @pl.when(jnp.logical_not(crosses))
            def _():
                act(self.copy(source, c.x, piece, 0, c.aside))

    def each_way(self, source, piece, up, down, act):
        c = self.chain
        if up:

            @pl.when(c.has_above)
            def _():
                act(self.copy(source, c.x, piece, 1, c.above))

        if down:

            @pl.when(c.has_below)
            def _():
                act(self.copy(source, c.x, piece, 2, c.below))

        if not (self.paired and up and down):
            self.over_x(source, piece, act)

    def start(self):
        for piece in range(PIECES):
            self.each_way(self.chain.z, piece, True, True, lambda copy: copy.start())
        if self.paired:
            self.cross_out()

    def relay(self, distance):
        c = self.chain
        for piece in range(PIECES):

            @pl.when(c.z - distance >= 0)
            def _():
                self.copy(c.z - distance, c.x, piece, 1, c.below).wait_recv()
                self.each_way(c.z - distance, piece, True, False, lambda copy: copy.start())

            @pl.when(c.z + distance <= c.reach - 1)
            def _():
                self.copy(c.z + distance, c.x, piece, 2, c.above).wait_recv()
                self.each_way(c.z + distance, piece, False, True, lambda copy: copy.start())

    def cross_copy(self, end):
        c = self.chain
        return self.copy(end, 1 - c.x, PIECES - 1, 3, c.below if end else c.above)

    def cross_out(self):
        c = self.chain
        for end in (0, c.reach - 1):

            @pl.when(c.z == end)
            def _():
                self.cross_copy(end).start()

    def cross_relay(self, distance):
        c = self.chain
        for end in (0, c.reach - 1):
            last = c.reach - 1 - end

            @pl.when(jnp.where(c.z > end, c.z - end, end - c.z) == distance)
            def _():
                self.cross_copy(end).wait_recv()

                @pl.when(c.z != last)
                def _():
                    self.cross_copy(end).start()

    def wait_aside(self, source):
        c = self.chain
        self.copy(source, 1 - c.x, 0, 0, c.aside).wait_recv()

        @pl.when(jnp.logical_not(jnp.logical_and(is_end(c, source), source != c.z)))
        def _():
            self.copy(source, 1 - c.x, PIECES - 1, 0, c.aside).wait_recv()

    def drain(self):
        c = self.chain
        for piece in range(PIECES):
            self.each_way(c.z, piece, True, True, lambda copy: copy.wait_send())
            for distance in range(1, c.reach):

                @pl.when(c.z - distance >= 0)
                def _():
                    self.each_way(
                        c.z - distance, piece, True, False, lambda copy: copy.wait_send()
                    )

                @pl.when(c.z + distance <= c.reach - 1)
                def _():
                    self.each_way(
                        c.z + distance, piece, False, True, lambda copy: copy.wait_send()
                    )

        for end in (0, c.reach - 1):

            @pl.when(c.z != c.reach - 1 - end)
            def _():
                self.cross_copy(end).wait_send()


PIECES = 2
TAIL_PIECES = 4


class Reduce:
    def __init__(self, chain, part_at, from_x, from_z, sems, pieces=PIECES, cross=None):
        self.chain, self.part_at, self.from_x, self.from_z = chain, part_at, from_x, from_z
        self.pieces = pieces
        self.cross = cross
        self.x_send, self.x_recv, self.z_send, self.z_recv = sems

    def part_copy(self, home, piece):
        c = self.chain
        return pltpu.make_async_remote_copy(
            src_ref=self.part_at(home, 1 - c.x, piece),
            dst_ref=self.from_x.at[home, piece],
            send_sem=self.x_send.at[home, piece],
            recv_sem=self.x_recv.at[home, piece],
            device_id=c.aside,
            device_id_type=MESH_ID,
        )

    def sum_copy(self, home, piece, slot, target):
        return pltpu.make_async_remote_copy(
            src_ref=self.part_at(home, self.chain.x, piece),
            dst_ref=self.from_z.at[slot, piece],
            send_sem=self.z_send.at[home, piece],
            recv_sem=self.z_recv.at[slot, piece],
            device_id=target,
            device_id_type=MESH_ID,
        )

    def over_x(self, home, piece, act):
        c = self.chain
        if self.cross is None:
            act()
        else:
            crosses = jnp.logical_and(is_end(c, home), home != c.z)

            @pl.when(jnp.logical_not(jnp.logical_and(crosses, piece == self.pieces - 1)))
            def _():
                act()

    def start(self, k, piece):
        home = self.chain.near(k)
        self.over_x(home, piece, lambda: self.part_copy(home, piece).start())

    def arrive(self, k, piece):
        home = self.chain.near(k)
        self.over_x(home, piece, lambda: self.part_copy(home, piece).wait_recv())

    def own(self, home, piece):
        c = self.chain
        mine = self.part_at(home, c.x, piece)[...].astype(jnp.float32)
        came = self.from_x[home, piece].astype(jnp.float32)
        if self.cross is not None:
            crosses = jnp.logical_and(is_end(c, home), home != c.z)
            came = jnp.where(jnp.logical_and(crosses, piece == self.pieces - 1), 0.0, came)
        return mine + came

    def cross_copy(self, end):
        c = self.chain
        from_cross, send_sem, recv_sem = self.cross
        at = 1 if end else 0
        return pltpu.make_async_remote_copy(
            src_ref=self.part_at(end, 1 - c.x, self.pieces - 1),
            dst_ref=from_cross.at[at],
            send_sem=send_sem.at[at],
            recv_sem=recv_sem.at[at],
            device_id=c.above if end else c.below,
            device_id_type=MESH_ID,
        )

    def cross_step(self, distance):
        c = self.chain
        for end in (0, c.reach - 1):

            @pl.when(jnp.where(c.z > end, c.z - end, end - c.z) == distance)
            def _():
                @pl.when(c.z != c.reach - 1 - end)
                def _():
                    self.cross_copy(end).wait_recv()
                    mine = self.part_at(end, 1 - c.x, self.pieces - 1)
                    mine[...] = (
                        mine[...].astype(jnp.float32)
                        + self.cross[0][1 if end else 0].astype(jnp.float32)
                    ).astype(mine.dtype)

                @pl.when(c.z != end)
                def _():
                    self.cross_copy(end).start()

    def pass_on(self, k, piece):
        c = self.chain
        home = c.near(k)
        up = home > c.z
        comes = jnp.logical_or(
            jnp.logical_and(up, c.has_below), jnp.logical_and(home < c.z, c.has_above)
        )
        mine = self.part_at(home, c.x, piece)

        @pl.when(comes)
        def _():
            self.sum_copy(home, piece, home, c.above).wait_recv()
            mine[...] = (
                self.own(home, piece) + self.from_z[home, piece].astype(jnp.float32)
            ).astype(mine.dtype)

        @pl.when(jnp.logical_not(comes))
        def _():
            mine[...] = self.own(home, piece).astype(mine.dtype)

        @pl.when(up)
        def _():
            self.sum_copy(home, piece, home, c.above).start()

        @pl.when(home < c.z)
        def _():
            slot = jnp.where(home == c.z - 1, c.reach, home)
            self.sum_copy(home, piece, slot, c.below).start()

    def finish(self, piece, act):
        c = self.chain
        home = c.z

        @pl.when(c.has_below)
        def _():
            self.sum_copy(home, piece, home, c.below).wait_recv()

        @pl.when(c.has_above)
        def _():
            self.sum_copy(home, piece, c.reach, c.above).wait_recv()

        @pl.when(c.has_below & c.has_above)
        def _():
            act(
                piece,
                self.own(home, piece)
                + self.from_z[home, piece].astype(jnp.float32)
                + self.from_z[c.reach, piece].astype(jnp.float32),
            )

        @pl.when(jnp.logical_not(c.has_above))
        def _():
            act(piece, self.own(home, piece) + self.from_z[home, piece].astype(jnp.float32))

        @pl.when(jnp.logical_not(c.has_below))
        def _():
            act(piece, self.own(home, piece) + self.from_z[c.reach, piece].astype(jnp.float32))

    def drain(self):
        c = self.chain

        def one(home, carry):
            for piece in range(self.pieces):
                self.over_x(home, piece, lambda: self.part_copy(home, piece).wait_send())

                @pl.when(home != c.z)
                def _():
                    self.sum_copy(home, piece, home, c.above).wait_send()

            return carry

        lax.fori_loop(0, c.reach, one, 0)
        if self.cross is not None:
            for end in (0, c.reach - 1):

                @pl.when(c.z != end)
                def _():
                    self.cross_copy(end).wait_send()


def masked_softmax(logits, kept):
    top = jnp.max(jnp.where(kept, logits, NEG_BIG), axis=0, keepdims=True)
    exponent = jnp.where(kept, jnp.exp(jnp.where(kept, logits - top, 0.0)), 0.0)
    return exponent / jnp.sum(exponent, axis=0, keepdims=True)


def slot_gates(picks, gate_row):
    return jnp.sum(picks.astype(jnp.float32) * gate_row, axis=1, keepdims=True)


def one_hot_slots(slot_row, cap):
    length = slot_row.shape[1]
    at = lax.broadcasted_iota(jnp.int32, (cap, length), 0).astype(jnp.float32)
    return jnp.where(at == slot_row, 1.0, 0.0).astype(jnp.bfloat16)


def finish_pieces(summed, act):
    def one(piece, carry):
        summed.arrive(0, piece)
        summed.finish(piece, act)
        return carry

    lax.fori_loop(0, PIECES, one, 0)


def reduced_in_order(reach, summed, act):
    count = PIECES * (reach - 1)
    ahead = 3

    def place(i):
        return reach - 1 - i // PIECES, i % PIECES

    summed.cross_step(reach - 1)
    for i in range(ahead):
        summed.start(*place(i))

    def step(i, carry):
        summed.arrive(*place(i))

        @pl.when(i + ahead < count)
        def _():
            summed.start(*place(i + ahead))

        summed.pass_on(*place(i))

        @pl.when(jnp.logical_and(i % PIECES == 1, i < count - 1))
        def _():
            summed.cross_step(reach - 2 - i // PIECES)

        return carry

    lax.fori_loop(0, count, step, 0)
    summed.cross_step(0)
    summed.start(0, PIECES - 1)
    finish_pieces(summed, act)


def gathered_steps(reach, chain, rows, summed, compute):
    rows.start()

    def step(k, carry):
        @pl.when(k + 1 < reach)
        def _():
            rows.relay(k + 1)

        source = chain.near(k)
        rows.wait_aside(source)

        @pl.when(k == 0)
        def _():
            rows.cross_out()

        @pl.when(k > 0)
        def _():
            rows.cross_relay(k)

        @pl.when(k + 1 == reach)
        def _():
            summed.start(0, 0)

        compute(k, source)
        return carry

    lax.fori_loop(0, reach, step, 0)


def whole_rows(block):
    return block.reshape(-1, block.shape[-1])


def moe_forward_kernel(
    reach,
    tick,
    last,
    own_ref,
    h1_ref,
    ids_ref,
    router_ref,
    wg_hbm,
    wu_hbm,
    wd_hbm,
    *refs,
):
    refs = list(refs)
    if tick == 0:
        tops_ref, *shards = refs[:3]
        refs = refs[3:]
    out_ref, gates_ref, slots_ref, own_gates_ref, picked_hbm, g_hbm, u_hbm = refs[:7]
    refs = refs[7:]
    if tick == 0:
        tops_hbm, *halves = refs[:3]
        refs = refs[3:]
    (
        blocks,
        parts,
        from_x,
        from_z,
        from_cross,
        wg_ref,
        wu_ref,
        wd_ref,
        rows_in,
        rows_out,
        g_slots,
        u_slots,
        picks_of,
        ids_all,
        gather_send,
        gather_recv,
        x_send,
        x_recv,
        z_send,
        z_recv,
        cross_send,
        cross_recv,
        weight_sem,
        keep_sem,
        id_send,
        id_recv,
    ) = refs[:26]
    local = wg_ref.shape[0]
    cap = rows_in.shape[2] // 2
    experts = router_ref.shape[0]
    length = own_ref.shape[0]
    section = lax.axis_index(SECTION)
    chain = Chain(reach)

    def weight_copies():
        return [
            pltpu.make_async_copy(hbm, vmem, weight_sem.at[i])
            for i, (hbm, vmem) in enumerate(
                ((wg_hbm, wg_ref), (wu_hbm, wu_ref), (wd_hbm, wd_ref))
            )
        ]

    def keep_copies(k):
        source = chain.near(k)
        slot = k % 2 if isinstance(k, int) else lax.rem(k, 2)
        return [
            pltpu.make_async_copy(rows_in.at[slot], picked_hbm.at[source], keep_sem.at[0, k]),
            pltpu.make_async_copy(g_slots.at[slot], g_hbm.at[source], keep_sem.at[1, k]),
            pltpu.make_async_copy(u_slots.at[slot], u_hbm.at[source], keep_sem.at[2, k]),
        ]

    def id_copy(target, at):
        return pltpu.make_async_remote_copy(
            src_ref=ids_ref,
            dst_ref=ids_all.at[at],
            send_sem=id_send.at[target],
            recv_sem=id_recv.at[at],
            device_id={EXPERT: target // 2, TENSOR: target % 2},
            device_id_type=MESH_ID,
        )

    def compute(k, source):
        slot = lax.rem(k, 2)

        @pl.when(k == 0)
        def _():
            for copy in weight_copies():
                copy.wait()

        @pl.when(k >= 2)
        def _():
            for copy in keep_copies(k - 2):
                copy.wait()

        gate_of = {}
        ahead = lax.broadcasted_iota(jnp.int32, (length, length), 0)
        behind = lax.broadcasted_iota(jnp.int32, (length, length), 1)
        before = jnp.where(ahead < behind, 1.0, 0.0).astype(jnp.bfloat16)
        named = lax.rem(
            lax.broadcasted_iota(jnp.int32, (experts, length), 0) + chain.me * local, experts
        )
        for i in range(2):
            at = 2 * source + i

            @pl.when(at != chain.me)
            def _():
                id_copy(at, at).wait_recv()

            ids = ids_all[at]
            member = ids[0:1, :] == named
            for pick in range(1, TOPK):
                member = jnp.logical_or(member, ids[pick : pick + 1, :] == named)
            rows = whole_rows(blocks[at])
            gates = masked_softmax(dot(router_ref[...], rows, NT), member)
            gates_ref[at] = gates

            @pl.when(at == chain.me)
            def _():
                own_gates_ref[...] = gates

            mine = jnp.where(member[:8], 1.0, 0.0).astype(jnp.bfloat16)
            taken = jnp.where(member[:8], dot(mine, before), -1.0)
            slots_ref[at] = taken
            for e in range(local):
                picks = one_hot_slots(taken[e : e + 1, :], cap)
                picks_of[i, e * cap : (e + 1) * cap, :] = picks
                gate_of[i, e] = slot_gates(picks, gates[e : e + 1, :])
            gathered = dot(picks_of[i], rows).astype(jnp.bfloat16)
            for e in range(local):
                rows_in[slot, e, i * cap : (i + 1) * cap, :] = gathered[e * cap : (e + 1) * cap, :]
        for e in range(local):
            rows = rows_in[slot, e]
            gate_pre = dot(rows, wg_ref[e])
            up_pre = dot(rows, wu_ref[e])
            g_slots[slot, e] = gate_pre.astype(jnp.bfloat16)
            u_slots[slot, e] = up_pre.astype(jnp.bfloat16)
            hidden = (gate_pre * jax.nn.sigmoid(gate_pre) * up_pre).astype(jnp.bfloat16)
            produced = dot(hidden, wd_ref[e])
            for i in range(2):
                rows_out[i, e * cap : (e + 1) * cap, :] = (
                    produced[i * cap : (i + 1) * cap, :] * gate_of[i, e]
                ).astype(jnp.bfloat16)
        for i in range(2):
            share = dot(picks_of[i], rows_out[i], TN).astype(jnp.bfloat16)
            parts[2 * source + i] = share.reshape(parts.shape[1:])
        for copy in keep_copies(k):
            copy.start()

    def finish(piece, total):
        at = pl.ds(pl.multiple_of(piece * total.shape[0], total.shape[0]), total.shape[0])
        out_ref[at, :] = (h1_ref[at, :] + total).astype(jnp.bfloat16)

    def run():
        for copy in weight_copies():
            copy.start()
        blocks[chain.me] = own_ref[...].reshape(blocks.shape[1:])
        ids_all[chain.me] = ids_ref[...]
        chain.greet_group()
        for target in range(2 * reach):

            @pl.when(target != chain.me)
            def _():
                id_copy(target, chain.me).start()

        rows = Gather(chain, blocks, gather_send, gather_recv)
        summed = Reduce(
            chain,
            lambda home, column, piece: parts.at[2 * home + column, piece],
            from_x,
            from_z,
            (x_send, x_recv, z_send, z_recv),
            cross=(from_cross, cross_send, cross_recv),
        )
        gathered_steps(reach, chain, rows, summed, compute)
        reduced_in_order(reach, summed, finish)
        rows.drain()
        summed.drain()
        for target in range(2 * reach):

            @pl.when(target != chain.me)
            def _():
                id_copy(target, chain.me).wait_send()

        for k in (reach - 2, reach - 1):
            for copy in keep_copies(k):
                copy.wait()

    if tick == 0:
        second_send, second_recv, tops_sem, *refs = refs[26:]
        landed, (stage_sem, own_sem, half_sem, wx_send, wx_recv, core_send, core_recv) = (
            refs[:2],
            refs[2:],
        )
        core = lax.axis_index(DP)
        partner = {DP: 1 - core}
        chunks = local
        pieces = [(i, chunk) for i in range(2) for chunk in range(chunks)]

        def span(i, of_core, chunk):
            rows = shards[i].shape[0] // (2 * chunks)
            return pl.ds((of_core * chunks + chunk) * rows, rows)

        def stage(i, chunk, mine):
            rows, columns = shards[i].shape[0] // (2 * chunks), shards[i].shape[1]
            if mine:
                return rows_in.at[i, chunk, pl.ds(0, rows), pl.ds(0, columns)]
            if i == 0:
                return rows_out.at[chunk // 2, pl.ds(chunk % 2 * rows, rows), pl.ds(0, columns)]
            return from_x.at[chunk, 0, pl.ds(0, rows)]

        def stage_copy(i, chunk, mine):
            at = span(i, core if mine else 1 - core, chunk)
            return pltpu.make_async_copy(
                shards[i].at[at], stage(i, chunk, mine), stage_sem.at[i, chunk, 1 - mine]
            )

        def own_copy(i, chunk, mine):
            at = span(i, core if mine else 1 - core, chunk)
            return pltpu.make_async_copy(
                stage(i, chunk, mine), halves[i].at[chain.x, at], own_sem.at[i, chunk, 1 - mine]
            )

        def half_copy(i):
            return pltpu.make_async_copy(landed[i], halves[i].at[1 - chain.x], half_sem.at[i])

        def weight_x_copy(i, chunk):
            return pltpu.make_async_remote_copy(
                src_ref=stage(i, chunk, 1),
                dst_ref=landed[i].at[span(i, core, chunk)],
                send_sem=wx_send.at[i, chunk],
                recv_sem=wx_recv.at[i, chunk],
                device_id=chain.aside,
                device_id_type=MESH_ID,
            )

        def weight_core_copy(i, chunk, of_core):
            at = landed[i].at[span(i, of_core, chunk)]
            return pltpu.make_async_remote_copy(
                src_ref=at,
                dst_ref=at,
                send_sem=core_send.at[i, chunk],
                recv_sem=core_recv.at[i, chunk],
                device_id=partner,
                device_id_type=MESH_ID,
            )

        @pl.when(section == 0)
        def _():
            run()

        @pl.when(section != 0)
        def _():
            for mine in (1, 0):
                for i, chunk in pieces:
                    stage_copy(i, chunk, mine).start()
            own_tops = [
                pltpu.make_async_copy(
                    tops_ref.at[micro], buffer.at[pl.ds(2 * chain.z, 2)], tops_sem.at[micro]
                )
                for micro, buffer in enumerate((blocks, parts))
            ]
            for copy in own_tops:
                copy.start()
            chain.greet_group(partner)
            for copy in own_tops:
                copy.wait()
            both = (
                Gather(chain, blocks, gather_send, gather_recv, True),
                Gather(chain, parts, second_send, second_recv, True),
            )
            copies = [
                pltpu.make_async_copy(blocks, tops_hbm.at[0], tops_sem.at[0]),
                pltpu.make_async_copy(parts, tops_hbm.at[1], tops_sem.at[1]),
            ]
            both[0].start()
            both[1].start()
            for i, chunk in pieces:
                stage_copy(i, chunk, 1).wait()
                weight_x_copy(i, chunk).start()
                own_copy(i, chunk, 1).start()
            for i, chunk in pieces:
                stage_copy(i, chunk, 0).wait()
                own_copy(i, chunk, 0).start()
            for rows in both:
                for distance in range(1, reach):
                    rows.relay(distance)
                    rows.cross_relay(distance)
            for i, chunk in pieces:
                weight_x_copy(i, chunk).wait_recv()
                weight_core_copy(i, chunk, core).start()
            for i in range(2):
                for chunk in range(chunks):
                    weight_core_copy(i, chunk, 1 - core).wait_recv()
                half_copy(i).start()
            for rows, copy in zip(both, copies):
                for k in range(1, reach):
                    rows.wait_aside(chain.near(k))
                copy.start()
            for rows in both:
                rows.drain()
            for i, chunk in pieces:
                weight_x_copy(i, chunk).wait_send()
                weight_core_copy(i, chunk, core).wait_send()
                for mine in (1, 0):
                    own_copy(i, chunk, mine).wait()
            for i in range(2):
                half_copy(i).wait()
            for copy in copies:
                copy.wait()

    elif tick == last:

        @pl.when(section != 0)
        def _():
            run()

    else:
        run()


def exchange_scratch(reach, length, width):
    piece = (PIECES, length // PIECES, width)
    return [
        pltpu.VMEM((2 * reach,) + piece, jnp.bfloat16),
        pltpu.VMEM((2 * reach,) + piece, jnp.bfloat16),
        pltpu.VMEM((reach,) + piece, jnp.bfloat16),
        pltpu.VMEM((reach + 1,) + piece, jnp.bfloat16),
        pltpu.VMEM((2,) + piece[1:], jnp.bfloat16),
    ]


def exchange_sems(reach):
    dma = pltpu.SemaphoreType.DMA
    return [
        dma((4, reach, PIECES)),
        dma((2 * reach, PIECES)),
        dma((reach, PIECES)),
        dma((reach, PIECES)),
        dma((reach, PIECES)),
        dma((reach + 1, PIECES)),
        dma((2,)),
        dma((2,)),
    ]


def moe_forward_call(reach, tick, last, own, h1, ids, router, wg, wu, wd, firsts):
    length, width = own.shape
    local, _, hidden = wg.shape
    cap = slot_count(length)
    experts = router.shape[0]
    vmem = pl.BlockSpec(memory_space=pltpu.VMEM)
    anywhere = pl.BlockSpec(memory_space=pl.ANY)
    slots = (reach, local, 2 * cap, hidden)
    first = tick == 0
    all_rows = (2 * reach, PIECES, length // PIECES, width)
    return pl.pallas_call(
        functools.partial(moe_forward_kernel, reach, tick, last),
        in_specs=[vmem] * 4 + [anywhere] * 3 + [anywhere] * 3 * first,
        out_specs=[vmem] * 4 + [anywhere] * 3 + [anywhere] * 3 * first,
        out_shape=[
            jax.ShapeDtypeStruct((length, width), jnp.bfloat16),
            jax.ShapeDtypeStruct((2 * reach, experts, length), jnp.float32),
            jax.ShapeDtypeStruct((2 * reach, 8, length), jnp.float32),
            jax.ShapeDtypeStruct((experts, length), jnp.float32),
            jax.ShapeDtypeStruct(slots[:3] + (width,), jnp.bfloat16),
            jax.ShapeDtypeStruct(slots, jnp.bfloat16),
            jax.ShapeDtypeStruct(slots, jnp.bfloat16),
        ]
        + (
            [jax.ShapeDtypeStruct((2,) + all_rows, jnp.bfloat16)]
            + [jax.ShapeDtypeStruct((2,) + shard.shape, shard.dtype) for shard in firsts[1:]]
        )
        * first,
        scratch_shapes=exchange_scratch(reach, length, width)
        + [
            pltpu.VMEM(wg.shape, jnp.bfloat16),
            pltpu.VMEM(wu.shape, jnp.bfloat16),
            pltpu.VMEM(wd.shape, jnp.bfloat16),
            pltpu.VMEM((2, local, 2 * cap, width), jnp.bfloat16),
            pltpu.VMEM((2, local * cap, width), jnp.bfloat16),
            pltpu.VMEM((2,) + slots[1:], jnp.bfloat16),
            pltpu.VMEM((2,) + slots[1:], jnp.bfloat16),
            pltpu.VMEM((2, local * cap, length), jnp.bfloat16),
            pltpu.VMEM((2 * reach, TOPK, length), jnp.int32),
        ]
        + exchange_sems(reach)
        + [
            pltpu.SemaphoreType.DMA((3,)),
            pltpu.SemaphoreType.DMA((3, reach)),
            pltpu.SemaphoreType.DMA((2 * reach,)),
            pltpu.SemaphoreType.DMA((2 * reach,)),
        ]
        + (
            exchange_sems(reach)[:2]
            + [pltpu.SemaphoreType.DMA((2,))]
            + [pltpu.VMEM(shard.shape, shard.dtype) for shard in firsts[1:]]
            + [
                pltpu.SemaphoreType.DMA((2, local, 2)),
                pltpu.SemaphoreType.DMA((2, local, 2)),
                pltpu.SemaphoreType.DMA((2,)),
            ]
            + [pltpu.SemaphoreType.DMA((2, local))] * 4
        )
        * first,
        compiler_params=pltpu.CompilerParams(
            collective_id=1 + tick, has_side_effects=True, vmem_limit_bytes=62 * MIB
        ),
        cost_estimate=pl.CostEstimate(
            flops=20 * 10**9, bytes_accessed=45 * 10**6, transcendentals=2 * 10**6
        ),
        name="moe_forward",
    )(own, h1, ids, router, wg, wu, wd, *(firsts * first))


def moe_backward_kernel(
    reach,
    tick,
    last,
    own_ref,
    slots_first,
    slots_second,
    gates_first,
    gates_second,
    g_first,
    g_second,
    u_first,
    u_second,
    wg_hbm,
    wu_hbm,
    wd_hbm,
    tops_hbm,
    after,
    *refs,
):
    if tick == last:
        refs = refs[4:]
    moe_backward_body(
        reach,
        tick,
        last,
        own_ref,
        (slots_first, slots_second),
        (gates_first, gates_second),
        (g_first, g_second, u_first, u_second),
        (wg_hbm, wu_hbm, wd_hbm),
        tops_hbm,
        *refs,
    )


def moe_backward_body(
    reach,
    tick,
    last,
    own_ref,
    slots_pair,
    gates_pair,
    pre_pairs,
    weights_hbm,
    tops_hbm,
    out_ref,
    home_gates_ref,
    picked_hbm,
    gg_hbm,
    gu_hbm,
    hg_hbm,
    blocks,
    parts,
    from_x,
    from_z,
    from_cross,
    wg_ref,
    wu_ref,
    wd_ref,
    rows_in,
    rows_out,
    g_slots,
    u_slots,
    gg_slots,
    gu_slots,
    hg_slots,
    picks_of,
    gate_parts,
    gate_from,
    gather_send,
    gather_recv,
    x_send,
    x_recv,
    z_send,
    z_recv,
    cross_send,
    cross_recv,
    weight_sem,
    keep_sem,
    load_sem,
    gate_send,
    gate_recv,
    tops_sem,
):
    slots_first, slots_second = slots_pair
    gates_first, gates_second = gates_pair
    g_first, g_second, u_first, u_second = pre_pairs
    wg_hbm, wu_hbm, wd_hbm = weights_hbm
    local = wg_ref.shape[0]
    cap = rows_in.shape[2] // 2
    section = lax.axis_index(SECTION)
    chain = Chain(reach)
    me = chain.me

    def weight_copies():
        return [
            pltpu.make_async_copy(hbm, vmem, weight_sem.at[i])
            for i, (hbm, vmem) in enumerate(
                ((wd_hbm, wd_ref), (wg_hbm, wg_ref), (wu_hbm, wu_ref))
            )
        ]

    def load_copies(step, source, first):
        slot = step % 2 if isinstance(step, int) else lax.rem(step, 2)
        return [
            pltpu.make_async_copy(
                (g_first if first else g_second).at[source], g_slots.at[slot], load_sem.at[0, step]
            ),
            pltpu.make_async_copy(
                (u_first if first else u_second).at[source], u_slots.at[slot], load_sem.at[1, step]
            ),
        ]

    def keep_copies(step, source):
        slot = step % 2 if isinstance(step, int) else lax.rem(step, 2)
        return [
            pltpu.make_async_copy(rows_in.at[slot], picked_hbm.at[source], keep_sem.at[0, step]),
            pltpu.make_async_copy(gg_slots.at[slot], gg_hbm.at[source], keep_sem.at[1, step]),
            pltpu.make_async_copy(gu_slots.at[slot], gu_hbm.at[source], keep_sem.at[2, step]),
            pltpu.make_async_copy(hg_slots.at[slot], hg_hbm.at[source], keep_sem.at[3, step]),
        ]

    def gate_copy(target, at):
        return pltpu.make_async_remote_copy(
            src_ref=gate_parts.at[target],
            dst_ref=gate_from.at[at],
            send_sem=gate_send.at[target],
            recv_sem=gate_recv.at[at],
            device_id={EXPERT: target // 2, TENSOR: target % 2},
            device_id_type=MESH_ID,
        )

    def compute(step, source_of, first):
        source = source_of(step)
        slot = lax.rem(step, 2)

        @pl.when(step == 0)
        def _():
            for copy in weight_copies():
                copy.wait()

        @pl.when(step >= 2)
        def _():
            for copy in keep_copies(step - 2, source_of(step - 2)):
                copy.wait()

        for copy in load_copies(step, source, first):
            copy.wait()
        slots_ref = slots_first if first else slots_second
        gates_ref = gates_first if first else gates_second
        gate_of = {}
        for i in range(2):
            at = 2 * source + i
            for e in range(local):
                picks = one_hot_slots(slots_ref[at, e : e + 1, :], cap)
                picks_of[i, e * cap : (e + 1) * cap, :] = picks
                gate_of[i, e] = slot_gates(picks, gates_ref[at, e : e + 1, :])
            gathered = dot(picks_of[i], whole_rows(blocks[at])).astype(jnp.bfloat16)
            for e in range(local):
                rows_in[slot, e, i * cap : (i + 1) * cap, :] = gathered[e * cap : (e + 1) * cap, :]
        for e in range(local):
            plain = dot(rows_in[slot, e], wd_ref[e], NT)
            gate_pre = g_slots[slot, e].astype(jnp.float32)
            up_pre = u_slots[slot, e].astype(jnp.float32)
            sg = jax.nn.sigmoid(gate_pre)
            hidden = gate_pre * sg * up_pre
            gate_col = jnp.concatenate([gate_of[i, e] for i in range(2)], axis=0)
            grad_gate_col = jnp.sum(hidden * plain, axis=1, keepdims=True)
            grad_hidden = plain * gate_col
            grad_gate = (grad_hidden * up_pre * sg * (1.0 + gate_pre * (1.0 - sg))).astype(
                jnp.bfloat16
            )
            grad_up = (grad_hidden * gate_pre * sg).astype(jnp.bfloat16)
            gg_slots[slot, e] = grad_gate
            gu_slots[slot, e] = grad_up
            hg_slots[slot, e] = (hidden * gate_col).astype(jnp.bfloat16)
            grad_rows = dot(grad_gate, wg_ref[e], NT) + dot(grad_up, wu_ref[e], NT)
            for i in range(2):
                at = 2 * source + i
                rows = slice(i * cap, (i + 1) * cap)
                rows_out[i, e * cap : (e + 1) * cap, :] = grad_rows[rows, :].astype(jnp.bfloat16)
                picks = picks_of[i, e * cap : (e + 1) * cap, :].astype(jnp.float32)
                gate_parts[at, e : e + 1, :] = jnp.sum(
                    picks * grad_gate_col[rows, :], axis=0, keepdims=True
                )
        for i in range(2):
            share = dot(picks_of[i], rows_out[i], TN).astype(jnp.bfloat16)
            parts[2 * source + i] = share.reshape(parts.shape[1:])
        for copy in keep_copies(step, source):
            copy.start()

        @pl.when(step + 2 < reach)
        def _():
            for copy in load_copies(step + 2, source_of(step + 2), first):
                copy.start()

        for i in range(2):
            at = 2 * source + i

            @pl.when(at != me)
            def _():
                gate_copy(at, me).start()

    def finish(piece, total):
        at = pl.ds(pl.multiple_of(piece * total.shape[0], total.shape[0]), total.shape[0])
        out_ref[at, :] = total

    def run(gathered):
        first = gathered

        def source_of(step):
            if isinstance(step, int):
                return chain.near(step if gathered else reach - 1 - step)
            return chain.near(step if gathered else reach - 1 - step)

        def top_copy(step):
            pair = pl.ds(2 * source_of(step), 2)
            return pltpu.make_async_copy(
                tops_hbm.at[min(tick, 1), pair], blocks.at[pair], tops_sem.at[step]
            )

        for step in range(2):
            for copy in load_copies(step, source_of(step), first):
                copy.start()
        if not gathered:
            for step in range(reach):
                top_copy(step).start()
        for copy in weight_copies():
            copy.start()
        chain.greet_group()
        summed = Reduce(
            chain,
            lambda home, column, piece: parts.at[2 * home + column, piece],
            from_x,
            from_z,
            (x_send, x_recv, z_send, z_recv),
            cross=(from_cross, cross_send, cross_recv),
        )
        if gathered:
            blocks[me] = own_ref[...].reshape(blocks.shape[1:])
            rows = Gather(chain, blocks, gather_send, gather_recv)
            gathered_steps(
                reach, chain, rows, summed, lambda step, source: compute(step, source_of, first)
            )
            reduced_in_order(reach, summed, finish)
            rows.drain()
        else:

            def step_back(step, carry):
                k = reach - 1 - step
                top_copy(step).wait()
                compute(step, source_of, first)
                summed.start(k, 0)

                @pl.when(k > 0)
                def _():
                    summed.start(k, PIECES - 1)
                    summed.cross_step(k)

                @pl.when(step >= 1)
                def _():
                    for piece in range(PIECES):
                        summed.arrive(k + 1, piece)
                        summed.pass_on(k + 1, piece)

                return carry

            lax.fori_loop(0, reach, step_back, 0)
            summed.cross_step(0)
            summed.start(0, PIECES - 1)
            finish_pieces(summed, finish)
        summed.drain()
        home_gates_ref[0] = gate_parts[me, :local]
        for at in range(2 * reach):

            @pl.when(at != me)
            def _():
                gate_copy(at, me).wait_send()
                gate_copy(at, at).wait_recv()
                home_gates_ref[lax.rem(at - me + 2 * reach, 2 * reach)] = gate_from[at, :local]

        for step in (reach - 2, reach - 1):
            for copy in keep_copies(step, source_of(step)):
                copy.wait()

    if tick > 0:

        @pl.when(section == 0)
        def _():
            run(True)

    if tick < last:

        @pl.when(section != 0)
        def _():
            run(False)


def moe_backward_call(
    reach, tick, last, own, slots_two, gates_two, g_two, u_two, wg, wu, wd, tops, after, over
):
    length, width = own.shape
    local, _, hidden = wg.shape
    cap = slot_count(length)
    vmem = pl.BlockSpec(memory_space=pltpu.VMEM)
    anywhere = pl.BlockSpec(memory_space=pl.ANY)
    slot_rows = (reach, local, 2 * cap, hidden)
    kept = jax.ShapeDtypeStruct(slot_rows, jnp.bfloat16)
    return pl.pallas_call(
        functools.partial(moe_backward_kernel, reach, tick, last),
        in_specs=[vmem] * 5 + [anywhere] * (9 + len(over)),
        input_output_aliases={14 + i: 2 + i for i in range(len(over))},
        out_specs=[vmem, vmem] + [anywhere] * 4,
        out_shape=[
            jax.ShapeDtypeStruct((length, width), jnp.float32),
            jax.ShapeDtypeStruct((2 * reach, local, length), jnp.float32),
            jax.ShapeDtypeStruct(slot_rows[:3] + (width,), jnp.bfloat16),
            kept,
            kept,
            kept,
        ],
        scratch_shapes=exchange_scratch(reach, length, width)
        + [
            pltpu.VMEM(wg.shape, jnp.bfloat16),
            pltpu.VMEM(wu.shape, jnp.bfloat16),
            pltpu.VMEM(wd.shape, jnp.bfloat16),
            pltpu.VMEM((2, local, 2 * cap, width), jnp.bfloat16),
            pltpu.VMEM((2, local * cap, width), jnp.bfloat16),
        ]
        + [pltpu.VMEM((2,) + slot_rows[1:], jnp.bfloat16)] * 5
        + [
            pltpu.VMEM((2, local * cap, length), jnp.bfloat16),
            pltpu.VMEM((2 * reach, 8, length), jnp.float32),
            pltpu.VMEM((2 * reach, 8, length), jnp.float32),
        ]
        + exchange_sems(reach)
        + [
            pltpu.SemaphoreType.DMA((3,)),
            pltpu.SemaphoreType.DMA((4, reach)),
            pltpu.SemaphoreType.DMA((2, reach)),
            pltpu.SemaphoreType.DMA((2 * reach,)),
            pltpu.SemaphoreType.DMA((2 * reach,)),
            pltpu.SemaphoreType.DMA((reach,)),
        ],
        compiler_params=pltpu.CompilerParams(
            collective_id=4 + tick, has_side_effects=True, vmem_limit_bytes=62 * MIB
        ),
        cost_estimate=pl.CostEstimate(
            flops=20 * 10**9, bytes_accessed=55 * 10**6, transcendentals=2 * 10**6
        ),
        name="moe_backward",
    )(own, *slots_two, *gates_two, *g_two, *u_two, wg, wu, wd, tops, after, *over)


def tick_weights_kernel(sides, *refs):
    x_refs, (dh_ref, gg_ref, gu_ref, hg_ref, _), refs = (
        refs[:sides],
        refs[sides : sides + 5],
        refs[sides + 5 :],
    )
    *before, wg_ref, wu_ref, wd_ref = refs
    hidden = gg_ref.shape[3]
    wide = dh_ref.shape[3]
    rows = (of_section(*x_refs) if sides == 2 else x_refs[0][...]).reshape(-1, wide)
    found = (
        dot(rows, gg_ref[...].reshape(-1, hidden), TN),
        dot(rows, gu_ref[...].reshape(-1, hidden), TN),
        dot(hg_ref[...].reshape(-1, hidden), dh_ref[...].reshape(-1, wide), TN),
    )
    for i, to in enumerate((wg_ref, wu_ref, wd_ref)):
        part = found[i] + before[i][0].astype(jnp.float32) if before else found[i]
        to[0] = part.astype(jnp.bfloat16)


def tick_weights(x_sides, dh, gg, gu, hg, after, before=()):
    groups, local, rows, width = dh.shape
    hidden = gg.shape[3]
    tiles = width // hidden
    wide = width // tiles
    tiled = pl.BlockSpec((groups, 1, rows, wide), lambda e, t: (0, e, 0, t))
    held = pl.BlockSpec((groups, 1, rows, hidden), lambda e, t: (0, e, 0, 0))
    up = jax.ShapeDtypeStruct((local, width, hidden), jnp.bfloat16)
    outs = [
        pl.BlockSpec((1, wide, hidden), lambda e, t: (e, t, 0)),
        pl.BlockSpec((1, wide, hidden), lambda e, t: (e, t, 0)),
        pl.BlockSpec((1, hidden, wide), lambda e, t: (e, 0, t)),
    ]
    return pl.pallas_call(
        functools.partial(tick_weights_kernel, len(x_sides)),
        grid=(local, tiles),
        in_specs=[tiled] * (len(x_sides) + 1)
        + [held] * 3
        + [pl.BlockSpec(memory_space=pl.ANY)]
        + (outs if before else []),
        out_specs=outs,
        out_shape=[up, up, jax.ShapeDtypeStruct((local, hidden, width), jnp.bfloat16)],
        compiler_params=pltpu.CompilerParams(vmem_limit_bytes=62 * MIB),
        cost_estimate=pl.CostEstimate(
            flops=30 * 10**9, bytes_accessed=60 * 10**6, transcendentals=0
        ),
        name="tick_weights",
    )(*x_sides, dh, gg, gu, hg, after, *before)


def ends_exchange_kernel(
    first_hbm, second_hbm, after, out_ref, held, came, load_sem, send_sem, recv_sem
):
    del after
    x = lax.axis_index(TENSOR)
    aside = {TENSOR: 1 - x}
    start_of_section(first_hbm, second_hbm, held, load_sem)
    barrier = pltpu.get_barrier_semaphore()
    pl.semaphore_signal(barrier, inc=1, device_id=aside, device_id_type=MESH_ID)
    pl.semaphore_wait(barrier, 1)
    pltpu.make_async_copy(first_hbm, held, load_sem).wait()
    copy = pltpu.make_async_remote_copy(
        src_ref=held,
        dst_ref=came,
        send_sem=send_sem,
        recv_sem=recv_sem,
        device_id=aside,
        device_id_type=MESH_ID,
    )
    copy.start()
    out_ref[x] = held[...]
    copy.wait()
    out_ref[1 - x] = came[...]


def ends_exchange(first, second, after):
    anywhere = pl.BlockSpec(memory_space=pl.ANY)
    return pl.pallas_call(
        ends_exchange_kernel,
        in_specs=[anywhere] * 3,
        out_specs=pl.BlockSpec(memory_space=pltpu.VMEM),
        out_shape=jax.ShapeDtypeStruct((2,) + first.shape, first.dtype),
        scratch_shapes=[pltpu.VMEM(first.shape, first.dtype)] * 2 + [pltpu.SemaphoreType.DMA] * 3,
        compiler_params=pltpu.CompilerParams(
            collective_id=10, has_side_effects=True, vmem_limit_bytes=62 * MIB
        ),
        cost_estimate=pl.CostEstimate(flops=0, bytes_accessed=4 * 10**6, transcendentals=0),
        name="ends_exchange",
    )(first, second, after)


def tail_kernel(
    reach,
    dense_hbm,
    small_first,
    small_both,
    small_last,
    ends_back,
    ends_forward,
    query_out,
    key_out,
    value_out,
    out_out,
    small_out,
    ends_out,
    mine,
    theirs,
    from_core,
    from_x,
    from_z,
    whole,
    small_held,
    small_came,
    small_z,
    ends_held,
    ends_came,
    mine_sem,
    theirs_sem,
    core_send,
    core_recv,
    x_send,
    x_recv,
    z_send,
    z_recv,
    ring_send,
    ring_recv,
    last_send,
    last_recv,
    out_sem,
    small_send,
    small_recv,
    ends_load,
    ends_keep,
    ends_send,
    ends_recv,
):
    section = lax.axis_index(SECTION)
    core = lax.axis_index(DP)
    partner = {DP: 1 - core}
    chain = Chain(reach)
    x = chain.x
    z = chain.z
    quarter = mine.shape[3]
    def mine_copy(half):
        return pltpu.make_async_copy(dense_hbm.at[half, core], mine.at[half], mine_sem.at[half])

    def theirs_copy(half, piece):
        return pltpu.make_async_copy(
            dense_hbm.at[half, 1 - core, :, piece],
            theirs.at[half, :, piece],
            theirs_sem.at[half, piece],
        )

    def core_copy(half, piece):
        return pltpu.make_async_remote_copy(
            src_ref=theirs.at[half, :, piece],
            dst_ref=from_core.at[half, :, piece],
            send_sem=core_send.at[half, piece],
            recv_sem=core_recv.at[half, piece],
            device_id=partner,
            device_id_type=MESH_ID,
        )

    def add_core(half, k, piece):
        home = chain.near(k)

        @pl.when(k == reach - 1)
        def _():
            core_copy(half, piece).wait_recv()

        mine[half, home, piece] = (
            mine[half, home, piece].astype(jnp.float32)
            + from_core[half, home, piece].astype(jnp.float32)
        ).astype(jnp.bfloat16)

    summed = Reduce(
        chain,
        lambda home, column, piece: mine.at[column, home, piece],
        from_x,
        from_z,
        (x_send, x_recv, z_send, z_recv),
        TAIL_PIECES,
    )

    def ring_copy(source, piece, way, target):
        return pltpu.make_async_remote_copy(
            src_ref=whole.at[core, source, piece],
            dst_ref=whole.at[core, source, piece],
            send_sem=ring_send.at[way, source, piece],
            recv_sem=ring_recv.at[source, piece],
            device_id=target,
            device_id_type=MESH_ID,
        )

    def last_copy(source, piece, side):
        return pltpu.make_async_remote_copy(
            src_ref=whole.at[side, source, piece],
            dst_ref=whole.at[side, source, piece],
            send_sem=last_send.at[source, piece],
            recv_sem=last_recv.at[source, piece],
            device_id=partner,
            device_id_type=MESH_ID,
        )

    def out_copies(side, source):
        block = whole.at[side, source]
        at = side * reach + source
        first = query_out.shape[3]
        second = first + key_out.shape[3]
        third = second + value_out.shape[3]
        half = block.shape[2] - third
        columns = pl.ds(pl.multiple_of(side * half, half), half)
        return [
            pltpu.make_async_copy(block.at[:, :, found], to, out_sem.at[side, source, i])
            for i, (found, to) in enumerate(
                (
                    (pl.ds(0, first), query_out.at[at]),
                    (pl.ds(first, second - first), key_out.at[at]),
                    (pl.ds(second, third - second), value_out.at[at]),
                    (pl.ds(third, half), out_out.at[source, :, :, columns]),
                )
            )
        ]

    def spread_block(source, piece, up, down):
        if up:

            @pl.when(chain.has_above)
            def _():
                ring_copy(source, piece, 0, chain.above).start()

        if down:

            @pl.when(chain.has_below)
            def _():
                ring_copy(source, piece, 1, chain.below).start()

        last_copy(source, piece, core).start()

        @pl.when(piece == TAIL_PIECES - 1)
        def _():
            for copy in out_copies(core, source):
                copy.start()

    def relay(distance, piece):
        @pl.when(z - distance >= 0)
        def _():
            ring_copy(z - distance, piece, 0, chain.below).wait_recv()
            spread_block(z - distance, piece, True, False)

        @pl.when(z + distance <= reach - 1)
        def _():
            ring_copy(z + distance, piece, 1, chain.above).wait_recv()
            spread_block(z + distance, piece, False, True)

    def small_copy(to, i):
        if i < 2:
            return pltpu.make_async_remote_copy(
                src_ref=small_held.at[i],
                dst_ref=small_came.at[i],
                send_sem=small_send.at[i],
                recv_sem=small_recv.at[i],
                device_id=to,
                device_id_type=MESH_ID,
            )
        return pltpu.make_async_remote_copy(
            src_ref=small_z.at[z],
            dst_ref=small_z.at[z],
            send_sem=small_send.at[2 + to],
            recv_sem=small_recv.at[2 + z],
            device_id={EXPERT: to},
            device_id_type=MESH_ID,
        )

    def others(act):
        for other in range(reach):

            @pl.when(other != z)
            def _():
                act(other)

    def small_step(stage):
        if stage == 0:
            total = small_both[...] + of_section(small_last, small_first)
            experts = (total.shape[0] - 8) // 8 * 8
            small_held[0, :experts] = pltpu.roll(total[:experts], chain.me * (experts // (2 * reach)), 0)
            small_held[0, experts:] = total[experts:]
            small_copy(partner, 0).start()
        elif stage == 1:
            small_copy(partner, 0).wait_recv()
            small_held[1] = small_held[0] + small_came[0]
            small_copy(chain.aside, 1).start()
        elif stage == 2:
            small_copy(chain.aside, 1).wait_recv()
            small_z[z] = small_held[1] + small_came[1]
            others(lambda other: small_copy(other, 2).start())
        else:

            def wait(other):
                pltpu.make_async_remote_copy(
                    src_ref=small_z.at[other],
                    dst_ref=small_z.at[other],
                    send_sem=small_send.at[2 + other],
                    recv_sem=small_recv.at[2 + other],
                    device_id={EXPERT: other},
                    device_id_type=MESH_ID,
                ).wait_recv()

            others(wait)
            total = small_z[0]
            for other in range(1, reach):
                total = total + small_z[other]
            small_out[...] = total

    def ends_copy():
        return pltpu.make_async_remote_copy(
            src_ref=ends_held,
            dst_ref=ends_came,
            send_sem=ends_send,
            recv_sem=ends_recv,
            device_id=chain.aside,
            device_id_type=MESH_ID,
        )

    def ends_store(other):
        found, at = (ends_came, 1 - x) if other else (ends_held, x)
        return pltpu.make_async_copy(found, ends_out.at[at], ends_keep.at[int(other)])

    for piece in range(TAIL_PIECES):
        for half in (1 - x, x):
            theirs_copy(half, piece).start()
    for half in range(2):
        mine_copy(half).start()
    start_of_section(ends_back, ends_forward, ends_held, ends_load)

    barrier = pltpu.get_barrier_semaphore()
    pl.semaphore_signal(barrier, inc=1, device_id=partner, device_id_type=MESH_ID)
    pl.semaphore_signal(barrier, inc=1, device_id=chain.aside, device_id_type=MESH_ID)
    others(
        lambda other: pl.semaphore_signal(
            barrier, inc=1, device_id={EXPERT: other}, device_id_type=MESH_ID
        )
    )
    pl.semaphore_wait(barrier, 1 + reach)

    def core_start(piece):
        for half in (1 - x, x):
            theirs_copy(half, piece).wait()
            core_copy(half, piece).start()

    for piece in range(2):
        core_start(piece)
    small_step(0)
    pltpu.make_async_copy(ends_back, ends_held, ends_load).wait()
    ends_store(False).start()
    for half in range(2):
        mine_copy(half).wait()

    steps = TAIL_PIECES * reach
    ahead = 3

    def place(i):
        return reach - 1 - i % reach, i // reach

    def launch(i):
        k, piece = place(i)
        add_core(1 - x, k, piece)
        summed.start(k, piece)

    def finish(piece, total):
        whole[core, z, piece] = total.astype(jnp.bfloat16)

    def late(i):
        def due(offset, act):
            since = i - offset
            if isinstance(i, int):
                if since >= 0 and since % reach == 0 and since // reach < TAIL_PIECES:
                    act(since // reach)
            else:

                @pl.when(jnp.logical_and(since >= 0, lax.rem(since, reach) == 0))
                def _():
                    act(since // reach)

        def own(piece):
            summed.finish(piece, finish)
            spread_block(z, piece, True, True)

        due(reach + 1, own)
        for distance in range(1, reach):
            due(reach + 1 + 2 * distance, functools.partial(relay, distance))

    for i in range(ahead):
        launch(i)
    small_step(1)

    def step(i, carry):
        k, piece = place(i)

        @pl.when(jnp.logical_and(k == reach - 1, piece + 2 < TAIL_PIECES))
        def _():
            core_start(piece + 2)

        @pl.when(i == reach)
        def _():
            small_step(2)

        summed.arrive(k, piece)

        @pl.when(i + ahead < steps)
        def _():
            launch(i + ahead)

        add_core(x, k, piece)

        @pl.when(k > 0)
        def _():
            summed.pass_on(k, piece)

        late(i)
        return carry

    lax.fori_loop(0, steps, step, 0)
    ends_copy().start()
    small_step(3)
    for i in range(steps, steps + 3 * reach):
        late(i)
    def settle_last(source, carry):
        for piece in range(TAIL_PIECES):
            last_copy(source, piece, 1 - core).wait_recv()
        for copy in out_copies(1 - core, source):
            copy.start()
        return carry

    lax.fori_loop(0, reach, settle_last, 0)
    ends_copy().wait_recv()
    ends_store(True).start()

    summed.drain()

    def settle_sends(source, carry):
        for piece in range(TAIL_PIECES):
            last_copy(source, piece, core).wait_send()

            @pl.when(jnp.logical_and(chain.has_above, z >= source))
            def _():
                ring_copy(source, piece, 0, chain.above).wait_send()

            @pl.when(jnp.logical_and(chain.has_below, z <= source))
            def _():
                ring_copy(source, piece, 1, chain.below).wait_send()

        for side in range(2):
            for copy in out_copies(side, source):
                copy.wait()
        return carry

    lax.fori_loop(0, reach, settle_sends, 0)
    for piece in range(TAIL_PIECES):
        for half in range(2):
            core_copy(half, piece).wait_send()
    ends_copy().wait_send()
    for other in (False, True):
        ends_store(other).wait()
    small_copy(partner, 0).wait_send()
    small_copy(chain.aside, 1).wait_send()
    others(lambda other: small_copy(other, 2).wait_send())


def tail_call(reach, widths, dense, smalls, ends):
    halves, cores, _, _, quarter, columns = dense.shape
    width = ends[0].shape[1]
    anywhere = pl.BlockSpec(memory_space=pl.ANY)
    vmem = pl.BlockSpec(memory_space=pltpu.VMEM)
    end = ends[0].shape
    block = (TAIL_PIECES, quarter, columns)
    dma = pltpu.SemaphoreType.DMA
    return pl.pallas_call(
        functools.partial(tail_kernel, reach),
        in_specs=[anywhere] + [vmem] * 3 + [anywhere] * 2,
        out_specs=[anywhere] * 4 + [vmem, anywhere],
        out_shape=[
            jax.ShapeDtypeStruct((cores * reach, TAIL_PIECES, quarter, one), jnp.bfloat16)
            for one in widths
        ]
        + [
            jax.ShapeDtypeStruct((reach, TAIL_PIECES, quarter, width), jnp.bfloat16),
            jax.ShapeDtypeStruct(smalls[0].shape, jnp.float32),
            jax.ShapeDtypeStruct((2,) + end, jnp.bfloat16),
        ],
        scratch_shapes=[
            pltpu.VMEM((halves, reach) + block, jnp.bfloat16),
            pltpu.VMEM((halves, reach) + block, jnp.bfloat16),
            pltpu.VMEM((halves, reach) + block, jnp.bfloat16),
            pltpu.VMEM((reach,) + block, jnp.bfloat16),
            pltpu.VMEM((reach + 1,) + block, jnp.bfloat16),
            pltpu.VMEM((cores, reach) + block, jnp.bfloat16),
        ]
        + [pltpu.VMEM((count,) + smalls[0].shape, jnp.float32) for count in (2, 2, reach)]
        + [pltpu.VMEM(end, jnp.bfloat16)] * 2
        + [
            dma((halves,)),
            dma((halves, TAIL_PIECES)),
            dma((halves, TAIL_PIECES)),
            dma((halves, TAIL_PIECES)),
            dma((reach, TAIL_PIECES)),
            dma((reach, TAIL_PIECES)),
            dma((reach, TAIL_PIECES)),
            dma((reach + 1, TAIL_PIECES)),
            dma((2, reach, TAIL_PIECES)),
            dma((reach, TAIL_PIECES)),
            dma((reach, TAIL_PIECES)),
            dma((reach, TAIL_PIECES)),
            dma((cores, reach, 4)),
            dma((2 + reach,)),
            dma((2 + reach,)),
            dma,
            dma((2,)),
            dma,
            dma,
        ],
        compiler_params=pltpu.CompilerParams(
            collective_id=7, has_side_effects=True, vmem_limit_bytes=62 * MIB
        ),
        cost_estimate=pl.CostEstimate(
            flops=10**9, bytes_accessed=300 * 10**6, transcendentals=0
        ),
        name="tail",
    )(dense, *smalls, *ends)


GROUP = (EXPERT, TENSOR)
ROWS = (DP, EXPERT)


def by_rows(
    boundary,
    segments,
    expert_ids,
    attn_gain,
    query_weight,
    key_weight,
    value_weight,
    out_weight,
    ffn_gain,
    router_weight,
    gate_weight,
    up_weight,
    down_weight,
):
    args = (
        boundary,
        segments,
        expert_ids,
        attn_gain,
        query_weight,
        key_weight,
        value_weight,
        out_weight,
        ffn_gain,
        router_weight,
        gate_weight,
        up_weight,
        down_weight,
    )
    share_rows = expert_ids.shape[2]
    local = gate_weight.shape[1]
    if (
        share_rows != LEN
        or lax.axis_size(TENSOR) != 2
        or lax.axis_size(SECTION) != 2
        or lax.axis_size(DP) != 2
        or query_weight.shape[2] % (4 * HD)
    ):
        return on_device(*args)
    section = lax.axis_index(SECTION)
    tensor = lax.axis_index(TENSOR)
    group_at = lax.axis_index(EXPERT) * lax.axis_size(TENSOR) + tensor
    micro_count = boundary.shape[1]
    reach = lax.axis_size(EXPERT)
    group = query_weight.shape[2] // key_weight.shape[2]
    own_rows = lax.dynamic_slice_in_dim(boundary[0], tensor * share_rows, share_rows, 1)
    own_seg = lax.dynamic_slice_in_dim(segments, tensor * share_rows, share_rows, 1)
    own_ids = jnp.swapaxes(expert_ids[0], 1, 2)
    gains = (attn_gain, ffn_gain)
    tables = pair_tables(LEN)

    wqkv_part = jnp.concatenate([query_weight[0], key_weight[0], value_weight[0]], axis=1)
    wo_part = out_weight[0]
    wqkv = wo = None
    router_local = jnp.roll(router_weight[0].T, -group_at * local, axis=0)
    wg, wu, wd = gate_weight[0], up_weight[0], down_weight[0]

    def pick(array, index):
        return lax.dynamic_index_in_dim(array, index, 0, keepdims=False)

    arrived = None
    kept = []
    wide = []
    outputs = []
    for tick in range(micro_count + 1):
        micro = jnp.clip(tick - section, 0, micro_count - 1)
        if tick == 0:
            layer_in = own_rows[0]
            h1, xn2 = attn_split(
                boundary[0, 0].reshape(2, share_rows, -1),
                segments[0].reshape(2, share_rows),
                gains,
                wqkv_part,
                wo_part,
                tables,
                group,
            )
        else:
            layer_in = arrived
            h1, xn1, qkv, att, xn2 = attn_forward(
                own_rows[tick] if tick < micro_count else arrived,
                arrived,
                pick(own_seg, micro),
                gains,
                wqkv,
                wo,
                tables,
                group,
                0 if tick == micro_count else -1,
            )
        h2, gates, slots, own_gates, picked, gate_pre, up_pre, *firsts = moe_forward_call(
            reach,
            tick,
            micro_count,
            xn2,
            h1,
            pick(own_ids, micro),
            router_local,
            wg,
            wu,
            wd,
            [
                boundary[0].reshape(micro_count, 2, PIECES, share_rows // PIECES, -1),
                wqkv_part,
                wo_part,
            ],
        )
        outputs.append(h2)
        arrived = shifted(h2, SECTION, 1)
        if tick == 0:
            tops, *before = firsts
            wqkv, wo = both_halves(wqkv_part, wo_part, h2, before)
            xn1, qkv, att = attn_again(own_rows[0], own_seg[0], attn_gain, wqkv, tables, group)
        kept.append((layer_in, h1, xn2, own_gates, qkv, slots, gates, xn1, att))
        wide.append((picked, gate_pre, up_pre))

    arrived = jnp.zeros(own_rows.shape[1:], jnp.bfloat16)
    backs = []
    slotted = []
    for tick in range(micro_count + 1):
        micro = jnp.clip(tick - (1 - section), 0, micro_count - 1)
        ticks = {0: (1, 1), 1: (0, 2), 2: (1, 1)}[tick]
        pairs = list(zip(*(kept[one] for one in ticks)))
        sides = [wide[one] for one in ticks]
        if tick == micro_count:
            pairs[0] = (own_rows[1], own_rows[1])
            pairs.insert(5, (arrived, arrived))
        elif tick == 0:
            pairs.insert(5, (own_rows[0], own_rows[0]))
        else:
            pairs.insert(5, (arrived, own_rows[1]))
        rows, grad_gates, *found = moe_backward_call(
            reach,
            tick,
            micro_count,
            arrived,
            pairs[6],
            pairs[7],
            [side[1] for side in sides],
            [side[2] for side in sides],
            wg,
            wu,
            wd,
            tops,
            ends[0] if tick == micro_count else tops,
            slotted[0] if tick == micro_count else (),
        )
        if tick == micro_count:
            expert_grads = tick_weights([wide[1][0]], *found, rows, before)
            expert_grads = [lax.psum(one, DP) for one in expert_grads]
        grad_in, mid, dqkv, small = attn_backward(
            pairs[:6],
            rows,
            grad_gates.reshape(EXPERTS, LEN),
            pick(own_seg, micro),
            gains,
            router_local,
            wqkv,
            wo,
            tables,
            group,
            {0: 0, micro_count: 1}.get(tick, -1),
        )
        arrived = shifted(grad_in, SECTION, -1)
        backs.append((grad_in, mid, dqkv, small))
        slotted.append(found)
        if tick == 1:
            before = tick_weights(
                [side[0] for side in sides], *found, grad_in
            )
            ends = [ends_exchange(grad_in, outputs[1], before[0])]

    grads_in, mids, dqkvs, smalls = zip(*backs)
    dense = attn_weights([one[7] for one in kept], [one[8] for one in kept], mids, dqkvs)
    width = dense.shape[1]
    dense = dense.reshape(
        2, 2, reach, TAIL_PIECES, width // (2 * reach * TAIL_PIECES), dense.shape[2]
    )
    widths = [one.shape[2] for one in (query_weight, key_weight, value_weight)]
    *dense, small, last_end = tail_call(
        reach, widths, dense, smalls, (grads_in[2], outputs[2])
    )
    ends = jnp.stack([ends[0], last_end])
    return (
        ends.reshape(1, micro_count, 2 * share_rows, -1),
        small[EXPERTS + 1][None],
        *[one.astype(jnp.float32).reshape(1, -1, one.shape[3]) for one in dense],
        small[EXPERTS][None],
        small[:EXPERTS].T[None],
        *[one.astype(jnp.float32)[None] for one in expert_grads],
    )


def solution(mesh):
    placed = (
        P(SECTION, None, (DP, EXPERT), None),
        P(None, (DP, EXPERT)),
        P(SECTION, None, (DP, EXPERT, TENSOR), None),
        P(SECTION, None),
        P(SECTION, None, TENSOR),
        P(SECTION, None, TENSOR),
        P(SECTION, None, TENSOR),
        P(SECTION, TENSOR, None),
        P(SECTION, None),
        P(SECTION, None, None),
        P(SECTION, (EXPERT, TENSOR), None, None),
        P(SECTION, (EXPERT, TENSOR), None, None),
        P(SECTION, (EXPERT, TENSOR), None, None),
    )
    return jax.shard_map(
        by_rows,
        mesh=mesh,
        in_specs=placed,
        out_specs=(
            P(SECTION, None, (DP, EXPERT), None),
            P(SECTION, None),
            P(SECTION, None, TENSOR),
            P(SECTION, None, TENSOR),
            P(SECTION, None, TENSOR),
            P(SECTION, TENSOR, None),
            P(SECTION, None),
            P(SECTION, None, None),
            P(SECTION, (EXPERT, TENSOR), None, None),
            P(SECTION, (EXPERT, TENSOR), None, None),
            P(SECTION, (EXPERT, TENSOR), None, None),
        ),
        check_vma=False,
    )
```

```python
import functools

import jax
import jax.numpy as jnp
from jax import lax
from jax.experimental import pallas as pl
from jax.experimental.pallas import tpu as pltpu
from jax.sharding import PartitionSpec as P

SECTION, DP, EXPERT, TENSOR = "section", "dp", "expert", "tensor"
HD = 64
TOPK = 8
EXPERTS = 32
LEN = 256


EPS = 1e-06
THETA = 10000.0
NEG_BIG = -1e30


def shifted(block, axis, distance):
    devices = range(lax.axis_size(axis))
    route = [(i - distance, i) for i in devices if i - distance in devices]
    return lax.ppermute(block, axis, route)


def rms_scale(values):
    return lax.rsqrt(jnp.mean(values * values, axis=-1, keepdims=True) + EPS)


def norm_back(grad_out, values, scale_col, gain_vec):
    weighted = grad_out * gain_vec
    inner_mean = jnp.mean(weighted * values, axis=-1, keepdims=True)
    grad_values = scale_col * weighted - values * (scale_col * scale_col * scale_col) * inner_mean
    grad_gain = jnp.sum(grad_out * values * scale_col, axis=0)
    return (grad_values, grad_gain)


def rope_tables(row_count, head_width, length):
    position = (jnp.arange(row_count) % length).astype(jnp.float32)
    frequency = THETA ** (-2.0 * jnp.arange(head_width // 2).astype(jnp.float32) / head_width)
    angles = position[:, None] * frequency[None, :]
    return (jnp.cos(angles), jnp.sin(angles))


def rotate(matrix, cosine_table, sine_table, head_width, direction):
    row_count = matrix.shape[0]
    by_head = matrix.reshape(row_count, -1, head_width)
    half_width = head_width // 2
    first_half = by_head[..., :half_width]
    second_half = by_head[..., half_width:]
    cosine = cosine_table[:, None, :]
    sine_val = sine_table[:, None, :] * direction
    turned = jnp.concatenate(
        [
            first_half * cosine - second_half * sine_val,
            second_half * cosine + first_half * sine_val,
        ],
        axis=-1,
    )
    return turned.reshape(row_count, -1)


def slot_count(share_rows):
    return share_rows * 3 // 8


def score_block(query_blk, key_blk, seg_row):
    length = query_blk.shape[0]
    kv_heads = key_blk.shape[1] // HD
    query_heads = query_blk.reshape(length, kv_heads, -1, HD)
    key_heads = key_blk.reshape(length, kv_heads, HD)
    scores = jnp.einsum(
        "qkgd,skd->kgqs", query_heads, key_heads, preferred_element_type=jnp.float32
    ) * HD ** (-0.5)
    position = jnp.arange(length)
    allowed = (position[:, None] >= position[None, :]) & (seg_row[:, None] == seg_row[None, :])
    return (jnp.where(allowed, scores, NEG_BIG), query_heads, key_heads)


def attend_forward(bundle):
    query_blk, key_blk, value_blk, seg_row = bundle
    length = query_blk.shape[0]
    scores, query_heads, key_heads = score_block(query_blk, key_blk, seg_row)
    top_score = jnp.max(scores, axis=-1, keepdims=True)
    exponent = jnp.exp(scores - top_score)
    row_total = jnp.sum(exponent, axis=-1, keepdims=True)
    probability = (exponent / row_total).astype(jnp.bfloat16)
    value_heads = value_blk.reshape(length, key_heads.shape[1], HD)
    mixture = jnp.einsum(
        "kgqs,skd->qkgd", probability, value_heads, preferred_element_type=jnp.float32
    )
    return (mixture.astype(jnp.bfloat16).reshape(length, -1), top_score + jnp.log(row_total))


def attend_backward(bundle):
    query_blk, key_blk, value_blk, seg_row, log_total, grad_mix = bundle
    length = query_blk.shape[0]
    scores, query_heads, key_heads = score_block(query_blk, key_blk, seg_row)
    kv_heads = key_heads.shape[1]
    probability = jnp.exp(scores - log_total)
    prob_low = probability.astype(jnp.bfloat16)
    grad_heads = grad_mix.reshape(length, kv_heads, -1, HD)
    value_heads = value_blk.reshape(length, kv_heads, HD)
    grad_value = jnp.einsum(
        "kgqs,qkgd->skd", prob_low, grad_heads, preferred_element_type=jnp.float32
    )
    grad_prob = jnp.einsum(
        "qkgd,skd->kgqs", grad_heads, value_heads, preferred_element_type=jnp.float32
    )
    centre = jnp.sum(probability * grad_prob, axis=-1, keepdims=True)
    grad_scores = (probability * (grad_prob - centre)).astype(jnp.bfloat16)
    grad_query = jnp.einsum(
        "kgqs,skd->qkgd", grad_scores, key_heads, preferred_element_type=jnp.float32
    ) * HD ** (-0.5)
    grad_key = jnp.einsum(
        "kgqs,qkgd->skd", grad_scores, query_heads, preferred_element_type=jnp.float32
    ) * HD ** (-0.5)
    return (
        grad_query.reshape(length, -1),
        grad_key.reshape(length, -1),
        grad_value.reshape(length, -1),
    )


def attention_forward(hidden_in, seg_rows, params):
    attn_gain, query_weight, key_weight, value_weight = params[:4]
    row_count = hidden_in.shape[0]
    scale_one = rms_scale(hidden_in)
    normed = (hidden_in * scale_one * attn_gain).astype(jnp.bfloat16)
    query_proj = jnp.dot(normed, query_weight, preferred_element_type=jnp.float32)
    key_proj = jnp.dot(normed, key_weight, preferred_element_type=jnp.float32)
    value_rot = jnp.dot(normed, value_weight, preferred_element_type=jnp.float32).astype(
        jnp.bfloat16
    )
    cosine_table, sine_table = rope_tables(row_count, HD, LEN)
    query_rot = rotate(query_proj, cosine_table, sine_table, HD, 1.0).astype(jnp.bfloat16)
    key_rot = rotate(key_proj, cosine_table, sine_table, HD, 1.0).astype(jnp.bfloat16)
    seq_count = row_count // LEN
    mixed, log_total = lax.map(
        attend_forward,
        (
            query_rot.reshape(seq_count, LEN, -1),
            key_rot.reshape(seq_count, LEN, -1),
            value_rot.reshape(seq_count, LEN, -1),
            seg_rows.reshape(seq_count, LEN),
        ),
    )
    attended = mixed.reshape(row_count, -1)
    return (
        scale_one,
        normed,
        query_rot,
        key_rot,
        value_rot,
        attended,
        log_total,
        cosine_table,
        sine_table,
    )


def expert_plan(route_rows, capacity):
    pair_ids = route_rows.reshape(-1)
    onehot = (pair_ids[:, None] == jnp.arange(EXPERTS, dtype=jnp.int32)[None, :]).astype(jnp.int32)
    earlier = jnp.cumsum(onehot, axis=0) - onehot
    slot_pos = jnp.sum(earlier * onehot, axis=1)
    target = pair_ids * capacity + slot_pos
    source = (
        jnp.zeros((EXPERTS * capacity,), jnp.int32)
        .at[target]
        .set(jnp.arange(pair_ids.shape[0], dtype=jnp.int32) + 1)
    )
    return (target.reshape(route_rows.shape), source)


def send_out(buffer):
    return lax.all_to_all(buffer, (EXPERT, TENSOR), split_axis=0, concat_axis=1, tiled=True)


def send_home(produced):
    return lax.all_to_all(produced, (EXPERT, TENSOR), split_axis=1, concat_axis=0, tiled=True)


def moe_forward(middle_share, route_rows, params, outward, homeward):
    ffn_gain, router_weight, gate_weight, up_weight, down_weight = params[5:]
    share_rows = middle_share.shape[0]
    capacity = slot_count(share_rows)
    scale_two = rms_scale(middle_share)
    normed_two = (middle_share * scale_two * ffn_gain).astype(jnp.bfloat16)
    logits = jnp.dot(normed_two, router_weight, preferred_element_type=jnp.float32)
    member = route_rows[:, :, None] == jnp.arange(EXPERTS, dtype=jnp.int32)[None, None, :]
    chosen = jnp.sum(jnp.where(member, logits[:, None, :], 0.0), axis=2)
    exponent = jnp.exp(chosen - jnp.max(chosen, axis=1, keepdims=True))
    gates = exponent / jnp.sum(exponent, axis=1, keepdims=True)
    target, source = expert_plan(route_rows, capacity)
    filled = (source > 0)[:, None]
    gathered = normed_two[jnp.maximum(source - 1, 0) // TOPK]
    buffer = jnp.where(filled, gathered, jnp.zeros_like(gathered)).reshape(EXPERTS, capacity, -1)
    received = outward(buffer)
    gate_pre = jnp.einsum("erd,edf->erf", received, gate_weight, preferred_element_type=jnp.float32)
    up_pre = jnp.einsum("erd,edf->erf", received, up_weight, preferred_element_type=jnp.float32)
    hidden = (jax.nn.silu(gate_pre) * up_pre).astype(jnp.bfloat16)
    produced = jnp.einsum(
        "erf,efd->erd", hidden, down_weight, preferred_element_type=jnp.float32
    ).astype(jnp.bfloat16)
    returned = homeward(produced)
    picked = returned.reshape(EXPERTS * capacity, -1)[target]
    addition = jnp.einsum("tk,tkd->td", gates, picked, preferred_element_type=jnp.float32)
    return (
        scale_two,
        normed_two,
        member,
        gates,
        target,
        source,
        received,
        gate_pre,
        up_pre,
        hidden,
        picked,
        addition,
    )


def section_forward(layer_in, seg_rows, route_rows, params, share_start, share_rows):
    hidden_in = layer_in.astype(jnp.float32)
    attn_parts = attention_forward(hidden_in, seg_rows, params)
    partial_sum = jnp.dot(attn_parts[5], params[4], preferred_element_type=jnp.float32)
    own_share = lax.dynamic_slice_in_dim(hidden_in, share_start, share_rows, 0)
    summed = lax.psum(partial_sum.astype(jnp.bfloat16), TENSOR).astype(jnp.float32)
    branch = lax.dynamic_slice_in_dim(summed, share_start, share_rows, 0)
    middle_share = own_share + branch
    moe_parts = moe_forward(middle_share, route_rows, params, send_out, send_home)
    block_share = middle_share + moe_parts[-1]
    block_full = lax.all_gather(
        block_share.astype(jnp.bfloat16), TENSOR, axis=0, tiled=True
    ).astype(block_share.dtype)
    return (block_full, middle_share, moe_parts)


def section_backward(layer_in, middle_share, grad_top, seg_rows, params, share_start, kept_parts):
    (
        attn_gain,
        query_weight,
        key_weight,
        value_weight,
        out_weight,
        ffn_gain,
        router_weight,
        gate_weight,
        up_weight,
        down_weight,
    ) = params
    hidden_in = layer_in.astype(jnp.float32)
    row_count = hidden_in.shape[0]
    share_rows = middle_share.shape[0]
    capacity = slot_count(share_rows)
    (
        scale_one,
        normed,
        query_rot,
        key_rot,
        value_rot,
        attended,
        log_total,
        cosine_table,
        sine_table,
    ) = attention_forward(hidden_in, seg_rows, params)
    (
        scale_two,
        normed_two,
        member,
        gates,
        target,
        source,
        received,
        gate_pre,
        up_pre,
        hidden,
        picked,
        addition,
    ) = kept_parts
    grad_share = lax.dynamic_slice_in_dim(grad_top, share_start, share_rows, 0)
    grad_picked = (gates[:, :, None] * grad_share[:, None, :]).astype(jnp.bfloat16)
    grad_gates = jnp.einsum("td,tkd->tk", grad_share, picked, preferred_element_type=jnp.float32)
    grad_chosen = gates * (grad_gates - jnp.sum(gates * grad_gates, axis=1, keepdims=True))
    grad_logits = jnp.sum(jnp.where(member, grad_chosen[:, :, None], 0.0), axis=1).astype(
        jnp.bfloat16
    )
    router_grad = jnp.einsum(
        "td,te->de", normed_two, grad_logits, preferred_element_type=jnp.float32
    )
    grad_normed = jnp.einsum(
        "te,de->td", grad_logits, router_weight, preferred_element_type=jnp.float32
    )
    filled = (source > 0)[:, None]
    flat_grad = grad_picked.reshape(share_rows * TOPK, -1)
    gathered = flat_grad[jnp.maximum(source - 1, 0)]
    grad_buffer = jnp.where(filled, gathered, jnp.zeros_like(gathered)).reshape(
        EXPERTS, capacity, -1
    )
    sent = lax.all_to_all(
        grad_buffer, (EXPERT, TENSOR), split_axis=0, concat_axis=1, tiled=True
    )
    grad_hidden = jnp.einsum("erd,efd->erf", sent, down_weight, preferred_element_type=jnp.float32)
    sigmoid_gate = jax.nn.sigmoid(gate_pre)
    grad_gate = (
        grad_hidden * up_pre * sigmoid_gate * (1.0 + gate_pre * (1.0 - sigmoid_gate))
    ).astype(jnp.bfloat16)
    grad_up = (grad_hidden * gate_pre * sigmoid_gate).astype(jnp.bfloat16)
    down_grad = jnp.einsum("erf,erd->efd", hidden, sent, preferred_element_type=jnp.float32)
    gate_grad = jnp.einsum("erd,erf->edf", received, grad_gate, preferred_element_type=jnp.float32)
    up_grad = jnp.einsum("erd,erf->edf", received, grad_up, preferred_element_type=jnp.float32)
    grad_rows = jnp.einsum(
        "erf,edf->erd", grad_gate, gate_weight, preferred_element_type=jnp.float32
    )
    grad_rows = (
        grad_rows
        + jnp.einsum("erf,edf->erd", grad_up, up_weight, preferred_element_type=jnp.float32)
    ).astype(jnp.bfloat16)
    back_rows = lax.all_to_all(
        grad_rows, (EXPERT, TENSOR), split_axis=1, concat_axis=0, tiled=True
    )
    grad_normed = grad_normed + jnp.sum(
        back_rows.reshape(EXPERTS * capacity, -1)[target].astype(jnp.float32), axis=1
    )
    grad_middle, ffn_gain_grad = norm_back(grad_normed, middle_share, scale_two, ffn_gain)
    grad_middle = grad_middle + grad_share
    grad_mid_full = lax.all_gather(
        grad_middle.astype(jnp.bfloat16), TENSOR, axis=0, tiled=True
    ).astype(grad_middle.dtype)
    grad_mid_low = grad_mid_full.astype(jnp.bfloat16)
    out_grad = jnp.einsum("rh,rd->hd", attended, grad_mid_low, preferred_element_type=jnp.float32)
    grad_attended = jnp.einsum(
        "rd,hd->rh", grad_mid_low, out_weight, preferred_element_type=jnp.float32
    ).astype(jnp.bfloat16)
    seq_count = row_count // LEN
    grad_query, grad_key, grad_value = lax.map(
        attend_backward,
        (
            query_rot.reshape(seq_count, LEN, -1),
            key_rot.reshape(seq_count, LEN, -1),
            value_rot.reshape(seq_count, LEN, -1),
            seg_rows.reshape(seq_count, LEN),
            log_total,
            grad_attended.reshape(seq_count, LEN, -1),
        ),
    )
    grad_query = rotate(
        grad_query.reshape(row_count, -1), cosine_table, sine_table, HD, -1.0
    ).astype(jnp.bfloat16)
    grad_key = rotate(grad_key.reshape(row_count, -1), cosine_table, sine_table, HD, -1.0).astype(
        jnp.bfloat16
    )
    grad_value = grad_value.reshape(row_count, -1).astype(jnp.bfloat16)
    query_grad = jnp.einsum("rd,rh->dh", normed, grad_query, preferred_element_type=jnp.float32)
    key_grad = jnp.einsum("rd,rh->dh", normed, grad_key, preferred_element_type=jnp.float32)
    value_grad = jnp.einsum("rd,rh->dh", normed, grad_value, preferred_element_type=jnp.float32)
    grad_normed_one = jnp.einsum(
        "rh,dh->rd", grad_query, query_weight, preferred_element_type=jnp.float32
    )
    grad_normed_one = grad_normed_one + jnp.einsum(
        "rh,dh->rd", grad_key, key_weight, preferred_element_type=jnp.float32
    )
    grad_normed_one = grad_normed_one + jnp.einsum(
        "rh,dh->rd", grad_value, value_weight, preferred_element_type=jnp.float32
    )
    grad_normed_one = lax.psum(grad_normed_one.astype(jnp.bfloat16), TENSOR).astype(jnp.float32)
    grad_input, attn_gain_grad = norm_back(grad_normed_one, hidden_in, scale_one, attn_gain)
    grad_input = grad_input + grad_mid_full
    return (
        grad_input,
        (
            attn_gain_grad,
            query_grad,
            key_grad,
            value_grad,
            out_grad,
            ffn_gain_grad,
            router_grad,
            gate_grad,
            up_grad,
            down_grad,
        ),
    )


def stack_zeros(piece_arr, count):
    return jnp.zeros((count,) + piece_arr.shape, piece_arr.dtype)


def on_device(
    boundary,
    segments,
    expert_ids,
    attn_gain,
    query_weight,
    key_weight,
    value_weight,
    out_weight,
    ffn_gain,
    router_weight,
    gate_weight,
    up_weight,
    down_weight,
):
    params = tuple(
        (
            array_in[0]
            for array_in in (
                attn_gain,
                query_weight,
                key_weight,
                value_weight,
                out_weight,
                ffn_gain,
                router_weight,
                gate_weight,
                up_weight,
                down_weight,
            )
        )
    )
    section_index = lax.axis_index(SECTION)
    tensor_index = lax.axis_index(TENSOR)
    own_rows = boundary[0]
    micro_count = own_rows.shape[0]
    row_count = own_rows.shape[1]
    model_width = own_rows.shape[2]
    share_rows = expert_ids.shape[2]
    share_start = tensor_index * share_rows
    routes = expert_ids[0]
    kept_inputs = jnp.zeros((micro_count, row_count, model_width), jnp.bfloat16)
    kept_middle = jnp.zeros((micro_count, share_rows, model_width), jnp.float32)
    block_outputs = jnp.zeros((micro_count, row_count, model_width), jnp.bfloat16)
    arrived = jnp.zeros((row_count, model_width), jnp.bfloat16)
    kept_moe = None
    for tick_idx in range(micro_count + 1):
        micro_idx = tick_idx - section_index
        is_valid = (micro_idx >= 0) & (micro_idx < micro_count)
        slot_idx = jnp.clip(micro_idx, 0, micro_count - 1)
        layer_in = jnp.where(section_index == 0, own_rows[min(tick_idx, micro_count - 1)], arrived)
        seg_rows = lax.dynamic_index_in_dim(segments, slot_idx, 0, keepdims=False)
        route_rows = lax.dynamic_index_in_dim(routes, slot_idx, 0, keepdims=False)
        block_full, middle_share, moe_parts = section_forward(
            layer_in, seg_rows, route_rows, params, share_start, share_rows
        )
        block_low = block_full.astype(jnp.bfloat16)
        kept_inputs = jnp.where(
            is_valid,
            lax.dynamic_update_index_in_dim(kept_inputs, layer_in, slot_idx, 0),
            kept_inputs,
        )
        kept_middle = jnp.where(
            is_valid,
            lax.dynamic_update_index_in_dim(kept_middle, middle_share, slot_idx, 0),
            kept_middle,
        )
        block_outputs = jnp.where(
            is_valid,
            lax.dynamic_update_index_in_dim(block_outputs, block_low, slot_idx, 0),
            block_outputs,
        )
        if kept_moe is None:
            kept_moe = tuple((stack_zeros(piece_arr, micro_count) for piece_arr in moe_parts))
        kept_moe = tuple(
            (
                jnp.where(
                    is_valid,
                    lax.dynamic_update_index_in_dim(stack_arr, piece_arr, slot_idx, 0),
                    stack_arr,
                )
                for stack_arr, piece_arr in zip(kept_moe, moe_parts)
            )
        )
        arrived = shifted(block_low, SECTION, 1)
    grads = tuple((jnp.zeros(param_arr.shape, jnp.float32) for param_arr in params))
    input_grads = jnp.zeros((micro_count, row_count, model_width), jnp.bfloat16)
    grad_arrived = jnp.zeros((row_count, model_width), jnp.bfloat16)
    for tick_idx in range(micro_count + 1):
        micro_idx = tick_idx - (1 - section_index)
        is_valid = (micro_idx >= 0) & (micro_idx < micro_count)
        slot_idx = jnp.clip(micro_idx, 0, micro_count - 1)
        grad_top = jnp.where(
            section_index == 1, own_rows[min(tick_idx, micro_count - 1)], grad_arrived
        ).astype(jnp.float32)
        layer_in = lax.dynamic_index_in_dim(kept_inputs, slot_idx, 0, keepdims=False)
        middle_share = lax.dynamic_index_in_dim(kept_middle, slot_idx, 0, keepdims=False)
        seg_rows = lax.dynamic_index_in_dim(segments, slot_idx, 0, keepdims=False)
        route_rows = lax.dynamic_index_in_dim(routes, slot_idx, 0, keepdims=False)
        tick_moe = tuple(
            (
                lax.dynamic_index_in_dim(stack_arr, slot_idx, 0, keepdims=False)
                for stack_arr in kept_moe
            )
        )
        grad_input, tick_grads = section_backward(
            layer_in, middle_share, grad_top, seg_rows, params, share_start, tick_moe
        )
        valid_weight = is_valid.astype(jnp.float32)
        grads = tuple(
            (
                total_grad + valid_weight * tick_part
                for total_grad, tick_part in zip(grads, tick_grads)
            )
        )
        grad_low = grad_input.astype(jnp.bfloat16)
        input_grads = jnp.where(
            is_valid,
            lax.dynamic_update_index_in_dim(input_grads, grad_low, slot_idx, 0),
            input_grads,
        )
        grad_arrived = shifted(grad_low, SECTION, -1)
    dense = (
        lax.psum(grads[0].astype(jnp.bfloat16), (DP, EXPERT)).astype(jnp.float32),
        lax.psum(grads[1].astype(jnp.bfloat16), (DP, EXPERT)).astype(jnp.float32),
        lax.psum(grads[2].astype(jnp.bfloat16), (DP, EXPERT)).astype(jnp.float32),
        lax.psum(grads[3].astype(jnp.bfloat16), (DP, EXPERT)).astype(jnp.float32),
        lax.psum(grads[4].astype(jnp.bfloat16), (DP, EXPERT)).astype(jnp.float32),
    )
    shared = lax.psum((grads[5], grads[6]), (DP, EXPERT, TENSOR))
    expert_sums = (
        lax.psum(grads[7].astype(jnp.bfloat16), DP).astype(jnp.float32),
        lax.psum(grads[8].astype(jnp.bfloat16), DP).astype(jnp.float32),
        lax.psum(grads[9].astype(jnp.bfloat16), DP).astype(jnp.float32),
    )
    ends_out = jnp.where(section_index == 0, input_grads, block_outputs)[None]
    return (
        ends_out,
        dense[0][None],
        dense[1][None],
        dense[2][None],
        dense[3][None],
        dense[4][None],
        shared[0][None],
        shared[1][None],
        expert_sums[0][None],
        expert_sums[1][None],
        expert_sums[2][None],
    )


MIB = 1024 * 1024
NT = (((1,), (1,)), ((), ()))
TN = (((0,), (0,)), ((), ()))


def dot(left, right, dims=None):
    if dims is None:
        return jnp.dot(left, right, preferred_element_type=jnp.float32)
    return lax.dot_general(left, right, dims, preferred_element_type=jnp.float32)


def lane_grid(rows):
    return lax.broadcasted_iota(jnp.int32, (rows, 2 * HD), 1)


def turn_pair(slab, cosine, sine):
    low_half = (lane_grid(slab.shape[0]) % HD) < HD // 2
    partner = jnp.where(
        low_half, pltpu.roll(slab, 2 * HD - HD // 2, 1), pltpu.roll(slab, HD // 2, 1)
    )
    return slab * cosine + partner * sine


def pair_tables(length):
    cosine, sine = rope_tables(length, HD, length)
    return (
        jnp.concatenate([cosine] * 4, axis=1),
        jnp.concatenate([-sine, sine, -sine, sine], axis=1),
    )


def aligned_head(slabs, head, side, scale):
    slab = slabs[head // 2]
    if head % 2 != side:
        slab = pltpu.roll(slab, HD, 1)
    keep = (lane_grid(slab.shape[0]) // HD) == side
    return jnp.where(keep, slab * scale, 0.0).astype(jnp.bfloat16)


def one_side(slab, side):
    return jnp.where((lane_grid(slab.shape[0]) // HD) == side, slab, jnp.zeros_like(slab))


def slabs_of(matrix, start, count):
    return [matrix[:, start + 2 * HD * i : start + 2 * HD * (i + 1)] for i in range(count)]


def attend_part(group, rows, weights, tables, allowed):
    width = weights.shape[1]
    query_width = width * group // (group + 2)
    key_width = (width - query_width) // 2
    cosine, sine = tables
    projected = dot(rows, weights)
    query = [
        turn_pair(slab, cosine, sine) for slab in slabs_of(projected, 0, query_width // (2 * HD))
    ]
    key = [
        turn_pair(slab, cosine, sine).astype(jnp.bfloat16)
        for slab in slabs_of(projected, query_width, key_width // (2 * HD))
    ]
    value = [
        slab.astype(jnp.bfloat16)
        for slab in slabs_of(projected, query_width + key_width, key_width // (2 * HD))
    ]
    turned = jnp.concatenate([slab.astype(jnp.bfloat16) for slab in query] + key + value, axis=1)
    query = [slab.astype(jnp.bfloat16).astype(jnp.float32) for slab in query]
    mixed = [None] * len(query)
    for kv_head in range(key_width // HD):
        side = kv_head % 2
        key_slab = key[kv_head // 2]
        value_side = one_side(value[kv_head // 2], side)
        for head in range(group * kv_head, group * (kv_head + 1)):
            scores = dot(aligned_head(query, head, side, HD**-0.5), key_slab, NT)
            scores = jnp.where(allowed, scores, NEG_BIG)
            exponent = jnp.exp(scores - jnp.max(scores, axis=1, keepdims=True))
            probability = exponent / jnp.sum(exponent, axis=1, keepdims=True)
            part = dot(probability.astype(jnp.bfloat16), value_side)
            if head % 2 != side:
                part = pltpu.roll(part, HD, 1)
            mixed[head // 2] = part if head % 2 == 0 else mixed[head // 2] + part
    return turned, jnp.concatenate([part.astype(jnp.bfloat16) for part in mixed], axis=1)


def allowed_pairs(seg_col, seg_row):
    length = seg_row.shape[1]
    row = lax.broadcasted_iota(jnp.int32, (length, length), 0)
    column = lax.broadcasted_iota(jnp.int32, (length, length), 1)
    return (row >= column) & (seg_col == seg_row)


def of_section(first, second):
    return jnp.where(lax.axis_index(SECTION) == 0, first[...], second[...])


def start_of_section(first, second, to, sem):
    @pl.when(lax.axis_index(SECTION) == 0)
    def _():
        pltpu.make_async_copy(first, to, sem).start()

    @pl.when(lax.axis_index(SECTION) != 0)
    def _():
        pltpu.make_async_copy(second, to, sem).start()


def attn_forward_kernel(
    group,
    skipped,
    x_first,
    x_second,
    gain_one_ref,
    wqkv_hbm,
    wo_hbm,
    cos_ref,
    sin_ref,
    seg_col_ref,
    seg_row_ref,
    gain_two_ref,
    h1_ref,
    xn1_ref,
    qkv_ref,
    att_ref,
    xn2_ref,
    x_ref,
    wqkv_ref,
    wo_ref,
    x_sem,
    weight_sem,
):
    @pl.when(lax.axis_index(SECTION) != skipped)
    def _():
        parts = wqkv_ref.shape[0]

        def weight_copies(half):
            return [
                pltpu.make_async_copy(hbm.at[half], ref.at[half], weight_sem.at[i, half])
                for i, (hbm, ref) in enumerate(((wqkv_hbm, wqkv_ref), (wo_hbm, wo_ref)))
            ]

        start_of_section(x_first, x_second, x_ref, x_sem)
        for copy in weight_copies(0):
            copy.start()
        pltpu.make_async_copy(x_first, x_ref, x_sem).wait()
        rows = x_ref[...].astype(jnp.float32)
        xn1_ref[...] = (rows * rms_scale(rows) * gain_one_ref[...]).astype(jnp.bfloat16)
        h1_ref[...] = rows

        def one(half, carry):
            for copy in weight_copies(half):
                copy.wait()

            @pl.when(half + 1 < parts)
            def _():
                for copy in weight_copies(half + 1):
                    copy.start()

            turned, attended = attend_part(
                group,
                xn1_ref[...],
                wqkv_ref[half],
                (cos_ref[...], sin_ref[...]),
                allowed_pairs(seg_col_ref[...], seg_row_ref[...]),
            )
            qkv_ref[half] = turned
            att_ref[half] = attended
            h1_ref[...] += dot(attended, wo_ref[half])
            return carry

        lax.fori_loop(0, parts, one, 0)
        middle = h1_ref[...]
        xn2_ref[...] = (middle * rms_scale(middle) * gain_two_ref[...]).astype(jnp.bfloat16)


def attn_forward(first, second, seg, gains, wqkv, wo, tables, group, skipped):
    length, width = first.shape
    parts, _, qkv_width = wqkv.shape
    att_width = wo.shape[1]
    vmem = pl.BlockSpec(memory_space=pltpu.VMEM)
    anywhere = pl.BlockSpec(memory_space=pl.ANY)
    return pl.pallas_call(
        functools.partial(attn_forward_kernel, group, skipped),
        in_specs=[anywhere] * 2 + [vmem] + [anywhere] * 2 + [vmem] * 5,
        out_specs=[vmem] * 5,
        out_shape=[
            jax.ShapeDtypeStruct((length, width), jnp.float32),
            jax.ShapeDtypeStruct((length, width), jnp.bfloat16),
            jax.ShapeDtypeStruct((parts, length, qkv_width), jnp.bfloat16),
            jax.ShapeDtypeStruct((parts, length, att_width), jnp.bfloat16),
            jax.ShapeDtypeStruct((length, width), jnp.bfloat16),
        ],
        scratch_shapes=[
            pltpu.VMEM((length, width), jnp.bfloat16),
            pltpu.VMEM(wqkv.shape, wqkv.dtype),
            pltpu.VMEM(wo.shape, wo.dtype),
            pltpu.SemaphoreType.DMA,
            pltpu.SemaphoreType.DMA((2, parts)),
        ],
        compiler_params=pltpu.CompilerParams(vmem_limit_bytes=62 * MIB),
        cost_estimate=pl.CostEstimate(
            flops=4 * 10**9, bytes_accessed=20 * 10**6, transcendentals=2 * 10**6
        ),
        name="attn_forward",
    )(first, second, gains[0], wqkv, wo, *tables, seg[:, None], seg[None, :], gains[1])


def attn_again_kernel(
    group,
    x_ref,
    gain_ref,
    wqkv_hbm,
    cos_ref,
    sin_ref,
    seg_col_ref,
    seg_row_ref,
    xn1_ref,
    qkv_ref,
    att_ref,
    wqkv_ref,
    sem,
):
    @pl.when(lax.axis_index(SECTION) == 0)
    def _():
        parts = wqkv_ref.shape[0]

        def copy(half):
            return pltpu.make_async_copy(wqkv_hbm.at[half], wqkv_ref.at[half], sem.at[half])

        for half in range(parts):
            copy(half).start()
        rows = x_ref[...].astype(jnp.float32)
        xn1_ref[...] = (rows * rms_scale(rows) * gain_ref[...]).astype(jnp.bfloat16)

        def one(half, carry):
            copy(half).wait()
            qkv_ref[half], att_ref[half] = attend_part(
                group,
                xn1_ref[...],
                wqkv_ref[half],
                (cos_ref[...], sin_ref[...]),
                allowed_pairs(seg_col_ref[...], seg_row_ref[...]),
            )
            return carry

        lax.fori_loop(0, parts, one, 0)


def attn_again(layer_in, seg, gain, wqkv, tables, group):
    length, width = layer_in.shape
    parts, _, qkv_width = wqkv.shape
    vmem = pl.BlockSpec(memory_space=pltpu.VMEM)
    return pl.pallas_call(
        functools.partial(attn_again_kernel, group),
        in_specs=[vmem] * 2 + [pl.BlockSpec(memory_space=pl.ANY)] + [vmem] * 4,
        out_specs=[vmem] * 3,
        out_shape=[
            jax.ShapeDtypeStruct((length, width), jnp.bfloat16),
            jax.ShapeDtypeStruct((parts, length, qkv_width), jnp.bfloat16),
            jax.ShapeDtypeStruct((parts, length, width // parts), jnp.bfloat16),
        ],
        scratch_shapes=[
            pltpu.VMEM(wqkv.shape, wqkv.dtype),
            pltpu.SemaphoreType.DMA((parts,)),
        ],
        compiler_params=pltpu.CompilerParams(vmem_limit_bytes=62 * MIB),
        cost_estimate=pl.CostEstimate(
            flops=3 * 10**9, bytes_accessed=12 * 10**6, transcendentals=2 * 10**6
        ),
        name="attn_again",
    )(layer_in, gain, wqkv, tables[0], tables[1], seg[:, None], seg[None, :])


def attn_split_kernel(
    group,
    x_ref,
    gain_one_ref,
    wqkv_ref,
    wo_ref,
    cos_ref,
    sin_ref,
    seg_col_ref,
    seg_row_ref,
    gain_two_ref,
    h1_ref,
    xn2_ref,
    part,
    arrived,
    send_sem,
    recv_sem,
):
    x = lax.axis_index(TENSOR)
    aside = {TENSOR: 1 - x}

    @pl.when(lax.axis_index(SECTION) == 0)
    def _():
        barrier = pltpu.get_barrier_semaphore()
        pl.semaphore_signal(barrier, inc=1, device_id=aside, device_id_type=pl.DeviceIdType.MESH)

        def one(i, carry):
            at = jnp.where(i == 0, 1 - x, x)
            rows = x_ref[at].astype(jnp.float32)
            normed = (rows * rms_scale(rows) * gain_one_ref[...]).astype(jnp.bfloat16)
            _, attended = attend_part(
                group,
                normed,
                wqkv_ref[...],
                (cos_ref[...], sin_ref[...]),
                allowed_pairs(seg_col_ref[at], seg_row_ref[at]),
            )
            branch = dot(attended, wo_ref[...])

            @pl.when(i == 0)
            def _():
                part[...] = branch.astype(jnp.bfloat16)
                pl.semaphore_wait(barrier, 1)
                copy().start()

            @pl.when(i == 1)
            def _():
                h1_ref[...] = rows + branch

            return carry

        def copy():
            return pltpu.make_async_remote_copy(
                src_ref=part,
                dst_ref=arrived,
                send_sem=send_sem,
                recv_sem=recv_sem,
                device_id=aside,
                device_id_type=pl.DeviceIdType.MESH,
            )

        lax.fori_loop(0, 2, one, 0)
        copy().wait()
        middle = h1_ref[...] + arrived[...].astype(jnp.float32)
        h1_ref[...] = middle
        xn2_ref[...] = (middle * rms_scale(middle) * gain_two_ref[...]).astype(jnp.bfloat16)


def attn_split(rows, seg, gains, wqkv, wo, tables, group):
    _, length, width = rows.shape
    vmem = pl.BlockSpec(memory_space=pltpu.VMEM)
    return pl.pallas_call(
        functools.partial(attn_split_kernel, group),
        in_specs=[vmem] * 9,
        out_specs=[vmem] * 2,
        out_shape=[
            jax.ShapeDtypeStruct((length, width), jnp.float32),
            jax.ShapeDtypeStruct((length, width), jnp.bfloat16),
        ],
        scratch_shapes=[
            pltpu.VMEM((length, width), jnp.bfloat16),
            pltpu.VMEM((length, width), jnp.bfloat16),
            pltpu.SemaphoreType.DMA,
            pltpu.SemaphoreType.DMA,
        ],
        compiler_params=pltpu.CompilerParams(
            collective_id=8, has_side_effects=True, vmem_limit_bytes=48 * MIB
        ),
        cost_estimate=pl.CostEstimate(
            flops=4 * 10**9, bytes_accessed=20 * 10**6, transcendentals=2 * 10**6
        ),
        name="attn_split",
    )(
        rows,
        gains[0],
        wqkv,
        wo,
        tables[0],
        tables[1],
        seg[:, :, None],
        seg[:, None, :],
        gains[1],
    )


def both_halves_kernel(
    chunks,
    wqkv,
    wo,
    after,
    wqkv_before,
    wo_before,
    wqkv_all,
    wo_all,
    wqkv_held,
    wo_held,
    own_sem,
    out_sem,
    x_send,
    x_recv,
    core_send,
    core_recv,
):
    del after, wqkv_before, wo_before
    x = lax.axis_index(TENSOR)
    core = lax.axis_index(DP)
    aside, partner = {TENSOR: 1 - x}, {DP: 1 - core}
    pairs = ((wqkv, wqkv_held, wqkv_all), (wo, wo_held, wo_all))

    def span(i, of_core, chunk):
        rows = pairs[i][0].shape[0] // (2 * chunks)
        return pl.ds((of_core * chunks + chunk) * rows, rows)

    def own_copy(i, of_core, chunk):
        shard, held, _ = pairs[i]
        at = span(i, of_core, chunk)
        return pltpu.make_async_copy(shard.at[at], held.at[x, at], own_sem.at[i, of_core, chunk])

    def out_copy(i, half):
        _, held, out = pairs[i]
        return pltpu.make_async_copy(held.at[half], out.at[half], out_sem.at[i, half])

    def x_copy(i, chunk, half):
        _, held, _ = pairs[i]
        at = held.at[half, span(i, core, chunk)]
        return pltpu.make_async_remote_copy(
            src_ref=at,
            dst_ref=at,
            send_sem=x_send.at[i, chunk],
            recv_sem=x_recv.at[i, chunk],
            device_id=aside,
            device_id_type=pl.DeviceIdType.MESH,
        )

    def core_copy(i, chunk, of_core):
        _, held, _ = pairs[i]
        at = held.at[1 - x, span(i, of_core, chunk)]
        return pltpu.make_async_remote_copy(
            src_ref=at,
            dst_ref=at,
            send_sem=core_send.at[i, chunk],
            recv_sem=core_recv.at[i, chunk],
            device_id=partner,
            device_id_type=pl.DeviceIdType.MESH,
        )

    steps = [(i, chunk) for i in range(2) for chunk in range(chunks)]

    @pl.when(lax.axis_index(SECTION) == 0)
    def _():
        for of_core in (core, 1 - core):
            for i, chunk in steps:
                own_copy(i, of_core, chunk).start()
        barrier = pltpu.get_barrier_semaphore()
        for other in (aside, partner):
            pl.semaphore_signal(barrier, inc=1, device_id=other, device_id_type=pl.DeviceIdType.MESH)
        pl.semaphore_wait(barrier, 2)
        for i, chunk in steps:
            own_copy(i, core, chunk).wait()
            x_copy(i, chunk, x).start()
        for i, chunk in steps:
            own_copy(i, 1 - core, chunk).wait()
        for i in range(2):
            out_copy(i, x).start()
        for i, chunk in steps:
            x_copy(i, chunk, 1 - x).wait_recv()
            core_copy(i, chunk, core).start()
        for i in range(2):
            for chunk in range(chunks):
                core_copy(i, chunk, 1 - core).wait_recv()
            out_copy(i, 1 - x).start()
        for i, chunk in steps:
            x_copy(i, chunk, x).wait_send()
            core_copy(i, chunk, core).wait_send()
        for i in range(2):
            for half in range(2):
                out_copy(i, half).wait()


def both_halves(wqkv, wo, after, before, chunks=4):
    anywhere = pl.BlockSpec(memory_space=pl.ANY)
    dma = pltpu.SemaphoreType.DMA
    return pl.pallas_call(
        functools.partial(both_halves_kernel, chunks),
        in_specs=[anywhere] * 5,
        out_specs=[anywhere] * 2,
        input_output_aliases={3: 0, 4: 1},
        out_shape=[
            jax.ShapeDtypeStruct((2,) + wqkv.shape, wqkv.dtype),
            jax.ShapeDtypeStruct((2,) + wo.shape, wo.dtype),
        ],
        scratch_shapes=[
            pltpu.VMEM((2,) + wqkv.shape, wqkv.dtype),
            pltpu.VMEM((2,) + wo.shape, wo.dtype),
            dma((2, 2, chunks)),
            dma((2, 2)),
        ]
        + [dma((2, chunks))] * 4,
        compiler_params=pltpu.CompilerParams(
            collective_id=9, has_side_effects=True, vmem_limit_bytes=62 * MIB
        ),
        cost_estimate=pl.CostEstimate(flops=0, bytes_accessed=30 * 10**6, transcendentals=0),
        name="both_halves",
    )(wqkv, wo, after, *before)


def attn_backward_kernel(group, skipped, *refs):
    @pl.when(lax.axis_index(SECTION) != skipped)
    def _():
        pairs = [refs[2 * i : 2 * i + 2] for i in range(6)]
        (
            wqkv_hbm,
            wo_hbm,
            rows_ref,
            grad_gates_ref,
            router_ref,
            gain_one_ref,
            gain_two_ref,
            cos_ref,
            sin_ref,
            seg_col_ref,
            seg_row_ref,
            grad_in_ref,
            mid_ref,
            dqkv_ref,
            small_ref,
            x_ref,
            h1_ref,
            xn2_ref,
            gates_ref,
            qkv_ref,
            top_ref,
            wqkv_ref,
            wo_ref,
            middle_acc,
            normed_acc,
            taken_sem,
            weight_sem,
        ) = refs[12:]
        taken = (x_ref, h1_ref, xn2_ref, gates_ref, qkv_ref, top_ref)
        experts = grad_gates_ref.shape[0]
        parts = wqkv_ref.shape[0]

        def weight_copies(half):
            return [
                pltpu.make_async_copy(hbm.at[half], ref.at[half], weight_sem.at[i, half])
                for i, (hbm, ref) in enumerate(((wqkv_hbm, wqkv_ref), (wo_hbm, wo_ref)))
            ]

        for i in (3, 2, 1, 5, 4, 0):
            start_of_section(*pairs[i], taken[i], taken_sem.at[i])

        def arrived(i):
            pltpu.make_async_copy(pairs[i][0], taken[i], taken_sem.at[i]).wait()
            return taken[i]

        gates = arrived(3)[...]
        grad_gates = grad_gates_ref[...]
        chosen = gates * (grad_gates - jnp.sum(gates * grad_gates, axis=0, keepdims=True))
        logits = chosen.astype(jnp.bfloat16)
        small_ref[0:experts, :] = dot(logits, arrived(2)[...])
        for copy in weight_copies(0):
            copy.start()
        grad_normed = dot(logits, router_ref[...], TN) + rows_ref[...].astype(jnp.float32)
        middle = arrived(1)[...]
        grad_middle, gain_grad = norm_back(grad_normed, middle, rms_scale(middle), gain_two_ref[...])
        small_ref[experts : experts + 1, :] = gain_grad[None, :]
        grad_middle = grad_middle + arrived(5)[...].astype(jnp.float32)
        middle_acc[...] = grad_middle
        mid_ref[...] = grad_middle.astype(jnp.bfloat16)
        normed_acc[...] = jnp.zeros_like(normed_acc)
        arrived(4)

        def one(half, carry):
            for copy in weight_copies(half):
                copy.wait()

            @pl.when(half + 1 < parts)
            def _():
                for copy in weight_copies(half + 1):
                    copy.start()

            attn_backward_part(
                group,
                half,
                mid_ref,
                wqkv_ref,
                wo_ref,
                (cos_ref[...], -sin_ref[...]),
                (seg_col_ref[...], seg_row_ref[...]),
                qkv_ref,
                dqkv_ref,
                normed_acc,
            )
            return carry

        lax.fori_loop(0, parts, one, 0)
        rows = arrived(0)[...].astype(jnp.float32)
        grad_rows, gain_grad = norm_back(normed_acc[...], rows, rms_scale(rows), gain_one_ref[...])
        grad_in_ref[...] = (grad_rows + middle_acc[...]).astype(jnp.bfloat16)
        small_ref[experts + 1 : experts + 2, :] = gain_grad[None, :]
        small_ref[experts + 2 :, :] = jnp.zeros_like(small_ref[experts + 2 :, :])


def attn_backward_part(
    group, part, mid_ref, wqkv_ref, wo_ref, tables, segs, qkv_ref, dqkv_ref, normed_acc
):
    length = mid_ref.shape[0]
    width = wqkv_ref.shape[2]
    query_width = width * group // (group + 2)
    key_width = (width - query_width) // 2
    cosine, sine = tables
    seg_col, seg_row = segs
    grad_att = dot(mid_ref[...], wo_ref[part], NT).astype(jnp.bfloat16).astype(jnp.float32)
    grad_out = slabs_of(grad_att, 0, query_width // (2 * HD))
    kept = qkv_ref[part]
    query = [slab.astype(jnp.float32) for slab in slabs_of(kept, 0, query_width // (2 * HD))]
    key = slabs_of(kept, query_width, key_width // (2 * HD))
    value = slabs_of(kept, query_width + key_width, key_width // (2 * HD))
    key_at = lax.broadcasted_iota(jnp.int32, (length, length), 0)
    query_at = lax.broadcasted_iota(jnp.int32, (length, length), 1)
    allowed = (query_at >= key_at) & (seg_col == seg_row)
    grad_query = [None] * len(query)
    grad_key = [None] * len(key)
    grad_value = [None] * len(value)
    for kv_head in range(key_width // HD):
        side = kv_head % 2
        slab_at = kv_head // 2
        key_slab = key[slab_at]
        key_side = one_side(key_slab, side)
        value_slab = value[slab_at]
        for head in range(group * kv_head, group * (kv_head + 1)):
            query_head = aligned_head(query, head, side, HD**-0.5)
            out_head = aligned_head(grad_out, head, side, 1.0)
            scores = dot(key_slab, query_head, NT)
            scores = jnp.where(allowed, scores, NEG_BIG)
            exponent = jnp.exp(scores - jnp.max(scores, axis=0, keepdims=True))
            probability = exponent / jnp.sum(exponent, axis=0, keepdims=True)
            grad_prob = dot(value_slab, out_head, NT)
            value_part = dot(probability.astype(jnp.bfloat16), out_head)
            centre = jnp.sum(probability * grad_prob, axis=0, keepdims=True)
            grad_scores = (probability * (grad_prob - centre)).astype(jnp.bfloat16)
            key_part = dot(grad_scores, query_head)
            query_part = dot(grad_scores, key_side, TN) * HD**-0.5
            if head % 2 != side:
                query_part = pltpu.roll(query_part, HD, 1)
            at = head // 2
            grad_query[at] = query_part if head % 2 == 0 else grad_query[at] + query_part
            first = head == 2 * group * slab_at
            grad_key[slab_at] = key_part if first else grad_key[slab_at] + key_part
            grad_value[slab_at] = value_part if first else grad_value[slab_at] + value_part
    turned = [turn_pair(slab, cosine, sine).astype(jnp.bfloat16) for slab in grad_query + grad_key]
    dqkv = jnp.concatenate(turned + [slab.astype(jnp.bfloat16) for slab in grad_value], axis=1)
    dqkv_ref[part] = dqkv
    normed_acc[...] += dot(dqkv, wqkv_ref[part], NT)


def attn_backward(
    kept, rows, grad_gates, seg, gains, router, wqkv, wo, tables, group, skipped
):
    length, width = rows.shape
    parts, _, qkv_width = wqkv.shape
    experts = router.shape[0]
    vmem = pl.BlockSpec(memory_space=pltpu.VMEM)
    anywhere = pl.BlockSpec(memory_space=pl.ANY)
    dma = pltpu.SemaphoreType.DMA
    return pl.pallas_call(
        functools.partial(attn_backward_kernel, group, skipped),
        in_specs=[anywhere] * 14 + [vmem] * 9,
        out_specs=[vmem] * 4,
        out_shape=[
            jax.ShapeDtypeStruct((length, width), jnp.bfloat16),
            jax.ShapeDtypeStruct((length, width), jnp.bfloat16),
            jax.ShapeDtypeStruct((parts, length, qkv_width), jnp.bfloat16),
            jax.ShapeDtypeStruct((experts + 8, width), jnp.float32),
        ],
        scratch_shapes=[pltpu.VMEM(one.shape, one.dtype) for one, _ in kept]
        + [
            pltpu.VMEM(wqkv.shape, wqkv.dtype),
            pltpu.VMEM(wo.shape, wo.dtype),
            pltpu.VMEM((length, width), jnp.float32),
            pltpu.VMEM((length, width), jnp.float32),
            dma((len(kept),)),
            dma((2, parts)),
        ],
        compiler_params=pltpu.CompilerParams(vmem_limit_bytes=62 * MIB),
        cost_estimate=pl.CostEstimate(
            flops=8 * 10**9, bytes_accessed=20 * 10**6, transcendentals=2 * 10**6
        ),
        name="attn_backward",
    )(
        *[one for pair in kept for one in pair],
        wqkv,
        wo,
        rows,
        grad_gates,
        router,
        gains[0],
        gains[1],
        tables[0],
        tables[1],
        seg[:, None],
        seg[None, :],
    )


def attn_weights_kernel(*refs):
    groups, out_ref = [refs[3 * i : 3 * i + 3] for i in range(4)], refs[12]
    width = out_ref.shape[1]

    def kept(group):
        one, both, three = group
        return jnp.concatenate([of_section(one, three), both[...]], axis=-2)

    def found(group):
        one, both, three = group
        return jnp.concatenate([both[...], of_section(three, one)], axis=-2)

    xn1, att = kept(groups[0]), kept(groups[1])[0]
    mid, dqkv = found(groups[2]), found(groups[3])[0]
    qkv_width = dqkv.shape[1]
    out_ref[0, :, :qkv_width] = dot(xn1, dqkv, TN).astype(jnp.bfloat16)
    half = width // 2
    for i in range(2):
        out_ref[0, i * half : (i + 1) * half, qkv_width:] = dot(
            att, mid[:, i * half : (i + 1) * half], TN
        ).astype(jnp.bfloat16)


def attn_weights(xn1, att, mid, dqkv):
    rows, width = xn1[0].shape
    parts, _, att_width = att[0].shape
    qkv_width = dqkv[0].shape[2]

    def whole(*shape):
        return pl.BlockSpec(shape, lambda i: (0,) * len(shape))

    def part(*shape):
        return pl.BlockSpec((1,) + shape, lambda i: (i, 0, 0))

    return pl.pallas_call(
        attn_weights_kernel,
        grid=(parts,),
        in_specs=[whole(rows, width)] * 3
        + [part(rows, att_width)] * 3
        + [whole(rows, width)] * 3
        + [part(rows, qkv_width)] * 3,
        out_specs=part(width, qkv_width + width // 2),
        out_shape=jax.ShapeDtypeStruct((parts, width, qkv_width + width // 2), jnp.bfloat16),
        compiler_params=pltpu.CompilerParams(vmem_limit_bytes=56 * MIB),
        cost_estimate=pl.CostEstimate(
            flops=7 * 10**9, bytes_accessed=20 * 10**6, transcendentals=0
        ),
        name="attn_weights",
    )(*xn1, *att, *mid, *dqkv)


def looked_up(place, values):
    found = values[0]
    for i, value in enumerate(values[1:]):
        found = jnp.where(place == i + 1, value, found)
    return found


def nearest_first(place, reach):
    table = []
    for at in range(reach):
        table.append(sorted(range(reach), key=lambda other: (abs(other - at), other)))
    return [looked_up(place, [table[at][k] for at in range(reach)]) for k in range(reach)]


MESH_ID = pl.DeviceIdType.MESH


class Chain:
    def __init__(self, reach):
        self.reach = reach
        self.z = lax.axis_index(EXPERT)
        self.x = lax.axis_index(TENSOR)
        self.me = 2 * self.z + self.x
        self.aside = {TENSOR: 1 - self.x}
        self.above = {EXPERT: self.z + 1}
        self.below = {EXPERT: self.z - 1}
        self.has_above = self.z < reach - 1
        self.has_below = self.z > 0
        self.order = nearest_first(self.z, reach)

    def near(self, k):
        return self.order[k] if isinstance(k, int) else looked_up(k, self.order)

    def greet_group(self, partner=None):
        barrier = pltpu.get_barrier_semaphore()
        if partner is not None:
            pl.semaphore_signal(barrier, inc=1, device_id=partner, device_id_type=MESH_ID)
        for other in range(2 * self.reach):

            @pl.when(other != self.me)
            def _():
                pl.semaphore_signal(
                    barrier,
                    inc=1,
                    device_id={EXPERT: other // 2, TENSOR: other % 2},
                    device_id_type=MESH_ID,
                )

        pl.semaphore_wait(barrier, 2 * self.reach - (1 if partner is None else 0))


def is_end(chain, source):
    return jnp.logical_or(source == 0, source == chain.reach - 1)


class Gather:
    def __init__(self, chain, blocks, send_sem, recv_sem, paired=False):
        self.chain, self.blocks, self.send_sem, self.recv_sem = chain, blocks, send_sem, recv_sem
        self.paired = paired

    def copy(self, source, column, piece, way, target):
        at = 2 * source + column
        return pltpu.make_async_remote_copy(
            src_ref=self.blocks.at[at, piece],
            dst_ref=self.blocks.at[at, piece],
            send_sem=self.send_sem.at[way, source, piece],
            recv_sem=self.recv_sem.at[at, piece],
            device_id=target,
            device_id_type=MESH_ID,
        )

    def over_x(self, source, piece, act):
        c = self.chain
        crosses = jnp.logical_and(is_end(c, source), source != c.z)
        if piece == 0:
            act(self.copy(source, c.x, 0, 0, c.aside))
        else:

            @pl.when(jnp.logical_not(crosses))
            def _():
                act(self.copy(source, c.x, piece, 0, c.aside))

    def each_way(self, source, piece, up, down, act):
        c = self.chain
        if up:

            @pl.when(c.has_above)
            def _():
                act(self.copy(source, c.x, piece, 1, c.above))

        if down:

            @pl.when(c.has_below)
            def _():
                act(self.copy(source, c.x, piece, 2, c.below))

        if not (self.paired and up and down):
            self.over_x(source, piece, act)

    def start(self):
        for piece in range(PIECES):
            self.each_way(self.chain.z, piece, True, True, lambda copy: copy.start())
        if self.paired:
            self.cross_out()

    def relay(self, distance):
        c = self.chain
        for piece in range(PIECES):

            @pl.when(c.z - distance >= 0)
            def _():
                self.copy(c.z - distance, c.x, piece, 1, c.below).wait_recv()
                self.each_way(c.z - distance, piece, True, False, lambda copy: copy.start())

            @pl.when(c.z + distance <= c.reach - 1)
            def _():
                self.copy(c.z + distance, c.x, piece, 2, c.above).wait_recv()
                self.each_way(c.z + distance, piece, False, True, lambda copy: copy.start())

    def cross_copy(self, end):
        c = self.chain
        return self.copy(end, 1 - c.x, PIECES - 1, 3, c.below if end else c.above)

    def cross_out(self):
        c = self.chain
        for end in (0, c.reach - 1):

            @pl.when(c.z == end)
            def _():
                self.cross_copy(end).start()

    def cross_relay(self, distance):
        c = self.chain
        for end in (0, c.reach - 1):
            last = c.reach - 1 - end

            @pl.when(jnp.where(c.z > end, c.z - end, end - c.z) == distance)
            def _():
                self.cross_copy(end).wait_recv()

                @pl.when(c.z != last)
                def _():
                    self.cross_copy(end).start()

    def wait_aside(self, source):
        c = self.chain
        self.copy(source, 1 - c.x, 0, 0, c.aside).wait_recv()

        @pl.when(jnp.logical_not(jnp.logical_and(is_end(c, source), source != c.z)))
        def _():
            self.copy(source, 1 - c.x, PIECES - 1, 0, c.aside).wait_recv()

    def drain(self):
        c = self.chain
        for piece in range(PIECES):
            self.each_way(c.z, piece, True, True, lambda copy: copy.wait_send())
            for distance in range(1, c.reach):

                @pl.when(c.z - distance >= 0)
                def _():
                    self.each_way(
                        c.z - distance, piece, True, False, lambda copy: copy.wait_send()
                    )

                @pl.when(c.z + distance <= c.reach - 1)
                def _():
                    self.each_way(
                        c.z + distance, piece, False, True, lambda copy: copy.wait_send()
                    )

        for end in (0, c.reach - 1):

            @pl.when(c.z != c.reach - 1 - end)
            def _():
                self.cross_copy(end).wait_send()


PIECES = 2
TAIL_PIECES = 4


class Reduce:
    def __init__(self, chain, part_at, from_x, from_z, sems, pieces=PIECES, cross=None):
        self.chain, self.part_at, self.from_x, self.from_z = chain, part_at, from_x, from_z
        self.pieces = pieces
        self.cross = cross
        self.x_send, self.x_recv, self.z_send, self.z_recv = sems

    def part_copy(self, home, piece):
        c = self.chain
        return pltpu.make_async_remote_copy(
            src_ref=self.part_at(home, 1 - c.x, piece),
            dst_ref=self.from_x.at[home, piece],
            send_sem=self.x_send.at[home, piece],
            recv_sem=self.x_recv.at[home, piece],
            device_id=c.aside,
            device_id_type=MESH_ID,
        )

    def sum_copy(self, home, piece, slot, target):
        return pltpu.make_async_remote_copy(
            src_ref=self.part_at(home, self.chain.x, piece),
            dst_ref=self.from_z.at[slot, piece],
            send_sem=self.z_send.at[home, piece],
            recv_sem=self.z_recv.at[slot, piece],
            device_id=target,
            device_id_type=MESH_ID,
        )

    def over_x(self, home, piece, act):
        c = self.chain
        if self.cross is None:
            act()
        else:
            crosses = jnp.logical_and(is_end(c, home), home != c.z)

            @pl.when(jnp.logical_not(jnp.logical_and(crosses, piece == self.pieces - 1)))
            def _():
                act()

    def start(self, k, piece):
        home = self.chain.near(k)
        self.over_x(home, piece, lambda: self.part_copy(home, piece).start())

    def arrive(self, k, piece):
        home = self.chain.near(k)
        self.over_x(home, piece, lambda: self.part_copy(home, piece).wait_recv())

    def own(self, home, piece):
        c = self.chain
        mine = self.part_at(home, c.x, piece)[...].astype(jnp.float32)
        came = self.from_x[home, piece].astype(jnp.float32)
        if self.cross is not None:
            crosses = jnp.logical_and(is_end(c, home), home != c.z)
            came = jnp.where(jnp.logical_and(crosses, piece == self.pieces - 1), 0.0, came)
        return mine + came

    def cross_copy(self, end):
        c = self.chain
        from_cross, send_sem, recv_sem = self.cross
        at = 1 if end else 0
        return pltpu.make_async_remote_copy(
            src_ref=self.part_at(end, 1 - c.x, self.pieces - 1),
            dst_ref=from_cross.at[at],
            send_sem=send_sem.at[at],
            recv_sem=recv_sem.at[at],
            device_id=c.above if end else c.below,
            device_id_type=MESH_ID,
        )

    def cross_step(self, distance):
        c = self.chain
        for end in (0, c.reach - 1):

            @pl.when(jnp.where(c.z > end, c.z - end, end - c.z) == distance)
            def _():
                @pl.when(c.z != c.reach - 1 - end)
                def _():
                    self.cross_copy(end).wait_recv()
                    mine = self.part_at(end, 1 - c.x, self.pieces - 1)
                    mine[...] = (
                        mine[...].astype(jnp.float32)
                        + self.cross[0][1 if end else 0].astype(jnp.float32)
                    ).astype(mine.dtype)

                @pl.when(c.z != end)
                def _():
                    self.cross_copy(end).start()

    def pass_on(self, k, piece):
        c = self.chain
        home = c.near(k)
        up = home > c.z
        comes = jnp.logical_or(
            jnp.logical_and(up, c.has_below), jnp.logical_and(home < c.z, c.has_above)
        )
        mine = self.part_at(home, c.x, piece)

        @pl.when(comes)
        def _():
            self.sum_copy(home, piece, home, c.above).wait_recv()
            mine[...] = (
                self.own(home, piece) + self.from_z[home, piece].astype(jnp.float32)
            ).astype(mine.dtype)

        @pl.when(jnp.logical_not(comes))
        def _():
            mine[...] = self.own(home, piece).astype(mine.dtype)

        @pl.when(up)
        def _():
            self.sum_copy(home, piece, home, c.above).start()

        @pl.when(home < c.z)
        def _():
            slot = jnp.where(home == c.z - 1, c.reach, home)
            self.sum_copy(home, piece, slot, c.below).start()

    def finish(self, piece, act):
        c = self.chain
        home = c.z

        @pl.when(c.has_below)
        def _():
            self.sum_copy(home, piece, home, c.below).wait_recv()

        @pl.when(c.has_above)
        def _():
            self.sum_copy(home, piece, c.reach, c.above).wait_recv()

        @pl.when(c.has_below & c.has_above)
        def _():
            act(
                piece,
                self.own(home, piece)
                + self.from_z[home, piece].astype(jnp.float32)
                + self.from_z[c.reach, piece].astype(jnp.float32),
            )

        @pl.when(jnp.logical_not(c.has_above))
        def _():
            act(piece, self.own(home, piece) + self.from_z[home, piece].astype(jnp.float32))

        @pl.when(jnp.logical_not(c.has_below))
        def _():
            act(piece, self.own(home, piece) + self.from_z[c.reach, piece].astype(jnp.float32))

    def drain(self):
        c = self.chain

        def one(home, carry):
            for piece in range(self.pieces):
                self.over_x(home, piece, lambda: self.part_copy(home, piece).wait_send())

                @pl.when(home != c.z)
                def _():
                    self.sum_copy(home, piece, home, c.above).wait_send()

            return carry

        lax.fori_loop(0, c.reach, one, 0)
        if self.cross is not None:
            for end in (0, c.reach - 1):

                @pl.when(c.z != end)
                def _():
                    self.cross_copy(end).wait_send()


def masked_softmax(logits, kept):
    top = jnp.max(jnp.where(kept, logits, NEG_BIG), axis=0, keepdims=True)
    exponent = jnp.where(kept, jnp.exp(jnp.where(kept, logits - top, 0.0)), 0.0)
    return exponent / jnp.sum(exponent, axis=0, keepdims=True)


def slot_gates(picks, gate_row):
    return jnp.sum(picks.astype(jnp.float32) * gate_row, axis=1, keepdims=True)


def one_hot_slots(slot_row, cap):
    length = slot_row.shape[1]
    at = lax.broadcasted_iota(jnp.int32, (cap, length), 0).astype(jnp.float32)
    return jnp.where(at == slot_row, 1.0, 0.0).astype(jnp.bfloat16)


def finish_pieces(summed, act):
    def one(piece, carry):
        summed.arrive(0, piece)
        summed.finish(piece, act)
        return carry

    lax.fori_loop(0, PIECES, one, 0)


def reduced_in_order(reach, summed, act):
    count = PIECES * (reach - 1)
    ahead = 3

    def place(i):
        return reach - 1 - i // PIECES, i % PIECES

    summed.cross_step(reach - 1)
    for i in range(ahead):
        summed.start(*place(i))

    def step(i, carry):
        summed.arrive(*place(i))

        @pl.when(i + ahead < count)
        def _():
            summed.start(*place(i + ahead))

        summed.pass_on(*place(i))

        @pl.when(jnp.logical_and(i % PIECES == 1, i < count - 1))
        def _():
            summed.cross_step(reach - 2 - i // PIECES)

        return carry

    lax.fori_loop(0, count, step, 0)
    summed.cross_step(0)
    summed.start(0, PIECES - 1)
    finish_pieces(summed, act)


def gathered_steps(reach, chain, rows, summed, compute):
    rows.start()

    def step(k, carry):
        @pl.when(k + 1 < reach)
        def _():
            rows.relay(k + 1)

        source = chain.near(k)
        rows.wait_aside(source)

        @pl.when(k == 0)
        def _():
            rows.cross_out()

        @pl.when(k > 0)
        def _():
            rows.cross_relay(k)

        @pl.when(k + 1 == reach)
        def _():
            summed.start(0, 0)

        compute(k, source)
        return carry

    lax.fori_loop(0, reach, step, 0)


def whole_rows(block):
    return block.reshape(-1, block.shape[-1])


def moe_forward_kernel(
    reach,
    tick,
    last,
    own_ref,
    h1_ref,
    ids_ref,
    router_ref,
    wg_hbm,
    wu_hbm,
    wd_hbm,
    *refs,
):
    refs = list(refs)
    if tick == 0:
        tops_ref, *shards = refs[:3]
        refs = refs[3:]
    out_ref, gates_ref, slots_ref, own_gates_ref, picked_hbm, g_hbm, u_hbm = refs[:7]
    refs = refs[7:]
    if tick == 0:
        tops_hbm, *halves = refs[:3]
        refs = refs[3:]
    (
        blocks,
        parts,
        from_x,
        from_z,
        from_cross,
        wg_ref,
        wu_ref,
        wd_ref,
        rows_in,
        rows_out,
        g_slots,
        u_slots,
        picks_of,
        ids_all,
        gather_send,
        gather_recv,
        x_send,
        x_recv,
        z_send,
        z_recv,
        cross_send,
        cross_recv,
        weight_sem,
        keep_sem,
        id_send,
        id_recv,
    ) = refs[:26]
    local = wg_ref.shape[0]
    cap = rows_in.shape[2] // 2
    experts = router_ref.shape[0]
    length = own_ref.shape[0]
    section = lax.axis_index(SECTION)
    chain = Chain(reach)

    def weight_copies():
        return [
            pltpu.make_async_copy(hbm, vmem, weight_sem.at[i])
            for i, (hbm, vmem) in enumerate(
                ((wg_hbm, wg_ref), (wu_hbm, wu_ref), (wd_hbm, wd_ref))
            )
        ]

    def keep_copies(k):
        source = chain.near(k)
        slot = k % 2 if isinstance(k, int) else lax.rem(k, 2)
        return [
            pltpu.make_async_copy(rows_in.at[slot], picked_hbm.at[source], keep_sem.at[0, k]),
            pltpu.make_async_copy(g_slots.at[slot], g_hbm.at[source], keep_sem.at[1, k]),
            pltpu.make_async_copy(u_slots.at[slot], u_hbm.at[source], keep_sem.at[2, k]),
        ]

    def id_copy(target, at):
        return pltpu.make_async_remote_copy(
            src_ref=ids_ref,
            dst_ref=ids_all.at[at],
            send_sem=id_send.at[target],
            recv_sem=id_recv.at[at],
            device_id={EXPERT: target // 2, TENSOR: target % 2},
            device_id_type=MESH_ID,
        )

    def compute(k, source):
        slot = lax.rem(k, 2)

        @pl.when(k == 0)
        def _():
            for copy in weight_copies():
                copy.wait()

        @pl.when(k >= 2)
        def _():
            for copy in keep_copies(k - 2):
                copy.wait()

        gate_of = {}
        ahead = lax.broadcasted_iota(jnp.int32, (length, length), 0)
        behind = lax.broadcasted_iota(jnp.int32, (length, length), 1)
        before = jnp.where(ahead < behind, 1.0, 0.0).astype(jnp.bfloat16)
        named = lax.rem(
            lax.broadcasted_iota(jnp.int32, (experts, length), 0) + chain.me * local, experts
        )
        for i in range(2):
            at = 2 * source + i

            @pl.when(at != chain.me)
            def _():
                id_copy(at, at).wait_recv()

            ids = ids_all[at]
            member = ids[0:1, :] == named
            for pick in range(1, TOPK):
                member = jnp.logical_or(member, ids[pick : pick + 1, :] == named)
            rows = whole_rows(blocks[at])
            gates = masked_softmax(dot(router_ref[...], rows, NT), member)
            gates_ref[at] = gates

            @pl.when(at == chain.me)
            def _():
                own_gates_ref[...] = gates

            mine = jnp.where(member[:8], 1.0, 0.0).astype(jnp.bfloat16)
            taken = jnp.where(member[:8], dot(mine, before), -1.0)
            slots_ref[at] = taken
            for e in range(local):
                picks = one_hot_slots(taken[e : e + 1, :], cap)
                picks_of[i, e * cap : (e + 1) * cap, :] = picks
                gate_of[i, e] = slot_gates(picks, gates[e : e + 1, :])
            gathered = dot(picks_of[i], rows).astype(jnp.bfloat16)
            for e in range(local):
                rows_in[slot, e, i * cap : (i + 1) * cap, :] = gathered[e * cap : (e + 1) * cap, :]
        for e in range(local):
            rows = rows_in[slot, e]
            gate_pre = dot(rows, wg_ref[e])
            up_pre = dot(rows, wu_ref[e])
            g_slots[slot, e] = gate_pre.astype(jnp.bfloat16)
            u_slots[slot, e] = up_pre.astype(jnp.bfloat16)
            hidden = (gate_pre * jax.nn.sigmoid(gate_pre) * up_pre).astype(jnp.bfloat16)
            produced = dot(hidden, wd_ref[e])
            for i in range(2):
                rows_out[i, e * cap : (e + 1) * cap, :] = (
                    produced[i * cap : (i + 1) * cap, :] * gate_of[i, e]
                ).astype(jnp.bfloat16)
        for i in range(2):
            share = dot(picks_of[i], rows_out[i], TN).astype(jnp.bfloat16)
            parts[2 * source + i] = share.reshape(parts.shape[1:])
        for copy in keep_copies(k):
            copy.start()

    def finish(piece, total):
        at = pl.ds(pl.multiple_of(piece * total.shape[0], total.shape[0]), total.shape[0])
        out_ref[at, :] = (h1_ref[at, :] + total).astype(jnp.bfloat16)

    def run():
        for copy in weight_copies():
            copy.start()
        blocks[chain.me] = own_ref[...].reshape(blocks.shape[1:])
        ids_all[chain.me] = ids_ref[...]
        chain.greet_group()
        for target in range(2 * reach):

            @pl.when(target != chain.me)
            def _():
                id_copy(target, chain.me).start()

        rows = Gather(chain, blocks, gather_send, gather_recv)
        summed = Reduce(
            chain,
            lambda home, column, piece: parts.at[2 * home + column, piece],
            from_x,
            from_z,
            (x_send, x_recv, z_send, z_recv),
            cross=(from_cross, cross_send, cross_recv),
        )
        gathered_steps(reach, chain, rows, summed, compute)
        reduced_in_order(reach, summed, finish)
        rows.drain()
        summed.drain()
        for target in range(2 * reach):

            @pl.when(target != chain.me)
            def _():
                id_copy(target, chain.me).wait_send()

        for k in (reach - 2, reach - 1):
            for copy in keep_copies(k):
                copy.wait()

    if tick == 0:
        second_send, second_recv, tops_sem, *refs = refs[26:]
        landed, (stage_sem, own_sem, half_sem, wx_send, wx_recv, core_send, core_recv) = (
            refs[:2],
            refs[2:],
        )
        core = lax.axis_index(DP)
        partner = {DP: 1 - core}
        chunks = local
        pieces = [(i, chunk) for i in range(2) for chunk in range(chunks)]

        def span(i, of_core, chunk):
            rows = shards[i].shape[0] // (2 * chunks)
            return pl.ds((of_core * chunks + chunk) * rows, rows)

        def stage(i, chunk, mine):
            rows, columns = shards[i].shape[0] // (2 * chunks), shards[i].shape[1]
            if mine:
                return rows_in.at[i, chunk, pl.ds(0, rows), pl.ds(0, columns)]
            if i == 0:
                return rows_out.at[chunk // 2, pl.ds(chunk % 2 * rows, rows), pl.ds(0, columns)]
            return from_x.at[chunk, 0, pl.ds(0, rows)]

        def stage_copy(i, chunk, mine):
            at = span(i, core if mine else 1 - core, chunk)
            return pltpu.make_async_copy(
                shards[i].at[at], stage(i, chunk, mine), stage_sem.at[i, chunk, 1 - mine]
            )

        def own_copy(i, chunk, mine):
            at = span(i, core if mine else 1 - core, chunk)
            return pltpu.make_async_copy(
                stage(i, chunk, mine), halves[i].at[chain.x, at], own_sem.at[i, chunk, 1 - mine]
            )

        def half_copy(i):
            return pltpu.make_async_copy(landed[i], halves[i].at[1 - chain.x], half_sem.at[i])

        def weight_x_copy(i, chunk):
            return pltpu.make_async_remote_copy(
                src_ref=stage(i, chunk, 1),
                dst_ref=landed[i].at[span(i, core, chunk)],
                send_sem=wx_send.at[i, chunk],
                recv_sem=wx_recv.at[i, chunk],
                device_id=chain.aside,
                device_id_type=MESH_ID,
            )

        def weight_core_copy(i, chunk, of_core):
            at = landed[i].at[span(i, of_core, chunk)]
            return pltpu.make_async_remote_copy(
                src_ref=at,
                dst_ref=at,
                send_sem=core_send.at[i, chunk],
                recv_sem=core_recv.at[i, chunk],
                device_id=partner,
                device_id_type=MESH_ID,
            )

        @pl.when(section == 0)
        def _():
            run()

        @pl.when(section != 0)
        def _():
            for mine in (1, 0):
                for i, chunk in pieces:
                    stage_copy(i, chunk, mine).start()
            own_tops = [
                pltpu.make_async_copy(
                    tops_ref.at[micro], buffer.at[pl.ds(2 * chain.z, 2)], tops_sem.at[micro]
                )
                for micro, buffer in enumerate((blocks, parts))
            ]
            for copy in own_tops:
                copy.start()
            chain.greet_group(partner)
            for copy in own_tops:
                copy.wait()
            both = (
                Gather(chain, blocks, gather_send, gather_recv, True),
                Gather(chain, parts, second_send, second_recv, True),
            )
            copies = [
                pltpu.make_async_copy(blocks, tops_hbm.at[0], tops_sem.at[0]),
                pltpu.make_async_copy(parts, tops_hbm.at[1], tops_sem.at[1]),
            ]
            both[0].start()
            both[1].start()
            for i, chunk in pieces:
                stage_copy(i, chunk, 1).wait()
                weight_x_copy(i, chunk).start()
                own_copy(i, chunk, 1).start()
            for i, chunk in pieces:
                stage_copy(i, chunk, 0).wait()
                own_copy(i, chunk, 0).start()
            for rows in both:
                for distance in range(1, reach):
                    rows.relay(distance)
                    rows.cross_relay(distance)
            for i, chunk in pieces:
                weight_x_copy(i, chunk).wait_recv()
                weight_core_copy(i, chunk, core).start()
            for i in range(2):
                for chunk in range(chunks):
                    weight_core_copy(i, chunk, 1 - core).wait_recv()
                half_copy(i).start()
            for rows, copy in zip(both, copies):
                for k in range(1, reach):
                    rows.wait_aside(chain.near(k))
                copy.start()
            for rows in both:
                rows.drain()
            for i, chunk in pieces:
                weight_x_copy(i, chunk).wait_send()
                weight_core_copy(i, chunk, core).wait_send()
                for mine in (1, 0):
                    own_copy(i, chunk, mine).wait()
            for i in range(2):
                half_copy(i).wait()
            for copy in copies:
                copy.wait()

    elif tick == last:

        @pl.when(section != 0)
        def _():
            run()

    else:
        run()


def exchange_scratch(reach, length, width):
    piece = (PIECES, length // PIECES, width)
    return [
        pltpu.VMEM((2 * reach,) + piece, jnp.bfloat16),
        pltpu.VMEM((2 * reach,) + piece, jnp.bfloat16),
        pltpu.VMEM((reach,) + piece, jnp.bfloat16),
        pltpu.VMEM((reach + 1,) + piece, jnp.bfloat16),
        pltpu.VMEM((2,) + piece[1:], jnp.bfloat16),
    ]


def exchange_sems(reach):
    dma = pltpu.SemaphoreType.DMA
    return [
        dma((4, reach, PIECES)),
        dma((2 * reach, PIECES)),
        dma((reach, PIECES)),
        dma((reach, PIECES)),
        dma((reach, PIECES)),
        dma((reach + 1, PIECES)),
        dma((2,)),
        dma((2,)),
    ]


def moe_forward_call(reach, tick, last, own, h1, ids, router, wg, wu, wd, firsts):
    length, width = own.shape
    local, _, hidden = wg.shape
    cap = slot_count(length)
    experts = router.shape[0]
    vmem = pl.BlockSpec(memory_space=pltpu.VMEM)
    anywhere = pl.BlockSpec(memory_space=pl.ANY)
    slots = (reach, local, 2 * cap, hidden)
    first = tick == 0
    all_rows = (2 * reach, PIECES, length // PIECES, width)
    return pl.pallas_call(
        functools.partial(moe_forward_kernel, reach, tick, last),
        in_specs=[vmem] * 4 + [anywhere] * 3 + [anywhere] * 3 * first,
        out_specs=[vmem] * 4 + [anywhere] * 3 + [anywhere] * 3 * first,
        out_shape=[
            jax.ShapeDtypeStruct((length, width), jnp.bfloat16),
            jax.ShapeDtypeStruct((2 * reach, experts, length), jnp.float32),
            jax.ShapeDtypeStruct((2 * reach, 8, length), jnp.float32),
            jax.ShapeDtypeStruct((experts, length), jnp.float32),
            jax.ShapeDtypeStruct(slots[:3] + (width,), jnp.bfloat16),
            jax.ShapeDtypeStruct(slots, jnp.bfloat16),
            jax.ShapeDtypeStruct(slots, jnp.bfloat16),
        ]
        + (
            [jax.ShapeDtypeStruct((2,) + all_rows, jnp.bfloat16)]
            + [jax.ShapeDtypeStruct((2,) + shard.shape, shard.dtype) for shard in firsts[1:]]
        )
        * first,
        scratch_shapes=exchange_scratch(reach, length, width)
        + [
            pltpu.VMEM(wg.shape, jnp.bfloat16),
            pltpu.VMEM(wu.shape, jnp.bfloat16),
            pltpu.VMEM(wd.shape, jnp.bfloat16),
            pltpu.VMEM((2, local, 2 * cap, width), jnp.bfloat16),
            pltpu.VMEM((2, local * cap, width), jnp.bfloat16),
            pltpu.VMEM((2,) + slots[1:], jnp.bfloat16),
            pltpu.VMEM((2,) + slots[1:], jnp.bfloat16),
            pltpu.VMEM((2, local * cap, length), jnp.bfloat16),
            pltpu.VMEM((2 * reach, TOPK, length), jnp.int32),
        ]
        + exchange_sems(reach)
        + [
            pltpu.SemaphoreType.DMA((3,)),
            pltpu.SemaphoreType.DMA((3, reach)),
            pltpu.SemaphoreType.DMA((2 * reach,)),
            pltpu.SemaphoreType.DMA((2 * reach,)),
        ]
        + (
            exchange_sems(reach)[:2]
            + [pltpu.SemaphoreType.DMA((2,))]
            + [pltpu.VMEM(shard.shape, shard.dtype) for shard in firsts[1:]]
            + [
                pltpu.SemaphoreType.DMA((2, local, 2)),
                pltpu.SemaphoreType.DMA((2, local, 2)),
                pltpu.SemaphoreType.DMA((2,)),
            ]
            + [pltpu.SemaphoreType.DMA((2, local))] * 4
        )
        * first,
        compiler_params=pltpu.CompilerParams(
            collective_id=1 + tick, has_side_effects=True, vmem_limit_bytes=62 * MIB
        ),
        cost_estimate=pl.CostEstimate(
            flops=20 * 10**9, bytes_accessed=45 * 10**6, transcendentals=2 * 10**6
        ),
        name="moe_forward",
    )(own, h1, ids, router, wg, wu, wd, *(firsts * first))


def moe_backward_kernel(
    reach,
    tick,
    last,
    own_ref,
    slots_first,
    slots_second,
    gates_first,
    gates_second,
    g_first,
    g_second,
    u_first,
    u_second,
    wg_hbm,
    wu_hbm,
    wd_hbm,
    tops_hbm,
    after,
    out_ref,
    home_gates_ref,
    picked_hbm,
    gg_hbm,
    gu_hbm,
    hg_hbm,
    blocks,
    parts,
    from_x,
    from_z,
    from_cross,
    wg_ref,
    wu_ref,
    wd_ref,
    rows_in,
    rows_out,
    g_slots,
    u_slots,
    gg_slots,
    gu_slots,
    hg_slots,
    picks_of,
    gate_parts,
    gate_from,
    gather_send,
    gather_recv,
    x_send,
    x_recv,
    z_send,
    z_recv,
    cross_send,
    cross_recv,
    weight_sem,
    keep_sem,
    load_sem,
    gate_send,
    gate_recv,
    tops_sem,
):
    del after
    local = wg_ref.shape[0]
    cap = rows_in.shape[2] // 2
    section = lax.axis_index(SECTION)
    chain = Chain(reach)
    me = chain.me

    def weight_copies():
        return [
            pltpu.make_async_copy(hbm, vmem, weight_sem.at[i])
            for i, (hbm, vmem) in enumerate(
                ((wd_hbm, wd_ref), (wg_hbm, wg_ref), (wu_hbm, wu_ref))
            )
        ]

    def load_copies(step, source, first):
        slot = step % 2 if isinstance(step, int) else lax.rem(step, 2)
        return [
            pltpu.make_async_copy(
                (g_first if first else g_second).at[source], g_slots.at[slot], load_sem.at[0, step]
            ),
            pltpu.make_async_copy(
                (u_first if first else u_second).at[source], u_slots.at[slot], load_sem.at[1, step]
            ),
        ]

    def keep_copies(step, source):
        slot = step % 2 if isinstance(step, int) else lax.rem(step, 2)
        return [
            pltpu.make_async_copy(rows_in.at[slot], picked_hbm.at[source], keep_sem.at[0, step]),
            pltpu.make_async_copy(gg_slots.at[slot], gg_hbm.at[source], keep_sem.at[1, step]),
            pltpu.make_async_copy(gu_slots.at[slot], gu_hbm.at[source], keep_sem.at[2, step]),
            pltpu.make_async_copy(hg_slots.at[slot], hg_hbm.at[source], keep_sem.at[3, step]),
        ]

    def gate_copy(target, at):
        return pltpu.make_async_remote_copy(
            src_ref=gate_parts.at[target],
            dst_ref=gate_from.at[at],
            send_sem=gate_send.at[target],
            recv_sem=gate_recv.at[at],
            device_id={EXPERT: target // 2, TENSOR: target % 2},
            device_id_type=MESH_ID,
        )

    def compute(step, source_of, first):
        source = source_of(step)
        slot = lax.rem(step, 2)

        @pl.when(step == 0)
        def _():
            for copy in weight_copies():
                copy.wait()

        @pl.when(step >= 2)
        def _():
            for copy in keep_copies(step - 2, source_of(step - 2)):
                copy.wait()

        for copy in load_copies(step, source, first):
            copy.wait()
        slots_ref = slots_first if first else slots_second
        gates_ref = gates_first if first else gates_second
        gate_of = {}
        for i in range(2):
            at = 2 * source + i
            for e in range(local):
                picks = one_hot_slots(slots_ref[at, e : e + 1, :], cap)
                picks_of[i, e * cap : (e + 1) * cap, :] = picks
                gate_of[i, e] = slot_gates(picks, gates_ref[at, e : e + 1, :])
            gathered = dot(picks_of[i], whole_rows(blocks[at])).astype(jnp.bfloat16)
            for e in range(local):
                rows_in[slot, e, i * cap : (i + 1) * cap, :] = gathered[e * cap : (e + 1) * cap, :]
        for e in range(local):
            plain = dot(rows_in[slot, e], wd_ref[e], NT)
            gate_pre = g_slots[slot, e].astype(jnp.float32)
            up_pre = u_slots[slot, e].astype(jnp.float32)
            sg = jax.nn.sigmoid(gate_pre)
            hidden = gate_pre * sg * up_pre
            gate_col = jnp.concatenate([gate_of[i, e] for i in range(2)], axis=0)
            grad_gate_col = jnp.sum(hidden * plain, axis=1, keepdims=True)
            grad_hidden = plain * gate_col
            grad_gate = (grad_hidden * up_pre * sg * (1.0 + gate_pre * (1.0 - sg))).astype(
                jnp.bfloat16
            )
            grad_up = (grad_hidden * gate_pre * sg).astype(jnp.bfloat16)
            gg_slots[slot, e] = grad_gate
            gu_slots[slot, e] = grad_up
            hg_slots[slot, e] = (hidden * gate_col).astype(jnp.bfloat16)
            grad_rows = dot(grad_gate, wg_ref[e], NT) + dot(grad_up, wu_ref[e], NT)
            for i in range(2):
                at = 2 * source + i
                rows = slice(i * cap, (i + 1) * cap)
                rows_out[i, e * cap : (e + 1) * cap, :] = grad_rows[rows, :].astype(jnp.bfloat16)
                picks = picks_of[i, e * cap : (e + 1) * cap, :].astype(jnp.float32)
                gate_parts[at, e : e + 1, :] = jnp.sum(
                    picks * grad_gate_col[rows, :], axis=0, keepdims=True
                )
        for i in range(2):
            share = dot(picks_of[i], rows_out[i], TN).astype(jnp.bfloat16)
            parts[2 * source + i] = share.reshape(parts.shape[1:])
        for copy in keep_copies(step, source):
            copy.start()

        @pl.when(step + 2 < reach)
        def _():
            for copy in load_copies(step + 2, source_of(step + 2), first):
                copy.start()

        for i in range(2):
            at = 2 * source + i

            @pl.when(at != me)
            def _():
                gate_copy(at, me).start()

    def finish(piece, total):
        at = pl.ds(pl.multiple_of(piece * total.shape[0], total.shape[0]), total.shape[0])
        out_ref[at, :] = total

    def run(gathered):
        first = gathered

        def source_of(step):
            if isinstance(step, int):
                return chain.near(step if gathered else reach - 1 - step)
            return chain.near(step if gathered else reach - 1 - step)

        def top_copy(step):
            pair = pl.ds(2 * source_of(step), 2)
            return pltpu.make_async_copy(
                tops_hbm.at[min(tick, 1), pair], blocks.at[pair], tops_sem.at[step]
            )

        for step in range(2):
            for copy in load_copies(step, source_of(step), first):
                copy.start()
        if not gathered:
            for step in range(reach):
                top_copy(step).start()
        for copy in weight_copies():
            copy.start()
        chain.greet_group()
        summed = Reduce(
            chain,
            lambda home, column, piece: parts.at[2 * home + column, piece],
            from_x,
            from_z,
            (x_send, x_recv, z_send, z_recv),
            cross=(from_cross, cross_send, cross_recv),
        )
        if gathered:
            blocks[me] = own_ref[...].reshape(blocks.shape[1:])
            rows = Gather(chain, blocks, gather_send, gather_recv)
            gathered_steps(
                reach, chain, rows, summed, lambda step, source: compute(step, source_of, first)
            )
            reduced_in_order(reach, summed, finish)
            rows.drain()
        else:

            def step_back(step, carry):
                k = reach - 1 - step
                top_copy(step).wait()
                compute(step, source_of, first)
                summed.start(k, 0)

                @pl.when(k > 0)
                def _():
                    summed.start(k, PIECES - 1)
                    summed.cross_step(k)

                @pl.when(step >= 1)
                def _():
                    for piece in range(PIECES):
                        summed.arrive(k + 1, piece)
                        summed.pass_on(k + 1, piece)

                return carry

            lax.fori_loop(0, reach, step_back, 0)
            summed.cross_step(0)
            summed.start(0, PIECES - 1)
            finish_pieces(summed, finish)
        summed.drain()
        home_gates_ref[0] = gate_parts[me, :local]
        for at in range(2 * reach):

            @pl.when(at != me)
            def _():
                gate_copy(at, me).wait_send()
                gate_copy(at, at).wait_recv()
                home_gates_ref[lax.rem(at - me + 2 * reach, 2 * reach)] = gate_from[at, :local]

        for step in (reach - 2, reach - 1):
            for copy in keep_copies(step, source_of(step)):
                copy.wait()

    if tick > 0:

        @pl.when(section == 0)
        def _():
            run(True)

    if tick < last:

        @pl.when(section != 0)
        def _():
            run(False)


def moe_backward_call(
    reach, tick, last, own, slots_two, gates_two, g_two, u_two, wg, wu, wd, tops, after
):
    length, width = own.shape
    local, _, hidden = wg.shape
    cap = slot_count(length)
    vmem = pl.BlockSpec(memory_space=pltpu.VMEM)
    anywhere = pl.BlockSpec(memory_space=pl.ANY)
    slot_rows = (reach, local, 2 * cap, hidden)
    kept = jax.ShapeDtypeStruct(slot_rows, jnp.bfloat16)
    return pl.pallas_call(
        functools.partial(moe_backward_kernel, reach, tick, last),
        in_specs=[vmem] * 5 + [anywhere] * 9,
        out_specs=[vmem, vmem] + [anywhere] * 4,
        out_shape=[
            jax.ShapeDtypeStruct((length, width), jnp.float32),
            jax.ShapeDtypeStruct((2 * reach, local, length), jnp.float32),
            jax.ShapeDtypeStruct(slot_rows[:3] + (width,), jnp.bfloat16),
            kept,
            kept,
            kept,
        ],
        scratch_shapes=exchange_scratch(reach, length, width)
        + [
            pltpu.VMEM(wg.shape, jnp.bfloat16),
            pltpu.VMEM(wu.shape, jnp.bfloat16),
            pltpu.VMEM(wd.shape, jnp.bfloat16),
            pltpu.VMEM((2, local, 2 * cap, width), jnp.bfloat16),
            pltpu.VMEM((2, local * cap, width), jnp.bfloat16),
        ]
        + [pltpu.VMEM((2,) + slot_rows[1:], jnp.bfloat16)] * 5
        + [
            pltpu.VMEM((2, local * cap, length), jnp.bfloat16),
            pltpu.VMEM((2 * reach, 8, length), jnp.float32),
            pltpu.VMEM((2 * reach, 8, length), jnp.float32),
        ]
        + exchange_sems(reach)
        + [
            pltpu.SemaphoreType.DMA((3,)),
            pltpu.SemaphoreType.DMA((4, reach)),
            pltpu.SemaphoreType.DMA((2, reach)),
            pltpu.SemaphoreType.DMA((2 * reach,)),
            pltpu.SemaphoreType.DMA((2 * reach,)),
            pltpu.SemaphoreType.DMA((reach,)),
        ],
        compiler_params=pltpu.CompilerParams(
            collective_id=4 + tick, has_side_effects=True, vmem_limit_bytes=62 * MIB
        ),
        cost_estimate=pl.CostEstimate(
            flops=20 * 10**9, bytes_accessed=55 * 10**6, transcendentals=2 * 10**6
        ),
        name="moe_backward",
    )(own, *slots_two, *gates_two, *g_two, *u_two, wg, wu, wd, tops, after)


def middle_weights_kernel(
    x_first, x_second, dh_ref, gg_ref, gu_ref, hg_ref, after, wg_ref, wu_ref, wd_ref
):
    del after
    hidden = gg_ref.shape[3]
    wide = dh_ref.shape[3]
    rows = of_section(x_first, x_second).reshape(-1, wide)
    wg_ref[0] = dot(rows, gg_ref[...].reshape(-1, hidden), TN).astype(jnp.bfloat16)
    wu_ref[0] = dot(rows, gu_ref[...].reshape(-1, hidden), TN).astype(jnp.bfloat16)
    wd_ref[0] = dot(
        hg_ref[...].reshape(-1, hidden), dh_ref[...].reshape(-1, wide), TN
    ).astype(jnp.bfloat16)


def middle_weights(x_two, dh, gg, gu, hg, after):
    groups, local, rows, width = dh.shape
    hidden = gg.shape[3]
    tiles = width // hidden
    wide = width // tiles
    tiled = pl.BlockSpec((groups, 1, rows, wide), lambda e, t: (0, e, 0, t))
    held = pl.BlockSpec((groups, 1, rows, hidden), lambda e, t: (0, e, 0, 0))
    up = jax.ShapeDtypeStruct((local, width, hidden), jnp.bfloat16)
    return pl.pallas_call(
        middle_weights_kernel,
        grid=(local, tiles),
        in_specs=[tiled] * 3 + [held] * 3 + [pl.BlockSpec(memory_space=pl.ANY)],
        out_specs=[
            pl.BlockSpec((1, wide, hidden), lambda e, t: (e, t, 0)),
            pl.BlockSpec((1, wide, hidden), lambda e, t: (e, t, 0)),
            pl.BlockSpec((1, hidden, wide), lambda e, t: (e, 0, t)),
        ],
        out_shape=[up, up, jax.ShapeDtypeStruct((local, hidden, width), jnp.bfloat16)],
        compiler_params=pltpu.CompilerParams(vmem_limit_bytes=62 * MIB),
        cost_estimate=pl.CostEstimate(
            flops=30 * 10**9, bytes_accessed=60 * 10**6, transcendentals=0
        ),
        name="middle_weights",
    )(*x_two, dh, gg, gu, hg, after)


def ends_exchange_kernel(
    first_hbm, second_hbm, after, out_ref, held, came, load_sem, send_sem, recv_sem
):
    del after
    x = lax.axis_index(TENSOR)
    aside = {TENSOR: 1 - x}
    start_of_section(first_hbm, second_hbm, held, load_sem)
    barrier = pltpu.get_barrier_semaphore()
    pl.semaphore_signal(barrier, inc=1, device_id=aside, device_id_type=MESH_ID)
    pl.semaphore_wait(barrier, 1)
    pltpu.make_async_copy(first_hbm, held, load_sem).wait()
    copy = pltpu.make_async_remote_copy(
        src_ref=held,
        dst_ref=came,
        send_sem=send_sem,
        recv_sem=recv_sem,
        device_id=aside,
        device_id_type=MESH_ID,
    )
    copy.start()
    out_ref[x] = held[...]
    copy.wait()
    out_ref[1 - x] = came[...]


def ends_exchange(first, second, after):
    anywhere = pl.BlockSpec(memory_space=pl.ANY)
    return pl.pallas_call(
        ends_exchange_kernel,
        in_specs=[anywhere] * 3,
        out_specs=pl.BlockSpec(memory_space=pltpu.VMEM),
        out_shape=jax.ShapeDtypeStruct((2,) + first.shape, first.dtype),
        scratch_shapes=[pltpu.VMEM(first.shape, first.dtype)] * 2 + [pltpu.SemaphoreType.DMA] * 3,
        compiler_params=pltpu.CompilerParams(
            collective_id=10, has_side_effects=True, vmem_limit_bytes=62 * MIB
        ),
        cost_estimate=pl.CostEstimate(flops=0, bytes_accessed=4 * 10**6, transcendentals=0),
        name="ends_exchange",
    )(first, second, after)


def tail_kernel(
    reach,
    tiles,
    dense_hbm,
    x_hbm,
    dh_first,
    dh_last,
    gg_first,
    gg_last,
    gu_first,
    gu_last,
    hg_first,
    hg_last,
    wg_before,
    wu_before,
    wd_before,
    small_first,
    small_both,
    small_last,
    ends_back,
    ends_forward,
    query_out,
    key_out,
    value_out,
    out_out,
    wg_out,
    wu_out,
    wd_out,
    small_out,
    ends_out,
    mine,
    theirs,
    from_core,
    from_x,
    from_z,
    whole,
    x_rows,
    dh_rows,
    slots,
    before,
    wg_tile,
    wu_tile,
    wd_tile,
    wg_from,
    wu_from,
    wd_from,
    small_held,
    small_came,
    small_z,
    ends_held,
    ends_came,
    mine_sem,
    theirs_sem,
    core_send,
    core_recv,
    x_send,
    x_recv,
    z_send,
    z_recv,
    ring_send,
    ring_recv,
    last_send,
    last_recv,
    out_sem,
    row_sem,
    slot_sem,
    before_sem,
    tile_sem,
    tile_send,
    tile_recv,
    free_sem,
    small_send,
    small_recv,
    ends_load,
    ends_keep,
    ends_send,
    ends_recv,
):
    section = lax.axis_index(SECTION)
    core = lax.axis_index(DP)
    partner = {DP: 1 - core}
    chain = Chain(reach)
    x = chain.x
    z = chain.z
    quarter = mine.shape[3]
    local = gg_first.shape[1]
    width = x_hbm.shape[3]
    hidden = gg_first.shape[3]
    wide = width // tiles

    def mine_copy(half):
        return pltpu.make_async_copy(dense_hbm.at[half, core], mine.at[half], mine_sem.at[half])

    def theirs_copy(half, piece):
        return pltpu.make_async_copy(
            dense_hbm.at[half, 1 - core, :, piece],
            theirs.at[half, :, piece],
            theirs_sem.at[half, piece],
        )

    def core_copy(half, piece):
        return pltpu.make_async_remote_copy(
            src_ref=theirs.at[half, :, piece],
            dst_ref=from_core.at[half, :, piece],
            send_sem=core_send.at[half, piece],
            recv_sem=core_recv.at[half, piece],
            device_id=partner,
            device_id_type=MESH_ID,
        )

    def add_core(half, k, piece):
        home = chain.near(k)

        @pl.when(k == reach - 1)
        def _():
            core_copy(half, piece).wait_recv()

        mine[half, home, piece] = (
            mine[half, home, piece].astype(jnp.float32)
            + from_core[half, home, piece].astype(jnp.float32)
        ).astype(jnp.bfloat16)

    summed = Reduce(
        chain,
        lambda home, column, piece: mine.at[column, home, piece],
        from_x,
        from_z,
        (x_send, x_recv, z_send, z_recv),
        TAIL_PIECES,
    )

    def ring_copy(source, piece, way, target):
        return pltpu.make_async_remote_copy(
            src_ref=whole.at[core, source, piece],
            dst_ref=whole.at[core, source, piece],
            send_sem=ring_send.at[way, source, piece],
            recv_sem=ring_recv.at[source, piece],
            device_id=target,
            device_id_type=MESH_ID,
        )

    def last_copy(source, piece, side):
        return pltpu.make_async_remote_copy(
            src_ref=whole.at[side, source, piece],
            dst_ref=whole.at[side, source, piece],
            send_sem=last_send.at[source, piece],
            recv_sem=last_recv.at[source, piece],
            device_id=partner,
            device_id_type=MESH_ID,
        )

    def out_copies(side, source):
        block = whole.at[side, source]
        at = side * reach + source
        first = query_out.shape[3]
        second = first + key_out.shape[3]
        third = second + value_out.shape[3]
        half = block.shape[2] - third
        columns = pl.ds(pl.multiple_of(side * half, half), half)
        return [
            pltpu.make_async_copy(block.at[:, :, found], to, out_sem.at[side, source, i])
            for i, (found, to) in enumerate(
                (
                    (pl.ds(0, first), query_out.at[at]),
                    (pl.ds(first, second - first), key_out.at[at]),
                    (pl.ds(second, third - second), value_out.at[at]),
                    (pl.ds(third, half), out_out.at[source, :, :, columns]),
                )
            )
        ]

    def spread_block(source, piece, up, down):
        if up:

            @pl.when(chain.has_above)
            def _():
                ring_copy(source, piece, 0, chain.above).start()

        if down:

            @pl.when(chain.has_below)
            def _():
                ring_copy(source, piece, 1, chain.below).start()

        last_copy(source, piece, core).start()

        @pl.when(piece == TAIL_PIECES - 1)
        def _():
            for copy in out_copies(core, source):
                copy.start()

    def relay(distance, piece):
        @pl.when(z - distance >= 0)
        def _():
            ring_copy(z - distance, piece, 0, chain.below).wait_recv()
            spread_block(z - distance, piece, True, False)

        @pl.when(z + distance <= reach - 1)
        def _():
            ring_copy(z + distance, piece, 1, chain.above).wait_recv()
            spread_block(z + distance, piece, False, True)

    depth = wg_tile.shape[0]

    def spot(index):
        expert = index // tiles
        return expert, pl.ds(pl.multiple_of(lax.rem(index, tiles) * wide, wide), wide)

    def tile_loads(index, first):
        expert, at = spot(index)
        slot = lax.rem(index, 2)
        back = dh_last if first else dh_first
        return [
            pltpu.make_async_copy(
                x_hbm.at[:, expert, :, at], x_rows.at[slot], row_sem.at[slot, 0]
            ),
            pltpu.make_async_copy(
                back.at[:, expert, :, at], dh_rows.at[slot], row_sem.at[slot, 1]
            ),
        ] + [
            pltpu.make_async_copy(ref, before.at[slot, i], before_sem.at[slot, i])
            for i, ref in enumerate(
                (wg_before.at[expert, at], wu_before.at[expert, at], wd_before.at[expert, :, at])
            )
        ]

    def slot_loads(expert, first):
        slot = lax.rem(expert, 2)
        return [
            pltpu.make_async_copy(
                (two if first else one).at[:, expert], slots.at[slot, i], slot_sem.at[slot, i]
            )
            for i, (one, two) in enumerate(
                ((gg_first, gg_last), (gu_first, gu_last), (hg_first, hg_last))
            )
        ]

    def start(copies):
        @pl.when(section == 0)
        def _():
            for copy in copies(True):
                copy.start()

        @pl.when(section != 0)
        def _():
            for copy in copies(False):
                copy.start()

    held = ((wg_tile, wg_from), (wu_tile, wu_from), (wd_tile, wd_from))

    def tile_sends(index):
        slot = lax.rem(index, depth)
        return [
            pltpu.make_async_remote_copy(
                src_ref=tile.at[slot],
                dst_ref=came.at[slot],
                send_sem=tile_send.at[slot, i],
                recv_sem=tile_recv.at[slot, i],
                device_id=partner,
                device_id_type=MESH_ID,
            )
            for i, (tile, came) in enumerate(held)
        ]

    def tile_stores(index):
        expert, at = spot(index)
        slot = lax.rem(index, depth)
        outs = (wg_out.at[expert, at], wu_out.at[expert, at], wd_out.at[expert, :, at])
        return [
            pltpu.make_async_copy(came.at[slot], out, tile_sem.at[slot, i])
            for i, ((_, came), out) in enumerate(zip(held, outs))
        ]

    count = local * tiles

    def sum_tile(index):
        slot = lax.rem(index, depth)
        for copy, (tile, came) in zip(tile_sends(index), held):
            copy.wait_recv()
            came[slot] = (
                tile[slot].astype(jnp.float32) + came[slot].astype(jnp.float32)
            ).astype(jnp.bfloat16)
        for copy in tile_stores(index):
            copy.start()

    def one_tile(index):
        slot = lax.rem(index, 2)
        expert = index // tiles
        taken = lax.rem(expert, 2)

        @pl.when(index + 1 < count)
        def _():
            start(functools.partial(tile_loads, index + 1))

        @pl.when(jnp.logical_and(lax.rem(index, tiles) == 0, expert + 1 < local))
        def _():
            start(functools.partial(slot_loads, expert + 1))

        @pl.when(lax.rem(index, tiles) == 0)
        def _():
            for copy in slot_loads(expert, True):
                copy.wait()

        for copy in tile_loads(index, True):
            copy.wait()

        @pl.when(index >= depth)
        def _():
            for copy in tile_sends(index - depth):
                copy.wait_send()
            for copy in tile_stores(index - depth):
                copy.wait()
            pl.semaphore_signal(free_sem, inc=1, device_id=partner, device_id_type=MESH_ID)
            pl.semaphore_wait(free_sem, 1)

        to = lax.rem(index, depth)
        rows = x_rows[slot].reshape(-1, wide)
        found = (
            dot(rows, slots[taken, 0].reshape(-1, hidden), TN),
            dot(rows, slots[taken, 1].reshape(-1, hidden), TN),
            dot(slots[taken, 2].reshape(-1, hidden), dh_rows[slot].reshape(-1, wide), TN),
        )
        for i, (one, (tile, _)) in enumerate(zip(found, held)):
            tile[to] = (one + before[slot, i].astype(jnp.float32)).astype(jnp.bfloat16)
        for copy in tile_sends(index):
            copy.start()

        @pl.when(index >= 3)
        def _():
            sum_tile(index - 3)

    def tile_run(low, high):
        lax.fori_loop(low, high, lambda index, carry: (one_tile(index), carry)[1], 0)

    def small_copy(to, i):
        if i < 2:
            return pltpu.make_async_remote_copy(
                src_ref=small_held.at[i],
                dst_ref=small_came.at[i],
                send_sem=small_send.at[i],
                recv_sem=small_recv.at[i],
                device_id=to,
                device_id_type=MESH_ID,
            )
        return pltpu.make_async_remote_copy(
            src_ref=small_z.at[z],
            dst_ref=small_z.at[z],
            send_sem=small_send.at[2 + to],
            recv_sem=small_recv.at[2 + z],
            device_id={EXPERT: to},
            device_id_type=MESH_ID,
        )

    def others(act):
        for other in range(reach):

            @pl.when(other != z)
            def _():
                act(other)

    def small_step(stage):
        if stage == 0:
            total = small_both[...] + of_section(small_last, small_first)
            experts = 2 * reach * local
            small_held[0, :experts] = pltpu.roll(total[:experts], chain.me * local, 0)
            small_held[0, experts:] = total[experts:]
            small_copy(partner, 0).start()
        elif stage == 1:
            small_copy(partner, 0).wait_recv()
            small_held[1] = small_held[0] + small_came[0]
            small_copy(chain.aside, 1).start()
        elif stage == 2:
            small_copy(chain.aside, 1).wait_recv()
            small_z[z] = small_held[1] + small_came[1]
            others(lambda other: small_copy(other, 2).start())
        else:

            def wait(other):
                pltpu.make_async_remote_copy(
                    src_ref=small_z.at[other],
                    dst_ref=small_z.at[other],
                    send_sem=small_send.at[2 + other],
                    recv_sem=small_recv.at[2 + other],
                    device_id={EXPERT: other},
                    device_id_type=MESH_ID,
                ).wait_recv()

            others(wait)
            total = small_z[0]
            for other in range(1, reach):
                total = total + small_z[other]
            small_out[...] = total

    def ends_copy():
        return pltpu.make_async_remote_copy(
            src_ref=ends_held,
            dst_ref=ends_came,
            send_sem=ends_send,
            recv_sem=ends_recv,
            device_id=chain.aside,
            device_id_type=MESH_ID,
        )

    def ends_store(other):
        found, at = (ends_came, 1 - x) if other else (ends_held, x)
        return pltpu.make_async_copy(found, ends_out.at[at], ends_keep.at[int(other)])

    for piece in range(TAIL_PIECES):
        for half in (1 - x, x):
            theirs_copy(half, piece).start()
    for half in range(2):
        mine_copy(half).start()
    start_of_section(ends_back, ends_forward, ends_held, ends_load)

    barrier = pltpu.get_barrier_semaphore()
    pl.semaphore_signal(barrier, inc=1, device_id=partner, device_id_type=MESH_ID)
    pl.semaphore_signal(barrier, inc=1, device_id=chain.aside, device_id_type=MESH_ID)
    others(
        lambda other: pl.semaphore_signal(
            barrier, inc=1, device_id={EXPERT: other}, device_id_type=MESH_ID
        )
    )
    pl.semaphore_wait(barrier, 1 + reach)

    def core_start(piece):
        for half in (1 - x, x):
            theirs_copy(half, piece).wait()
            core_copy(half, piece).start()

    for piece in range(2):
        core_start(piece)
    small_step(0)
    start(functools.partial(slot_loads, 0))
    start(functools.partial(tile_loads, 0))
    pltpu.make_async_copy(ends_back, ends_held, ends_load).wait()
    ends_store(False).start()
    for half in range(2):
        mine_copy(half).wait()

    steps = TAIL_PIECES * reach
    ahead = 3

    def place(i):
        return reach - 1 - i % reach, i // reach

    def launch(i):
        k, piece = place(i)
        add_core(1 - x, k, piece)
        summed.start(k, piece)

    def finish(piece, total):
        whole[core, z, piece] = total.astype(jnp.bfloat16)

    def late(i):
        def due(offset, act):
            since = i - offset
            if isinstance(i, int):
                if since >= 0 and since % reach == 0 and since // reach < TAIL_PIECES:
                    act(since // reach)
            else:

                @pl.when(jnp.logical_and(since >= 0, lax.rem(since, reach) == 0))
                def _():
                    act(since // reach)

        def own(piece):
            summed.finish(piece, finish)
            spread_block(z, piece, True, True)

        due(reach + 1, own)
        for distance in range(1, reach):
            due(reach + 1 + 2 * distance, functools.partial(relay, distance))

    for i in range(ahead):
        launch(i)
    for piece in range(2, TAIL_PIECES):
        core_start(piece)
    small_step(1)

    def step(i, carry):
        k, piece = place(i)

        @pl.when(jnp.logical_and(k > 0, piece * (reach - 1) + reach - 1 - k < count))
        def _():
            one_tile(piece * (reach - 1) + reach - 1 - k)

        @pl.when(i == reach)
        def _():
            small_step(2)

        summed.arrive(k, piece)

        @pl.when(i + ahead < steps)
        def _():
            launch(i + ahead)

        add_core(x, k, piece)

        @pl.when(k > 0)
        def _():
            summed.pass_on(k, piece)

        late(i)
        return carry

    lax.fori_loop(0, steps, step, 0)
    done = min(count, TAIL_PIECES * (reach - 1))
    ends_copy().start()
    small_step(3)
    for i in range(steps, steps + 3 * reach):
        late(i)
    tile_run(done, count)
    for index in range(count - 3, count):
        sum_tile(index)

    def settle_last(source, carry):
        for piece in range(TAIL_PIECES):
            last_copy(source, piece, 1 - core).wait_recv()
        for copy in out_copies(1 - core, source):
            copy.start()
        return carry

    lax.fori_loop(0, reach, settle_last, 0)
    ends_copy().wait_recv()
    ends_store(True).start()

    summed.drain()

    def settle_sends(source, carry):
        for piece in range(TAIL_PIECES):
            last_copy(source, piece, core).wait_send()

            @pl.when(jnp.logical_and(chain.has_above, z >= source))
            def _():
                ring_copy(source, piece, 0, chain.above).wait_send()

            @pl.when(jnp.logical_and(chain.has_below, z <= source))
            def _():
                ring_copy(source, piece, 1, chain.below).wait_send()

        for side in range(2):
            for copy in out_copies(side, source):
                copy.wait()
        return carry

    lax.fori_loop(0, reach, settle_sends, 0)
    for piece in range(TAIL_PIECES):
        for half in range(2):
            core_copy(half, piece).wait_send()
    ends_copy().wait_send()
    for other in (False, True):
        ends_store(other).wait()
    small_copy(partner, 0).wait_send()
    small_copy(chain.aside, 1).wait_send()
    others(lambda other: small_copy(other, 2).wait_send())
    def settle_tiles(index, carry):
        for copy in tile_sends(index):
            copy.wait_send()
        for copy in tile_stores(index):
            copy.wait()
        return carry

    lax.fori_loop(count - depth, count, settle_tiles, 0)


def tail_call(reach, widths, dense, x_rows, dh_two, gg_two, gu_two, hg_two, before, smalls, ends):
    halves, cores, _, _, quarter, columns = dense.shape
    groups, local, slot_rows, width = x_rows.shape
    hidden = gg_two[0].shape[3]
    tiles = width // hidden
    wide = width // tiles
    anywhere = pl.BlockSpec(memory_space=pl.ANY)
    vmem = pl.BlockSpec(memory_space=pltpu.VMEM)
    end = ends[0].shape
    up = jax.ShapeDtypeStruct((local, width, hidden), jnp.bfloat16)
    down = jax.ShapeDtypeStruct((local, hidden, width), jnp.bfloat16)
    block = (TAIL_PIECES, quarter, columns)
    dma = pltpu.SemaphoreType.DMA
    return pl.pallas_call(
        functools.partial(tail_kernel, reach, tiles),
        in_specs=[anywhere] * 13 + [vmem] * 3 + [anywhere] * 2,
        out_specs=[anywhere] * 7 + [vmem, anywhere],
        out_shape=[
            jax.ShapeDtypeStruct((cores * reach, TAIL_PIECES, quarter, one), jnp.bfloat16)
            for one in widths
        ]
        + [
            jax.ShapeDtypeStruct((reach, TAIL_PIECES, quarter, width), jnp.bfloat16),
            up,
            up,
            down,
            jax.ShapeDtypeStruct(smalls[0].shape, jnp.float32),
            jax.ShapeDtypeStruct((2,) + end, jnp.bfloat16),
        ],
        scratch_shapes=[
            pltpu.VMEM((halves, reach) + block, jnp.bfloat16),
            pltpu.VMEM((halves, reach) + block, jnp.bfloat16),
            pltpu.VMEM((halves, reach) + block, jnp.bfloat16),
            pltpu.VMEM((reach,) + block, jnp.bfloat16),
            pltpu.VMEM((reach + 1,) + block, jnp.bfloat16),
            pltpu.VMEM((cores, reach) + block, jnp.bfloat16),
            pltpu.VMEM((2, groups, slot_rows, wide), jnp.bfloat16),
            pltpu.VMEM((2, groups, slot_rows, wide), jnp.bfloat16),
            pltpu.VMEM((2, 3, groups, slot_rows, hidden), jnp.bfloat16),
            pltpu.VMEM((2, 3, wide, hidden), jnp.bfloat16),
        ]
        + [pltpu.VMEM((4, wide, hidden), jnp.bfloat16)] * 6
        + [pltpu.VMEM((count,) + smalls[0].shape, jnp.float32) for count in (2, 2, reach)]
        + [pltpu.VMEM(end, jnp.bfloat16)] * 2
        + [
            dma((halves,)),
            dma((halves, TAIL_PIECES)),
            dma((halves, TAIL_PIECES)),
            dma((halves, TAIL_PIECES)),
            dma((reach, TAIL_PIECES)),
            dma((reach, TAIL_PIECES)),
            dma((reach, TAIL_PIECES)),
            dma((reach + 1, TAIL_PIECES)),
            dma((2, reach, TAIL_PIECES)),
            dma((reach, TAIL_PIECES)),
            dma((reach, TAIL_PIECES)),
            dma((reach, TAIL_PIECES)),
            dma((cores, reach, 4)),
            dma((2, 2)),
            dma((2, 3)),
            dma((2, 3)),
            dma((4, 3)),
            dma((4, 3)),
            dma((4, 3)),
            pltpu.SemaphoreType.REGULAR,
            dma((2 + reach,)),
            dma((2 + reach,)),
            dma,
            dma((2,)),
            dma,
            dma,
        ],
        compiler_params=pltpu.CompilerParams(
            collective_id=7, has_side_effects=True, vmem_limit_bytes=62 * MIB
        ),
        cost_estimate=pl.CostEstimate(
            flops=60 * 10**9, bytes_accessed=120 * 10**6, transcendentals=0
        ),
        name="tail",
    )(dense, x_rows, *dh_two, *gg_two, *gu_two, *hg_two, *before, *smalls, *ends)


GROUP = (EXPERT, TENSOR)
ROWS = (DP, EXPERT)


def by_rows(
    boundary,
    segments,
    expert_ids,
    attn_gain,
    query_weight,
    key_weight,
    value_weight,
    out_weight,
    ffn_gain,
    router_weight,
    gate_weight,
    up_weight,
    down_weight,
):
    args = (
        boundary,
        segments,
        expert_ids,
        attn_gain,
        query_weight,
        key_weight,
        value_weight,
        out_weight,
        ffn_gain,
        router_weight,
        gate_weight,
        up_weight,
        down_weight,
    )
    share_rows = expert_ids.shape[2]
    local = gate_weight.shape[1]
    if (
        share_rows != LEN
        or lax.axis_size(TENSOR) != 2
        or lax.axis_size(SECTION) != 2
        or lax.axis_size(DP) != 2
        or query_weight.shape[2] % (4 * HD)
    ):
        return on_device(*args)
    section = lax.axis_index(SECTION)
    tensor = lax.axis_index(TENSOR)
    group_at = lax.axis_index(EXPERT) * lax.axis_size(TENSOR) + tensor
    micro_count = boundary.shape[1]
    reach = lax.axis_size(EXPERT)
    group = query_weight.shape[2] // key_weight.shape[2]
    own_rows = lax.dynamic_slice_in_dim(boundary[0], tensor * share_rows, share_rows, 1)
    own_seg = lax.dynamic_slice_in_dim(segments, tensor * share_rows, share_rows, 1)
    own_ids = jnp.swapaxes(expert_ids[0], 1, 2)
    gains = (attn_gain, ffn_gain)
    tables = pair_tables(LEN)

    wqkv_part = jnp.concatenate([query_weight[0], key_weight[0], value_weight[0]], axis=1)
    wo_part = out_weight[0]
    wqkv = wo = None
    router_local = jnp.roll(router_weight[0].T, -group_at * local, axis=0)
    wg, wu, wd = gate_weight[0], up_weight[0], down_weight[0]

    def pick(array, index):
        return lax.dynamic_index_in_dim(array, index, 0, keepdims=False)

    arrived = None
    kept = []
    wide = []
    outputs = []
    for tick in range(micro_count + 1):
        micro = jnp.clip(tick - section, 0, micro_count - 1)
        if tick == 0:
            layer_in = own_rows[0]
            h1, xn2 = attn_split(
                boundary[0, 0].reshape(2, share_rows, -1),
                segments[0].reshape(2, share_rows),
                gains,
                wqkv_part,
                wo_part,
                tables,
                group,
            )
        else:
            layer_in = arrived
            h1, xn1, qkv, att, xn2 = attn_forward(
                own_rows[tick] if tick < micro_count else arrived,
                arrived,
                pick(own_seg, micro),
                gains,
                wqkv,
                wo,
                tables,
                group,
                0 if tick == micro_count else -1,
            )
        h2, gates, slots, own_gates, picked, gate_pre, up_pre, *firsts = moe_forward_call(
            reach,
            tick,
            micro_count,
            xn2,
            h1,
            pick(own_ids, micro),
            router_local,
            wg,
            wu,
            wd,
            [
                boundary[0].reshape(micro_count, 2, PIECES, share_rows // PIECES, -1),
                wqkv_part,
                wo_part,
            ],
        )
        outputs.append(h2)
        arrived = shifted(h2, SECTION, 1)
        if tick == 0:
            tops, *before = firsts
            wqkv, wo = both_halves(wqkv_part, wo_part, h2, before)
            xn1, qkv, att = attn_again(own_rows[0], own_seg[0], attn_gain, wqkv, tables, group)
        kept.append((layer_in, h1, xn2, own_gates, qkv, slots, gates, xn1, att))
        wide.append((picked, gate_pre, up_pre))

    arrived = jnp.zeros(own_rows.shape[1:], jnp.bfloat16)
    backs = []
    slotted = []
    for tick in range(micro_count + 1):
        micro = jnp.clip(tick - (1 - section), 0, micro_count - 1)
        ticks = {0: (1, 1), 1: (0, 2), 2: (1, 1)}[tick]
        pairs = list(zip(*(kept[one] for one in ticks)))
        sides = [wide[one] for one in ticks]
        if tick == micro_count:
            pairs[0] = (own_rows[1], own_rows[1])
            pairs.insert(5, (arrived, arrived))
        elif tick == 0:
            pairs.insert(5, (own_rows[0], own_rows[0]))
        else:
            pairs.insert(5, (arrived, own_rows[1]))
        rows, grad_gates, picked, gg, gu, hg = moe_backward_call(
            reach,
            tick,
            micro_count,
            arrived,
            pairs[6],
            pairs[7],
            [side[1] for side in sides],
            [side[2] for side in sides],
            wg,
            wu,
            wd,
            tops,
            first_end if tick == micro_count else tops,
        )
        grad_in, mid, dqkv, small = attn_backward(
            pairs[:6],
            rows,
            grad_gates.reshape(EXPERTS, LEN),
            pick(own_seg, micro),
            gains,
            router_local,
            wqkv,
            wo,
            tables,
            group,
            {0: 0, micro_count: 1}.get(tick, -1),
        )
        arrived = shifted(grad_in, SECTION, -1)
        backs.append((grad_in, mid, dqkv, small))
        slotted.append((picked, gg, gu, hg))
        if tick == 1:
            before = middle_weights([side[0] for side in sides], picked, gg, gu, hg, grad_in)
            first_end = ends_exchange(grad_in, outputs[1], before[0])

    grads_in, mids, dqkvs, smalls = zip(*backs)
    dense = attn_weights([one[7] for one in kept], [one[8] for one in kept], mids, dqkvs)
    width = dense.shape[1]
    dense = dense.reshape(
        2, 2, reach, TAIL_PIECES, width // (2 * reach * TAIL_PIECES), dense.shape[2]
    )
    widths = [one.shape[2] for one in (query_weight, key_weight, value_weight)]
    ends = (grads_in[2], outputs[2])
    *dense, wg_sum, wu_sum, wd_sum, small, last_end = tail_call(
        reach, widths, dense, wide[1][0], *zip(slotted[0], slotted[2]), before, smalls, ends
    )
    return (
        jnp.stack([first_end, last_end]).reshape(1, micro_count, 2 * share_rows, -1),
        small[EXPERTS + 1][None],
        *[one.astype(jnp.float32).reshape(1, -1, one.shape[3]) for one in dense],
        small[EXPERTS][None],
        small[:EXPERTS].T[None],
        *[one.astype(jnp.float32)[None] for one in (wg_sum, wu_sum, wd_sum)],
    )


def solution(mesh):
    placed = (
        P(SECTION, None, (DP, EXPERT), None),
        P(None, (DP, EXPERT)),
        P(SECTION, None, (DP, EXPERT, TENSOR), None),
        P(SECTION, None),
        P(SECTION, None, TENSOR),
        P(SECTION, None, TENSOR),
        P(SECTION, None, TENSOR),
        P(SECTION, TENSOR, None),
        P(SECTION, None),
        P(SECTION, None, None),
        P(SECTION, (EXPERT, TENSOR), None, None),
        P(SECTION, (EXPERT, TENSOR), None, None),
        P(SECTION, (EXPERT, TENSOR), None, None),
    )
    return jax.shard_map(
        by_rows,
        mesh=mesh,
        in_specs=placed,
        out_specs=(
            P(SECTION, None, (DP, EXPERT), None),
            P(SECTION, None),
            P(SECTION, None, TENSOR),
            P(SECTION, None, TENSOR),
            P(SECTION, None, TENSOR),
            P(SECTION, TENSOR, None),
            P(SECTION, None),
            P(SECTION, None, None),
            P(SECTION, (EXPERT, TENSOR), None, None),
            P(SECTION, (EXPERT, TENSOR), None, None),
            P(SECTION, (EXPERT, TENSOR), None, None),
        ),
        check_vma=False,
    )
```
